128 devices in a mesh: expert: 8 (over y, core), frame: 16 (over z, x).
Axes of the slice: x: 4, y: 4, z: 4, core: 2. Of those that a mesh axis runs over, the one named last changes fastest.
Arguments:
- tokens: bfloat16 [4096, 4096], P('frame'), may hold values from -6 to 6
- routes: int32 [4096, 2], P('frame'), may hold values from 0 to 7, all different within a row; in each aligned block of 256 rows (0 to 255, 256 to 511, ...) at most 96 rows name the same one
- route_weight: float32 [4096, 2], P('frame'), may hold values from 0.2 to 1
- moe_gain: float32 [4096], replicated, may hold values from 0.1 to 1.9
- gate_weight: bfloat16 [8, 7168, 4096], P('expert', 'frame'), may hold values from -0.09375 to 0.09375
- up_weight: bfloat16 [8, 7168, 4096], P('expert', 'frame'), may hold values from -0.09375 to 0.09375
- down_weight: bfloat16 [8, 7168, 4096], P('expert', 'frame'), may hold values from -0.0625 to 0.0625
- ssd_gain: float32 [4096], replicated, may hold values from 0.1 to 1.9
- input_weight: bfloat16 [4096, 8192], P(None, 'expert'), may hold values from -0.09375 to 0.09375
- write_weight: bfloat16 [4096, 1024], P(None, 'expert'), may hold values from -0.0078125 to 0.0078125
- read_weight: bfloat16 [4096, 1024], P(None, 'expert'), may hold values from -0.0078125 to 0.0078125
- step_weight: bfloat16 [4096, 128], P(None, 'expert'), may hold values from -0.375 to 0.375
- step_bias: float32 [128], P('expert'), may hold values from -5 to -4.2
- decay_log: float32 [128], P('expert'), may hold values from -9.1 to 1.39
- skip_gain: float32 [128], P('expert'), may hold values from -3 to 3
Outputs:
- mixed: bfloat16 [4096, 4096], P('frame', 'expert')
- ssd_out: bfloat16 [4096, 8192], P('frame', 'expert')
The draws below stay inside these ranges and needn't reach their ends.
Inputs may be any that keep to these rules, and one draw needn't show every extreme that they name: `routes`: each token names two different experts. In each aligned block of 256 tokens no expert is named by more than 96 tokens, and in every draw some expert is named by exactly 96 tokens of some block.
All inputs are finite; a program needn't handle non-finite values.
Results may differ from the reference program's by a relative error of at most 0.034.
Values may be sent and summed in bfloat16 or wider, within the bound.
No kernel may reach another device: no remote copies, remote signals or barrier semaphores. Data moves between devices by JAX's collectives and lax.ppermute only.
A program may use at most 128 MiB of HBM per device.

```python
import math
import jax
import jax.numpy as jnp
import numpy as np
from jax import lax

D = 4096
FF = 7168
EXPERTS = 8
TOK_DEV = 256
TOKENS = 4096
CAP = 96
HEADS = 128
HEAD_DIM = 64
STATE = 128
GROUPS = 8
SPAN = 128
N_FRAME = 16


def draw_decay_log(key, part):
    key = jax.random.fold_in(key, 11)
    pick_key, slow_key, fast_key = jax.random.split(key, 3)
    slow_share = 0.5
    slow = jax.random.uniform(pick_key, (HEADS,), jnp.float32) < slow_share
    slow_rate = jax.random.uniform(slow_key, (HEADS,), jnp.float32, math.log(2.0 / TOKENS), math.log(8.0 / TOKENS))
    fast_rate = jax.random.uniform(fast_key, (HEADS,), jnp.float32, 0.0, math.log(4.0))
    return jnp.where(slow, slow_rate, fast_rate).astype(jnp.float32)


def levels(key, shape, cuts, least, largest):
    factor_of = 1.0
    for position, shards_of in cuts:
        draws = jax.random.uniform(jax.random.fold_in(jax.random.fold_in(key, 6), position), (shards_of,), jnp.float32, least / len(cuts), largest / len(cuts))
        factor_of = factor_of * jnp.repeat(jnp.exp(draws), shape[position] // shards_of).reshape((-1,) + (1,) * (len(shape) - 1 - position))
    return factor_of


def routed_block(own_key, own, number, rows, number_of, top, bound, lean):
    order = jax.random.permutation(own_key, number_of)
    heavy_load, usual = load_shares(number_of, rows * top, bound, lean, True), load_shares(number_of, rows * top, bound, lean, False)
    places = jnp.arange(number_of)

    def named(lengths, offset_by):
        used = int((lengths > 0).sum())
        fixed = max(1, used // 4)
        shifted = fixed + (places - fixed + offset_by * (used - fixed)) % max(1, number_of - fixed)
        return jnp.zeros((number_of,), jnp.int32).at[order[jnp.where(places < fixed, places, shifted)]].set(jnp.asarray(lengths, jnp.int32))

    lengths = jnp.where(number % 4 == 0, named(heavy_load, number // 4), named(usual, number - number // 4 - 1))
    mixed = jax.random.permutation(jax.random.fold_in(own, 3), number_of)
    giver, taker = mixed[0:number_of // 2 * 2:2], mixed[1:number_of // 2 * 2:2]
    slack = jnp.minimum(lengths[giver] - 1, bound - lengths[taker]) // 2
    slack = jnp.where((giver == order[0]) | (taker == order[0]) | (lengths[taker] == 0), 0, jnp.maximum(slack, 0))
    shifted = jax.random.randint(jax.random.fold_in(own, 4), (number_of // 2,), 0, 1 << 20) % (slack + 1)
    lengths = lengths.at[giver].add(-shifted).at[taker].add(shifted)
    items = jnp.searchsorted(jnp.cumsum(lengths), jnp.arange(rows * top), side="right").astype(jnp.int32)
    grid = items.reshape(top, rows).T
    grid = grid[jax.random.permutation(jax.random.fold_in(own, 1), rows)]
    offset_by = jax.random.randint(jax.random.fold_in(own, 2), (rows, 1), 0, top)
    return jnp.take_along_axis(grid, (jnp.arange(top)[None, :] + offset_by) % top, axis=1)


def load_shares(number_of, total, bound, skew, full):
    portions = [(1 << 20) // math.isqrt(standing ** skew) + 1 for standing in range(1, number_of + 1)]
    largest = bound if full else min(bound, max(-(-total // number_of), total * portions[0] // sum(portions)))
    least = 1 if total - largest >= number_of - 1 else 0
    holding, surplus = [largest] + [least] * (number_of - 1), total - largest - least * (number_of - 1)
    while surplus > 0:
        movable = [i for i in range(1, number_of) if holding[i] < largest] or [i for i in range(1, number_of) if holding[i] < bound]
        pool, remaining = sum([portions[i] for i in movable]), surplus
        for i in movable:
            extra = min(bound - holding[i], max(1, remaining * portions[i] // pool), surplus)
            holding[i] = holding[i] + extra
            surplus = surplus - extra
    return np.array(holding)


def bell_draw(key, dims, deviation, limit, cuts=(), kind=jnp.bfloat16):
    array = jax.random.normal(key, dims, jnp.float32) * deviation
    if len(cuts) > 0:
        array = levels(key, dims, cuts, -0.22, 0.18) * array
    return jnp.clip(array, min=-limit, max=limit).astype(kind)


def setup_inputs(seed: int = 0) -> dict:
    key_of = jax.random.split(jax.random.key(seed), 16)
    tokens = bell_draw(key_of[0], (TOKENS, D), 1.0, 6.0, ((0, 16),))
    routes_keys = jax.random.split(jax.random.fold_in(key_of[1], 1), TOKENS // TOK_DEV)
    routes_turns = jax.random.permutation(jax.random.fold_in(key_of[1], 3), TOKENS // TOK_DEV)
    routes = jax.vmap(lambda own, number: routed_block(jax.random.fold_in(key_of[1], 2), own, number, TOK_DEV, EXPERTS, 2, CAP, 2))(routes_keys, routes_turns).reshape((TOKENS, 2))
    route_weight = jnp.clip(0.2 + 0.8 * jax.random.uniform(key_of[2], (TOKENS, 2), jnp.float32) ** levels(key_of[2], (TOKENS, 2), ((0, 16),), -0.2, 0.2), 0.2, 1.0)
    moe_gain = jnp.clip(1.0 + 0.18 * jax.random.normal(key_of[3], (D,), jnp.float32), 0.1, 1.9)
    gate_weight = bell_draw(key_of[4], (EXPERTS, FF, D), D ** -0.5, 0.09375, ((0, 8), (1, 16)))
    up_weight = bell_draw(key_of[5], (EXPERTS, FF, D), D ** -0.5, 0.09375, ((0, 8), (1, 16)))
    down_weight = bell_draw(key_of[6], (EXPERTS, FF, D), FF ** -0.5, 0.0625, ((0, 8), (1, 16)))
    ssd_gain = jnp.clip(1.0 + 0.18 * jax.random.normal(key_of[7], (D,), jnp.float32), 0.1, 1.9)
    input_weight = bell_draw(key_of[8], (D, HEADS * HEAD_DIM), D ** -0.5, 0.09375, ((1, 8),))
    write_weight = bell_draw(key_of[9], (D, GROUPS * STATE), (D * STATE) ** -0.5, 0.0078125, ((1, 8),))
    read_weight = bell_draw(key_of[10], (D, GROUPS * STATE), (D * STATE) ** -0.5, 0.0078125, ((1, 8),))
    step_weight = bell_draw(key_of[11], (D, HEADS), (D // 16) ** -0.5, 0.375, ((1, 8),))
    step_bias = jnp.clip(-5.0 + 0.8000002 * jax.random.uniform(key_of[12], (HEADS,), jnp.float32) ** levels(key_of[12], (HEADS,), ((0, 8),), -0.2, 0.2), -5.0, -4.2)
    decay_log = draw_decay_log(jax.random.fold_in(key_of[15], 71), 0)
    skip_gain = jnp.clip(jax.random.uniform(key_of[14], (HEADS,), jnp.float32, -3.0, 3.0) * levels(key_of[14], (HEADS,), ((0, 8),), -0.4, 0.0), -3.0, 3.0)
    return dict(tokens=tokens, routes=routes, route_weight=route_weight, moe_gain=moe_gain, gate_weight=gate_weight, up_weight=up_weight, down_weight=down_weight, ssd_gain=ssd_gain, input_weight=input_weight, write_weight=write_weight, read_weight=read_weight, step_weight=step_weight, step_bias=step_bias, decay_log=decay_log, skip_gain=skip_gain)


EPSILON = 1e-06
PRECISE = lax.Precision.HIGHEST

def rms_scale(values, gain):
    mean_sq = lax.optimization_barrier(jnp.mean(values * values, axis=-1, keepdims=True))
    return values * lax.rsqrt(mean_sq + EPSILON) * gain

def expert_rows(routes, route_weight, expert):
    hits = routes == expert
    chosen = jnp.any(hits, axis=1)
    weights = lax.optimization_barrier(jnp.sum(jnp.where(hits, route_weight, 0.0), axis=1))
    shard_mask = chosen.reshape(N_FRAME, TOK_DEV).astype(jnp.int32)
    slot_index = (jnp.cumsum(shard_mask, axis=1) - 1).astype(jnp.int32)
    frame_ids = jnp.arange(N_FRAME, dtype=jnp.int32)[:, None]
    target = jnp.where(shard_mask > 0, frame_ids * CAP + slot_index, N_FRAME * CAP).astype(jnp.int32)
    token_ids = jnp.arange(TOKENS, dtype=jnp.int32)
    index = jnp.zeros((N_FRAME * CAP + 1,), jnp.int32).at[target.reshape(-1)].set(token_ids)
    used = jnp.zeros((N_FRAME * CAP + 1,), jnp.float32).at[target.reshape(-1)].set(1.0)
    return (index[:-1], used[:-1], weights)

def expert_output(normed, gate_w, up_w, down_w, index):
    rows = normed[index]
    gate = jnp.dot(rows, gate_w.T, preferred_element_type=jnp.float32)
    upper = jnp.dot(rows, up_w.T, preferred_element_type=jnp.float32)
    hidden = (jax.nn.silu(gate) * upper).astype(jnp.bfloat16)
    block_units = FF // N_FRAME
    hidden_blocks = jnp.moveaxis(hidden.reshape(rows.shape[0], N_FRAME, block_units), 1, 0)
    down_blocks = down_w.reshape(N_FRAME, block_units, D)

    def one_block(totals, pair):
        hidden_part, down_part = pair
        partial_sum = jnp.dot(hidden_part, down_part, preferred_element_type=jnp.float32).astype(jnp.bfloat16)
        partial_sum = lax.optimization_barrier(partial_sum)
        return (totals + partial_sum.astype(jnp.float32), None)
    totals, _ = lax.scan(one_block, jnp.zeros((rows.shape[0], D), jnp.float32), (hidden_blocks, down_blocks))
    return totals

def span_terms(span_x, span_b, span_c, span_dt, span_decay):
    cumulative = jnp.cumsum(span_decay, axis=0)
    length = span_x.shape[0]
    gaps = cumulative[:, None, :] - cumulative[None, :, :]
    causal = jnp.arange(length)[:, None] >= jnp.arange(length)[None, :]
    decays = jnp.exp(jnp.where(causal[:, :, None], gaps, -jnp.inf))
    scores = jnp.einsum('ihn,jhn->ijh', span_c, span_b, precision=PRECISE)
    mixing = scores * decays * span_dt[None, :, :]
    inside = jnp.einsum('ijh,jhp->ihp', mixing, span_x, precision=PRECISE)
    to_end = jnp.exp(cumulative[-1][None, :] - cumulative) * span_dt
    states = jnp.einsum('jh,jhn,jhp->hnp', to_end, span_b, span_x, precision=PRECISE)
    return (cumulative, inside, states)

def reference(tokens, routes, route_weight, moe_gain, gate_weight, up_weight, down_weight, ssd_gain, input_weight, write_weight, read_weight, step_weight, step_bias, decay_log, skip_gain):
    normed = rms_scale(tokens.astype(jnp.float32), moe_gain).astype(jnp.bfloat16)

    def per_expert(totals, stacked):
        gate_w, up_w, down_w, expert = stacked
        index, used, weights = expert_rows(routes, route_weight, expert)
        outputs = expert_output(normed, gate_w, up_w, down_w, index)
        slot_weight = weights[index] * used
        return (totals.at[index].add(slot_weight[:, None] * outputs), None)
    experts_out, _ = lax.scan(per_expert, jnp.zeros((TOKENS, D), jnp.float32), (gate_weight, up_weight, down_weight, jnp.arange(EXPERTS, dtype=jnp.int32)))
    mixed = (tokens.astype(jnp.float32) + experts_out).astype(jnp.bfloat16)
    ssd_in = rms_scale(mixed.astype(jnp.float32), ssd_gain).astype(jnp.bfloat16)
    inputs = jnp.dot(ssd_in, input_weight, preferred_element_type=jnp.float32).astype(jnp.bfloat16)
    writes = jnp.dot(ssd_in, write_weight, preferred_element_type=jnp.float32).astype(jnp.bfloat16)
    reads = jnp.dot(ssd_in, read_weight, preferred_element_type=jnp.float32).astype(jnp.bfloat16)
    step_size = jax.nn.softplus(jnp.dot(ssd_in, step_weight, preferred_element_type=jnp.float32) + step_bias)
    log_decay = -step_size * jnp.exp(decay_log)
    blocks = TOKENS // SPAN
    per_group = HEADS // GROUPS
    span_x = inputs.astype(jnp.float32).reshape(blocks, SPAN, HEADS, HEAD_DIM)
    span_b = writes.astype(jnp.float32).reshape(blocks, SPAN, GROUPS, STATE)
    span_c = reads.astype(jnp.float32).reshape(blocks, SPAN, GROUPS, STATE)
    span_dt = step_size.reshape(blocks, SPAN, HEADS)
    span_decay = log_decay.reshape(blocks, SPAN, HEADS)

    def advance(carried, pieces):
        block_x, block_b, block_c, block_dt, block_decay = pieces
        wide_b = jnp.repeat(block_b, per_group, axis=1)
        wide_c = jnp.repeat(block_c, per_group, axis=1)
        cumulative, inside, states = span_terms(block_x, wide_b, wide_c, block_dt, block_decay)
        from_prior = jnp.exp(cumulative)[:, :, None] * jnp.einsum('ihn,hnp->ihp', wide_c, carried, precision=PRECISE)
        result = inside + from_prior + skip_gain[None, :, None] * block_x
        carried = jnp.exp(cumulative[-1])[:, None, None] * carried + states
        return (carried, result.astype(jnp.bfloat16))
    start_state = jnp.zeros((HEADS, STATE, HEAD_DIM), jnp.float32)
    _, outputs = lax.scan(advance, start_state, (span_x, span_b, span_c, span_dt, span_decay))
    ssd_out = outputs.reshape(TOKENS, HEADS * HEAD_DIM)
    return (mixed, ssd_out)
```

```python
import functools

import jax
import jax.numpy as jnp
from jax import lax
from jax.experimental import pallas as pl
from jax.experimental.pallas import tpu as pltpu
from jax.sharding import PartitionSpec as P

HEAD_DIM = 64
STATE = 128
SLOTS = 96
SIDE = 4
EPSILON = 1e-06
PRECISE = lax.Precision.HIGHEST
AXES = ("expert", "frame")
VMEM_BYTES = 48 * 1024 * 1024
F32, BF16 = jnp.float32, jnp.bfloat16


def routes_of(rule):
    pairs = []
    for y in range(SIDE):
        for core in range(2):
            for z in range(SIDE):
                for x in range(SIDE):
                    ny, nc, nz, nx = rule(y, core, z, x)
                    source = (y * 2 + core) * 16 + z * SIDE + x
                    target = ((ny % SIDE) * 2 + nc % 2) * 16 + (nz % SIDE) * SIDE + nx % SIDE
                    pairs.append((source, target))
    return pairs


def send(array, rule):
    return lax.ppermute(array, AXES, routes_of(rule))


def along_first(array, by):
    return send(array, lambda y, c, z, x: (y, c, z + by * c, x + by * (1 - c)))


def along_second(array, by):
    return send(array, lambda y, c, z, x: (y, c, z + by * (1 - c), x + by * c))


def along_x(array, by):
    return send(array, lambda y, c, z, x: (y, c, z, x + by))


def along_z(array, by):
    return send(array, lambda y, c, z, x: (y, c, z + by, x))


def along_y(array, by):
    return send(array, lambda y, c, z, x: (y + by, c, z, x))


def to_sibling(array):
    return send(array, lambda y, c, z, x: (y, 1 - c, z, x))


def shape(dims, kind):
    return jax.ShapeDtypeStruct(dims, kind)


def params():
    return pltpu.CompilerParams(vmem_limit_bytes=VMEM_BYTES)


def pick_kernel(where_ref, tokens_ref, routes_ref, weight_ref, gain_ref, rows_ref, onehot_ref, slot_weight_ref):
    count = tokens_ref.shape[0]
    hits = routes_ref[...] == where_ref[0]
    chosen = jnp.max(hits.astype(F32), axis=1, keepdims=True)
    weights = jnp.sum(jnp.where(hits, weight_ref[...], 0.0), axis=1, keepdims=True)
    lower = lax.broadcasted_iota(jnp.int32, (count, count), 0) >= lax.broadcasted_iota(jnp.int32, (count, count), 1)
    wide = jnp.broadcast_to(chosen, (count, SLOTS))
    place = jnp.dot(lower.astype(BF16), wide.astype(BF16), preferred_element_type=F32) - 1.0
    slot = lax.broadcasted_iota(jnp.int32, (count, SLOTS), 1)
    onehot = jnp.where((place.astype(jnp.int32) == slot) & (wide > 0.0), 1.0, 0.0).astype(BF16)
    onehot_ref[...] = onehot
    slot_weight_ref[...] = jnp.broadcast_to(weights, slot_weight_ref.shape)
    picked = lax.dot_general(onehot, tokens_ref[...], (((0,), (0,)), ((), ())), preferred_element_type=F32)
    mean_sq = jnp.mean(picked * picked, axis=1, keepdims=True)
    rows_ref[...] = (picked * lax.rsqrt(mean_sq + EPSILON) * gain_ref[...]).astype(BF16)


def pick(where, tokens, routes, route_weight, gain):
    count, width = tokens.shape
    smem, vmem = pl.BlockSpec(memory_space=pltpu.SMEM), pl.BlockSpec(memory_space=pltpu.VMEM)
    return pl.pallas_call(
        pick_kernel,
        out_shape=(shape((SLOTS, width), BF16), shape((count, SLOTS), BF16), shape((count, 128), F32)),
        in_specs=[smem, vmem, vmem, vmem, vmem],
        out_specs=(vmem, vmem, vmem),
        compiler_params=params(),
        name="pick",
    )(where, tokens, routes, route_weight, gain.reshape(1, width))


def expert_hidden(rows, gate_w, up_w):
    gate = jnp.einsum("rd,fd->rf", rows, gate_w, preferred_element_type=F32)
    upper = jnp.einsum("rd,fd->rf", rows, up_w, preferred_element_type=F32)
    return (jax.nn.silu(gate) * upper).astype(BF16)


def expert_out(rows, gate_w, up_w, down_w):
    return jnp.dot(expert_hidden(rows, gate_w, up_w), down_w, preferred_element_type=F32).astype(BF16)


def plus(a, b):
    return (a.astype(F32) + b.astype(F32)).astype(BF16)


def experts(rows, gate_w, up_w, down_w):
    half = 2 * SLOTS
    near = jnp.concatenate([rows, along_first(rows, 1), along_first(rows, -1), along_first(rows, 2)], axis=0)
    before = along_second(near, 1)
    after = along_second(near, -1)
    far_top = along_second(before[:half], 1)
    far_bottom = along_second(after[half:], -1)
    out_near = expert_out(near, gate_w, up_w, down_w)
    out_before = expert_out(before, gate_w, up_w, down_w)
    out_after = expert_out(after, gate_w, up_w, down_w)
    far = jnp.concatenate([far_top, far_bottom], axis=0)
    out_far = expert_out(far, gate_w, up_w, down_w)
    relay_down = along_second(out_far[:half], 1)
    relay_up = along_second(out_far[half:], -1)
    to_after = jnp.concatenate([plus(out_after[:half], relay_down), out_after[half:]], axis=0)
    to_before = jnp.concatenate([out_before[:half], plus(out_before[half:], relay_up)], axis=0)
    from_before = along_second(to_after, 1)
    from_after = along_second(to_before, -1)
    total = (out_near.astype(F32) + from_before.astype(F32) + from_after.astype(F32)).astype(BF16)
    own, down, up, across = [total[k * SLOTS : (k + 1) * SLOTS] for k in range(4)]
    return own, along_first(down, -1), along_first(up, 1), along_first(across, 2)


def place_kernel(where_ref, a_ref, b_ref, c_ref, d_ref, onehot_ref, weight_ref, keep_ref, give_ref):
    rows = (a_ref[...].astype(F32) + b_ref[...].astype(F32)) + (c_ref[...].astype(F32) + d_ref[...].astype(F32))
    placed = jnp.dot(onehot_ref[...], rows.astype(BF16), preferred_element_type=F32)
    weighted = (placed * weight_ref[:, :1]).astype(BF16)

    @pl.when(pl.program_id(1) == 0)
    def _():
        keep_ref[0] = weighted

    @pl.when(pl.program_id(1) == 1)
    def _():
        give_ref[0] = weighted


def place(where, terms, onehot, slot_weight, width):
    count = onehot.shape[0]
    cols = width // 8
    term = pl.BlockSpec((SLOTS, cols), lambda k, p, where: (0, 2 * k + (p + where[1]) % 2))
    block = pl.BlockSpec((1, count, cols), lambda k, p, where: (k, 0, 0))
    return pl.pallas_call(
        place_kernel,
        out_shape=(shape((SIDE, count, cols), BF16),) * 2,
        grid_spec=pltpu.PrefetchScalarGridSpec(
            num_scalar_prefetch=1,
            grid=(SIDE, 2),
            in_specs=[term] * 4
            + [
                pl.BlockSpec(onehot.shape, lambda k, p, where: (0, 0)),
                pl.BlockSpec(slot_weight.shape, lambda k, p, where: (0, 0)),
            ],
            out_specs=(block, block),
        ),
        compiler_params=params(),
        name="place",
    )(where, *terms, onehot, slot_weight)


def pair_kernel(where_ref, keep_ref, got_ref, own_ref, next_ref, last_ref, across_ref):
    for by, out in ((0, own_ref), (1, next_ref), (3, last_ref), (2, across_ref)):
        k = (where_ref[2] + by) % SIDE
        out[...] = (keep_ref[k].astype(F32) + got_ref[k].astype(F32)).astype(out.dtype)


def pair(where, keep, got):
    _, count, cols = keep.shape
    vmem = pl.BlockSpec(memory_space=pltpu.VMEM)
    return pl.pallas_call(
        pair_kernel,
        out_shape=(shape((count, cols), F32),) + (shape((count, cols), BF16),) * 3,
        in_specs=[pl.BlockSpec(memory_space=pltpu.SMEM), vmem, vmem],
        out_specs=(vmem,) * 4,
        compiler_params=params(),
        name="pair",
    )(where, keep, got)


def residual_kernel(where_ref, tokens_ref, own_ref, a_ref, b_ref, c_ref, mixed_ref):
    summed = (own_ref[...] + a_ref[...].astype(F32)) + (b_ref[...].astype(F32) + c_ref[...].astype(F32))
    mixed_ref[...] = (tokens_ref[...].astype(F32) + summed).astype(BF16)


def residual(where, tokens, own, others):
    count, cols = own.shape
    whole = pl.BlockSpec((count, cols), lambda i, where: (0, 0))
    return pl.pallas_call(
        residual_kernel,
        out_shape=shape((count, cols), BF16),
        grid_spec=pltpu.PrefetchScalarGridSpec(
            num_scalar_prefetch=1,
            grid=(1,),
            in_specs=[pl.BlockSpec((count, cols), lambda i, where: (0, where[0]))] + [whole] * 4,
            out_specs=whole,
        ),
        compiler_params=params(),
        name="residual",
    )(where, tokens, own, *others)


def spread(per_head, lanes):
    heads = per_head.shape[1]
    pairs = []
    first = lax.broadcasted_iota(jnp.int32, (per_head.shape[0], 2 * HEAD_DIM), 1) < HEAD_DIM
    for k in range(heads // 2):
        pairs.append(jnp.where(first, per_head[:, 2 * k : 2 * k + 1], per_head[:, 2 * k + 1 : 2 * k + 2]))
    return jnp.concatenate(pairs, axis=1)


def project_kernel(
    where_ref, mine_ref, other_ref, gain_ref, in_w_ref, write_w_ref, read_w_ref, step_w_ref, bias_ref, decay_ref,
    x_ref, write_ref, read_ref, step_ref, cum_ref, state_ref,
    in_acc, write_acc, read_acc, step_acc, square_acc,
):
    at = pl.program_id(0)

    @pl.when(at == 0)
    def _():
        for acc in (in_acc, write_acc, read_acc, step_acc, square_acc):
            acc[...] = jnp.zeros_like(acc)

    def add(block):
        values = block.astype(F32)
        square_acc[...] += jnp.sum(values * values, axis=1, keepdims=True)
        scaled = (values * gain_ref[...]).astype(BF16)
        for acc, weight in (
            (in_acc, in_w_ref), (write_acc, write_w_ref), (read_acc, read_w_ref), (step_acc, step_w_ref)
        ):
            acc[...] += jnp.dot(scaled, weight[...], preferred_element_type=F32)

    @pl.when(at < SIDE)
    def _():
        add(mine_ref[0])

    @pl.when(at >= SIDE)
    def _():
        add(other_ref[0])

    @pl.when(at == 2 * SIDE - 1)
    def _():
        count, heads = step_acc.shape
        scale = lax.rsqrt(square_acc[:, :1] / gain_ref.shape[1] / (2 * SIDE) + EPSILON)
        x = (in_acc[...] * scale).astype(BF16)
        x_ref[...] = x
        write = (write_acc[...] * scale).astype(BF16)
        write_ref[...] = write
        read_ref[...] = (read_acc[...] * scale).astype(BF16)
        raw = step_acc[...] * scale + bias_ref[...]
        step = jnp.maximum(raw, 0.0) + jnp.log1p(jnp.exp(-jnp.abs(raw)))
        step_ref[...] = step
        log_decay = -step * jnp.exp(decay_ref[...])
        lower = lax.broadcasted_iota(jnp.int32, (count, count), 0) >= lax.broadcasted_iota(jnp.int32, (count, count), 1)
        cum = jnp.dot(lower.astype(F32), log_decay, preferred_element_type=F32, precision=PRECISE)
        cum_ref[...] = cum
        last = cum[count - 1 :, :]
        to_end = jnp.exp(last - cum) * step
        weighted = (x.astype(F32) * spread(to_end, x.shape[1])).astype(BF16)
        state = lax.dot_general(write, weighted, (((0,), (0,)), ((), ())), preferred_element_type=F32)
        state_ref[:STATE, :] = state.astype(BF16)
        total = spread(last, x.shape[1])
        high = total.astype(BF16).astype(F32)
        row = lax.broadcasted_iota(jnp.int32, (16, x.shape[1]), 0)
        state_ref[STATE:, :] = jnp.where(row == 0, high, jnp.where(row == 1, total - high, 0.0)).astype(BF16)


def project(order, mine, other, gain, in_w, write_w, read_w, step_w, bias, decay_log):
    _, count, cols = mine.shape
    lanes, heads = in_w.shape[1], step_w.shape[1]
    by_rows = lambda w: pl.BlockSpec((cols, w.shape[1]), lambda i, order: (order[i], 0))
    fixed = lambda dims: pl.BlockSpec(dims, lambda i, order: (0,) * len(dims))
    outs = (
        shape((count, lanes), BF16), shape((count, STATE), BF16), shape((count, STATE), BF16),
        shape((count, heads), F32), shape((count, heads), F32), shape((STATE + 16, lanes), BF16),
    )
    return pl.pallas_call(
        project_kernel,
        out_shape=outs,
        grid_spec=pltpu.PrefetchScalarGridSpec(
            num_scalar_prefetch=1,
            grid=(2 * SIDE,),
            in_specs=[
                pl.BlockSpec((1, count, cols), lambda i, order: (jnp.minimum(i, SIDE - 1), 0, 0)),
                pl.BlockSpec((1, count, cols), lambda i, order: (jnp.maximum(i - SIDE, 0), 0, 0)),
                pl.BlockSpec((1, cols), lambda i, order: (0, order[i])),
                by_rows(in_w), by_rows(write_w), by_rows(read_w), by_rows(step_w),
                fixed((1, heads)), fixed((1, heads)),
            ],
            out_specs=tuple(fixed(o.shape) for o in outs),
            scratch_shapes=[
                pltpu.VMEM((count, lanes), F32), pltpu.VMEM((count, STATE), F32), pltpu.VMEM((count, STATE), F32),
                pltpu.VMEM((count, heads), F32), pltpu.VMEM((count, 128), F32),
            ],
        ),
        compiler_params=params(),
        name="project",
    )(
        order, mine, other, gain.reshape(1, -1), in_w, write_w, read_w, step_w,
        bias.reshape(1, -1), decay_log.reshape(1, -1),
    )


def inside_kernel(x_ref, write_ref, read_ref, step_ref, cum_ref, skip_ref, out_ref):
    count, heads = step_ref.shape
    span = count // 2
    scores = lax.dot_general(read_ref[...], write_ref[...], (((1,), (1,)), ((), ())), preferred_element_type=F32)
    cum = cum_ref[...]
    cum_t, step_t = cum.T, step_ref[...].T
    causal = lax.broadcasted_iota(jnp.int32, (span, span), 0) >= lax.broadcasted_iota(jnp.int32, (span, span), 1)
    low, high = slice(0, span), slice(span, count)

    def mixing(h, rows, columns):
        gaps = cum[rows, h : h + 1] - cum_t[h : h + 1, columns]
        if rows == columns:
            gaps = jnp.where(causal, gaps, -jnp.inf)
        return (scores[rows, columns] * jnp.exp(gaps) * step_t[h : h + 1, columns]).astype(BF16)

    for h in range(heads):
        lanes = slice(h * HEAD_DIM, (h + 1) * HEAD_DIM)
        x = x_ref[:, lanes]
        skipped = skip_ref[0, h] * x.astype(F32)
        top = jnp.dot(mixing(h, low, low), x[low], preferred_element_type=F32)
        below = jnp.concatenate([mixing(h, high, low), mixing(h, high, high)], axis=1)
        bottom = jnp.dot(below, x, preferred_element_type=F32)
        out_ref[:, lanes] = jnp.concatenate([top, bottom], axis=0) + skipped


def inside(x, write, read, step, cum, skip_gain):
    vmem = pl.BlockSpec(memory_space=pltpu.VMEM)
    return pl.pallas_call(
        inside_kernel,
        out_shape=shape(x.shape, F32),
        in_specs=[vmem] * 5 + [pl.BlockSpec(memory_space=pltpu.SMEM)],
        out_specs=vmem,
        compiler_params=params(),
        cost_estimate=pl.CostEstimate(flops=2 * 10**9, bytes_accessed=2 * 10**6, transcendentals=10**6),
        name="inside",
    )(x, write, read, step, cum, skip_gain.reshape(1, -1))


def log_of(ref):
    return ref[STATE : STATE + 1, :].astype(F32) + ref[STATE + 1 : STATE + 2, :].astype(F32)


def weights_before(here, places, logs):
    terms = []
    for s in places:
        between = sum(jnp.where((s < u) & (u < here), log, 0.0) for u, log in zip(places, logs))
        terms.append(jnp.where(s < here, jnp.exp(between), 0.0))
    return terms


def ring_kernel(where_ref, own_ref, last_ref, next_ref, across_ref, prior_ref, total_ref):
    here = where_ref[3]
    refs = (own_ref, last_ref, next_ref, across_ref)
    places = [here, (here + 3) % SIDE, (here + 1) % SIDE, (here + 2) % SIDE]
    logs = [log_of(ref) for ref in refs]
    before = weights_before(here, places, logs)
    until_end = [jnp.exp(sum(jnp.where(s < u, log, 0.0) for u, log in zip(places, logs))) for s in places]
    states = [ref[:STATE, :].astype(F32) for ref in refs]
    prior_ref[:STATE, :] = sum(w * s for w, s in zip(before, states))
    gone = sum(jnp.where(s < here, log, 0.0) for s, log in zip(places, logs))
    prior_ref[STATE:, :] = jnp.broadcast_to(jnp.exp(gone), (8, gone.shape[1]))
    total_ref[:STATE, :] = sum(w * s for w, s in zip(until_end, states)).astype(BF16)
    whole = sum(logs)
    top = whole.astype(BF16).astype(F32)
    row = lax.broadcasted_iota(jnp.int32, (16, whole.shape[1]), 0)
    total_ref[STATE:, :] = jnp.where(row == 0, top, jnp.where(row == 1, whole - top, 0.0)).astype(BF16)


def ring(where, parts):
    vmem = pl.BlockSpec(memory_space=pltpu.VMEM)
    lanes = parts[0].shape[1]
    return pl.pallas_call(
        ring_kernel,
        out_shape=(shape((STATE + 8, lanes), F32), shape((STATE + 16, lanes), BF16)),
        in_specs=[pl.BlockSpec(memory_space=pltpu.SMEM)] + [vmem] * 4,
        out_specs=(vmem, vmem),
        compiler_params=params(),
        name="ring",
    )(where, *parts)


def finish_kernel(where_ref, prior_ref, last_ref, next_ref, across_ref, read_ref, cum_ref, inside_ref, out_ref):
    here = where_ref[4]
    refs = (last_ref, next_ref, across_ref)
    places = [(here + 3) % SIDE, (here + 1) % SIDE, (here + 2) % SIDE]
    logs = [log_of(ref) for ref in refs]
    before = weights_before(here, places, logs)
    earlier = sum(w * ref[:STATE, :].astype(F32) for w, ref in zip(before, refs))
    carried = (prior_ref[:STATE, :] + prior_ref[STATE : STATE + 1, :] * earlier).astype(BF16)
    from_prior = jnp.dot(read_ref[...], carried, preferred_element_type=F32)
    decayed = spread(jnp.exp(cum_ref[...]), carried.shape[1])
    out_ref[...] = (inside_ref[...] + decayed * from_prior).astype(BF16)


def finish(where, prior, parts, read, cum, within):
    vmem = pl.BlockSpec(memory_space=pltpu.VMEM)
    return pl.pallas_call(
        finish_kernel,
        out_shape=shape(within.shape, BF16),
        in_specs=[pl.BlockSpec(memory_space=pltpu.SMEM)] + [vmem] * 7,
        out_specs=vmem,
        compiler_params=params(),
        name="finish",
    )(where, prior, *parts, read, cum, within)


def body(
    tokens,
    routes,
    route_weight,
    moe_gain,
    gate_weight,
    up_weight,
    down_weight,
    ssd_gain,
    input_weight,
    write_weight,
    read_weight,
    step_weight,
    step_bias,
    decay_log,
    skip_gain,
):
    width = tokens.shape[1]
    expert, frame = lax.axis_index("expert"), lax.axis_index("frame")
    y, core, z, x = expert // 2, expert % 2, frame // SIDE, frame % SIDE
    where = jnp.stack([expert, core, y, x, z]).astype(jnp.int32)
    rows, onehot, slot_weight = pick(where, tokens, routes, route_weight, moe_gain)
    terms = experts(rows, gate_weight[0], up_weight[0], down_weight[0])
    keep, give = place(where, terms, onehot, slot_weight, width)
    own, to_next, to_last, to_across = pair(where, keep, to_sibling(give))
    others = (along_y(to_next, 1), along_y(to_last, -1), along_y(to_across, 2))
    mixed = residual(where, tokens, own, others)
    mine = jnp.stack([mixed, along_y(mixed, 1), along_y(mixed, -1), along_y(mixed, 2)])
    other = to_sibling(mine)
    around = jnp.stack([y, (y + 3) % SIDE, (y + 1) % SIDE, (y + 2) % SIDE])
    order = jnp.concatenate([2 * around + core, 2 * around + 1 - core]).astype(jnp.int32)
    inputs, write, read, step, cum, state = project(
        order, mine, other, ssd_gain, input_weight, write_weight, read_weight, step_weight, step_bias, decay_log
    )
    parts = (state, along_x(state, 1), along_x(state, -1), along_x(state, 2))
    prior, total = ring(where, parts)
    earlier = (along_z(total, 1), along_z(total, -1), along_z(total, 2))
    within = inside(inputs, write, read, step, cum, skip_gain)
    ssd_out = finish(where, prior, earlier, read, cum, within)
    return (mixed, ssd_out)


def solution(mesh):
    placed = (
        P("frame", None),
        P("frame", None),
        P("frame", None),
        P(),
        P("expert", "frame", None),
        P("expert", "frame", None),
        P("expert", "frame", None),
        P(),
        P(None, "expert"),
        P(None, "expert"),
        P(None, "expert"),
        P(None, "expert"),
        P("expert"),
        P("expert"),
        P("expert"),
    )
    return jax.shard_map(
        body,
        mesh=mesh,
        in_specs=placed,
        out_specs=(P("frame", "expert"), P("frame", "expert")),
        check_vma=False,
    )
```

```python
import functools

import jax
import jax.numpy as jnp
from jax import lax
from jax.experimental import pallas as pl
from jax.experimental.pallas import tpu as pltpu
from jax.sharding import PartitionSpec as P

HEAD_DIM = 64
STATE = 128
SLOTS = 96
SIDE = 4
EPSILON = 1e-06
PRECISE = lax.Precision.HIGHEST
AXES = ("expert", "frame")
VMEM_BYTES = 48 * 1024 * 1024
F32, BF16 = jnp.float32, jnp.bfloat16


def routes_of(rule):
    pairs = []
    for y in range(SIDE):
        for core in range(2):
            for z in range(SIDE):
                for x in range(SIDE):
                    ny, nc, nz, nx = rule(y, core, z, x)
                    source = (y * 2 + core) * 16 + z * SIDE + x
                    target = ((ny % SIDE) * 2 + nc % 2) * 16 + (nz % SIDE) * SIDE + nx % SIDE
                    pairs.append((source, target))
    return pairs


def send(array, rule):
    return lax.ppermute(array, AXES, routes_of(rule))


def along_first(array, by):
    return send(array, lambda y, c, z, x: (y, c, z + by * c, x + by * (1 - c)))


def along_second(array, by):
    return send(array, lambda y, c, z, x: (y, c, z + by * (1 - c), x + by * c))


def along_x(array, by):
    return send(array, lambda y, c, z, x: (y, c, z, x + by))


def along_z(array, by):
    return send(array, lambda y, c, z, x: (y, c, z + by, x))


def along_y(array, by):
    return send(array, lambda y, c, z, x: (y + by, c, z, x))


def to_sibling(array):
    return send(array, lambda y, c, z, x: (y, 1 - c, z, x))


def shape(dims, kind):
    return jax.ShapeDtypeStruct(dims, kind)


def params():
    return pltpu.CompilerParams(vmem_limit_bytes=VMEM_BYTES)


def pick_kernel(where_ref, tokens_ref, routes_ref, weight_ref, gain_ref, rows_ref, onehot_ref, slot_weight_ref):
    count = tokens_ref.shape[0]
    hits = routes_ref[...] == where_ref[0]
    chosen = jnp.max(hits.astype(F32), axis=0, keepdims=True)
    weights = jnp.sum(jnp.where(hits, weight_ref[...], 0.0), axis=0, keepdims=True)
    upper = lax.broadcasted_iota(jnp.int32, (count, count), 0) <= lax.broadcasted_iota(jnp.int32, (count, count), 1)
    wide = jnp.broadcast_to(chosen, (SLOTS, count))
    place = jnp.dot(wide.astype(BF16), upper.astype(BF16), preferred_element_type=F32) - 1.0
    slot = lax.broadcasted_iota(jnp.int32, (SLOTS, count), 0)
    named = (place.astype(jnp.int32) == slot) & (wide > 0.0)
    onehot = jnp.where(named, 1.0, 0.0).astype(BF16)
    onehot_ref[...] = onehot
    slot_weight = jnp.sum(jnp.where(named, weights, 0.0), axis=1, keepdims=True)
    slot_weight_ref[...] = jnp.broadcast_to(slot_weight, slot_weight_ref.shape)
    picked = jnp.dot(onehot, tokens_ref[...], preferred_element_type=F32)
    mean_sq = jnp.mean(picked * picked, axis=1, keepdims=True)
    rows_ref[...] = (picked * lax.rsqrt(mean_sq + EPSILON) * gain_ref[...]).astype(BF16)


def pick(where, tokens, routes, route_weight, gain):
    count, width = tokens.shape
    smem, vmem = pl.BlockSpec(memory_space=pltpu.SMEM), pl.BlockSpec(memory_space=pltpu.VMEM)
    return pl.pallas_call(
        pick_kernel,
        out_shape=(shape((SLOTS, width), BF16), shape((SLOTS, count), BF16), shape((SLOTS, 128), F32)),
        in_specs=[smem, vmem, vmem, vmem, vmem],
        out_specs=(vmem, vmem, vmem),
        compiler_params=params(),
        name="pick",
    )(where, tokens, routes.T, route_weight.T, gain.reshape(1, width))


def expert_kernel(top_ref, bottom_ref, gate_ref, up_ref, down_ref, out_top_ref, out_bottom_ref):
    half = top_ref.shape[0]
    rows = jnp.concatenate([top_ref[...], bottom_ref[...]], axis=0)
    by_row = (((1,), (1,)), ((), ()))
    gate = lax.dot_general(rows, gate_ref[...], by_row, preferred_element_type=F32)
    upper = lax.dot_general(rows, up_ref[...], by_row, preferred_element_type=F32)
    hidden = (gate / (1.0 + jnp.exp(-gate)) * upper).astype(BF16)
    out = jnp.dot(hidden, down_ref[...], preferred_element_type=F32).astype(BF16)
    out_top_ref[...] = out[:half]
    out_bottom_ref[...] = out[half:]


def expert(top, bottom, weights):
    vmem = pl.BlockSpec(memory_space=pltpu.VMEM)
    rows, width = top.shape
    units = weights[0].shape[0]
    return pl.pallas_call(
        expert_kernel,
        out_shape=(shape(top.shape, BF16),) * 2,
        in_specs=[vmem] * 5,
        out_specs=(vmem, vmem),
        compiler_params=params(),
        cost_estimate=pl.CostEstimate(
            flops=12 * rows * width * units, bytes_accessed=6 * units * width + 8 * rows * width, transcendentals=0
        ),
        name="expert",
    )(top, bottom, *weights)


def half_columns(c, block):
    return [slice(k * 512 + c * 256, k * 512 + c * 256 + 256) for k in range(block // 512)]


def relay_kernel(c, after_ref, down_ref, before_ref, up_ref, to_after_ref, to_before_ref):
    for k, lanes in enumerate(half_columns(c, after_ref.shape[1])):
        to = slice(k * 256, k * 256 + 256)
        to_after_ref[:, to] = (after_ref[:, lanes].astype(F32) + down_ref[:, lanes].astype(F32)).astype(BF16)
        to_before_ref[:, to] = (before_ref[:, lanes].astype(F32) + up_ref[:, lanes].astype(F32)).astype(BF16)


def relay(c, *arrays):
    rows, width = arrays[0].shape
    steps = 4
    full = pl.BlockSpec((rows, width // steps), lambda j: (0, j))
    part = pl.BlockSpec((rows, width // steps // 2), lambda j: (0, j))
    return pl.pallas_call(
        functools.partial(relay_kernel, c),
        out_shape=(shape((rows, width // 2), BF16),) * 2,
        grid=(steps,),
        in_specs=[full] * 4,
        out_specs=(part, part),
        compiler_params=params(),
        name="relay",
    )(*arrays)


def total_kernel(c, near_top, top_a, top_b, near_bottom, bottom_a, bottom_b, own, down, up, across):
    for k, lanes in enumerate(half_columns(c, near_top.shape[1])):
        at = slice(k * 256, k * 256 + 256)
        for near, a, b, first, second in (
            (near_top, top_a, top_b, own, down), (near_bottom, bottom_a, bottom_b, up, across)
        ):
            total = near[:, lanes].astype(F32) + a[:, lanes].astype(F32) + b[:, at].astype(F32)
            first[:, at] = total[:SLOTS].astype(BF16)
            second[:, at] = total[SLOTS:].astype(BF16)


def total(c, *arrays):
    rows, width = arrays[0].shape
    steps = 4
    full = pl.BlockSpec((rows, width // steps), lambda j: (0, j))
    part = pl.BlockSpec((rows, width // steps // 2), lambda j: (0, j))
    piece = pl.BlockSpec((SLOTS, width // steps // 2), lambda j: (0, j))
    return pl.pallas_call(
        functools.partial(total_kernel, c),
        out_shape=(shape((SLOTS, width // 2), BF16),) * 4,
        grid=(steps,),
        in_specs=[full, full, part, full, full, part],
        out_specs=(piece,) * 4,
        compiler_params=params(),
        name="total",
    )(*arrays)


def after(values, *earlier):
    return lax.optimization_barrier((values, earlier))[0]


def experts(rows, weights):
    near_top = jnp.concatenate([rows, along_first(rows, 1)], axis=0)
    near_bottom = jnp.concatenate([along_first(rows, -1), along_first(rows, 2)], axis=0)
    before_top = along_second(near_top, 1)
    after_bottom = along_second(near_bottom, -1)
    out_near_top, out_near_bottom = expert(near_top, near_bottom, weights)
    later_top, later_bottom = after((near_top, near_bottom), out_near_top)
    after_top = along_second(later_top, -1)
    before_bottom = along_second(later_bottom, 1)
    far_top = along_second(before_top, 1)
    far_bottom = along_second(after_bottom, -1)
    out_before_top, out_after_bottom = expert(before_top, after_bottom, weights)
    second = after((after_top, before_bottom), out_before_top)
    out_after_top, out_before_bottom = expert(*second, weights)
    far_top, far_bottom = after((far_top, far_bottom), out_after_top)
    first_back = after((out_before_top, out_after_bottom), far_top, far_bottom)
    top_a = along_second(first_back[0], -1)
    bottom_a = along_second(first_back[1], 1)
    out_far_top, out_far_bottom = after(expert(far_top, far_bottom, weights), top_a, bottom_a)
    relay_down = along_second(out_far_top, 1)
    relay_up = along_second(out_far_bottom, -1)
    terms, order = [], ()
    for c in range(2):
        arrays = after((out_after_top, relay_down, out_before_bottom, relay_up), *order)
        to_after, to_before = relay(c, *arrays)
        order = (to_after,)
        top_b = along_second(to_after, 1)
        bottom_b = along_second(to_before, -1)
        own, down, up, across = total(c, out_near_top, top_a, top_b, out_near_bottom, bottom_a, bottom_b)
        terms.append((own, along_first(down, -1), along_first(up, 1), along_first(across, 2)))
    return terms


def place_kernel(where_ref, a_ref, b_ref, c_ref, d_ref, onehot_ref, weight_ref, keep_ref, give_ref):
    rows = (a_ref[...].astype(F32) + b_ref[...].astype(F32)) + (c_ref[...].astype(F32) + d_ref[...].astype(F32))
    weighted = (rows * weight_ref[:, :1]).astype(BF16)
    placed = lax.dot_general(
        onehot_ref[...], weighted, (((0,), (0,)), ((), ())), preferred_element_type=F32
    ).astype(BF16)
    for core in range(2):

        @pl.when(where_ref[1] == core)
        def _():
            for k in range(SIDE):
                for out, e in ((keep_ref, 2 * k + core), (give_ref, 2 * k + 1 - core)):
                    out[k] = placed[:, e * 256 : (e + 1) * 256]


def place(where, terms, onehot, slot_weight):
    count = onehot.shape[1]
    vmem = pl.BlockSpec(memory_space=pltpu.VMEM)
    return pl.pallas_call(
        place_kernel,
        out_shape=(shape((SIDE, count, 256), BF16),) * 2,
        in_specs=[pl.BlockSpec(memory_space=pltpu.SMEM)] + [vmem] * 6,
        out_specs=(vmem, vmem),
        compiler_params=params(),
        name="place",
    )(where, *terms, onehot, slot_weight)


def pair_kernel(where_ref, keep_ref, got_ref, own_ref, next_ref, last_ref, across_ref):
    for by, out in ((0, own_ref), (1, next_ref), (3, last_ref), (2, across_ref)):
        k = (where_ref[2] + by) % SIDE
        out[...] = (keep_ref[k].astype(F32) + got_ref[k].astype(F32)).astype(out.dtype)


def pair(where, keep, got):
    _, count, cols = keep.shape
    vmem = pl.BlockSpec(memory_space=pltpu.VMEM)
    return pl.pallas_call(
        pair_kernel,
        out_shape=(shape((count, cols), F32),) + (shape((count, cols), BF16),) * 3,
        in_specs=[pl.BlockSpec(memory_space=pltpu.SMEM), vmem, vmem],
        out_specs=(vmem,) * 4,
        compiler_params=params(),
        name="pair",
    )(where, keep, got)


def residual_kernel(where_ref, tokens_ref, own_ref, a_ref, b_ref, c_ref, mixed_ref):
    summed = (own_ref[...] + a_ref[...].astype(F32)) + (b_ref[...].astype(F32) + c_ref[...].astype(F32))
    mixed_ref[...] = (tokens_ref[...].astype(F32) + summed).astype(BF16)


def residual(c, where, tokens, own, others):
    count, cols = own.shape
    whole = pl.BlockSpec((count, cols), lambda i, where: (0, 0))
    return pl.pallas_call(
        residual_kernel,
        out_shape=shape((count, cols), BF16),
        grid_spec=pltpu.PrefetchScalarGridSpec(
            num_scalar_prefetch=1,
            grid=(1,),
            in_specs=[pl.BlockSpec((count, cols), lambda i, where: (0, 2 * where[0] + c))] + [whole] * 4,
            out_specs=whole,
        ),
        compiler_params=params(),
        name="residual",
    )(where, tokens, own, *others)


def spread(per_head, lanes):
    heads = per_head.shape[1]
    pairs = []
    first = lax.broadcasted_iota(jnp.int32, (per_head.shape[0], 2 * HEAD_DIM), 1) < HEAD_DIM
    for k in range(heads // 2):
        pairs.append(jnp.where(first, per_head[:, 2 * k : 2 * k + 1], per_head[:, 2 * k + 1 : 2 * k + 2]))
    return jnp.concatenate(pairs, axis=1)


def project_kernel(
    c, where_ref, mine_ref, other_ref, gain_ref, in_w_ref, write_w_ref, read_w_ref, step_w_ref, *refs
):
    if c == 0:
        out_accs, accs = refs[:5], refs[5:]
    else:
        in_accs, (bias_ref, decay_ref) = refs[:5], refs[5:7]
        outs, accs, state_scr = refs[7:16], refs[16:21], refs[21]
    in_acc, write_acc, read_acc, step_acc, square_acc = accs
    at = pl.program_id(0)

    @pl.when(at == 0)
    def _():
        for k, acc in enumerate(accs):
            acc[...] = jnp.zeros_like(acc) if c == 0 else in_accs[k][...]

    away = (at + SIDE - where_ref[2]) % SIDE
    slot = jnp.where(away == 0, 0, jnp.where(away == 3, 1, away + 1))
    for ref, core in ((mine_ref, where_ref[1]), (other_ref, 1 - where_ref[1])):
        values = ref[slot].astype(F32)
        square_acc[...] += jnp.sum(values * values, axis=1, keepdims=True)
        scaled = (values * gain_ref[core, 0]).astype(BF16)
        for acc, weight in (
            (in_acc, in_w_ref), (write_acc, write_w_ref), (read_acc, read_w_ref), (step_acc, step_w_ref)
        ):
            acc[...] += jnp.dot(scaled, weight[core, 0], preferred_element_type=F32)

    @pl.when(at == SIDE - 1)
    def _():
        if c == 0:
            for acc, out in zip(accs, out_accs):
                out[...] = acc[...]
        else:
            projected(where_ref, bias_ref, decay_ref, outs, accs, state_scr, 8 * 512)


def projected(where_ref, bias_ref, decay_ref, outs, accs, state_scr, width):
    in_acc, write_acc, read_acc, step_acc, square_acc = accs
    x_ref, write_ref, read_ref, step_ref, cum_ref = outs[:5]
    count, heads = step_acc.shape
    scale = lax.rsqrt(square_acc[:, :1] / width + EPSILON)
    x = (in_acc[...] * scale).astype(BF16)
    x_ref[...] = x
    write = (write_acc[...] * scale).astype(BF16)
    write_ref[...] = write
    read_ref[...] = (read_acc[...] * scale).astype(BF16)
    raw = step_acc[...] * scale + bias_ref[...]
    step = jnp.maximum(raw, 0.0) + jnp.log1p(jnp.exp(-jnp.abs(raw)))
    step_ref[...] = step
    log_decay = -step * jnp.exp(decay_ref[...])
    lower = lax.broadcasted_iota(jnp.int32, (count, count), 0) >= lax.broadcasted_iota(jnp.int32, (count, count), 1)
    cum = jnp.dot(lower.astype(F32), log_decay, preferred_element_type=F32, precision=PRECISE)
    cum_ref[...] = cum
    last = cum[count - 1 :, :]
    to_end = jnp.exp(last - cum) * step
    weighted = (x.astype(F32) * spread(to_end, x.shape[1])).astype(BF16)
    state = lax.dot_general(write, weighted, (((0,), (0,)), ((), ())), preferred_element_type=F32)
    whole = spread(last, x.shape[1])
    high = whole.astype(BF16).astype(F32)
    row = lax.broadcasted_iota(jnp.int32, (16, x.shape[1]), 0)
    log_rows = jnp.where(row == 0, high, jnp.where(row == 1, whole - high, 0.0)).astype(BF16)
    cols = x.shape[1] // SIDE
    for q in range(SIDE):
        lanes = slice(q * cols, (q + 1) * cols)
        state_scr[q, :STATE, :] = state[:, lanes].astype(BF16)
        state_scr[q, STATE:, :] = log_rows[:, lanes]
    for by, out in zip((0, 1, 3, 2), outs[5:]):
        out[...] = state_scr[(where_ref[3] + by) % SIDE]


def project(c, where, mine, other, gain, weights, *more):
    _, count, cols = mine.shape
    lanes, heads = weights[0].shape[1], weights[3].shape[1]
    cut = lambda w: w.reshape(8, 2, cols, w.shape[1])
    by_rows = lambda w: pl.BlockSpec((2, 1, cols, w.shape[1]), lambda i, where: (i, c, 0, 0))
    fixed = lambda dims: pl.BlockSpec(dims, lambda i, where: (0,) * len(dims))
    accs = [(count, lanes), (count, STATE), (count, STATE), (count, heads), (count, 128)]
    scratch = [pltpu.VMEM(dims, F32) for dims in accs]
    if c == 0:
        outs = tuple(shape(dims, F32) for dims in accs)
    else:
        quarter = (STATE + 16, lanes // SIDE)
        outs = (
            shape((count, lanes), BF16), shape((count, STATE), BF16), shape((count, STATE), BF16),
            shape((count, heads), F32), shape((count, heads), F32),
        ) + (shape(quarter, BF16),) * 4
        scratch.append(pltpu.VMEM((SIDE,) + quarter, BF16))
    return pl.pallas_call(
        functools.partial(project_kernel, c),
        out_shape=outs,
        grid_spec=pltpu.PrefetchScalarGridSpec(
            num_scalar_prefetch=1,
            grid=(SIDE,),
            in_specs=[
                fixed(mine.shape), fixed(other.shape),
                pl.BlockSpec((2, 1, 1, cols), lambda i, where: (i, c, 0, 0)),
                *[by_rows(w) for w in weights],
                *[fixed(m.shape) for m in more],
            ],
            out_specs=tuple(fixed(o.shape) for o in outs),
            scratch_shapes=scratch,
        ),
        compiler_params=params(),
        name="project",
    )(where, mine, other, gain.reshape(8, 2, 1, cols), *[cut(w) for w in weights], *more)


def inside_kernel(x_ref, write_ref, read_ref, step_ref, cum_ref, skip_ref, out_ref):
    count, heads = step_ref.shape
    span = count // 2
    scores = lax.dot_general(read_ref[...], write_ref[...], (((1,), (1,)), ((), ())), preferred_element_type=F32)
    cum = cum_ref[...]
    cum_t, step_t = cum.T, step_ref[...].T
    causal = lax.broadcasted_iota(jnp.int32, (span, span), 0) >= lax.broadcasted_iota(jnp.int32, (span, span), 1)
    low, high = slice(0, span), slice(span, count)

    def mixing(h, rows, columns):
        gaps = cum[rows, h : h + 1] - cum_t[h : h + 1, columns]
        if rows == columns:
            gaps = jnp.where(causal, gaps, -jnp.inf)
        return (scores[rows, columns] * jnp.exp(gaps) * step_t[h : h + 1, columns]).astype(BF16)

    for h in range(heads):
        lanes = slice(h * HEAD_DIM, (h + 1) * HEAD_DIM)
        x = x_ref[:, lanes]
        skipped = skip_ref[0, h] * x.astype(F32)
        top = jnp.dot(mixing(h, low, low), x[low], preferred_element_type=F32)
        below = jnp.concatenate([mixing(h, high, low), mixing(h, high, high)], axis=1)
        bottom = jnp.dot(below, x, preferred_element_type=F32)
        out_ref[:, lanes] = jnp.concatenate([top, bottom], axis=0) + skipped


def inside(x, write, read, step, cum, skip_gain):
    vmem = pl.BlockSpec(memory_space=pltpu.VMEM)
    return pl.pallas_call(
        inside_kernel,
        out_shape=shape(x.shape, F32),
        in_specs=[vmem] * 5 + [pl.BlockSpec(memory_space=pltpu.SMEM)],
        out_specs=vmem,
        compiler_params=params(),
        cost_estimate=pl.CostEstimate(flops=2 * 10**9, bytes_accessed=2 * 10**6, transcendentals=10**6),
        name="inside",
    )(x, write, read, step, cum, skip_gain.reshape(1, -1))


def log_of(ref):
    return ref[STATE : STATE + 1, :].astype(F32) + ref[STATE + 1 : STATE + 2, :].astype(F32)


def weights_before(here, places, logs):
    terms = []
    for s in places:
        between = sum(jnp.where((s < u) & (u < here), log, 0.0) for u, log in zip(places, logs))
        terms.append(jnp.where(s < here, jnp.exp(between), 0.0))
    return terms


def row_total_kernel(where_ref, own_ref, last_ref, next_ref, across_ref, total_ref):
    here = where_ref[3]
    refs = (own_ref, last_ref, next_ref, across_ref)
    places = [here, (here + 3) % SIDE, (here + 1) % SIDE, (here + 2) % SIDE]
    logs = [log_of(ref) for ref in refs]
    until_end = [jnp.exp(sum(jnp.where(s < u, log, 0.0) for u, log in zip(places, logs))) for s in places]
    total_ref[:STATE, :] = sum(w * ref[:STATE, :].astype(F32) for w, ref in zip(until_end, refs)).astype(BF16)
    whole = sum(logs)
    top = whole.astype(BF16).astype(F32)
    row = lax.broadcasted_iota(jnp.int32, (16, whole.shape[1]), 0)
    total_ref[STATE:, :] = jnp.where(row == 0, top, jnp.where(row == 1, whole - top, 0.0)).astype(BF16)


def row_total(where, parts):
    vmem = pl.BlockSpec(memory_space=pltpu.VMEM)
    return pl.pallas_call(
        row_total_kernel,
        out_shape=shape(parts[0].shape, BF16),
        in_specs=[pl.BlockSpec(memory_space=pltpu.SMEM)] + [vmem] * 4,
        out_specs=vmem,
        compiler_params=params(),
        name="row_total",
    )(where, *parts)


def carry_kernel(where_ref, *refs):
    parts, earlier, outs = refs[:4], refs[4:7], refs[7:]
    here = where_ref[4]
    rows = [(here + 3) % SIDE, (here + 1) % SIDE, (here + 2) % SIDE]
    before = weights_before(here, rows, [log_of(ref) for ref in earlier])
    to_row = sum(w * ref[:STATE, :].astype(F32) for w, ref in zip(before, earlier))
    here = where_ref[3]
    places = [here, (here + 3) % SIDE, (here + 1) % SIDE, (here + 2) % SIDE]
    logs = [log_of(ref) for ref in parts]
    for by, out in zip((0, 1, 3, 2), outs):
        target = (here + by) % SIDE
        gone = sum(jnp.where(s < target, log, 0.0) for s, log in zip(places, logs))
        state = jnp.exp(gone) * to_row
        for w, ref in zip(weights_before(target, places, logs), parts):
            state += w * ref[:STATE, :].astype(F32)
        out[...] = state.astype(BF16)


def carry(where, parts, earlier):
    vmem = pl.BlockSpec(memory_space=pltpu.VMEM)
    return pl.pallas_call(
        carry_kernel,
        out_shape=(shape((STATE, parts[0].shape[1]), BF16),) * 4,
        in_specs=[pl.BlockSpec(memory_space=pltpu.SMEM)] + [vmem] * 7,
        out_specs=(vmem,) * 4,
        compiler_params=params(),
        name="carry",
    )(where, *parts, *earlier)


def finish_kernel(where_ref, own_ref, last_ref, next_ref, across_ref, read_ref, cum_ref, inside_ref, out_ref, scr):
    for by, ref in ((0, own_ref), (3, last_ref), (1, next_ref), (2, across_ref)):
        scr[(where_ref[3] + by) % SIDE] = ref[...]
    cols = own_ref.shape[1]
    decayed = spread(jnp.exp(cum_ref[...]), SIDE * cols)
    for q in range(SIDE):
        lanes = slice(q * cols, (q + 1) * cols)
        from_prior = jnp.dot(read_ref[...], scr[q], preferred_element_type=F32)
        out_ref[:, lanes] = (inside_ref[:, lanes] + decayed[:, lanes] * from_prior).astype(BF16)


def finish(where, parts, read, cum, within):
    vmem = pl.BlockSpec(memory_space=pltpu.VMEM)
    return pl.pallas_call(
        finish_kernel,
        out_shape=shape(within.shape, BF16),
        in_specs=[pl.BlockSpec(memory_space=pltpu.SMEM)] + [vmem] * 7,
        out_specs=vmem,
        scratch_shapes=[pltpu.VMEM((SIDE,) + parts[0].shape, BF16)],
        compiler_params=params(),
        name="finish",
    )(where, *parts, read, cum, within)


def body(
    tokens,
    routes,
    route_weight,
    moe_gain,
    gate_weight,
    up_weight,
    down_weight,
    ssd_gain,
    input_weight,
    write_weight,
    read_weight,
    step_weight,
    step_bias,
    decay_log,
    skip_gain,
):
    expert_at, frame = lax.axis_index("expert"), lax.axis_index("frame")
    y, core, z, x = expert_at // 2, expert_at % 2, frame // SIDE, frame % SIDE
    where = jnp.stack([expert_at, core, y, x, z]).astype(jnp.int32)
    rows, onehot, slot_weight = pick(where, tokens, routes, route_weight, moe_gain)
    halves = experts(rows, (gate_weight[0], up_weight[0], down_weight[0]))
    weights = (input_weight, write_weight, read_weight, step_weight)
    mixed, more = [], ()
    for c in range(2):
        keep, give = place(where, halves[c], onehot, slot_weight)
        own, to_next, to_last, to_across = pair(where, keep, to_sibling(give))
        others = (along_y(to_next, 1), along_y(to_last, -1), along_y(to_across, 2))
        half = residual(c, where, tokens, own, others)
        mixed.append(half)
        mine = jnp.stack([half, along_y(half, 1), along_y(half, -1), along_y(half, 2)])
        if c == 1:
            more = (*more, step_bias.reshape(1, -1), decay_log.reshape(1, -1))
        more = project(c, where, mine, to_sibling(mine), ssd_gain, weights, *more)
    inputs, write, read, step, cum, state, to_next, to_last, to_across = more
    parts = (state, along_x(to_next, 1), along_x(to_last, -1), along_x(to_across, 2))
    row = row_total(where, parts)
    earlier = (along_z(row, 1), along_z(row, -1), along_z(row, 2))
    within = inside(inputs, write, read, step, cum, skip_gain)
    prior, to_next, to_last, to_across = carry(where, parts, earlier)
    carried = (prior, along_x(to_next, 1), along_x(to_last, -1), along_x(to_across, 2))
    ssd_out = finish(where, carried, read, cum, within)
    return (jnp.concatenate(mixed, axis=1), ssd_out)


def solution(mesh):
    placed = (
        P("frame", None),
        P("frame", None),
        P("frame", None),
        P(),
        P("expert", "frame", None),
        P("expert", "frame", None),
        P("expert", "frame", None),
        P(),
        P(None, "expert"),
        P(None, "expert"),
        P(None, "expert"),
        P(None, "expert"),
        P("expert"),
        P("expert"),
        P("expert"),
    )
    return jax.shard_map(
        body,
        mesh=mesh,
        in_specs=placed,
        out_specs=(P("frame", "expert"), P("frame", "expert")),
        check_vma=False,
    )
```

```python
import functools

import jax
import jax.numpy as jnp
from jax import lax
from jax.experimental import pallas as pl
from jax.experimental.pallas import tpu as pltpu
from jax.sharding import PartitionSpec as P

HEAD_DIM = 64
STATE = 128
SLOTS = 96
SIDE = 4
EPSILON = 1e-06
PRECISE = lax.Precision.HIGHEST
AXES = ("expert", "frame")
VMEM_BYTES = 48 * 1024 * 1024
F32, BF16 = jnp.float32, jnp.bfloat16


def routes_of(rule):
    pairs = []
    for y in range(SIDE):
        for core in range(2):
            for z in range(SIDE):
                for x in range(SIDE):
                    ny, nc, nz, nx = rule(y, core, z, x)
                    source = (y * 2 + core) * 16 + z * SIDE + x
                    target = ((ny % SIDE) * 2 + nc % 2) * 16 + (nz % SIDE) * SIDE + nx % SIDE
                    pairs.append((source, target))
    return pairs


def send(array, rule):
    return lax.ppermute(array, AXES, routes_of(rule))


def along_first(array, by):
    return send(array, lambda y, c, z, x: (y, c, z + by * c, x + by * (1 - c)))


def along_second(array, by):
    return send(array, lambda y, c, z, x: (y, c, z + by * (1 - c), x + by * c))


def along_x(array, by):
    return send(array, lambda y, c, z, x: (y, c, z, x + by))


def along_z(array, by):
    return send(array, lambda y, c, z, x: (y, c, z + by, x))


def along_y(array, by):
    return send(array, lambda y, c, z, x: (y + by, c, z, x))


def to_sibling(array):
    return send(array, lambda y, c, z, x: (y, 1 - c, z, x))


def shape(dims, kind):
    return jax.ShapeDtypeStruct(dims, kind)


def params():
    return pltpu.CompilerParams(vmem_limit_bytes=VMEM_BYTES)


def pick_kernel(where_ref, tokens_ref, routes_ref, weight_ref, gain_ref, rows_ref, onehot_ref, slot_weight_ref):
    count = tokens_ref.shape[0]
    hits = routes_ref[...] == where_ref[0]
    chosen = jnp.max(hits.astype(F32), axis=0, keepdims=True)
    weights = jnp.sum(jnp.where(hits, weight_ref[...], 0.0), axis=0, keepdims=True)
    upper = lax.broadcasted_iota(jnp.int32, (count, count), 0) <= lax.broadcasted_iota(jnp.int32, (count, count), 1)
    wide = jnp.broadcast_to(chosen, (SLOTS, count))
    place = jnp.dot(wide.astype(BF16), upper.astype(BF16), preferred_element_type=F32) - 1.0
    slot = lax.broadcasted_iota(jnp.int32, (SLOTS, count), 0)
    named = (place.astype(jnp.int32) == slot) & (wide > 0.0)
    onehot = jnp.where(named, 1.0, 0.0).astype(BF16)
    onehot_ref[...] = onehot
    slot_weight = jnp.sum(jnp.where(named, weights, 0.0), axis=1, keepdims=True)
    slot_weight_ref[...] = jnp.broadcast_to(slot_weight, slot_weight_ref.shape)
    picked = jnp.dot(onehot, tokens_ref[...], preferred_element_type=F32)
    mean_sq = jnp.mean(picked * picked, axis=1, keepdims=True)
    rows_ref[...] = (picked * lax.rsqrt(mean_sq + EPSILON) * gain_ref[...]).astype(BF16)


def pick(where, tokens, routes, route_weight, gain):
    count, width = tokens.shape
    outs = (shape((SLOTS, width), BF16), shape((SLOTS, count), BF16), shape((SLOTS, 128), F32))
    block = lambda dims: pl.BlockSpec(dims, lambda i, where: (0, 0))
    arrays = (tokens, routes.T, route_weight.T, gain.reshape(1, width))
    return pl.pallas_call(
        pick_kernel,
        out_shape=outs,
        grid_spec=pltpu.PrefetchScalarGridSpec(
            num_scalar_prefetch=1,
            grid=(1,),
            in_specs=[block(array.shape) for array in arrays],
            out_specs=tuple(block(out.shape) for out in outs),
        ),
        compiler_params=params(),
        name="pick",
    )(where, *arrays)


def expert_kernel(top_ref, bottom_ref, gate_ref, up_ref, down_ref, out_top_ref, out_bottom_ref):
    half = top_ref.shape[0]
    rows = jnp.concatenate([top_ref[...], bottom_ref[...]], axis=0)
    by_row = (((1,), (1,)), ((), ()))
    gate = lax.dot_general(rows, gate_ref[...], by_row, preferred_element_type=F32)
    upper = lax.dot_general(rows, up_ref[...], by_row, preferred_element_type=F32)
    hidden = (gate / (1.0 + jnp.exp(-gate)) * upper).astype(BF16)
    out = jnp.dot(hidden, down_ref[...], preferred_element_type=F32).astype(BF16)
    out_top_ref[...] = out[:half]
    out_bottom_ref[...] = out[half:]


def expert(top, bottom, weights):
    vmem = pl.BlockSpec(memory_space=pltpu.VMEM)
    rows, width = top.shape
    units = weights[0].shape[0]
    return pl.pallas_call(
        expert_kernel,
        out_shape=(shape(top.shape, BF16),) * 2,
        in_specs=[vmem] * 5,
        out_specs=(vmem, vmem),
        compiler_params=params(),
        cost_estimate=pl.CostEstimate(
            flops=12 * rows * width * units, bytes_accessed=6 * units * width + 8 * rows * width, transcendentals=0
        ),
        name="expert",
    )(top, bottom, *weights)


def half_columns(c, block):
    return [slice(k * 512 + c * 256, k * 512 + c * 256 + 256) for k in range(block // 512)]


def relay_kernel(c, after_ref, down_ref, before_ref, up_ref, to_after_ref, to_before_ref):
    for k, lanes in enumerate(half_columns(c, after_ref.shape[1])):
        to = slice(k * 256, k * 256 + 256)
        to_after_ref[:, to] = (after_ref[:, lanes].astype(F32) + down_ref[:, lanes].astype(F32)).astype(BF16)
        to_before_ref[:, to] = (before_ref[:, lanes].astype(F32) + up_ref[:, lanes].astype(F32)).astype(BF16)


def relay(c, *arrays):
    rows, width = arrays[0].shape
    steps = 4
    full = pl.BlockSpec((rows, width // steps), lambda j: (0, j))
    part = pl.BlockSpec((rows, width // steps // 2), lambda j: (0, j))
    return pl.pallas_call(
        functools.partial(relay_kernel, c),
        out_shape=(shape((rows, width // 2), BF16),) * 2,
        grid=(steps,),
        in_specs=[full] * 4,
        out_specs=(part, part),
        compiler_params=params(),
        name="relay",
    )(*arrays)


def total_kernel(c, near_top, top_a, top_b, near_bottom, bottom_a, bottom_b, own, down, up, across):
    for k, lanes in enumerate(half_columns(c, near_top.shape[1])):
        at = slice(k * 256, k * 256 + 256)
        for near, a, b, first, second in (
            (near_top, top_a, top_b, own, down), (near_bottom, bottom_a, bottom_b, up, across)
        ):
            total = near[:, lanes].astype(F32) + a[:, lanes].astype(F32) + b[:, at].astype(F32)
            first[:, at] = total[:SLOTS].astype(BF16)
            second[:, at] = total[SLOTS:].astype(BF16)


def total(c, *arrays):
    rows, width = arrays[0].shape
    steps = 4
    full = pl.BlockSpec((rows, width // steps), lambda j: (0, j))
    part = pl.BlockSpec((rows, width // steps // 2), lambda j: (0, j))
    piece = pl.BlockSpec((SLOTS, width // steps // 2), lambda j: (0, j))
    return pl.pallas_call(
        functools.partial(total_kernel, c),
        out_shape=(shape((SLOTS, width // 2), BF16),) * 4,
        grid=(steps,),
        in_specs=[full, full, part, full, full, part],
        out_specs=(piece,) * 4,
        compiler_params=params(),
        name="total",
    )(*arrays)


def after(values, *earlier):
    return lax.optimization_barrier((values, earlier))[0]


def experts(rows, weights):
    near_top = jnp.concatenate([rows, along_first(rows, 1)], axis=0)
    near_bottom = jnp.concatenate([along_first(rows, -1), along_first(rows, 2)], axis=0)
    before_top = along_second(near_top, 1)
    after_bottom = along_second(near_bottom, -1)
    out_near_top, out_near_bottom = expert(near_top, near_bottom, weights)
    far_top = along_second(before_top, 1)
    far_bottom = along_second(after_bottom, -1)
    out_before_top, out_after_bottom = expert(*after((before_top, after_bottom), out_near_top), weights)
    later_top, later_bottom = after((near_top, near_bottom), out_before_top)
    after_top = along_second(later_top, -1)
    before_bottom = along_second(later_bottom, 1)
    out_far_top, out_far_bottom = expert(*after((far_top, far_bottom), out_before_top), weights)
    relay_down = along_second(out_far_top, 1)
    relay_up = along_second(out_far_bottom, -1)
    first_back = after((out_before_top, out_after_bottom), out_far_top)
    top_a = along_second(first_back[0], -1)
    bottom_a = along_second(first_back[1], 1)
    second = after((after_top, before_bottom), relay_down, relay_up)
    out_after_top, out_before_bottom = expert(*second, weights)
    terms, order = [], ()
    for c in range(2):
        arrays = after((out_after_top, relay_down, out_before_bottom, relay_up), *order)
        to_after, to_before = relay(c, *arrays)
        order = (to_after,)
        top_b = along_second(to_after, 1)
        bottom_b = along_second(to_before, -1)
        own, down, up, across = total(c, out_near_top, top_a, top_b, out_near_bottom, bottom_a, bottom_b)
        terms.append((own, along_first(down, -1), along_first(up, 1), along_first(across, 2)))
    return terms


def place_kernel(where_ref, a_ref, b_ref, c_ref, d_ref, onehot_ref, weight_ref, keep_ref, give_ref):
    rows = (a_ref[...].astype(F32) + b_ref[...].astype(F32)) + (c_ref[...].astype(F32) + d_ref[...].astype(F32))
    weighted = (rows * weight_ref[:, :1]).astype(BF16)
    placed = lax.dot_general(
        onehot_ref[...], weighted, (((0,), (0,)), ((), ())), preferred_element_type=F32
    ).astype(BF16)
    for core in range(2):

        @pl.when(where_ref[1] == core)
        def _():
            for k in range(SIDE):
                for out, e in ((keep_ref, 2 * k + core), (give_ref, 2 * k + 1 - core)):
                    out[k] = placed[:, e * 256 : (e + 1) * 256]


def place(where, terms, onehot, slot_weight):
    count = onehot.shape[1]
    vmem = pl.BlockSpec(memory_space=pltpu.VMEM)
    return pl.pallas_call(
        place_kernel,
        out_shape=(shape((SIDE, count, 256), BF16),) * 2,
        in_specs=[pl.BlockSpec(memory_space=pltpu.SMEM)] + [vmem] * 6,
        out_specs=(vmem, vmem),
        compiler_params=params(),
        name="place",
    )(where, *terms, onehot, slot_weight)


def pair_kernel(where_ref, keep_ref, got_ref, own_ref, next_ref, last_ref, across_ref):
    for by, out in ((0, own_ref), (1, next_ref), (3, last_ref), (2, across_ref)):
        k = (where_ref[2] + by) % SIDE
        out[...] = (keep_ref[k].astype(F32) + got_ref[k].astype(F32)).astype(out.dtype)


def pair(where, keep, got):
    _, count, cols = keep.shape
    vmem = pl.BlockSpec(memory_space=pltpu.VMEM)
    return pl.pallas_call(
        pair_kernel,
        out_shape=(shape((count, cols), F32),) + (shape((count, cols), BF16),) * 3,
        in_specs=[pl.BlockSpec(memory_space=pltpu.SMEM), vmem, vmem],
        out_specs=(vmem,) * 4,
        compiler_params=params(),
        name="pair",
    )(where, keep, got)


def residual_kernel(where_ref, tokens_ref, own_ref, a_ref, b_ref, c_ref, mixed_ref):
    summed = (own_ref[...] + a_ref[...].astype(F32)) + (b_ref[...].astype(F32) + c_ref[...].astype(F32))
    mixed_ref[...] = (tokens_ref[...].astype(F32) + summed).astype(BF16)


def residual(c, where, tokens, own, others):
    count, cols = own.shape
    whole = pl.BlockSpec((count, cols), lambda i, where: (0, 0))
    return pl.pallas_call(
        residual_kernel,
        out_shape=shape((count, cols), BF16),
        grid_spec=pltpu.PrefetchScalarGridSpec(
            num_scalar_prefetch=1,
            grid=(1,),
            in_specs=[pl.BlockSpec((count, cols), lambda i, where: (0, 2 * where[0] + c))] + [whole] * 4,
            out_specs=whole,
        ),
        compiler_params=params(),
        name="residual",
    )(where, tokens, own, *others)


def spread(per_head, lanes):
    heads = per_head.shape[1]
    pairs = []
    first = lax.broadcasted_iota(jnp.int32, (per_head.shape[0], 2 * HEAD_DIM), 1) < HEAD_DIM
    for k in range(heads // 2):
        pairs.append(jnp.where(first, per_head[:, 2 * k : 2 * k + 1], per_head[:, 2 * k + 1 : 2 * k + 2]))
    return jnp.concatenate(pairs, axis=1)


def project_kernel(
    c, where_ref, mine_ref, other_ref, gain_ref, in_w_ref, write_w_ref, read_w_ref, step_w_ref, *refs
):
    if c == 0:
        out_accs, accs = refs[:5], refs[5:]
    else:
        in_accs, (bias_ref, decay_ref) = refs[:5], refs[5:7]
        outs, accs, state_scr = refs[7:16], refs[16:21], refs[21]
    in_acc, write_acc, read_acc, step_acc, square_acc = accs
    at = pl.program_id(0)

    @pl.when(at == 0)
    def _():
        for k, acc in enumerate(accs):
            acc[...] = jnp.zeros_like(acc) if c == 0 else in_accs[k][...]

    away = (at + SIDE - where_ref[2]) % SIDE
    slot = jnp.where(away == 0, 0, jnp.where(away == 3, 1, away + 1))
    mine, other = mine_ref[slot], other_ref[slot]
    even = where_ref[1] == 0
    values = jnp.concatenate([jnp.where(even, mine, other), jnp.where(even, other, mine)], axis=1).astype(F32)
    square_acc[...] += jnp.sum(values * values, axis=1, keepdims=True)
    scaled = (values * jnp.concatenate([gain_ref[0, 0], gain_ref[1, 0]], axis=1)).astype(BF16)

    def rows(weight):
        return weight[...].reshape(scaled.shape[1], weight.shape[3])

    in_acc[...] += jnp.dot(scaled, rows(in_w_ref), preferred_element_type=F32)
    both = jnp.concatenate([rows(write_w_ref), rows(read_w_ref)], axis=1)
    write_read = jnp.dot(scaled, both, preferred_element_type=F32)
    write_acc[...] += write_read[:, :STATE]
    read_acc[...] += write_read[:, STATE:]
    step_acc[...] += jnp.dot(scaled, rows(step_w_ref), preferred_element_type=F32)

    @pl.when(at == SIDE - 1)
    def _():
        if c == 0:
            for acc, out in zip(accs, out_accs):
                out[...] = acc[...]
        else:
            projected(where_ref, bias_ref, decay_ref, outs, accs, state_scr, 8 * 512)


def projected(where_ref, bias_ref, decay_ref, outs, accs, state_scr, width):
    in_acc, write_acc, read_acc, step_acc, square_acc = accs
    x_ref, write_ref, read_ref, step_ref, cum_ref = outs[:5]
    count, heads = step_acc.shape
    scale = lax.rsqrt(square_acc[:, :1] / width + EPSILON)
    x = (in_acc[...] * scale).astype(BF16)
    x_ref[...] = x
    write = (write_acc[...] * scale).astype(BF16)
    write_ref[...] = write
    read_ref[...] = (read_acc[...] * scale).astype(BF16)
    raw = step_acc[...] * scale + bias_ref[...]
    step = jnp.maximum(raw, 0.0) + jnp.log1p(jnp.exp(-jnp.abs(raw)))
    step_ref[...] = step
    log_decay = -step * jnp.exp(decay_ref[...])
    lower = lax.broadcasted_iota(jnp.int32, (count, count), 0) >= lax.broadcasted_iota(jnp.int32, (count, count), 1)
    cum = jnp.dot(lower.astype(F32), log_decay, preferred_element_type=F32, precision=PRECISE)
    cum_ref[...] = cum
    last = cum[count - 1 :, :]
    to_end = jnp.exp(last - cum) * step
    weighted = (x.astype(F32) * spread(to_end, x.shape[1])).astype(BF16)
    state = lax.dot_general(write, weighted, (((0,), (0,)), ((), ())), preferred_element_type=F32)
    whole = spread(last, x.shape[1])
    high = whole.astype(BF16).astype(F32)
    row = lax.broadcasted_iota(jnp.int32, (16, x.shape[1]), 0)
    log_rows = jnp.where(row == 0, high, jnp.where(row == 1, whole - high, 0.0)).astype(BF16)
    cols = x.shape[1] // SIDE
    for q in range(SIDE):
        lanes = slice(q * cols, (q + 1) * cols)
        state_scr[q, :STATE, :] = state[:, lanes].astype(BF16)
        state_scr[q, STATE:, :] = log_rows[:, lanes]
    for by, out in zip((0, 1, 3, 2), outs[5:]):
        out[...] = state_scr[(where_ref[3] + by) % SIDE]


def project(c, where, mine, other, gain, weights, *more):
    _, count, cols = mine.shape
    lanes, heads = weights[0].shape[1], weights[3].shape[1]
    cut = lambda w: w.reshape(8, 2, cols, w.shape[1])
    by_rows = lambda w: pl.BlockSpec((2, 1, cols, w.shape[1]), lambda i, where: (i, c, 0, 0))
    fixed = lambda dims: pl.BlockSpec(dims, lambda i, where: (0,) * len(dims))
    accs = [(count, lanes), (count, STATE), (count, STATE), (count, heads), (count, 128)]
    scratch = [pltpu.VMEM(dims, F32) for dims in accs]
    if c == 0:
        outs = tuple(shape(dims, F32) for dims in accs)
    else:
        quarter = (STATE + 16, lanes // SIDE)
        outs = (
            shape((count, lanes), BF16), shape((count, STATE), BF16), shape((count, STATE), BF16),
            shape((count, heads), F32), shape((count, heads), F32),
        ) + (shape(quarter, BF16),) * 4
        scratch.append(pltpu.VMEM((SIDE,) + quarter, BF16))
    return pl.pallas_call(
        functools.partial(project_kernel, c),
        out_shape=outs,
        grid_spec=pltpu.PrefetchScalarGridSpec(
            num_scalar_prefetch=1,
            grid=(SIDE,),
            in_specs=[
                fixed(mine.shape), fixed(other.shape),
                pl.BlockSpec((2, 1, 1, cols), lambda i, where: (i, c, 0, 0)),
                *[by_rows(w) for w in weights],
                *[fixed(m.shape) for m in more],
            ],
            out_specs=tuple(fixed(o.shape) for o in outs),
            scratch_shapes=scratch,
        ),
        compiler_params=params(),
        name="project",
    )(where, mine, other, gain.reshape(8, 2, 1, cols), *[cut(w) for w in weights], *more)


def inside_kernel(x_ref, write_ref, read_ref, step_ref, cum_ref, skip_ref, out_ref):
    count, heads = step_ref.shape
    span = count // 2
    scores = lax.dot_general(read_ref[...], write_ref[...], (((1,), (1,)), ((), ())), preferred_element_type=F32)
    cum = cum_ref[...]
    cum_t, step_t = cum.T, step_ref[...].T
    causal = lax.broadcasted_iota(jnp.int32, (span, span), 0) >= lax.broadcasted_iota(jnp.int32, (span, span), 1)
    low, high = slice(0, span), slice(span, count)

    def mixing(h, rows, columns):
        gaps = cum[rows, h : h + 1] - cum_t[h : h + 1, columns]
        if rows == columns:
            gaps = jnp.where(causal, gaps, -jnp.inf)
        return (scores[rows, columns] * jnp.exp(gaps) * step_t[h : h + 1, columns]).astype(BF16)

    for h in range(heads):
        lanes = slice(h * HEAD_DIM, (h + 1) * HEAD_DIM)
        x = x_ref[:, lanes]
        skipped = skip_ref[0, h] * x.astype(F32)
        top = jnp.dot(mixing(h, low, low), x[low], preferred_element_type=F32)
        below = jnp.concatenate([mixing(h, high, low), mixing(h, high, high)], axis=1)
        bottom = jnp.dot(below, x, preferred_element_type=F32)
        out_ref[:, lanes] = jnp.concatenate([top, bottom], axis=0) + skipped


def inside(x, write, read, step, cum, skip_gain):
    vmem = pl.BlockSpec(memory_space=pltpu.VMEM)
    return pl.pallas_call(
        inside_kernel,
        out_shape=shape(x.shape, F32),
        in_specs=[vmem] * 5 + [pl.BlockSpec(memory_space=pltpu.SMEM)],
        out_specs=vmem,
        compiler_params=params(),
        cost_estimate=pl.CostEstimate(flops=2 * 10**9, bytes_accessed=2 * 10**6, transcendentals=10**6),
        name="inside",
    )(x, write, read, step, cum, skip_gain.reshape(1, -1))


def log_of(ref):
    return ref[STATE : STATE + 1, :].astype(F32) + ref[STATE + 1 : STATE + 2, :].astype(F32)


def weights_before(here, places, logs):
    terms = []
    for s in places:
        between = sum(jnp.where((s < u) & (u < here), log, 0.0) for u, log in zip(places, logs))
        terms.append(jnp.where(s < here, jnp.exp(between), 0.0))
    return terms


def row_total_kernel(where_ref, own_ref, last_ref, next_ref, across_ref, total_ref):
    here = where_ref[3]
    refs = (own_ref, last_ref, next_ref, across_ref)
    places = [here, (here + 3) % SIDE, (here + 1) % SIDE, (here + 2) % SIDE]
    logs = [log_of(ref) for ref in refs]
    until_end = [jnp.exp(sum(jnp.where(s < u, log, 0.0) for u, log in zip(places, logs))) for s in places]
    total_ref[:STATE, :] = sum(w * ref[:STATE, :].astype(F32) for w, ref in zip(until_end, refs)).astype(BF16)
    whole = sum(logs)
    top = whole.astype(BF16).astype(F32)
    row = lax.broadcasted_iota(jnp.int32, (16, whole.shape[1]), 0)
    total_ref[STATE:, :] = jnp.where(row == 0, top, jnp.where(row == 1, whole - top, 0.0)).astype(BF16)


def row_total(where, parts):
    vmem = pl.BlockSpec(memory_space=pltpu.VMEM)
    return pl.pallas_call(
        row_total_kernel,
        out_shape=shape(parts[0].shape, BF16),
        in_specs=[pl.BlockSpec(memory_space=pltpu.SMEM)] + [vmem] * 4,
        out_specs=vmem,
        compiler_params=params(),
        name="row_total",
    )(where, *parts)


def carry_kernel(where_ref, *refs):
    parts, earlier, outs = refs[:4], refs[4:7], refs[7:]
    here = where_ref[4]
    rows = [(here + 3) % SIDE, (here + 1) % SIDE, (here + 2) % SIDE]
    before = weights_before(here, rows, [log_of(ref) for ref in earlier])
    to_row = sum(w * ref[:STATE, :].astype(F32) for w, ref in zip(before, earlier))
    here = where_ref[3]
    places = [here, (here + 3) % SIDE, (here + 1) % SIDE, (here + 2) % SIDE]
    logs = [log_of(ref) for ref in parts]
    for by, out in zip((0, 1, 3, 2), outs):
        target = (here + by) % SIDE
        gone = sum(jnp.where(s < target, log, 0.0) for s, log in zip(places, logs))
        state = jnp.exp(gone) * to_row
        for w, ref in zip(weights_before(target, places, logs), parts):
            state += w * ref[:STATE, :].astype(F32)
        out[...] = state.astype(BF16)


def carry(where, parts, earlier):
    vmem = pl.BlockSpec(memory_space=pltpu.VMEM)
    return pl.pallas_call(
        carry_kernel,
        out_shape=(shape((STATE, parts[0].shape[1]), BF16),) * 4,
        in_specs=[pl.BlockSpec(memory_space=pltpu.SMEM)] + [vmem] * 7,
        out_specs=(vmem,) * 4,
        compiler_params=params(),
        name="carry",
    )(where, *parts, *earlier)


def finish_kernel(where_ref, own_ref, last_ref, next_ref, across_ref, read_ref, cum_ref, inside_ref, out_ref, scr):
    for by, ref in ((0, own_ref), (3, last_ref), (1, next_ref), (2, across_ref)):
        scr[(where_ref[3] + by) % SIDE] = ref[...]
    cols = own_ref.shape[1]
    decayed = spread(jnp.exp(cum_ref[...]), SIDE * cols)
    for q in range(SIDE):
        lanes = slice(q * cols, (q + 1) * cols)
        from_prior = jnp.dot(read_ref[...], scr[q], preferred_element_type=F32)
        out_ref[:, lanes] = (inside_ref[:, lanes] + decayed[:, lanes] * from_prior).astype(BF16)


def finish(where, parts, read, cum, within):
    vmem = pl.BlockSpec(memory_space=pltpu.VMEM)
    return pl.pallas_call(
        finish_kernel,
        out_shape=shape(within.shape, BF16),
        in_specs=[pl.BlockSpec(memory_space=pltpu.SMEM)] + [vmem] * 7,
        out_specs=vmem,
        scratch_shapes=[pltpu.VMEM((SIDE,) + parts[0].shape, BF16)],
        compiler_params=params(),
        name="finish",
    )(where, *parts, read, cum, within)


def body(
    tokens,
    routes,
    route_weight,
    moe_gain,
    gate_weight,
    up_weight,
    down_weight,
    ssd_gain,
    input_weight,
    write_weight,
    read_weight,
    step_weight,
    step_bias,
    decay_log,
    skip_gain,
):
    expert_at, frame = lax.axis_index("expert"), lax.axis_index("frame")
    y, core, z, x = expert_at // 2, expert_at % 2, frame // SIDE, frame % SIDE
    where = jnp.stack([expert_at, core, y, x, z]).astype(jnp.int32)
    rows, onehot, slot_weight = pick(where, tokens, routes, route_weight, moe_gain)
    halves = experts(rows, (gate_weight[0], up_weight[0], down_weight[0]))
    weights = (input_weight, write_weight, read_weight, step_weight)
    mixed, more = [], ()
    for c in range(2):
        keep, give = place(where, halves[c], onehot, slot_weight)
        own, to_next, to_last, to_across = pair(where, keep, to_sibling(give))
        others = (along_y(to_next, 1), along_y(to_last, -1), along_y(to_across, 2))
        half = residual(c, where, tokens, own, others)
        mixed.append(half)
        mine = jnp.stack([half, along_y(half, 1), along_y(half, -1), along_y(half, 2)])
        if c == 1:
            more = (*more, step_bias.reshape(1, -1), decay_log.reshape(1, -1))
        more = project(c, where, mine, to_sibling(mine), ssd_gain, weights, *more)
    inputs, write, read, step, cum, state, to_next, to_last, to_across = more
    parts = (state, along_x(to_next, 1), along_x(to_last, -1), along_x(to_across, 2))
    row = row_total(where, parts)
    earlier = (along_z(row, 1), along_z(row, -1), along_z(row, 2))
    within = inside(inputs, write, read, step, cum, skip_gain)
    prior, to_next, to_last, to_across = carry(where, parts, earlier)
    carried = (prior, along_x(to_next, 1), along_x(to_last, -1), along_x(to_across, 2))
    ssd_out = finish(where, carried, read, cum, within)
    return (jnp.concatenate(mixed, axis=1), ssd_out)


def solution(mesh):
    placed = (
        P("frame", None),
        P("frame", None),
        P("frame", None),
        P(),
        P("expert", "frame", None),
        P("expert", "frame", None),
        P("expert", "frame", None),
        P(),
        P(None, "expert"),
        P(None, "expert"),
        P(None, "expert"),
        P(None, "expert"),
        P("expert"),
        P("expert"),
        P("expert"),
    )
    return jax.shard_map(
        body,
        mesh=mesh,
        in_specs=placed,
        out_specs=(P("frame", "expert"), P("frame", "expert")),
        check_vma=False,
    )
```

```python
import functools

import jax
import jax.numpy as jnp
from jax import lax
from jax.experimental import pallas as pl
from jax.experimental.pallas import tpu as pltpu
from jax.sharding import PartitionSpec as P

HEAD_DIM = 64
STATE = 128
SLOTS = 96
SIDE = 4
EPSILON = 1e-06
PRECISE = lax.Precision.HIGHEST
AXES = ("expert", "frame")
F32, BF16 = jnp.float32, jnp.bfloat16


def routes_of(rule):
    pairs = []
    for y in range(SIDE):
        for core in range(2):
            for z in range(SIDE):
                for x in range(SIDE):
                    ny, nc, nz, nx = rule(y, core, z, x)
                    source = (y * 2 + core) * 16 + z * SIDE + x
                    target = ((ny % SIDE) * 2 + nc % 2) * 16 + (nz % SIDE) * SIDE + nx % SIDE
                    pairs.append((source, target))
    return pairs


def send(array, rule):
    return lax.ppermute(array, AXES, routes_of(rule))


def along_first(array, by):
    return send(array, lambda y, c, z, x: (y, c, z + by * c, x + by * (1 - c)))


def along_second(array, by):
    return send(array, lambda y, c, z, x: (y, c, z + by * (1 - c), x + by * c))


def along_x(array, by):
    return send(array, lambda y, c, z, x: (y, c, z, x + by))


def along_z(array, by):
    return send(array, lambda y, c, z, x: (y, c, z + by, x))


def along_y(array, by):
    return send(array, lambda y, c, z, x: (y + by, c, z, x))


def to_sibling(array):
    return send(array, lambda y, c, z, x: (y, 1 - c, z, x))


def shape(dims, kind):
    return jax.ShapeDtypeStruct(dims, kind)


def params(mebibytes=20):
    return pltpu.CompilerParams(vmem_limit_bytes=mebibytes * 1024 * 1024)


def place_of(where_ref):
    return where_ref[0] >> 1, where_ref[0] & 1, where_ref[1] >> 2, where_ref[1] & 3


def pick_kernel(where_ref, tokens_ref, routes_ref, weight_ref, gain_ref, rows_ref, onehot_ref, slot_weight_ref):
    count = tokens_ref.shape[0]
    hits = routes_ref[...] == where_ref[0]
    chosen = jnp.max(hits.astype(F32), axis=0, keepdims=True)
    weights = jnp.sum(jnp.where(hits, weight_ref[...], 0.0), axis=0, keepdims=True)
    upper = lax.broadcasted_iota(jnp.int32, (count, count), 0) <= lax.broadcasted_iota(jnp.int32, (count, count), 1)
    wide = jnp.broadcast_to(chosen, (SLOTS, count))
    place = jnp.dot(wide.astype(BF16), upper.astype(BF16), preferred_element_type=F32) - 1.0
    slot = lax.broadcasted_iota(jnp.int32, (SLOTS, count), 0)
    named = (place.astype(jnp.int32) == slot) & (wide > 0.0)
    onehot = jnp.where(named, 1.0, 0.0).astype(BF16)
    onehot_ref[...] = onehot
    slot_weight = jnp.sum(jnp.where(named, weights, 0.0), axis=1, keepdims=True)
    slot_weight_ref[...] = jnp.broadcast_to(slot_weight, slot_weight_ref.shape)
    picked = jnp.dot(onehot, tokens_ref[...], preferred_element_type=F32)
    mean_sq = jnp.mean(picked * picked, axis=1, keepdims=True)
    rows_ref[...] = (picked * lax.rsqrt(mean_sq + EPSILON) * gain_ref[...]).astype(BF16)


def pick(where, tokens, routes, route_weight, gain):
    count, width = tokens.shape
    outs = (shape((SLOTS, width), BF16), shape((SLOTS, count), BF16), shape((SLOTS, 128), F32))
    block = lambda dims: pl.BlockSpec(dims, lambda i, where: (0, 0))
    arrays = (tokens, routes.T, route_weight.T, gain.reshape(1, width))
    return pl.pallas_call(
        pick_kernel,
        out_shape=outs,
        grid_spec=pltpu.PrefetchScalarGridSpec(
            num_scalar_prefetch=1,
            grid=(1,),
            in_specs=[block(array.shape) for array in arrays],
            out_specs=tuple(block(out.shape) for out in outs),
        ),
        compiler_params=params(60),
        name="pick",
    )(where, *arrays)


def expert_kernel(top_ref, bottom_ref, gate_ref, up_ref, down_ref, out_top_ref, out_bottom_ref):
    half = top_ref.shape[0]
    rows = jnp.concatenate([top_ref[...], bottom_ref[...]], axis=0)
    by_row = (((1,), (1,)), ((), ()))
    gate = lax.dot_general(rows, gate_ref[...], by_row, preferred_element_type=F32)
    upper = lax.dot_general(rows, up_ref[...], by_row, preferred_element_type=F32)
    hidden = (gate / (1.0 + jnp.exp(-gate)) * upper).astype(BF16)
    out = jnp.dot(hidden, down_ref[...], preferred_element_type=F32).astype(BF16)
    out_top_ref[...] = out[:half]
    out_bottom_ref[...] = out[half:]


def expert(top, bottom, weights):
    vmem = pl.BlockSpec(memory_space=pltpu.VMEM)
    rows, width = top.shape
    units = weights[0].shape[0]
    return pl.pallas_call(
        expert_kernel,
        out_shape=(shape(top.shape, BF16),) * 2,
        in_specs=[vmem] * 5,
        out_specs=(vmem, vmem),
        compiler_params=params(28),
        cost_estimate=pl.CostEstimate(
            flops=12 * rows * width * units, bytes_accessed=6 * units * width + 8 * rows * width, transcendentals=0
        ),
        name="expert",
    )(top, bottom, *weights)


def half_columns(c, block):
    return [slice(k * 512 + c * 256, k * 512 + c * 256 + 256) for k in range(block // 512)]


def relay_kernel(c, after_ref, down_ref, before_ref, up_ref, to_after_ref, to_before_ref):
    for k, lanes in enumerate(half_columns(c, after_ref.shape[1])):
        to = slice(k * 256, k * 256 + 256)
        to_after_ref[:, to] = (after_ref[:, lanes].astype(F32) + down_ref[:, lanes].astype(F32)).astype(BF16)
        to_before_ref[:, to] = (before_ref[:, lanes].astype(F32) + up_ref[:, lanes].astype(F32)).astype(BF16)


def relay(c, *arrays):
    rows, width = arrays[0].shape
    vmem = pl.BlockSpec(memory_space=pltpu.VMEM)
    return pl.pallas_call(
        functools.partial(relay_kernel, c),
        out_shape=(shape((rows, width // 2), BF16),) * 2,
        in_specs=[vmem] * 4,
        out_specs=(vmem, vmem),
        compiler_params=params(),
        name="relay",
    )(*arrays)


def total_kernel(c, near_top, top_a, top_b, near_bottom, bottom_a, bottom_b, *refs):
    own, down, up, across = refs[-4:]
    for k, lanes in enumerate(half_columns(c, near_top.shape[1])):
        at = slice(k * 256, k * 256 + 256)
        for near, a, b, first, second in (
            (near_top, top_a, top_b, own, down), (near_bottom, bottom_a, bottom_b, up, across)
        ):
            total = near[:, lanes].astype(F32) + a[:, lanes].astype(F32) + b[:, at].astype(F32)
            first[:, at] = total[:SLOTS].astype(BF16)
            second[:, at] = total[SLOTS:].astype(BF16)


def total(c, *arrays):
    rows, width = arrays[0].shape
    vmem = pl.BlockSpec(memory_space=pltpu.VMEM)
    return pl.pallas_call(
        functools.partial(total_kernel, c),
        out_shape=(shape((SLOTS, width // 2), BF16),) * 4,
        in_specs=[vmem] * 6 + [pl.BlockSpec(memory_space=pl.ANY)] * (len(arrays) - 6),
        out_specs=(vmem,) * 4,
        compiler_params=params(),
        name="total",
    )(*arrays)


def after(values, *earlier):
    return lax.optimization_barrier((values, earlier))[0]


def experts(rows, weights):
    near_top = jnp.concatenate([rows, along_first(rows, 1)], axis=0)
    near_bottom = jnp.concatenate([along_first(rows, -1), along_first(rows, 2)], axis=0)
    before_top = along_second(near_top, 1)
    after_bottom = along_second(near_bottom, -1)
    out_near_top, out_near_bottom = expert(near_top, near_bottom, weights)
    before_top, after_bottom = after((before_top, after_bottom), out_near_top)
    far_top = along_second(before_top, 1)
    far_bottom = along_second(after_bottom, -1)
    out_before_top, out_after_bottom = expert(before_top, after_bottom, weights)
    later_top, later_bottom = after((near_top, near_bottom), out_before_top)
    after_top = along_second(later_top, -1)
    before_bottom = along_second(later_bottom, 1)
    out_far_top, out_far_bottom = expert(*after((far_top, far_bottom), out_before_top), weights)
    relay_down = along_second(out_far_top, 1)
    relay_up = along_second(out_far_bottom, -1)
    first_back = after((out_before_top, out_after_bottom), out_far_top)
    top_a = along_second(first_back[0], -1)
    bottom_a = along_second(first_back[1], 1)
    second = after((after_top, before_bottom), relay_down, relay_up)
    out_after_top, out_before_bottom = expert(*second, weights)
    terms, order = [], ()
    for c in range(2):
        arrays = after((out_after_top, relay_down, out_before_bottom, relay_up), *order)
        to_after, to_before = relay(c, *arrays)
        order = (to_after,)
        top_b = along_second(to_after, 1)
        bottom_b = along_second(to_before, -1)
        sums = (out_near_top, top_a, top_b, out_near_bottom, bottom_a, bottom_b)
        level = (to_sibling(top_b[:16, :128]),) if c == 0 else ()
        own, down, up, across = total(c, *sums, *level)
        terms.append((own, along_first(down, -1), along_first(up, 1), along_first(across, 2)))
    return terms


def place_kernel(where_ref, a_ref, b_ref, c_ref, d_ref, onehot_ref, weight_ref, keep_ref, give_ref):
    rows = (a_ref[...].astype(F32) + b_ref[...].astype(F32)) + (c_ref[...].astype(F32) + d_ref[...].astype(F32))
    weighted = (rows * weight_ref[:, :1]).astype(BF16)
    placed = lax.dot_general(
        onehot_ref[...], weighted, (((0,), (0,)), ((), ())), preferred_element_type=F32
    ).astype(BF16)
    _, mine, _, _ = place_of(where_ref)
    for core in range(2):

        @pl.when(mine == core)
        def _():
            for k in range(SIDE):
                for out, e in ((keep_ref, 2 * k + core), (give_ref, 2 * k + 1 - core)):
                    out[k] = placed[:, e * 256 : (e + 1) * 256]


def place(where, terms, onehot, slot_weight):
    count = onehot.shape[1]
    vmem = pl.BlockSpec(memory_space=pltpu.VMEM)
    return pl.pallas_call(
        place_kernel,
        out_shape=(shape((SIDE, count, 256), BF16),) * 2,
        in_specs=[pl.BlockSpec(memory_space=pltpu.SMEM)] + [vmem] * 6,
        out_specs=(vmem, vmem),
        compiler_params=params(),
        name="place",
    )(where, *terms, onehot, slot_weight)


def pair_kernel(where_ref, keep_ref, got_ref, own_ref, next_ref, last_ref, across_ref):
    y, _, _, _ = place_of(where_ref)
    for by, out in ((0, own_ref), (1, next_ref), (3, last_ref), (2, across_ref)):
        k = (y + by) & 3
        out[...] = (keep_ref[k].astype(F32) + got_ref[k].astype(F32)).astype(out.dtype)


def pair(where, keep, got):
    _, count, cols = keep.shape
    vmem = pl.BlockSpec(memory_space=pltpu.VMEM)
    return pl.pallas_call(
        pair_kernel,
        out_shape=(shape((count, cols), F32),) + (shape((count, cols), BF16),) * 3,
        in_specs=[pl.BlockSpec(memory_space=pltpu.SMEM), vmem, vmem],
        out_specs=(vmem,) * 4,
        compiler_params=params(),
        name="pair",
    )(where, keep, got)


def residual_kernel(where_ref, tokens_ref, own_ref, a_ref, b_ref, c_ref, mixed_ref):
    summed = (own_ref[...] + a_ref[...].astype(F32)) + (b_ref[...].astype(F32) + c_ref[...].astype(F32))
    mixed_ref[...] = (tokens_ref[...].astype(F32) + summed).astype(BF16)


def residual(c, where, tokens, own, others):
    count, cols = own.shape
    whole = pl.BlockSpec((count, cols), lambda i, where: (0, 0))
    return pl.pallas_call(
        residual_kernel,
        out_shape=shape((count, cols), BF16),
        grid_spec=pltpu.PrefetchScalarGridSpec(
            num_scalar_prefetch=1,
            grid=(1,),
            in_specs=[pl.BlockSpec((count, cols), lambda i, where: (0, 2 * where[0] + c))] + [whole] * 4,
            out_specs=whole,
        ),
        compiler_params=params(),
        name="residual",
    )(where, tokens, own, *others)


def spread(per_head, lanes):
    heads = per_head.shape[1]
    pairs = []
    first = lax.broadcasted_iota(jnp.int32, (per_head.shape[0], 2 * HEAD_DIM), 1) < HEAD_DIM
    for k in range(heads // 2):
        pairs.append(jnp.where(first, per_head[:, 2 * k : 2 * k + 1], per_head[:, 2 * k + 1 : 2 * k + 2]))
    return jnp.concatenate(pairs, axis=1)


def project_kernel(c, where_ref, mine_ref, other_ref, gain_ref, in_w_ref, write_w_ref, read_w_ref, step_w_ref, *refs):
    y, core, _, _ = place_of(where_ref)
    squares, scaled, step_w = 0.0, [], []
    for e in range(8):
        away = (e // 2 + SIDE - y) & 3
        slot = jnp.where(away == 0, 0, jnp.where(away == 3, 1, away + 1))
        values = jnp.where(core == e % 2, mine_ref[slot], other_ref[slot]).astype(F32)
        squares += jnp.sum(values * values, axis=1, keepdims=True)
        scaled.append((values * gain_ref[e, c]).astype(BF16))
        step_w.append(step_w_ref[:, e * 512 + c * 256 : e * 512 + c * 256 + 256])
    scaled = jnp.concatenate(scaled, axis=1)

    def rows(ref):
        return ref[:, c].reshape(scaled.shape[1], ref.shape[3])

    write_read = jnp.concatenate([rows(write_w_ref), rows(read_w_ref)], axis=1)
    accs = [
        jnp.dot(scaled, rows(in_w_ref), preferred_element_type=F32),
        jnp.dot(scaled, write_read, preferred_element_type=F32),
        lax.dot_general(
            scaled, jnp.concatenate(step_w, axis=1), (((1,), (1,)), ((), ())), preferred_element_type=F32
        ),
        jnp.broadcast_to(squares, (squares.shape[0], 128)),
    ]
    if c == 0:
        for out, acc in zip(refs, accs):
            out[...] = acc
    else:
        before, (bias_ref, decay_ref) = refs[:4], refs[4:6]
        accs = [acc + ref[...] for acc, ref in zip(accs, before)]
        projected(where_ref, bias_ref, decay_ref, refs[6:15], accs, refs[15], 8 * 512)


def projected(where_ref, bias_ref, decay_ref, outs, accs, state_scr, width):
    in_acc, write_read, step_acc, square_acc = accs
    x_ref, write_ref, read_ref, step_ref, cum_ref = outs[:5]
    count, heads = step_acc.shape
    scale = lax.rsqrt(square_acc[:, :1] / width + EPSILON)
    x = (in_acc * scale).astype(BF16)
    x_ref[...] = x
    write = (write_read[:, :STATE] * scale).astype(BF16)
    write_ref[...] = write
    read_ref[...] = (write_read[:, STATE:] * scale).astype(BF16)
    raw = step_acc * scale + bias_ref[...]
    step = jnp.maximum(raw, 0.0) + jnp.log1p(jnp.exp(-jnp.abs(raw)))
    step_ref[...] = step
    log_decay = -step * jnp.exp(decay_ref[...])
    lower = lax.broadcasted_iota(jnp.int32, (count, count), 0) >= lax.broadcasted_iota(jnp.int32, (count, count), 1)
    cum = jnp.dot(lower.astype(F32), log_decay, preferred_element_type=F32, precision=PRECISE)
    cum_ref[...] = cum
    last = cum[count - 1 :, :]
    to_end = jnp.exp(last - cum) * step
    weighted = (x.astype(F32) * spread(to_end, x.shape[1])).astype(BF16)
    state = lax.dot_general(write, weighted, (((0,), (0,)), ((), ())), preferred_element_type=F32)
    whole = spread(last, x.shape[1])
    high = whole.astype(BF16).astype(F32)
    row = lax.broadcasted_iota(jnp.int32, (16, x.shape[1]), 0)
    log_rows = jnp.where(row == 0, high, jnp.where(row == 1, whole - high, 0.0)).astype(BF16)
    cols = x.shape[1] // SIDE
    for q in range(SIDE):
        lanes = slice(q * cols, (q + 1) * cols)
        state_scr[q, :STATE, :] = state[:, lanes].astype(BF16)
        state_scr[q, STATE:, :] = log_rows[:, lanes]
    _, _, _, at = place_of(where_ref)
    for by, out in zip((0, 1, 3, 2), outs[5:]):
        out[...] = state_scr[(at + by) & 3]


def project(c, where, mine, other, gain, weights, *more):
    _, count, cols = mine.shape
    lanes, heads = weights[0].shape[1], weights[3].shape[1]
    smem, vmem = pl.BlockSpec(memory_space=pltpu.SMEM), pl.BlockSpec(memory_space=pltpu.VMEM)
    cut = [w.reshape(8, 2, cols, w.shape[1]) for w in weights[:3]]
    if c == 0:
        outs = tuple(shape((count, n), F32) for n in (lanes, 2 * STATE, heads, 128))
        scratch = []
    else:
        quarter = (STATE + 16, lanes // SIDE)
        outs = (
            shape((count, lanes), BF16), shape((count, STATE), BF16), shape((count, STATE), BF16),
            shape((count, heads), F32), shape((count, heads), F32),
        ) + (shape(quarter, BF16),) * 4
        scratch = [pltpu.VMEM((SIDE,) + quarter, BF16)]
    return pl.pallas_call(
        functools.partial(project_kernel, c),
        out_shape=outs,
        in_specs=[smem] + [vmem] * (7 + len(more)),
        out_specs=(vmem,) * len(outs),
        scratch_shapes=scratch,
        compiler_params=params(),
        name="project",
    )(where, mine, other, gain.reshape(8, 2, 1, cols), *cut, weights[3].T, *more)


def inside_kernel(x_ref, write_ref, read_ref, step_ref, cum_ref, skip_ref, out_ref):
    count, heads = step_ref.shape
    span = count // 2
    scores = lax.dot_general(read_ref[...], write_ref[...], (((1,), (1,)), ((), ())), preferred_element_type=F32)
    cum = cum_ref[...]
    cum_t, step_t = cum.T, step_ref[...].T
    causal = lax.broadcasted_iota(jnp.int32, (span, span), 0) >= lax.broadcasted_iota(jnp.int32, (span, span), 1)
    low, high = slice(0, span), slice(span, count)

    def mixing(h, rows, columns):
        gaps = cum[rows, h : h + 1] - cum_t[h : h + 1, columns]
        if rows == columns:
            gaps = jnp.where(causal, gaps, -jnp.inf)
        return (scores[rows, columns] * jnp.exp(gaps) * step_t[h : h + 1, columns]).astype(BF16)

    for h in range(heads):
        lanes = slice(h * HEAD_DIM, (h + 1) * HEAD_DIM)
        x = x_ref[:, lanes]
        skipped = skip_ref[0, h] * x.astype(F32)
        top = jnp.dot(mixing(h, low, low), x[low], preferred_element_type=F32)
        below = jnp.concatenate([mixing(h, high, low), mixing(h, high, high)], axis=1)
        bottom = jnp.dot(below, x, preferred_element_type=F32)
        out_ref[:, lanes] = jnp.concatenate([top, bottom], axis=0) + skipped


def inside(x, write, read, step, cum, skip_gain):
    vmem = pl.BlockSpec(memory_space=pltpu.VMEM)
    return pl.pallas_call(
        inside_kernel,
        out_shape=shape(x.shape, F32),
        in_specs=[vmem] * 5 + [pl.BlockSpec(memory_space=pltpu.SMEM)],
        out_specs=vmem,
        compiler_params=params(),
        cost_estimate=pl.CostEstimate(flops=2 * 10**9, bytes_accessed=2 * 10**6, transcendentals=10**6),
        name="inside",
    )(x, write, read, step, cum, skip_gain.reshape(1, -1))


def log_of(ref):
    return ref[STATE : STATE + 1, :].astype(F32) + ref[STATE + 1 : STATE + 2, :].astype(F32)


def weights_before(here, places, logs):
    terms = []
    for s in places:
        between = sum(jnp.where((s < u) & (u < here), log, 0.0) for u, log in zip(places, logs))
        terms.append(jnp.where(s < here, jnp.exp(between), 0.0))
    return terms


def row_total_kernel(where_ref, own_ref, last_ref, next_ref, across_ref, total_ref):
    _, _, _, here = place_of(where_ref)
    refs = (own_ref, last_ref, next_ref, across_ref)
    places = [here, (here + 3) & 3, (here + 1) & 3, (here + 2) & 3]
    logs = [log_of(ref) for ref in refs]
    until_end = [jnp.exp(sum(jnp.where(s < u, log, 0.0) for u, log in zip(places, logs))) for s in places]
    total_ref[:STATE, :] = sum(w * ref[:STATE, :].astype(F32) for w, ref in zip(until_end, refs)).astype(BF16)
    whole = sum(logs)
    top = whole.astype(BF16).astype(F32)
    row = lax.broadcasted_iota(jnp.int32, (16, whole.shape[1]), 0)
    total_ref[STATE:, :] = jnp.where(row == 0, top, jnp.where(row == 1, whole - top, 0.0)).astype(BF16)


def row_total(where, parts):
    vmem = pl.BlockSpec(memory_space=pltpu.VMEM)
    return pl.pallas_call(
        row_total_kernel,
        out_shape=shape(parts[0].shape, BF16),
        in_specs=[pl.BlockSpec(memory_space=pltpu.SMEM)] + [vmem] * 4,
        out_specs=vmem,
        compiler_params=params(),
        name="row_total",
    )(where, *parts)


def carry_kernel(where_ref, *refs):
    parts, earlier, outs = refs[:4], refs[4:7], refs[7:]
    _, _, z, here = place_of(where_ref)
    rows = [(z + 3) & 3, (z + 1) & 3, (z + 2) & 3]
    before = weights_before(z, rows, [log_of(ref) for ref in earlier])
    to_row = sum(w * ref[:STATE, :].astype(F32) for w, ref in zip(before, earlier))
    places = [here, (here + 3) & 3, (here + 1) & 3, (here + 2) & 3]
    logs = [log_of(ref) for ref in parts]
    for by, out in zip((0, 1, 3, 2), outs):
        target = (here + by) & 3
        gone = sum(jnp.where(s < target, log, 0.0) for s, log in zip(places, logs))
        state = jnp.exp(gone) * to_row
        for w, ref in zip(weights_before(target, places, logs), parts):
            state += w * ref[:STATE, :].astype(F32)
        out[...] = state.astype(BF16)


def carry(where, parts, earlier):
    vmem = pl.BlockSpec(memory_space=pltpu.VMEM)
    return pl.pallas_call(
        carry_kernel,
        out_shape=(shape((STATE, parts[0].shape[1]), BF16),) * 4,
        in_specs=[pl.BlockSpec(memory_space=pltpu.SMEM)] + [vmem] * 7,
        out_specs=(vmem,) * 4,
        compiler_params=params(),
        name="carry",
    )(where, *parts, *earlier)


def finish_kernel(where_ref, own_ref, last_ref, next_ref, across_ref, read_ref, cum_ref, inside_ref, out_ref, scr):
    _, _, _, here = place_of(where_ref)
    for by, ref in ((0, own_ref), (3, last_ref), (1, next_ref), (2, across_ref)):
        scr[(here + by) & 3] = ref[...]
    cols = own_ref.shape[1]
    decayed = spread(jnp.exp(cum_ref[...]), SIDE * cols)
    for q in range(SIDE):
        lanes = slice(q * cols, (q + 1) * cols)
        from_prior = jnp.dot(read_ref[...], scr[q], preferred_element_type=F32)
        out_ref[:, lanes] = (inside_ref[:, lanes] + decayed[:, lanes] * from_prior).astype(BF16)


def finish(where, parts, read, cum, within):
    vmem = pl.BlockSpec(memory_space=pltpu.VMEM)
    return pl.pallas_call(
        finish_kernel,
        out_shape=shape(within.shape, BF16),
        in_specs=[pl.BlockSpec(memory_space=pltpu.SMEM)] + [vmem] * 7,
        out_specs=vmem,
        scratch_shapes=[pltpu.VMEM((SIDE,) + parts[0].shape, BF16)],
        compiler_params=params(),
        name="finish",
    )(where, *parts, read, cum, within)


def body(
    tokens,
    routes,
    route_weight,
    moe_gain,
    gate_weight,
    up_weight,
    down_weight,
    ssd_gain,
    input_weight,
    write_weight,
    read_weight,
    step_weight,
    step_bias,
    decay_log,
    skip_gain,
):
    where = jnp.stack([lax.axis_index("expert"), lax.axis_index("frame")]).astype(jnp.int32)
    rows, onehot, slot_weight = pick(where, tokens, routes, route_weight, moe_gain)
    halves = experts(rows, (gate_weight[0], up_weight[0], down_weight[0]))
    weights = (input_weight, write_weight, read_weight, step_weight)
    mixed, more = [], ()
    for c in range(2):
        keep, give = place(where, halves[c], onehot, slot_weight)
        own, to_next, to_last, to_across = pair(where, keep, to_sibling(give))
        others = (along_y(to_next, 1), along_y(to_last, -1), along_y(to_across, 2))
        half = residual(c, where, tokens, own, others)
        mixed.append(half)
        mine = jnp.stack([half, along_y(half, 1), along_y(half, -1), along_y(half, 2)])
        if c == 1:
            more = (*more, step_bias.reshape(1, -1), decay_log.reshape(1, -1))
        more = project(c, where, mine, to_sibling(mine), ssd_gain, weights, *more)
    inputs, write, read, step, cum, state, to_next, to_last, to_across = more
    parts = (state, along_x(to_next, 1), along_x(to_last, -1), along_x(to_across, 2))
    row = row_total(where, parts)
    earlier = (along_z(row, 1), along_z(row, -1), along_z(row, 2))
    within = inside(inputs, write, read, step, cum, skip_gain)
    prior, to_next, to_last, to_across = carry(where, parts, earlier)
    carried = (prior, along_x(to_next, 1), along_x(to_last, -1), along_x(to_across, 2))
    ssd_out = finish(where, carried, read, cum, within)
    return (jnp.concatenate(mixed, axis=1), ssd_out)


def solution(mesh):
    placed = (
        P("frame", None),
        P("frame", None),
        P("frame", None),
        P(),
        P("expert", "frame", None),
        P("expert", "frame", None),
        P("expert", "frame", None),
        P(),
        P(None, "expert"),
        P(None, "expert"),
        P(None, "expert"),
        P(None, "expert"),
        P("expert"),
        P("expert"),
        P("expert"),
    )
    return jax.shard_map(
        body,
        mesh=mesh,
        in_specs=placed,
        out_specs=(P("frame", "expert"), P("frame", "expert")),
        check_vma=False,
    )
```

```python
import functools

import jax
import jax.numpy as jnp
from jax import lax
from jax.experimental import pallas as pl
from jax.experimental.pallas import tpu as pltpu
from jax.sharding import PartitionSpec as P

HEAD_DIM = 64
STATE = 128
SLOTS = 96
SIDE = 4
EPSILON = 1e-06
PRECISE = lax.Precision.HIGHEST
AXES = ("expert", "frame")
F32, BF16 = jnp.float32, jnp.bfloat16


def routes_of(rule):
    pairs = []
    for y in range(SIDE):
        for core in range(2):
            for z in range(SIDE):
                for x in range(SIDE):
                    ny, nc, nz, nx = rule(y, core, z, x)
                    source = (y * 2 + core) * 16 + z * SIDE + x
                    target = ((ny % SIDE) * 2 + nc % 2) * 16 + (nz % SIDE) * SIDE + nx % SIDE
                    pairs.append((source, target))
    return pairs


def send(array, rule):
    return lax.ppermute(array, AXES, routes_of(rule))


def along_first(array, by):
    return send(array, lambda y, c, z, x: (y, c, z + by * c, x + by * (1 - c)))


def along_second(array, by):
    return send(array, lambda y, c, z, x: (y, c, z + by * (1 - c), x + by * c))


def along_x(array, by):
    return send(array, lambda y, c, z, x: (y, c, z, x + by))


def along_z(array, by):
    return send(array, lambda y, c, z, x: (y, c, z + by, x))


def along_y(array, by):
    return send(array, lambda y, c, z, x: (y + by, c, z, x))


def to_sibling(array):
    return send(array, lambda y, c, z, x: (y, 1 - c, z, x))


def shape(dims, kind):
    return jax.ShapeDtypeStruct(dims, kind)


def params(mebibytes=20):
    return pltpu.CompilerParams(vmem_limit_bytes=mebibytes * 1024 * 1024)


def place_of(where_ref):
    return where_ref[0] >> 1, where_ref[0] & 1, where_ref[1] >> 2, where_ref[1] & 3


def pick_kernel(where_ref, *refs):
    arrays, (rows_ref, onehot_ref, slot_weight_ref), held, sems = refs[:4], refs[4:7], refs[7:11], refs[11]
    copies = [pltpu.make_async_copy(source, to, sems.at[k]) for k, (source, to) in enumerate(zip(arrays, held))]
    for copy in copies:
        copy.start()
    tokens_ref, routes_ref, weight_ref, gain_ref = held
    count = tokens_ref.shape[0]
    upper = lax.broadcasted_iota(jnp.int32, (count, count), 0) <= lax.broadcasted_iota(jnp.int32, (count, count), 1)
    slot = lax.broadcasted_iota(jnp.int32, (SLOTS, count), 0)
    copies[1].wait()
    copies[2].wait()
    onehots = []
    for sibling in range(2):
        hits = routes_ref[...] == where_ref[0] ^ sibling
        chosen = jnp.max(hits.astype(F32), axis=0, keepdims=True)
        wide = jnp.broadcast_to(chosen, (SLOTS, count))
        place = jnp.dot(wide.astype(BF16), upper.astype(BF16), preferred_element_type=F32) - 1.0
        named = (place.astype(jnp.int32) == slot) & (wide > 0.0)
        onehots.append(jnp.where(named, 1.0, 0.0).astype(BF16))
        if sibling == 0:
            weights = jnp.sum(jnp.where(hits, weight_ref[...], 0.0), axis=0, keepdims=True)
            slot_weight = jnp.sum(jnp.where(named, weights, 0.0), axis=1, keepdims=True)
    onehot_ref[...] = jnp.concatenate(onehots, axis=0)
    slot_weight_ref[...] = jnp.broadcast_to(slot_weight, slot_weight_ref.shape)
    copies[0].wait()
    copies[3].wait()
    picked = jnp.dot(onehots[0], tokens_ref[...], preferred_element_type=F32)
    mean_sq = jnp.mean(picked * picked, axis=1, keepdims=True)
    rows_ref[...] = (picked * lax.rsqrt(mean_sq + EPSILON) * gain_ref[...]).astype(BF16)


def pick(where, tokens, routes, route_weight, gain):
    count, width = tokens.shape
    smem, vmem = pl.BlockSpec(memory_space=pltpu.SMEM), pl.BlockSpec(memory_space=pltpu.VMEM)
    arrays = (tokens, routes.T, route_weight.T, gain.reshape(1, width))
    return pl.pallas_call(
        pick_kernel,
        out_shape=(shape((SLOTS, width), BF16), shape((2 * SLOTS, count), BF16), shape((SLOTS, 128), F32)),
        in_specs=[smem] + [pl.BlockSpec(memory_space=pltpu.HBM)] * 4,
        out_specs=(vmem, vmem, vmem),
        scratch_shapes=[pltpu.VMEM(array.shape, array.dtype) for array in arrays] + [pltpu.SemaphoreType.DMA((4,))],
        compiler_params=params(),
        name="pick",
    )(where, *arrays)


def expert_kernel(top_ref, bottom_ref, gate_ref, up_ref, down_ref, out_top_ref, out_bottom_ref):
    half = top_ref.shape[0]
    rows = jnp.concatenate([top_ref[...], bottom_ref[...]], axis=0)
    by_row = (((1,), (1,)), ((), ()))
    gate = lax.dot_general(rows, gate_ref[...], by_row, preferred_element_type=F32)
    upper = lax.dot_general(rows, up_ref[...], by_row, preferred_element_type=F32)
    hidden = (gate / (1.0 + jnp.exp(-gate)) * upper).astype(BF16)
    out = jnp.dot(hidden, down_ref[...], preferred_element_type=F32).astype(BF16)
    out_top_ref[...] = out[:half]
    out_bottom_ref[...] = out[half:]


def expert(top, bottom, weights):
    vmem = pl.BlockSpec(memory_space=pltpu.VMEM)
    rows, width = top.shape
    units = weights[0].shape[0]
    return pl.pallas_call(
        expert_kernel,
        out_shape=(shape(top.shape, BF16),) * 2,
        in_specs=[vmem] * 5,
        out_specs=(vmem, vmem),
        compiler_params=params(28),
        cost_estimate=pl.CostEstimate(
            flops=12 * rows * width * units, bytes_accessed=6 * units * width + 8 * rows * width, transcendentals=0
        ),
        name="expert",
    )(top, bottom, *weights)


def half_columns(c, block):
    return [slice(k * 512 + c * 256, k * 512 + c * 256 + 256) for k in range(block // 512)]


def relay_kernel(c, after_ref, down_ref, before_ref, up_ref, to_after_ref, to_before_ref):
    for k, lanes in enumerate(half_columns(c, after_ref.shape[1])):
        to = slice(k * 256, k * 256 + 256)
        to_after_ref[:, to] = (after_ref[:, lanes].astype(F32) + down_ref[:, lanes].astype(F32)).astype(BF16)
        to_before_ref[:, to] = (before_ref[:, lanes].astype(F32) + up_ref[:, lanes].astype(F32)).astype(BF16)


def relay(c, *arrays):
    rows, width = arrays[0].shape
    vmem = pl.BlockSpec(memory_space=pltpu.VMEM)
    return pl.pallas_call(
        functools.partial(relay_kernel, c),
        out_shape=(shape((rows, width // 2), BF16),) * 2,
        in_specs=[vmem] * 4,
        out_specs=(vmem, vmem),
        compiler_params=params(),
        name="relay",
    )(*arrays)


def total_kernel(c, near_top, top_a, top_b, near_bottom, bottom_a, bottom_b, *refs):
    own, down, up, across = refs[-4:]
    for k, lanes in enumerate(half_columns(c, near_top.shape[1])):
        at = slice(k * 256, k * 256 + 256)
        for near, a, b, first, second in (
            (near_top, top_a, top_b, own, down), (near_bottom, bottom_a, bottom_b, up, across)
        ):
            total = near[:, lanes].astype(F32) + a[:, lanes].astype(F32) + b[:, at].astype(F32)
            first[:, at] = total[:SLOTS].astype(BF16)
            second[:, at] = total[SLOTS:].astype(BF16)


def total(c, *arrays):
    rows, width = arrays[0].shape
    vmem = pl.BlockSpec(memory_space=pltpu.VMEM)
    return pl.pallas_call(
        functools.partial(total_kernel, c),
        out_shape=(shape((SLOTS, width // 2), BF16),) * 4,
        in_specs=[vmem] * 6 + [pl.BlockSpec(memory_space=pl.ANY)] * (len(arrays) - 6),
        out_specs=(vmem,) * 4,
        compiler_params=params(),
        name="total",
    )(*arrays)


def after(values, *earlier):
    return lax.optimization_barrier((values, earlier))[0]


def experts(rows, weights):
    last, following = along_first(rows, 1), along_first(rows, -1)
    across_top = along_first(last[: SLOTS // 2], 1)
    across_bottom = along_first(following[SLOTS // 2 :], -1)
    near_top = jnp.concatenate([rows, last], axis=0)
    near_bottom = jnp.concatenate([following, across_top, across_bottom], axis=0)
    before_top = along_second(near_top, 1)
    after_bottom = along_second(near_bottom, -1)
    out_near_top, out_near_bottom = expert(near_top, near_bottom, weights)
    before_top, after_bottom = after((before_top, after_bottom), out_near_top)
    far_top = along_second(before_top, 1)
    far_bottom = along_second(after_bottom, -1)
    out_before_top, out_after_bottom = expert(before_top, after_bottom, weights)
    later_top, later_bottom = after((near_top, near_bottom), out_before_top)
    after_top = along_second(later_top, -1)
    before_bottom = along_second(later_bottom, 1)
    out_far_top, out_far_bottom = expert(*after((far_top, far_bottom), out_before_top), weights)
    relay_down = along_second(out_far_top, 1)
    relay_up = along_second(out_far_bottom, -1)
    first_back = after((out_before_top, out_after_bottom), out_far_top)
    top_a = along_second(first_back[0], -1)
    bottom_a = along_second(first_back[1], 1)
    second = after((after_top, before_bottom), relay_down, relay_up)
    out_after_top, out_before_bottom = expert(*second, weights)
    terms, order = [], ()
    for c in range(2):
        arrays = after((out_after_top, relay_down, out_before_bottom, relay_up), *order)
        to_after, to_before = relay(c, *arrays)
        order = (to_after,)
        top_b = along_second(to_after, 1)
        bottom_b = along_second(to_before, -1)
        sums = (out_near_top, top_a, top_b, out_near_bottom, bottom_a, bottom_b)
        level = (to_sibling(top_b[:16, :128]),) if c == 0 else ()
        own, down, up, across = total(c, *sums, *level)
        terms.append((own, along_first(down, -1), along_first(up, 1), along_first(across, 2)))
    return terms


def weigh_kernel(where_ref, a_ref, b_ref, c_ref, d_ref, weight_ref, keep_ref, give_ref):
    rows = (a_ref[...].astype(F32) + b_ref[...].astype(F32)) + (c_ref[...].astype(F32) + d_ref[...].astype(F32))
    weighted = (rows * weight_ref[:, :1]).astype(BF16)
    _, mine, _, _ = place_of(where_ref)
    for core in range(2):

        @pl.when(mine == core)
        def _():
            for k in range(SIDE):
                to = slice(k * 256, (k + 1) * 256)
                for out, e in ((keep_ref, 2 * k + core), (give_ref, 2 * k + 1 - core)):
                    out[:, to] = weighted[:, e * 256 : (e + 1) * 256]


def weigh(where, terms, slot_weight):
    vmem = pl.BlockSpec(memory_space=pltpu.VMEM)
    return pl.pallas_call(
        weigh_kernel,
        out_shape=(shape((SLOTS, SIDE * 256), BF16),) * 2,
        in_specs=[pl.BlockSpec(memory_space=pltpu.SMEM)] + [vmem] * 5,
        out_specs=(vmem, vmem),
        compiler_params=params(),
        name="weigh",
    )(where, *terms, slot_weight)


def place_kernel(where_ref, keep_ref, got_ref, onehot_ref, own_ref, next_ref, last_ref, across_ref, scr):
    rows = jnp.concatenate([keep_ref[...], got_ref[...]], axis=0)
    placed = lax.dot_general(onehot_ref[...], rows, (((0,), (0,)), ((), ())), preferred_element_type=F32)
    for k in range(SIDE):
        scr[k] = placed[:, k * 256 : (k + 1) * 256]
    y, _, _, _ = place_of(where_ref)
    for by, out in ((0, own_ref), (1, next_ref), (3, last_ref), (2, across_ref)):
        out[...] = scr[(y + by) & 3].astype(out.dtype)


def place(where, keep, got, onehot):
    count = onehot.shape[1]
    vmem = pl.BlockSpec(memory_space=pltpu.VMEM)
    return pl.pallas_call(
        place_kernel,
        out_shape=(shape((count, 256), F32),) + (shape((count, 256), BF16),) * 3,
        in_specs=[pl.BlockSpec(memory_space=pltpu.SMEM)] + [vmem] * 3,
        out_specs=(vmem,) * 4,
        scratch_shapes=[pltpu.VMEM((SIDE, count, 256), F32)],
        compiler_params=params(),
        name="place",
    )(where, keep, got, onehot)


def residual_kernel(where_ref, tokens_ref, own_ref, a_ref, b_ref, c_ref, mixed_ref):
    summed = (own_ref[...] + a_ref[...].astype(F32)) + (b_ref[...].astype(F32) + c_ref[...].astype(F32))
    mixed_ref[...] = (tokens_ref[...].astype(F32) + summed).astype(BF16)


def residual(c, where, tokens, own, others):
    count, cols = own.shape
    whole = pl.BlockSpec((count, cols), lambda i, where: (0, 0))
    return pl.pallas_call(
        residual_kernel,
        out_shape=shape((count, cols), BF16),
        grid_spec=pltpu.PrefetchScalarGridSpec(
            num_scalar_prefetch=1,
            grid=(1,),
            in_specs=[pl.BlockSpec((count, cols), lambda i, where: (0, 2 * where[0] + c))] + [whole] * 4,
            out_specs=whole,
        ),
        compiler_params=params(),
        name="residual",
    )(where, tokens, own, *others)


def spread(per_head, lanes):
    heads = per_head.shape[1]
    pairs = []
    first = lax.broadcasted_iota(jnp.int32, (per_head.shape[0], 2 * HEAD_DIM), 1) < HEAD_DIM
    for k in range(heads // 2):
        pairs.append(jnp.where(first, per_head[:, 2 * k : 2 * k + 1], per_head[:, 2 * k + 1 : 2 * k + 2]))
    return jnp.concatenate(pairs, axis=1)


def project_kernel(c, where_ref, mine_ref, other_ref, gain_ref, in_w_ref, write_w_ref, read_w_ref, step_w_ref, *refs):
    y, core, _, _ = place_of(where_ref)
    squares, scaled, step_w = 0.0, [], []
    for e in range(8):
        away = (e // 2 + SIDE - y) & 3
        slot = jnp.where(away == 0, 0, jnp.where(away == 3, 1, away + 1))
        values = jnp.where(core == e % 2, mine_ref[slot], other_ref[slot]).astype(F32)
        squares += jnp.sum(values * values, axis=1, keepdims=True)
        scaled.append((values * gain_ref[e, c]).astype(BF16))
        step_w.append(step_w_ref[:, e * 512 + c * 256 : e * 512 + c * 256 + 256])
    scaled = jnp.concatenate(scaled, axis=1)

    def rows(ref):
        return ref[:, c].reshape(scaled.shape[1], ref.shape[3])

    write_read = jnp.concatenate([rows(write_w_ref), rows(read_w_ref)], axis=1)
    accs = [
        jnp.dot(scaled, rows(in_w_ref), preferred_element_type=F32),
        jnp.dot(scaled, write_read, preferred_element_type=F32),
        lax.dot_general(
            scaled, jnp.concatenate(step_w, axis=1), (((1,), (1,)), ((), ())), preferred_element_type=F32
        ),
        jnp.broadcast_to(squares, (squares.shape[0], 128)),
    ]
    if c == 0:
        for out, acc in zip(refs, accs):
            out[...] = acc
    else:
        before, (bias_ref, decay_ref) = refs[:4], refs[4:6]
        accs = [acc + ref[...] for acc, ref in zip(accs, before)]
        projected(where_ref, bias_ref, decay_ref, refs[6:15], accs, refs[15], 8 * 512)


def projected(where_ref, bias_ref, decay_ref, outs, accs, state_scr, width):
    in_acc, write_read, step_acc, square_acc = accs
    x_ref, write_ref, read_ref, step_ref, cum_ref = outs[:5]
    count, heads = step_acc.shape
    scale = lax.rsqrt(square_acc[:, :1] / width + EPSILON)
    x = (in_acc * scale).astype(BF16)
    x_ref[...] = x
    write = (write_read[:, :STATE] * scale).astype(BF16)
    write_ref[...] = write
    read_ref[...] = (write_read[:, STATE:] * scale).astype(BF16)
    raw = step_acc * scale + bias_ref[...]
    step = jnp.maximum(raw, 0.0) + jnp.log1p(jnp.exp(-jnp.abs(raw)))
    step_ref[...] = step
    log_decay = -step * jnp.exp(decay_ref[...])
    lower = lax.broadcasted_iota(jnp.int32, (count, count), 0) >= lax.broadcasted_iota(jnp.int32, (count, count), 1)
    cum = jnp.dot(lower.astype(F32), log_decay, preferred_element_type=F32, precision=PRECISE)
    cum_ref[...] = cum
    last = cum[count - 1 :, :]
    to_end = jnp.exp(last - cum) * step
    weighted = (x.astype(F32) * spread(to_end, x.shape[1])).astype(BF16)
    state = lax.dot_general(write, weighted, (((0,), (0,)), ((), ())), preferred_element_type=F32)
    whole = spread(last, x.shape[1])
    high = whole.astype(BF16).astype(F32)
    row = lax.broadcasted_iota(jnp.int32, (16, x.shape[1]), 0)
    log_rows = jnp.where(row == 0, high, jnp.where(row == 1, whole - high, 0.0)).astype(BF16)
    cols = x.shape[1] // SIDE
    for q in range(SIDE):
        lanes = slice(q * cols, (q + 1) * cols)
        state_scr[q, :STATE, :] = state[:, lanes].astype(BF16)
        state_scr[q, STATE:, :] = log_rows[:, lanes]
    _, _, _, at = place_of(where_ref)
    for by, out in zip((0, 1, 3, 2), outs[5:]):
        out[...] = state_scr[(at + by) & 3]


def project(c, where, mine, other, gain, weights, *more):
    _, count, cols = mine.shape
    lanes, heads = weights[0].shape[1], weights[3].shape[1]
    smem, vmem = pl.BlockSpec(memory_space=pltpu.SMEM), pl.BlockSpec(memory_space=pltpu.VMEM)
    cut = [w.reshape(8, 2, cols, w.shape[1]) for w in weights[:3]]
    if c == 0:
        outs = tuple(shape((count, n), F32) for n in (lanes, 2 * STATE, heads, 128))
        scratch = []
    else:
        quarter = (STATE + 16, lanes // SIDE)
        outs = (
            shape((count, lanes), BF16), shape((count, STATE), BF16), shape((count, STATE), BF16),
            shape((count, heads), F32), shape((count, heads), F32),
        ) + (shape(quarter, BF16),) * 4
        scratch = [pltpu.VMEM((SIDE,) + quarter, BF16)]
    return pl.pallas_call(
        functools.partial(project_kernel, c),
        out_shape=outs,
        in_specs=[smem] + [vmem] * (7 + len(more)),
        out_specs=(vmem,) * len(outs),
        scratch_shapes=scratch,
        compiler_params=params(),
        name="project",
    )(where, mine, other, gain.reshape(8, 2, 1, cols), *cut, weights[3].T, *more)


def inside_kernel(x_ref, write_ref, read_ref, step_ref, cum_ref, skip_ref, out_ref):
    count, heads = step_ref.shape
    span = count // 2
    scores = lax.dot_general(read_ref[...], write_ref[...], (((1,), (1,)), ((), ())), preferred_element_type=F32)
    cum = cum_ref[...]
    cum_t, step_t = cum.T, step_ref[...].T
    causal = lax.broadcasted_iota(jnp.int32, (span, span), 0) >= lax.broadcasted_iota(jnp.int32, (span, span), 1)
    low, high = slice(0, span), slice(span, count)

    def mixing(h, rows, columns):
        gaps = cum[rows, h : h + 1] - cum_t[h : h + 1, columns]
        if rows == columns:
            gaps = jnp.where(causal, gaps, -jnp.inf)
        return (scores[rows, columns] * jnp.exp(gaps) * step_t[h : h + 1, columns]).astype(BF16)

    for h in range(heads):
        lanes = slice(h * HEAD_DIM, (h + 1) * HEAD_DIM)
        x = x_ref[:, lanes]
        skipped = skip_ref[0, h] * x.astype(F32)
        top = jnp.dot(mixing(h, low, low), x[low], preferred_element_type=F32)
        below = jnp.concatenate([mixing(h, high, low), mixing(h, high, high)], axis=1)
        bottom = jnp.dot(below, x, preferred_element_type=F32)
        out_ref[:, lanes] = jnp.concatenate([top, bottom], axis=0) + skipped


def inside(x, write, read, step, cum, skip_gain):
    vmem = pl.BlockSpec(memory_space=pltpu.VMEM)
    return pl.pallas_call(
        inside_kernel,
        out_shape=shape(x.shape, F32),
        in_specs=[vmem] * 5 + [pl.BlockSpec(memory_space=pltpu.SMEM)],
        out_specs=vmem,
        compiler_params=params(),
        cost_estimate=pl.CostEstimate(flops=2 * 10**9, bytes_accessed=2 * 10**6, transcendentals=10**6),
        name="inside",
    )(x, write, read, step, cum, skip_gain.reshape(1, -1))


def log_of(ref):
    return ref[STATE : STATE + 1, :].astype(F32) + ref[STATE + 1 : STATE + 2, :].astype(F32)


def weights_before(here, places, logs):
    terms = []
    for s in places:
        between = sum(jnp.where((s < u) & (u < here), log, 0.0) for u, log in zip(places, logs))
        terms.append(jnp.where(s < here, jnp.exp(between), 0.0))
    return terms


def row_total_kernel(where_ref, own_ref, last_ref, next_ref, across_ref, total_ref):
    _, _, _, here = place_of(where_ref)
    refs = (own_ref, last_ref, next_ref, across_ref)
    places = [here, (here + 3) & 3, (here + 1) & 3, (here + 2) & 3]
    logs = [log_of(ref) for ref in refs]
    until_end = [jnp.exp(sum(jnp.where(s < u, log, 0.0) for u, log in zip(places, logs))) for s in places]
    total_ref[:STATE, :] = sum(w * ref[:STATE, :].astype(F32) for w, ref in zip(until_end, refs)).astype(BF16)
    whole = sum(logs)
    top = whole.astype(BF16).astype(F32)
    row = lax.broadcasted_iota(jnp.int32, (16, whole.shape[1]), 0)
    total_ref[STATE:, :] = jnp.where(row == 0, top, jnp.where(row == 1, whole - top, 0.0)).astype(BF16)


def row_total(where, parts):
    vmem = pl.BlockSpec(memory_space=pltpu.VMEM)
    return pl.pallas_call(
        row_total_kernel,
        out_shape=shape(parts[0].shape, BF16),
        in_specs=[pl.BlockSpec(memory_space=pltpu.SMEM)] + [vmem] * 4,
        out_specs=vmem,
        compiler_params=params(),
        name="row_total",
    )(where, *parts)


def carry_kernel(where_ref, *refs):
    parts, earlier, outs = refs[:4], refs[4:7], refs[7:]
    _, _, z, here = place_of(where_ref)
    rows = [(z + 3) & 3, (z + 1) & 3, (z + 2) & 3]
    before = weights_before(z, rows, [log_of(ref) for ref in earlier])
    to_row = sum(w * ref[:STATE, :].astype(F32) for w, ref in zip(before, earlier))
    places = [here, (here + 3) & 3, (here + 1) & 3, (here + 2) & 3]
    logs = [log_of(ref) for ref in parts]
    for by, out in zip((0, 1, 3, 2), outs):
        target = (here + by) & 3
        gone = sum(jnp.where(s < target, log, 0.0) for s, log in zip(places, logs))
        state = jnp.exp(gone) * to_row
        for w, ref in zip(weights_before(target, places, logs), parts):
            state += w * ref[:STATE, :].astype(F32)
        out[...] = state.astype(BF16)


def carry(where, parts, earlier):
    vmem = pl.BlockSpec(memory_space=pltpu.VMEM)
    return pl.pallas_call(
        carry_kernel,
        out_shape=(shape((STATE, parts[0].shape[1]), BF16),) * 4,
        in_specs=[pl.BlockSpec(memory_space=pltpu.SMEM)] + [vmem] * 7,
        out_specs=(vmem,) * 4,
        compiler_params=params(),
        name="carry",
    )(where, *parts, *earlier)


def finish_kernel(where_ref, own_ref, last_ref, next_ref, across_ref, read_ref, cum_ref, inside_ref, out_ref, scr):
    _, _, _, here = place_of(where_ref)
    for by, ref in ((0, own_ref), (3, last_ref), (1, next_ref), (2, across_ref)):
        scr[(here + by) & 3] = ref[...]
    cols = own_ref.shape[1]
    decayed = spread(jnp.exp(cum_ref[...]), SIDE * cols)
    for q in range(SIDE):
        lanes = slice(q * cols, (q + 1) * cols)
        from_prior = jnp.dot(read_ref[...], scr[q], preferred_element_type=F32)
        out_ref[:, lanes] = (inside_ref[:, lanes] + decayed[:, lanes] * from_prior).astype(BF16)


def finish(where, parts, read, cum, within):
    vmem = pl.BlockSpec(memory_space=pltpu.VMEM)
    return pl.pallas_call(
        finish_kernel,
        out_shape=shape(within.shape, BF16),
        in_specs=[pl.BlockSpec(memory_space=pltpu.SMEM)] + [vmem] * 7,
        out_specs=vmem,
        scratch_shapes=[pltpu.VMEM((SIDE,) + parts[0].shape, BF16)],
        compiler_params=params(),
        name="finish",
    )(where, *parts, read, cum, within)


def body(
    tokens,
    routes,
    route_weight,
    moe_gain,
    gate_weight,
    up_weight,
    down_weight,
    ssd_gain,
    input_weight,
    write_weight,
    read_weight,
    step_weight,
    step_bias,
    decay_log,
    skip_gain,
):
    where = jnp.stack([lax.axis_index("expert"), lax.axis_index("frame")]).astype(jnp.int32)
    rows, onehot, slot_weight = pick(where, tokens, routes, route_weight, moe_gain)
    halves = experts(rows, (gate_weight[0], up_weight[0], down_weight[0]))
    weights = (input_weight, write_weight, read_weight, step_weight)
    mixed, more, order = [], (), ()
    for c in range(2):
        keep, give = weigh(where, after(halves[c], *order), slot_weight)
        own, to_next, to_last, to_across = place(where, keep, to_sibling(give), onehot)
        order = (own,)
        others = (along_y(to_next, 1), along_y(to_last, -1), along_y(to_across, 2))
        half = residual(c, where, tokens, own, others)
        mixed.append(half)
        mine = jnp.stack([half, along_y(half, 1), along_y(half, -1), along_y(half, 2)])
        if c == 1:
            more = (*more, step_bias.reshape(1, -1), decay_log.reshape(1, -1))
        more = project(c, where, mine, to_sibling(mine), ssd_gain, weights, *more)
    inputs, write, read, step, cum, state, to_next, to_last, to_across = more
    parts = (state, along_x(to_next, 1), along_x(to_last, -1), along_x(to_across, 2))
    row = row_total(where, parts)
    earlier = (along_z(row, 1), along_z(row, -1), along_z(row, 2))
    within = inside(inputs, write, read, step, cum, skip_gain)
    prior, to_next, to_last, to_across = carry(where, parts, earlier)
    carried = (prior, along_x(to_next, 1), along_x(to_last, -1), along_x(to_across, 2))
    ssd_out = finish(where, carried, read, cum, within)
    return (jnp.concatenate(mixed, axis=1), ssd_out)


def solution(mesh):
    placed = (
        P("frame", None),
        P("frame", None),
        P("frame", None),
        P(),
        P("expert", "frame", None),
        P("expert", "frame", None),
        P("expert", "frame", None),
        P(),
        P(None, "expert"),
        P(None, "expert"),
        P(None, "expert"),
        P(None, "expert"),
        P("expert"),
        P("expert"),
        P("expert"),
    )
    return jax.shard_map(
        body,
        mesh=mesh,
        in_specs=placed,
        out_specs=(P("frame", "expert"), P("frame", "expert")),
        check_vma=False,
    )
```

```python
import functools

import jax
import jax.numpy as jnp
from jax import lax
from jax.experimental import pallas as pl
from jax.experimental.pallas import tpu as pltpu
from jax.sharding import PartitionSpec as P

HEAD_DIM = 64
STATE = 128
SLOTS = 96
SIDE = 4
EPSILON = 1e-06
PRECISE = lax.Precision.HIGHEST
AXES = ("expert", "frame")
F32, BF16 = jnp.float32, jnp.bfloat16


def routes_of(rule):
    pairs = []
    for y in range(SIDE):
        for core in range(2):
            for z in range(SIDE):
                for x in range(SIDE):
                    ny, nc, nz, nx = rule(y, core, z, x)
                    source = (y * 2 + core) * 16 + z * SIDE + x
                    target = ((ny % SIDE) * 2 + nc % 2) * 16 + (nz % SIDE) * SIDE + nx % SIDE
                    pairs.append((source, target))
    return pairs


def send(array, rule):
    return lax.ppermute(array, AXES, routes_of(rule))


def along_first(array, by):
    return send(array, lambda y, c, z, x: (y, c, z + by * c, x + by * (1 - c)))


def along_second(array, by):
    return send(array, lambda y, c, z, x: (y, c, z + by * (1 - c), x + by * c))


def along_x(array, by):
    return send(array, lambda y, c, z, x: (y, c, z, x + by))


def along_z(array, by):
    return send(array, lambda y, c, z, x: (y, c, z + by, x))


def along_y(array, by):
    return send(array, lambda y, c, z, x: (y + by, c, z, x))


def to_sibling(array):
    return send(array, lambda y, c, z, x: (y, 1 - c, z, x))


def shape(dims, kind):
    return jax.ShapeDtypeStruct(dims, kind)


def params(mebibytes=20):
    return pltpu.CompilerParams(vmem_limit_bytes=mebibytes * 1024 * 1024)


SMALL = pl.CostEstimate(flops=10**6, bytes_accessed=10**5, transcendentals=0)


def place_of(where_ref):
    return where_ref[0] >> 1, where_ref[0] & 1, where_ref[1] >> 2, where_ref[1] & 3


def pick_kernel(where_ref, *refs):
    arrays, (rows_ref, onehot_ref, slot_weight_ref), held, sems = refs[:4], refs[4:7], refs[7:11], refs[11]
    copies = [pltpu.make_async_copy(source, to, sems.at[k]) for k, (source, to) in enumerate(zip(arrays, held))]
    for copy in copies:
        copy.start()
    tokens_ref, routes_ref, weight_ref, gain_ref = held
    count = tokens_ref.shape[0]
    upper = lax.broadcasted_iota(jnp.int32, (count, count), 0) <= lax.broadcasted_iota(jnp.int32, (count, count), 1)
    slot = lax.broadcasted_iota(jnp.int32, (SLOTS, count), 0)
    copies[1].wait()
    copies[2].wait()
    onehots = []
    for sibling in range(2):
        hits = routes_ref[...] == where_ref[0] ^ sibling
        chosen = jnp.max(hits.astype(F32), axis=0, keepdims=True)
        wide = jnp.broadcast_to(chosen, (SLOTS, count))
        place = jnp.dot(wide.astype(BF16), upper.astype(BF16), preferred_element_type=F32) - 1.0
        named = (place.astype(jnp.int32) == slot) & (wide > 0.0)
        onehots.append(jnp.where(named, 1.0, 0.0).astype(BF16))
        if sibling == 0:
            weights = jnp.sum(jnp.where(hits, weight_ref[...], 0.0), axis=0, keepdims=True)
            slot_weight = jnp.sum(jnp.where(named, weights, 0.0), axis=1, keepdims=True)
    onehot_ref[...] = jnp.concatenate(onehots, axis=0)
    slot_weight_ref[...] = jnp.broadcast_to(slot_weight, slot_weight_ref.shape)
    copies[0].wait()
    copies[3].wait()
    picked = jnp.dot(onehots[0], tokens_ref[...], preferred_element_type=F32)
    mean_sq = jnp.mean(picked * picked, axis=1, keepdims=True)
    rows_ref[...] = (picked * lax.rsqrt(mean_sq + EPSILON) * gain_ref[...]).astype(BF16)


def pick(where, tokens, routes, route_weight, gain):
    count, width = tokens.shape
    smem, vmem = pl.BlockSpec(memory_space=pltpu.SMEM), pl.BlockSpec(memory_space=pltpu.VMEM)
    arrays = (tokens, routes.T, route_weight.T, gain.reshape(1, width))
    return pl.pallas_call(
        pick_kernel,
        out_shape=(shape((SLOTS, width), BF16), shape((2 * SLOTS, count), BF16), shape((SLOTS, 128), F32)),
        in_specs=[smem] + [pl.BlockSpec(memory_space=pltpu.HBM)] * 4,
        out_specs=(vmem, vmem, vmem),
        scratch_shapes=[pltpu.VMEM(array.shape, array.dtype) for array in arrays] + [pltpu.SemaphoreType.DMA((4,))],
        compiler_params=params(),
        name="pick",
    )(where, *arrays)


def expert_kernel(top_ref, bottom_ref, gate_ref, up_ref, down_ref, out_top_ref, out_bottom_ref):
    half = top_ref.shape[0]
    rows = jnp.concatenate([top_ref[...], bottom_ref[...]], axis=0)
    by_row = (((1,), (1,)), ((), ()))
    gate = lax.dot_general(rows, gate_ref[...], by_row, preferred_element_type=F32)
    upper = lax.dot_general(rows, up_ref[...], by_row, preferred_element_type=F32)
    hidden = (gate / (1.0 + jnp.exp(-gate)) * upper).astype(BF16)
    out = jnp.dot(hidden, down_ref[...], preferred_element_type=F32).astype(BF16)
    out_top_ref[...] = out[:half]
    out_bottom_ref[...] = out[half:]


def expert(top, bottom, weights):
    vmem = pl.BlockSpec(memory_space=pltpu.VMEM)
    rows, width = top.shape
    units = weights[0].shape[0]
    return pl.pallas_call(
        expert_kernel,
        out_shape=(shape(top.shape, BF16),) * 2,
        in_specs=[vmem] * 5,
        out_specs=(vmem, vmem),
        compiler_params=params(28),
        cost_estimate=pl.CostEstimate(
            flops=12 * rows * width * units, bytes_accessed=6 * units * width + 8 * rows * width, transcendentals=0
        ),
        name="expert",
    )(top, bottom, *weights)


def half_columns(c, block):
    return [slice(k * 512 + c * 256, k * 512 + c * 256 + 256) for k in range(block // 512)]


def relay_kernel(c, after_ref, down_ref, before_ref, up_ref, to_after_ref, to_before_ref):
    for k, lanes in enumerate(half_columns(c, after_ref.shape[1])):
        to = slice(k * 256, k * 256 + 256)
        to_after_ref[:, to] = (after_ref[:, lanes].astype(F32) + down_ref[:, lanes].astype(F32)).astype(BF16)
        to_before_ref[:, to] = (before_ref[:, lanes].astype(F32) + up_ref[:, lanes].astype(F32)).astype(BF16)


def relay(c, *arrays):
    rows, width = arrays[0].shape
    vmem = pl.BlockSpec(memory_space=pltpu.VMEM)
    return pl.pallas_call(
        functools.partial(relay_kernel, c),
        out_shape=(shape((rows, width // 2), BF16),) * 2,
        in_specs=[vmem] * 4,
        out_specs=(vmem, vmem),
        compiler_params=params(),
        cost_estimate=SMALL,
        name="relay",
    )(*arrays)


def total_kernel(c, near_top, top_a, top_b, near_bottom, bottom_a, bottom_b, *refs):
    own, down, up, across = refs[-4:]
    for k, lanes in enumerate(half_columns(c, near_top.shape[1])):
        at = slice(k * 256, k * 256 + 256)
        for near, a, b, first, second in (
            (near_top, top_a, top_b, own, down), (near_bottom, bottom_a, bottom_b, up, across)
        ):
            total = near[:, lanes].astype(F32) + a[:, lanes].astype(F32) + b[:, at].astype(F32)
            first[:, at] = total[:SLOTS].astype(BF16)
            second[:, at] = total[SLOTS:].astype(BF16)


def total(c, *arrays):
    rows, width = arrays[0].shape
    vmem = pl.BlockSpec(memory_space=pltpu.VMEM)
    return pl.pallas_call(
        functools.partial(total_kernel, c),
        out_shape=(shape((SLOTS, width // 2), BF16),) * 4,
        in_specs=[vmem] * 6 + [pl.BlockSpec(memory_space=pl.ANY)] * (len(arrays) - 6),
        out_specs=(vmem,) * 4,
        compiler_params=params(),
        cost_estimate=SMALL,
        name="total",
    )(*arrays)


def after(values, *earlier):
    return lax.optimization_barrier((values, earlier))[0]


def experts(rows, weights):
    last, following = along_first(rows, 1), along_first(rows, -1)
    across_top = along_first(last[: SLOTS // 2], 1)
    across_bottom = along_first(following[SLOTS // 2 :], -1)
    near_top = jnp.concatenate([rows, last], axis=0)
    near_bottom = jnp.concatenate([following, across_top, across_bottom], axis=0)
    before_top = along_second(near_top, 1)
    after_bottom = along_second(near_bottom, -1)
    out_near_top, out_near_bottom = expert(near_top, near_bottom, weights)
    before_top, after_bottom = after((before_top, after_bottom), out_near_top)
    far_top = along_second(before_top, 1)
    far_bottom = along_second(after_bottom, -1)
    out_before_top, out_after_bottom = expert(before_top, after_bottom, weights)
    later_top, later_bottom = after((near_top, near_bottom), out_before_top)
    after_top = along_second(later_top, -1)
    before_bottom = along_second(later_bottom, 1)
    out_far_top, out_far_bottom = expert(*after((far_top, far_bottom), out_before_top), weights)
    relay_down = along_second(out_far_top, 1)
    relay_up = along_second(out_far_bottom, -1)
    first_back = after((out_before_top, out_after_bottom), out_far_top)
    top_a = along_second(first_back[0], -1)
    bottom_a = along_second(first_back[1], 1)
    second = after((after_top, before_bottom), relay_down, relay_up)
    out_after_top, out_before_bottom = expert(*second, weights)
    received, order = [], ()
    for c in range(2):
        arrays = after((out_after_top, relay_down, out_before_bottom, relay_up), *order)
        to_after, to_before = relay(c, *arrays)
        order = (to_after,)
        received.append((along_second(to_after, 1), along_second(to_before, -1)))
    level = to_sibling(received[1][0][:16, :128])
    terms = []
    for c, (top_b, bottom_b) in enumerate(received):
        sums = (out_near_top, top_a, top_b, out_near_bottom, bottom_a, bottom_b)
        own, down, up, across = total(c, *sums, level)
        terms.append((own, along_first(down, -1), along_first(up, 1), along_first(across, 2)))
    return terms


def weigh_kernel(where_ref, a_ref, b_ref, c_ref, d_ref, weight_ref, keep_ref, give_ref):
    rows = (a_ref[...].astype(F32) + b_ref[...].astype(F32)) + (c_ref[...].astype(F32) + d_ref[...].astype(F32))
    weighted = (rows * weight_ref[:, :1]).astype(BF16)
    _, mine, _, _ = place_of(where_ref)
    for core in range(2):

        @pl.when(mine == core)
        def _():
            for k in range(SIDE):
                to = slice(k * 256, (k + 1) * 256)
                for out, e in ((keep_ref, 2 * k + core), (give_ref, 2 * k + 1 - core)):
                    out[:, to] = weighted[:, e * 256 : (e + 1) * 256]


def weigh(where, terms, slot_weight):
    vmem = pl.BlockSpec(memory_space=pltpu.VMEM)
    return pl.pallas_call(
        weigh_kernel,
        out_shape=(shape((SLOTS, SIDE * 256), BF16),) * 2,
        in_specs=[pl.BlockSpec(memory_space=pltpu.SMEM)] + [vmem] * 5,
        out_specs=(vmem, vmem),
        compiler_params=params(),
        cost_estimate=SMALL,
        name="weigh",
    )(where, *terms, slot_weight)


def place_kernel(where_ref, keep_ref, got_ref, onehot_ref, own_ref, next_ref, last_ref, across_ref, scr):
    rows = jnp.concatenate([keep_ref[...], got_ref[...]], axis=0)
    placed = lax.dot_general(onehot_ref[...], rows, (((0,), (0,)), ((), ())), preferred_element_type=F32)
    for k in range(SIDE):
        scr[k] = placed[:, k * 256 : (k + 1) * 256]
    y, _, _, _ = place_of(where_ref)
    for by, out in ((0, own_ref), (1, next_ref), (3, last_ref), (2, across_ref)):
        out[...] = scr[(y + by) & 3].astype(out.dtype)


def place(where, keep, got, onehot):
    count = onehot.shape[1]
    vmem = pl.BlockSpec(memory_space=pltpu.VMEM)
    return pl.pallas_call(
        place_kernel,
        out_shape=(shape((count, 256), F32),) + (shape((count, 256), BF16),) * 3,
        in_specs=[pl.BlockSpec(memory_space=pltpu.SMEM)] + [vmem] * 3,
        out_specs=(vmem,) * 4,
        scratch_shapes=[pltpu.VMEM((SIDE, count, 256), F32)],
        compiler_params=params(),
        cost_estimate=SMALL,
        name="place",
    )(where, keep, got, onehot)


def residual_kernel(where_ref, tokens_ref, own_ref, a_ref, b_ref, c_ref, mixed_ref):
    summed = (own_ref[...] + a_ref[...].astype(F32)) + (b_ref[...].astype(F32) + c_ref[...].astype(F32))
    mixed_ref[...] = (tokens_ref[...].astype(F32) + summed).astype(BF16)


def residual(c, where, tokens, own, others):
    count, cols = own.shape
    whole = pl.BlockSpec((count, cols), lambda i, where: (0, 0))
    return pl.pallas_call(
        residual_kernel,
        out_shape=shape((count, cols), BF16),
        grid_spec=pltpu.PrefetchScalarGridSpec(
            num_scalar_prefetch=1,
            grid=(1,),
            in_specs=[pl.BlockSpec((count, cols), lambda i, where: (0, 2 * where[0] + c))] + [whole] * 4,
            out_specs=whole,
        ),
        compiler_params=params(),
        cost_estimate=SMALL,
        name="residual",
    )(where, tokens, own, *others)


def spread(per_head, lanes):
    heads = per_head.shape[1]
    pairs = []
    first = lax.broadcasted_iota(jnp.int32, (per_head.shape[0], 2 * HEAD_DIM), 1) < HEAD_DIM
    for k in range(heads // 2):
        pairs.append(jnp.where(first, per_head[:, 2 * k : 2 * k + 1], per_head[:, 2 * k + 1 : 2 * k + 2]))
    return jnp.concatenate(pairs, axis=1)


def project_kernel(c, where_ref, mine_ref, other_ref, gain_ref, in_w_ref, write_w_ref, read_w_ref, step_w_ref, *refs):
    y, core, _, _ = place_of(where_ref)
    squares, scaled, step_w = 0.0, [], []
    for e in range(8):
        away = (e // 2 + SIDE - y) & 3
        slot = jnp.where(away == 0, 0, jnp.where(away == 3, 1, away + 1))
        values = jnp.where(core == e % 2, mine_ref[slot], other_ref[slot]).astype(F32)
        squares += jnp.sum(values * values, axis=1, keepdims=True)
        scaled.append((values * gain_ref[e, c]).astype(BF16))
        step_w.append(step_w_ref[:, e * 512 + c * 256 : e * 512 + c * 256 + 256])
    scaled = jnp.concatenate(scaled, axis=1)

    def rows(ref):
        return ref[:, c].reshape(scaled.shape[1], ref.shape[3])

    write_read = jnp.concatenate([rows(write_w_ref), rows(read_w_ref)], axis=1)
    accs = [
        jnp.dot(scaled, rows(in_w_ref), preferred_element_type=F32),
        jnp.dot(scaled, write_read, preferred_element_type=F32),
        lax.dot_general(
            scaled, jnp.concatenate(step_w, axis=1), (((1,), (1,)), ((), ())), preferred_element_type=F32
        ),
        jnp.broadcast_to(squares, (squares.shape[0], 128)),
    ]
    if c == 0:
        for out, acc in zip(refs, accs):
            out[...] = acc
    else:
        before, (bias_ref, decay_ref) = refs[:4], refs[4:6]
        accs = [acc + ref[...] for acc, ref in zip(accs, before)]
        projected(where_ref, bias_ref, decay_ref, refs[6:15], accs, refs[15], 8 * 512)


def projected(where_ref, bias_ref, decay_ref, outs, accs, state_scr, width):
    in_acc, write_read, step_acc, square_acc = accs
    x_ref, write_ref, read_ref, step_ref, cum_ref = outs[:5]
    count, heads = step_acc.shape
    scale = lax.rsqrt(square_acc[:, :1] / width + EPSILON)
    x = (in_acc * scale).astype(BF16)
    x_ref[...] = x
    write = (write_read[:, :STATE] * scale).astype(BF16)
    write_ref[...] = write
    read_ref[...] = (write_read[:, STATE:] * scale).astype(BF16)
    raw = step_acc * scale + bias_ref[...]
    step = jnp.maximum(raw, 0.0) + jnp.log1p(jnp.exp(-jnp.abs(raw)))
    step_ref[...] = step
    log_decay = -step * jnp.exp(decay_ref[...])
    lower = lax.broadcasted_iota(jnp.int32, (count, count), 0) >= lax.broadcasted_iota(jnp.int32, (count, count), 1)
    cum = jnp.dot(lower.astype(F32), log_decay, preferred_element_type=F32, precision=PRECISE)
    cum_ref[...] = cum
    last = cum[count - 1 :, :]
    to_end = jnp.exp(last - cum) * step
    weighted = (x.astype(F32) * spread(to_end, x.shape[1])).astype(BF16)
    state = lax.dot_general(write, weighted, (((0,), (0,)), ((), ())), preferred_element_type=F32)
    whole = spread(last, x.shape[1])
    high = whole.astype(BF16).astype(F32)
    row = lax.broadcasted_iota(jnp.int32, (16, x.shape[1]), 0)
    log_rows = jnp.where(row == 0, high, jnp.where(row == 1, whole - high, 0.0)).astype(BF16)
    cols = x.shape[1] // SIDE
    for q in range(SIDE):
        lanes = slice(q * cols, (q + 1) * cols)
        state_scr[q, :STATE, :] = state[:, lanes].astype(BF16)
        state_scr[q, STATE:, :] = log_rows[:, lanes]
    _, _, _, at = place_of(where_ref)
    for by, out in zip((0, 1, 3, 2), outs[5:]):
        out[...] = state_scr[(at + by) & 3]


def project(c, where, mine, other, gain, weights, *more):
    _, count, cols = mine.shape
    lanes, heads = weights[0].shape[1], weights[3].shape[1]
    smem, vmem = pl.BlockSpec(memory_space=pltpu.SMEM), pl.BlockSpec(memory_space=pltpu.VMEM)
    cut = [w.reshape(8, 2, cols, w.shape[1]) for w in weights[:3]]
    if c == 0:
        outs = tuple(shape((count, n), F32) for n in (lanes, 2 * STATE, heads, 128))
        scratch = []
    else:
        quarter = (STATE + 16, lanes // SIDE)
        outs = (
            shape((count, lanes), BF16), shape((count, STATE), BF16), shape((count, STATE), BF16),
            shape((count, heads), F32), shape((count, heads), F32),
        ) + (shape(quarter, BF16),) * 4
        scratch = [pltpu.VMEM((SIDE,) + quarter, BF16)]
    return pl.pallas_call(
        functools.partial(project_kernel, c),
        out_shape=outs,
        in_specs=[smem] + [vmem] * (7 + len(more)),
        out_specs=(vmem,) * len(outs),
        scratch_shapes=scratch,
        compiler_params=params(),
        cost_estimate=pl.CostEstimate(flops=3 * 10**9, bytes_accessed=10**6, transcendentals=0),
        name="project",
    )(where, mine, other, gain.reshape(8, 2, 1, cols), *cut, weights[3].T, *more)


def inside_kernel(x_ref, write_ref, read_ref, step_ref, cum_ref, skip_ref, out_ref):
    count, heads = step_ref.shape
    span = count // 2
    scores = lax.dot_general(read_ref[...], write_ref[...], (((1,), (1,)), ((), ())), preferred_element_type=F32)
    cum = cum_ref[...]
    cum_t, step_t = cum.T, step_ref[...].T
    causal = lax.broadcasted_iota(jnp.int32, (span, span), 0) >= lax.broadcasted_iota(jnp.int32, (span, span), 1)
    low, high = slice(0, span), slice(span, count)

    def mixing(h, rows, columns):
        gaps = cum[rows, h : h + 1] - cum_t[h : h + 1, columns]
        if rows == columns:
            gaps = jnp.where(causal, gaps, -jnp.inf)
        return (scores[rows, columns] * jnp.exp(gaps) * step_t[h : h + 1, columns]).astype(BF16)

    for h in range(heads):
        lanes = slice(h * HEAD_DIM, (h + 1) * HEAD_DIM)
        x = x_ref[:, lanes]
        skipped = skip_ref[0, h] * x.astype(F32)
        top = jnp.dot(mixing(h, low, low), x[low], preferred_element_type=F32)
        below = jnp.concatenate([mixing(h, high, low), mixing(h, high, high)], axis=1)
        bottom = jnp.dot(below, x, preferred_element_type=F32)
        out_ref[:, lanes] = jnp.concatenate([top, bottom], axis=0) + skipped


def inside(x, write, read, step, cum, skip_gain):
    vmem = pl.BlockSpec(memory_space=pltpu.VMEM)
    return pl.pallas_call(
        inside_kernel,
        out_shape=shape(x.shape, F32),
        in_specs=[vmem] * 5 + [pl.BlockSpec(memory_space=pltpu.SMEM)],
        out_specs=vmem,
        compiler_params=params(),
        cost_estimate=pl.CostEstimate(flops=2 * 10**9, bytes_accessed=2 * 10**6, transcendentals=10**6),
        name="inside",
    )(x, write, read, step, cum, skip_gain.reshape(1, -1))


def log_of(ref):
    return ref[STATE : STATE + 1, :].astype(F32) + ref[STATE + 1 : STATE + 2, :].astype(F32)


def weights_before(here, places, logs):
    terms = []
    for s in places:
        between = sum(jnp.where((s < u) & (u < here), log, 0.0) for u, log in zip(places, logs))
        terms.append(jnp.where(s < here, jnp.exp(between), 0.0))
    return terms


def row_total_kernel(where_ref, own_ref, last_ref, next_ref, across_ref, total_ref):
    _, _, _, here = place_of(where_ref)
    refs = (own_ref, last_ref, next_ref, across_ref)
    places = [here, (here + 3) & 3, (here + 1) & 3, (here + 2) & 3]
    logs = [log_of(ref) for ref in refs]
    until_end = [jnp.exp(sum(jnp.where(s < u, log, 0.0) for u, log in zip(places, logs))) for s in places]
    total_ref[:STATE, :] = sum(w * ref[:STATE, :].astype(F32) for w, ref in zip(until_end, refs)).astype(BF16)
    whole = sum(logs)
    top = whole.astype(BF16).astype(F32)
    row = lax.broadcasted_iota(jnp.int32, (16, whole.shape[1]), 0)
    total_ref[STATE:, :] = jnp.where(row == 0, top, jnp.where(row == 1, whole - top, 0.0)).astype(BF16)


def row_total(where, parts):
    vmem = pl.BlockSpec(memory_space=pltpu.VMEM)
    return pl.pallas_call(
        row_total_kernel,
        out_shape=shape(parts[0].shape, BF16),
        in_specs=[pl.BlockSpec(memory_space=pltpu.SMEM)] + [vmem] * 4,
        out_specs=vmem,
        compiler_params=params(),
        cost_estimate=SMALL,
        name="row_total",
    )(where, *parts)


def carry_kernel(where_ref, *refs):
    parts, earlier, outs = refs[:4], refs[4:7], refs[7:]
    _, _, z, here = place_of(where_ref)
    rows = [(z + 3) & 3, (z + 1) & 3, (z + 2) & 3]
    before = weights_before(z, rows, [log_of(ref) for ref in earlier])
    to_row = sum(w * ref[:STATE, :].astype(F32) for w, ref in zip(before, earlier))
    places = [here, (here + 3) & 3, (here + 1) & 3, (here + 2) & 3]
    logs = [log_of(ref) for ref in parts]
    for by, out in zip((0, 1, 3, 2), outs):
        target = (here + by) & 3
        gone = sum(jnp.where(s < target, log, 0.0) for s, log in zip(places, logs))
        state = jnp.exp(gone) * to_row
        for w, ref in zip(weights_before(target, places, logs), parts):
            state += w * ref[:STATE, :].astype(F32)
        out[...] = state.astype(BF16)


def carry(where, parts, earlier):
    vmem = pl.BlockSpec(memory_space=pltpu.VMEM)
    return pl.pallas_call(
        carry_kernel,
        out_shape=(shape((STATE, parts[0].shape[1]), BF16),) * 4,
        in_specs=[pl.BlockSpec(memory_space=pltpu.SMEM)] + [vmem] * 7,
        out_specs=(vmem,) * 4,
        compiler_params=params(),
        cost_estimate=SMALL,
        name="carry",
    )(where, *parts, *earlier)


def finish_kernel(where_ref, own_ref, last_ref, next_ref, across_ref, read_ref, cum_ref, inside_ref, out_ref, scr):
    _, _, _, here = place_of(where_ref)
    for by, ref in ((0, own_ref), (3, last_ref), (1, next_ref), (2, across_ref)):
        scr[(here + by) & 3] = ref[...]
    cols = own_ref.shape[1]
    decayed = spread(jnp.exp(cum_ref[...]), SIDE * cols)
    for q in range(SIDE):
        lanes = slice(q * cols, (q + 1) * cols)
        from_prior = jnp.dot(read_ref[...], scr[q], preferred_element_type=F32)
        out_ref[:, lanes] = (inside_ref[:, lanes] + decayed[:, lanes] * from_prior).astype(BF16)


def finish(where, parts, read, cum, within):
    vmem = pl.BlockSpec(memory_space=pltpu.VMEM)
    return pl.pallas_call(
        finish_kernel,
        out_shape=shape(within.shape, BF16),
        in_specs=[pl.BlockSpec(memory_space=pltpu.SMEM)] + [vmem] * 7,
        out_specs=vmem,
        scratch_shapes=[pltpu.VMEM((SIDE,) + parts[0].shape, BF16)],
        compiler_params=params(),
        cost_estimate=SMALL,
        name="finish",
    )(where, *parts, read, cum, within)


def body(
    tokens,
    routes,
    route_weight,
    moe_gain,
    gate_weight,
    up_weight,
    down_weight,
    ssd_gain,
    input_weight,
    write_weight,
    read_weight,
    step_weight,
    step_bias,
    decay_log,
    skip_gain,
):
    where = jnp.stack([lax.axis_index("expert"), lax.axis_index("frame")]).astype(jnp.int32)
    rows, onehot, slot_weight = pick(where, tokens, routes, route_weight, moe_gain)
    halves = experts(rows, (gate_weight[0], up_weight[0], down_weight[0]))
    weights = (input_weight, write_weight, read_weight, step_weight)
    mixed, more, order = [], (), ()
    for c in range(2):
        keep, give = weigh(where, after(halves[c], *order), slot_weight)
        own, to_next, to_last, to_across = place(where, keep, to_sibling(give), onehot)
        others = (along_y(to_next, 1), along_y(to_last, -1), along_y(to_across, 2))
        half = residual(c, where, tokens, own, others)
        order = (own,)
        mixed.append(half)
        mine = jnp.stack([half, along_y(half, 1), along_y(half, -1), along_y(half, 2)])
        if c == 1:
            more = (*more, step_bias.reshape(1, -1), decay_log.reshape(1, -1))
        more = project(c, where, mine, to_sibling(mine), ssd_gain, weights, *more)
    inputs, write, read, step, cum, state, to_next, to_last, to_across = more
    parts = (state, along_x(to_next, 1), along_x(to_last, -1), along_x(to_across, 2))
    row = row_total(where, parts)
    earlier = (along_z(row, 1), along_z(row, -1), along_z(row, 2))
    within = inside(inputs, write, read, step, cum, skip_gain)
    prior, to_next, to_last, to_across = carry(where, parts, earlier)
    carried = (prior, along_x(to_next, 1), along_x(to_last, -1), along_x(to_across, 2))
    ssd_out = finish(where, carried, read, cum, within)
    return (jnp.concatenate(mixed, axis=1), ssd_out)


def solution(mesh):
    placed = (
        P("frame", None),
        P("frame", None),
        P("frame", None),
        P(),
        P("expert", "frame", None),
        P("expert", "frame", None),
        P("expert", "frame", None),
        P(),
        P(None, "expert"),
        P(None, "expert"),
        P(None, "expert"),
        P(None, "expert"),
        P("expert"),
        P("expert"),
        P("expert"),
    )
    return jax.shard_map(
        body,
        mesh=mesh,
        in_specs=placed,
        out_specs=(P("frame", "expert"), P("frame", "expert")),
        check_vma=False,
    )
```

```python
import functools

import jax
import jax.numpy as jnp
from jax import lax
from jax.experimental import pallas as pl
from jax.experimental.pallas import tpu as pltpu
from jax.sharding import PartitionSpec as P

HEAD_DIM = 64
STATE = 128
SLOTS = 96
SIDE = 4
EPSILON = 1e-06
PRECISE = lax.Precision.HIGHEST
AXES = ("expert", "frame")
F32, BF16 = jnp.float32, jnp.bfloat16


def routes_of(rule):
    pairs = []
    for y in range(SIDE):
        for core in range(2):
            for z in range(SIDE):
                for x in range(SIDE):
                    ny, nc, nz, nx = rule(y, core, z, x)
                    source = (y * 2 + core) * 16 + z * SIDE + x
                    target = ((ny % SIDE) * 2 + nc % 2) * 16 + (nz % SIDE) * SIDE + nx % SIDE
                    pairs.append((source, target))
    return pairs


def send(array, rule):
    return lax.ppermute(array, AXES, routes_of(rule))


def along_first(array, by):
    return send(array, lambda y, c, z, x: (y, c, z + by * c, x + by * (1 - c)))


def along_second(array, by):
    return send(array, lambda y, c, z, x: (y, c, z + by * (1 - c), x + by * c))


def along_x(array, by):
    return send(array, lambda y, c, z, x: (y, c, z, x + by))


def along_z(array, by):
    return send(array, lambda y, c, z, x: (y, c, z + by, x))


def along_y(array, by):
    return send(array, lambda y, c, z, x: (y + by, c, z, x))


def to_sibling(array):
    return send(array, lambda y, c, z, x: (y, 1 - c, z, x))


def shape(dims, kind):
    return jax.ShapeDtypeStruct(dims, kind)


def params(mebibytes=20):
    return pltpu.CompilerParams(vmem_limit_bytes=mebibytes * 1024 * 1024)


SMALL = pl.CostEstimate(flops=10**6, bytes_accessed=10**5, transcendentals=0)


def place_of(where_ref):
    return where_ref[0] >> 1, where_ref[0] & 1, where_ref[1] >> 2, where_ref[1] & 3


def pick_kernel(where_ref, *refs):
    arrays, (rows_ref, onehot_ref, slot_weight_ref), held, sems = refs[:4], refs[4:7], refs[7:11], refs[11]
    copies = [pltpu.make_async_copy(source, to, sems.at[k]) for k, (source, to) in enumerate(zip(arrays, held))]
    for copy in copies:
        copy.start()
    tokens_ref, routes_ref, weight_ref, gain_ref = held
    count = tokens_ref.shape[0]
    upper = lax.broadcasted_iota(jnp.int32, (count, count), 0) <= lax.broadcasted_iota(jnp.int32, (count, count), 1)
    slot = lax.broadcasted_iota(jnp.int32, (SLOTS, count), 0)
    copies[1].wait()
    copies[2].wait()
    onehots = []
    for sibling in range(2):
        hits = routes_ref[...] == where_ref[0] ^ sibling
        chosen = jnp.max(hits.astype(F32), axis=0, keepdims=True)
        wide = jnp.broadcast_to(chosen, (SLOTS, count))
        place = jnp.dot(wide.astype(BF16), upper.astype(BF16), preferred_element_type=F32) - 1.0
        named = (place.astype(jnp.int32) == slot) & (wide > 0.0)
        onehots.append(jnp.where(named, 1.0, 0.0).astype(BF16))
        if sibling == 0:
            weights = jnp.sum(jnp.where(hits, weight_ref[...], 0.0), axis=0, keepdims=True)
            slot_weight = jnp.sum(jnp.where(named, weights, 0.0), axis=1, keepdims=True)
    onehot_ref[...] = jnp.concatenate(onehots, axis=0)
    slot_weight_ref[...] = jnp.broadcast_to(slot_weight, slot_weight_ref.shape)
    copies[0].wait()
    copies[3].wait()
    picked = jnp.dot(onehots[0], tokens_ref[...], preferred_element_type=F32)
    mean_sq = jnp.mean(picked * picked, axis=1, keepdims=True)
    rows_ref[...] = (picked * lax.rsqrt(mean_sq + EPSILON) * gain_ref[...]).astype(BF16)


def pick(where, tokens, routes, route_weight, gain):
    count, width = tokens.shape
    smem, vmem = pl.BlockSpec(memory_space=pltpu.SMEM), pl.BlockSpec(memory_space=pltpu.VMEM)
    arrays = (tokens, routes.T, route_weight.T, gain.reshape(1, width))
    return pl.pallas_call(
        pick_kernel,
        out_shape=(shape((SLOTS, width), BF16), shape((2 * SLOTS, count), BF16), shape((SLOTS, 128), F32)),
        in_specs=[smem] + [pl.BlockSpec(memory_space=pltpu.HBM)] * 4,
        out_specs=(vmem, vmem, vmem),
        scratch_shapes=[pltpu.VMEM(array.shape, array.dtype) for array in arrays] + [pltpu.SemaphoreType.DMA((4,))],
        compiler_params=params(),
        name="pick",
    )(where, *arrays)


def expert_kernel(top_ref, bottom_ref, gate_ref, up_ref, down_ref, out_top_ref, out_bottom_ref):
    half = top_ref.shape[0]
    rows = jnp.concatenate([top_ref[...], bottom_ref[...]], axis=0)
    by_row = (((1,), (1,)), ((), ()))
    gate = lax.dot_general(rows, gate_ref[...], by_row, preferred_element_type=F32)
    upper = lax.dot_general(rows, up_ref[...], by_row, preferred_element_type=F32)
    hidden = (gate / (1.0 + jnp.exp(-gate)) * upper).astype(BF16)
    out = jnp.dot(hidden, down_ref[...], preferred_element_type=F32).astype(BF16)
    out_top_ref[...] = out[:half]
    out_bottom_ref[...] = out[half:]


def expert(top, bottom, weights):
    vmem = pl.BlockSpec(memory_space=pltpu.VMEM)
    rows, width = top.shape
    units = weights[0].shape[0]
    return pl.pallas_call(
        expert_kernel,
        out_shape=(shape(top.shape, BF16),) * 2,
        in_specs=[vmem] * 5,
        out_specs=(vmem, vmem),
        compiler_params=params(28),
        cost_estimate=pl.CostEstimate(
            flops=12 * rows * width * units, bytes_accessed=6 * units * width + 8 * rows * width, transcendentals=0
        ),
        name="expert",
    )(top, bottom, *weights)


def relay_kernel(after_ref, down_ref, before_ref, up_ref, to_after_ref, to_before_ref):
    to_after_ref[...] = (after_ref[...].astype(F32) + down_ref[...].astype(F32)).astype(BF16)
    to_before_ref[...] = (before_ref[...].astype(F32) + up_ref[...].astype(F32)).astype(BF16)


def relay(*arrays):
    vmem = pl.BlockSpec(memory_space=pltpu.VMEM)
    return pl.pallas_call(
        relay_kernel,
        out_shape=(shape(arrays[0].shape, BF16),) * 2,
        in_specs=[vmem] * 4,
        out_specs=(vmem, vmem),
        compiler_params=params(),
        cost_estimate=SMALL,
        name="relay",
    )(*arrays)


def total_kernel(near_top, top_a, top_b, near_bottom, bottom_a, bottom_b, level, *outs):
    for c in range(2):
        own, down, up, across = outs[4 * c : 4 * c + 4]
        for e in range(8):
            lanes, at = slice(e * 512 + c * 256, e * 512 + c * 256 + 256), slice(e * 256, e * 256 + 256)
            for near, a, b, first, second in (
                (near_top, top_a, top_b, own, down), (near_bottom, bottom_a, bottom_b, up, across)
            ):
                total = near[:, lanes].astype(F32) + a[:, lanes].astype(F32) + b[:, lanes].astype(F32)
                first[:, at] = total[:SLOTS].astype(BF16)
                second[:, at] = total[SLOTS:].astype(BF16)


def total(level, *arrays):
    vmem = pl.BlockSpec(memory_space=pltpu.VMEM)
    return pl.pallas_call(
        total_kernel,
        out_shape=(shape((SLOTS, arrays[0].shape[1] // 2), BF16),) * 8,
        in_specs=[vmem] * 6 + [pl.BlockSpec(memory_space=pl.ANY)],
        out_specs=(vmem,) * 8,
        compiler_params=params(),
        cost_estimate=SMALL,
        name="total",
    )(*arrays, level)


def plus(a, b):
    return (a.astype(F32) + b.astype(F32)).astype(BF16)


def after(values, *earlier):
    return lax.optimization_barrier((values, earlier))[0]


def experts(rows, weights):
    last, following = along_first(rows, 1), along_first(rows, -1)
    across_top = along_first(last[: SLOTS // 2], 1)
    across_bottom = along_first(following[SLOTS // 2 :], -1)
    near_top = jnp.concatenate([rows, last], axis=0)
    near_bottom = jnp.concatenate([following, across_top, across_bottom], axis=0)
    near_top = after(near_top, across_top, across_bottom)
    before_top = along_second(near_top, 1)
    after_bottom = along_second(near_bottom, -1)
    out_near_top, out_near_bottom = expert(near_top, near_bottom, weights)
    before_top, after_bottom = after((before_top, after_bottom), out_near_top)
    far_top = along_second(before_top, 1)
    far_bottom = along_second(after_bottom, -1)
    out_before_top, out_after_bottom = expert(before_top, after_bottom, weights)
    later_top, later_bottom = after((near_top, near_bottom), out_before_top)
    after_top = along_second(later_top, -1)
    before_bottom = along_second(later_bottom, 1)
    out_far_top, out_far_bottom = expert(*after((far_top, far_bottom), out_before_top), weights)
    relay_down = along_second(out_far_top, 1)
    relay_up = along_second(out_far_bottom, -1)
    first_back = after((out_before_top, out_after_bottom), out_far_top)
    top_a = along_second(first_back[0], -1)
    bottom_a = along_second(first_back[1], 1)
    second = after((after_top, before_bottom), relay_down, relay_up)
    out_after_top, out_before_bottom = expert(*second, weights)
    to_after, to_before = relay(out_after_top, relay_down, out_before_bottom, relay_up)
    top_b = along_second(to_after, 1)
    bottom_b = along_second(to_before, -1)
    level = to_sibling(sum(array[:16, :128] for array in (top_a, bottom_a, top_b, bottom_b)))
    sums = total(level, out_near_top, top_a, top_b, out_near_bottom, bottom_a, bottom_b)
    terms = []
    for c in range(2):
        own, down, up, across = sums[4 * c : 4 * c + 4]
        terms.append((own, along_first(down, -1), along_first(up, 1), along_first(across, 2)))
    return terms


def weigh_kernel(where_ref, a_ref, b_ref, c_ref, d_ref, weight_ref, keep_ref, give_ref):
    rows = (a_ref[...].astype(F32) + b_ref[...].astype(F32)) + (c_ref[...].astype(F32) + d_ref[...].astype(F32))
    weighted = (rows * weight_ref[:, :1]).astype(BF16)
    _, mine, _, _ = place_of(where_ref)
    for core in range(2):

        @pl.when(mine == core)
        def _():
            for k in range(SIDE):
                to = slice(k * 256, (k + 1) * 256)
                for out, e in ((keep_ref, 2 * k + core), (give_ref, 2 * k + 1 - core)):
                    out[:, to] = weighted[:, e * 256 : (e + 1) * 256]


def weigh(where, terms, slot_weight):
    vmem = pl.BlockSpec(memory_space=pltpu.VMEM)
    return pl.pallas_call(
        weigh_kernel,
        out_shape=(shape((SLOTS, SIDE * 256), BF16),) * 2,
        in_specs=[pl.BlockSpec(memory_space=pltpu.SMEM)] + [vmem] * 5,
        out_specs=(vmem, vmem),
        compiler_params=params(),
        cost_estimate=SMALL,
        name="weigh",
    )(where, *terms, slot_weight)


def place_kernel(where_ref, keep_ref, got_ref, onehot_ref, own_ref, next_ref, last_ref, across_ref, scr):
    rows = jnp.concatenate([keep_ref[...], got_ref[...]], axis=0)
    placed = lax.dot_general(onehot_ref[...], rows, (((0,), (0,)), ((), ())), preferred_element_type=F32)
    for k in range(SIDE):
        scr[k] = placed[:, k * 256 : (k + 1) * 256]
    y, _, _, _ = place_of(where_ref)
    for by, out in ((0, own_ref), (1, next_ref), (3, last_ref), (2, across_ref)):
        out[...] = scr[(y + by) & 3].astype(out.dtype)


def place(where, keep, got, onehot):
    count = onehot.shape[1]
    vmem = pl.BlockSpec(memory_space=pltpu.VMEM)
    return pl.pallas_call(
        place_kernel,
        out_shape=(shape((count, 256), F32),) + (shape((count, 256), BF16),) * 3,
        in_specs=[pl.BlockSpec(memory_space=pltpu.SMEM)] + [vmem] * 3,
        out_specs=(vmem,) * 4,
        scratch_shapes=[pltpu.VMEM((SIDE, count, 256), F32)],
        compiler_params=params(),
        cost_estimate=SMALL,
        name="place",
    )(where, keep, got, onehot)


def residual_kernel(where_ref, tokens_ref, own_ref, a_ref, b_ref, c_ref, mixed_ref):
    summed = (own_ref[...] + a_ref[...].astype(F32)) + (b_ref[...].astype(F32) + c_ref[...].astype(F32))
    mixed_ref[...] = (tokens_ref[...].astype(F32) + summed).astype(BF16)


def residual(c, where, tokens, own, others):
    count, cols = own.shape
    whole = pl.BlockSpec((count, cols), lambda i, where: (0, 0))
    return pl.pallas_call(
        residual_kernel,
        out_shape=shape((count, cols), BF16),
        grid_spec=pltpu.PrefetchScalarGridSpec(
            num_scalar_prefetch=1,
            grid=(1,),
            in_specs=[pl.BlockSpec((count, cols), lambda i, where: (0, 2 * where[0] + c))] + [whole] * 4,
            out_specs=whole,
        ),
        compiler_params=params(),
        cost_estimate=SMALL,
        name="residual",
    )(where, tokens, own, *others)


def spread(per_head, lanes):
    heads = per_head.shape[1]
    pairs = []
    first = lax.broadcasted_iota(jnp.int32, (per_head.shape[0], 2 * HEAD_DIM), 1) < HEAD_DIM
    for k in range(heads // 2):
        pairs.append(jnp.where(first, per_head[:, 2 * k : 2 * k + 1], per_head[:, 2 * k + 1 : 2 * k + 2]))
    return jnp.concatenate(pairs, axis=1)


def project_kernel(c, where_ref, mine_ref, other_ref, gain_ref, in_w_ref, write_w_ref, read_w_ref, step_w_ref, *refs):
    y, core, _, _ = place_of(where_ref)
    squares, scaled, step_w = 0.0, [], []
    for e in range(8):
        away = (e // 2 + SIDE - y) & 3
        slot = jnp.where(away == 0, 0, jnp.where(away == 3, 1, away + 1))
        values = jnp.where(core == e % 2, mine_ref[slot], other_ref[slot]).astype(F32)
        squares += jnp.sum(values * values, axis=1, keepdims=True)
        scaled.append((values * gain_ref[e, c]).astype(BF16))
        step_w.append(step_w_ref[:, e * 512 + c * 256 : e * 512 + c * 256 + 256])
    scaled = jnp.concatenate(scaled, axis=1)

    def rows(ref):
        return ref[:, c].reshape(scaled.shape[1], ref.shape[3])

    write_read = jnp.concatenate([rows(write_w_ref), rows(read_w_ref)], axis=1)
    accs = [
        jnp.dot(scaled, rows(in_w_ref), preferred_element_type=F32),
        jnp.dot(scaled, write_read, preferred_element_type=F32),
        lax.dot_general(
            scaled, jnp.concatenate(step_w, axis=1), (((1,), (1,)), ((), ())), preferred_element_type=F32
        ),
        jnp.broadcast_to(squares, (squares.shape[0], 128)),
    ]
    if c == 0:
        for out, acc in zip(refs, accs):
            out[...] = acc
    else:
        before, (bias_ref, decay_ref) = refs[:4], refs[4:6]
        accs = [acc + ref[...] for acc, ref in zip(accs, before)]
        projected(where_ref, bias_ref, decay_ref, refs[6:15], accs, refs[15], 8 * 512)


def projected(where_ref, bias_ref, decay_ref, outs, accs, state_scr, width):
    in_acc, write_read, step_acc, square_acc = accs
    x_ref, write_ref, read_ref, step_ref, cum_ref = outs[:5]
    count, heads = step_acc.shape
    scale = lax.rsqrt(square_acc[:, :1] / width + EPSILON)
    x = (in_acc * scale).astype(BF16)
    x_ref[...] = x
    write = (write_read[:, :STATE] * scale).astype(BF16)
    write_ref[...] = write
    read_ref[...] = (write_read[:, STATE:] * scale).astype(BF16)
    raw = step_acc * scale + bias_ref[...]
    step = jnp.maximum(raw, 0.0) + jnp.log1p(jnp.exp(-jnp.abs(raw)))
    step_ref[...] = step
    log_decay = -step * jnp.exp(decay_ref[...])
    lower = lax.broadcasted_iota(jnp.int32, (count, count), 0) >= lax.broadcasted_iota(jnp.int32, (count, count), 1)
    cum = jnp.dot(lower.astype(F32), log_decay, preferred_element_type=F32, precision=PRECISE)
    cum_ref[...] = cum
    last = cum[count - 1 :, :]
    to_end = jnp.exp(last - cum) * step
    weighted = (x.astype(F32) * spread(to_end, x.shape[1])).astype(BF16)
    state = lax.dot_general(write, weighted, (((0,), (0,)), ((), ())), preferred_element_type=F32)
    whole = spread(last, x.shape[1])
    high = whole.astype(BF16).astype(F32)
    row = lax.broadcasted_iota(jnp.int32, (16, x.shape[1]), 0)
    log_rows = jnp.where(row == 0, high, jnp.where(row == 1, whole - high, 0.0)).astype(BF16)
    cols = x.shape[1] // SIDE
    for q in range(SIDE):
        lanes = slice(q * cols, (q + 1) * cols)
        state_scr[q, :STATE, :] = state[:, lanes].astype(BF16)
        state_scr[q, STATE:, :] = log_rows[:, lanes]
    _, _, _, at = place_of(where_ref)
    for by, out in zip((0, 1, 3, 2), outs[5:]):
        out[...] = state_scr[(at + by) & 3]


def project(c, where, mine, other, gain, weights, *more):
    _, count, cols = mine.shape
    lanes, heads = weights[0].shape[1], weights[3].shape[1]
    smem, vmem = pl.BlockSpec(memory_space=pltpu.SMEM), pl.BlockSpec(memory_space=pltpu.VMEM)
    cut = [w.reshape(8, 2, cols, w.shape[1]) for w in weights[:3]]
    if c == 0:
        outs = tuple(shape((count, n), F32) for n in (lanes, 2 * STATE, heads, 128))
        scratch = []
    else:
        quarter = (STATE + 16, lanes // SIDE)
        outs = (
            shape((count, lanes), BF16), shape((count, STATE), BF16), shape((count, STATE), BF16),
            shape((count, heads), F32), shape((count, heads), F32),
        ) + (shape(quarter, BF16),) * 4
        scratch = [pltpu.VMEM((SIDE,) + quarter, BF16)]
    return pl.pallas_call(
        functools.partial(project_kernel, c),
        out_shape=outs,
        in_specs=[smem] + [vmem] * (7 + len(more)),
        out_specs=(vmem,) * len(outs),
        scratch_shapes=scratch,
        compiler_params=params(),
        cost_estimate=pl.CostEstimate(flops=3 * 10**9, bytes_accessed=10**6, transcendentals=0),
        name="project",
    )(where, mine, other, gain.reshape(8, 2, 1, cols), *cut, weights[3].T, *more)


def inside_kernel(x_ref, write_ref, read_ref, step_ref, cum_ref, skip_ref, out_ref):
    count, heads = step_ref.shape
    span = count // 2
    scores = lax.dot_general(read_ref[...], write_ref[...], (((1,), (1,)), ((), ())), preferred_element_type=F32)
    cum = cum_ref[...]
    cum_t, step_t = cum.T, step_ref[...].T
    causal = lax.broadcasted_iota(jnp.int32, (span, span), 0) >= lax.broadcasted_iota(jnp.int32, (span, span), 1)
    low, high = slice(0, span), slice(span, count)

    def mixing(h, rows, columns):
        gaps = cum[rows, h : h + 1] - cum_t[h : h + 1, columns]
        if rows == columns:
            gaps = jnp.where(causal, gaps, -jnp.inf)
        return (scores[rows, columns] * jnp.exp(gaps) * step_t[h : h + 1, columns]).astype(BF16)

    for h in range(heads):
        lanes = slice(h * HEAD_DIM, (h + 1) * HEAD_DIM)
        x = x_ref[:, lanes]
        skipped = skip_ref[0, h] * x.astype(F32)
        top = jnp.dot(mixing(h, low, low), x[low], preferred_element_type=F32)
        below = jnp.concatenate([mixing(h, high, low), mixing(h, high, high)], axis=1)
        bottom = jnp.dot(below, x, preferred_element_type=F32)
        out_ref[:, lanes] = jnp.concatenate([top, bottom], axis=0) + skipped


def inside(x, write, read, step, cum, skip_gain):
    vmem = pl.BlockSpec(memory_space=pltpu.VMEM)
    return pl.pallas_call(
        inside_kernel,
        out_shape=shape(x.shape, F32),
        in_specs=[vmem] * 5 + [pl.BlockSpec(memory_space=pltpu.SMEM)],
        out_specs=vmem,
        compiler_params=params(),
        cost_estimate=pl.CostEstimate(flops=2 * 10**9, bytes_accessed=2 * 10**6, transcendentals=10**6),
        name="inside",
    )(x, write, read, step, cum, skip_gain.reshape(1, -1))


def log_of(ref):
    return ref[STATE : STATE + 1, :].astype(F32) + ref[STATE + 1 : STATE + 2, :].astype(F32)


def weights_before(here, places, logs):
    terms = []
    for s in places:
        between = sum(jnp.where((s < u) & (u < here), log, 0.0) for u, log in zip(places, logs))
        terms.append(jnp.where(s < here, jnp.exp(between), 0.0))
    return terms


def row_total_kernel(where_ref, own_ref, last_ref, next_ref, across_ref, total_ref):
    _, _, _, here = place_of(where_ref)
    refs = (own_ref, last_ref, next_ref, across_ref)
    places = [here, (here + 3) & 3, (here + 1) & 3, (here + 2) & 3]
    logs = [log_of(ref) for ref in refs]
    until_end = [jnp.exp(sum(jnp.where(s < u, log, 0.0) for u, log in zip(places, logs))) for s in places]
    total_ref[:STATE, :] = sum(w * ref[:STATE, :].astype(F32) for w, ref in zip(until_end, refs)).astype(BF16)
    whole = sum(logs)
    top = whole.astype(BF16).astype(F32)
    row = lax.broadcasted_iota(jnp.int32, (16, whole.shape[1]), 0)
    total_ref[STATE:, :] = jnp.where(row == 0, top, jnp.where(row == 1, whole - top, 0.0)).astype(BF16)


def row_total(where, parts):
    vmem = pl.BlockSpec(memory_space=pltpu.VMEM)
    return pl.pallas_call(
        row_total_kernel,
        out_shape=shape(parts[0].shape, BF16),
        in_specs=[pl.BlockSpec(memory_space=pltpu.SMEM)] + [vmem] * 4,
        out_specs=vmem,
        compiler_params=params(),
        cost_estimate=SMALL,
        name="row_total",
    )(where, *parts)


def carry_kernel(where_ref, *refs):
    parts, earlier, outs = refs[:4], refs[4:7], refs[7:]
    _, _, z, here = place_of(where_ref)
    rows = [(z + 3) & 3, (z + 1) & 3, (z + 2) & 3]
    before = weights_before(z, rows, [log_of(ref) for ref in earlier])
    to_row = sum(w * ref[:STATE, :].astype(F32) for w, ref in zip(before, earlier))
    places = [here, (here + 3) & 3, (here + 1) & 3, (here + 2) & 3]
    logs = [log_of(ref) for ref in parts]
    for by, out in zip((0, 1, 3, 2), outs):
        target = (here + by) & 3
        gone = sum(jnp.where(s < target, log, 0.0) for s, log in zip(places, logs))
        state = jnp.exp(gone) * to_row
        for w, ref in zip(weights_before(target, places, logs), parts):
            state += w * ref[:STATE, :].astype(F32)
        out[...] = state.astype(BF16)


def carry(where, parts, earlier):
    vmem = pl.BlockSpec(memory_space=pltpu.VMEM)
    return pl.pallas_call(
        carry_kernel,
        out_shape=(shape((STATE, parts[0].shape[1]), BF16),) * 4,
        in_specs=[pl.BlockSpec(memory_space=pltpu.SMEM)] + [vmem] * 7,
        out_specs=(vmem,) * 4,
        compiler_params=params(),
        cost_estimate=SMALL,
        name="carry",
    )(where, *parts, *earlier)


def finish_kernel(where_ref, own_ref, last_ref, next_ref, across_ref, read_ref, cum_ref, inside_ref, out_ref, scr):
    _, _, _, here = place_of(where_ref)
    for by, ref in ((0, own_ref), (3, last_ref), (1, next_ref), (2, across_ref)):
        scr[(here + by) & 3] = ref[...]
    cols = own_ref.shape[1]
    decayed = spread(jnp.exp(cum_ref[...]), SIDE * cols)
    for q in range(SIDE):
        lanes = slice(q * cols, (q + 1) * cols)
        from_prior = jnp.dot(read_ref[...], scr[q], preferred_element_type=F32)
        out_ref[:, lanes] = (inside_ref[:, lanes] + decayed[:, lanes] * from_prior).astype(BF16)


def finish(where, parts, read, cum, within):
    vmem = pl.BlockSpec(memory_space=pltpu.VMEM)
    return pl.pallas_call(
        finish_kernel,
        out_shape=shape(within.shape, BF16),
        in_specs=[pl.BlockSpec(memory_space=pltpu.SMEM)] + [vmem] * 7,
        out_specs=vmem,
        scratch_shapes=[pltpu.VMEM((SIDE,) + parts[0].shape, BF16)],
        compiler_params=params(),
        cost_estimate=SMALL,
        name="finish",
    )(where, *parts, read, cum, within)


def body(
    tokens,
    routes,
    route_weight,
    moe_gain,
    gate_weight,
    up_weight,
    down_weight,
    ssd_gain,
    input_weight,
    write_weight,
    read_weight,
    step_weight,
    step_bias,
    decay_log,
    skip_gain,
):
    where = jnp.stack([lax.axis_index("expert"), lax.axis_index("frame")]).astype(jnp.int32)
    rows, onehot, slot_weight = pick(where, tokens, routes, route_weight, moe_gain)
    halves = experts(rows, (gate_weight[0], up_weight[0], down_weight[0]))
    weights = (input_weight, write_weight, read_weight, step_weight)
    mixed, more, order = [], (), ()
    for c in range(2):
        keep, give = weigh(where, after(halves[c], *order), slot_weight)
        own, to_next, to_last, to_across = place(where, keep, to_sibling(give), onehot)
        others = (along_y(to_next, 1), along_y(to_last, -1), along_y(to_across, 2))
        half = residual(c, where, tokens, own, others)
        order = (own,)
        mixed.append(half)
        mine = jnp.stack([half, along_y(half, 1), along_y(half, -1), along_y(half, 2)])
        if c == 1:
            more = (*more, step_bias.reshape(1, -1), decay_log.reshape(1, -1))
        more = project(c, where, mine, to_sibling(mine), ssd_gain, weights, *more)
    inputs, write, read, step, cum, state, to_next, to_last, to_across = more
    parts = (state, along_x(to_next, 1), along_x(to_last, -1), along_x(to_across, 2))
    row = row_total(where, parts)
    earlier = (along_z(row, 1), along_z(row, -1), along_z(row, 2))
    within = inside(inputs, write, read, step, cum, skip_gain)
    prior, to_next, to_last, to_across = carry(where, parts, earlier)
    carried = (prior, along_x(to_next, 1), along_x(to_last, -1), along_x(to_across, 2))
    ssd_out = finish(where, carried, read, cum, within)
    return (jnp.concatenate(mixed, axis=1), ssd_out)


def solution(mesh):
    placed = (
        P("frame", None),
        P("frame", None),
        P("frame", None),
        P(),
        P("expert", "frame", None),
        P("expert", "frame", None),
        P("expert", "frame", None),
        P(),
        P(None, "expert"),
        P(None, "expert"),
        P(None, "expert"),
        P(None, "expert"),
        P("expert"),
        P("expert"),
        P("expert"),
    )
    return jax.shard_map(
        body,
        mesh=mesh,
        in_specs=placed,
        out_specs=(P("frame", "expert"), P("frame", "expert")),
        check_vma=False,
    )
```

```python
import functools

import jax
import jax.numpy as jnp
from jax import lax
from jax.experimental import pallas as pl
from jax.experimental.pallas import tpu as pltpu
from jax.sharding import PartitionSpec as P

HEAD_DIM = 64
STATE = 128
SLOTS = 96
SIDE = 4
EPSILON = 1e-06
PRECISE = lax.Precision.HIGHEST
AXES = ("expert", "frame")
F32, BF16 = jnp.float32, jnp.bfloat16


def routes_of(rule):
    pairs = []
    for y in range(SIDE):
        for core in range(2):
            for z in range(SIDE):
                for x in range(SIDE):
                    ny, nc, nz, nx = rule(y, core, z, x)
                    source = (y * 2 + core) * 16 + z * SIDE + x
                    target = ((ny % SIDE) * 2 + nc % 2) * 16 + (nz % SIDE) * SIDE + nx % SIDE
                    pairs.append((source, target))
    return pairs


def send(array, rule):
    return lax.ppermute(array, AXES, routes_of(rule))


def along_first(array, by):
    return send(array, lambda y, c, z, x: (y, c, z + by * c, x + by * (1 - c)))


def along_second(array, by):
    return send(array, lambda y, c, z, x: (y, c, z + by * (1 - c), x + by * c))


def along_x(array, by):
    return send(array, lambda y, c, z, x: (y, c, z, x + by))


def along_z(array, by):
    return send(array, lambda y, c, z, x: (y, c, z + by, x))


def along_y(array, by):
    return send(array, lambda y, c, z, x: (y + by, c, z, x))


def to_sibling(array):
    return send(array, lambda y, c, z, x: (y, 1 - c, z, x))


def shape(dims, kind):
    return jax.ShapeDtypeStruct(dims, kind)


def params(mebibytes=20):
    return pltpu.CompilerParams(vmem_limit_bytes=mebibytes * 1024 * 1024)


SMALL = pl.CostEstimate(flops=10**6, bytes_accessed=10**5, transcendentals=0)


def place_of(where_ref):
    return where_ref[0] >> 1, where_ref[0] & 1, where_ref[1] >> 2, where_ref[1] & 3


def pick_kernel(where_ref, *refs):
    arrays, (rows_ref, onehot_ref, slot_weight_ref), held, sems = refs[:4], refs[4:7], refs[7:11], refs[11]
    copies = [pltpu.make_async_copy(source, to, sems.at[k]) for k, (source, to) in enumerate(zip(arrays, held))]
    for copy in copies:
        copy.start()
    tokens_ref, routes_ref, weight_ref, gain_ref = held
    count = tokens_ref.shape[0]
    upper = lax.broadcasted_iota(jnp.int32, (count, count), 0) <= lax.broadcasted_iota(jnp.int32, (count, count), 1)
    slot = lax.broadcasted_iota(jnp.int32, (SLOTS, count), 0)
    copies[1].wait()
    copies[2].wait()
    onehots = []
    for sibling in range(2):
        hits = routes_ref[...] == where_ref[0] ^ sibling
        chosen = jnp.max(hits.astype(F32), axis=0, keepdims=True)
        wide = jnp.broadcast_to(chosen, (SLOTS, count))
        place = jnp.dot(wide.astype(BF16), upper.astype(BF16), preferred_element_type=F32) - 1.0
        named = (place.astype(jnp.int32) == slot) & (wide > 0.0)
        onehots.append(jnp.where(named, 1.0, 0.0).astype(BF16))
        if sibling == 0:
            weights = jnp.sum(jnp.where(hits, weight_ref[...], 0.0), axis=0, keepdims=True)
            slot_weight = jnp.sum(jnp.where(named, weights, 0.0), axis=1, keepdims=True)
    onehot_ref[...] = jnp.concatenate(onehots, axis=0)
    slot_weight_ref[...] = jnp.broadcast_to(slot_weight, slot_weight_ref.shape)
    copies[0].wait()
    copies[3].wait()
    picked = jnp.dot(onehots[0], tokens_ref[...], preferred_element_type=F32)
    mean_sq = jnp.mean(picked * picked, axis=1, keepdims=True)
    rows_ref[...] = (picked * lax.rsqrt(mean_sq + EPSILON) * gain_ref[...]).astype(BF16)


def pick(where, tokens, routes, route_weight, gain):
    count, width = tokens.shape
    smem, vmem = pl.BlockSpec(memory_space=pltpu.SMEM), pl.BlockSpec(memory_space=pltpu.VMEM)
    arrays = (tokens, routes.T, route_weight.T, gain.reshape(1, width))
    return pl.pallas_call(
        pick_kernel,
        out_shape=(shape((SLOTS, width), BF16), shape((2 * SLOTS, count), BF16), shape((SLOTS, 128), F32)),
        in_specs=[smem] + [pl.BlockSpec(memory_space=pltpu.HBM)] * 4,
        out_specs=(vmem, vmem, vmem),
        scratch_shapes=[pltpu.VMEM(array.shape, array.dtype) for array in arrays] + [pltpu.SemaphoreType.DMA((4,))],
        compiler_params=params(60),
        name="pick",
    )(where, *arrays)


def expert_kernel(pieces, *refs):
    gate_ref, up_ref, down_ref, out_top_ref, out_bottom_ref = refs[pieces:]
    half = out_top_ref.shape[0]
    rows = jnp.concatenate([ref[...] for ref in refs[:pieces]], axis=0)
    by_row = (((1,), (1,)), ((), ()))
    gate = lax.dot_general(rows, gate_ref[...], by_row, preferred_element_type=F32)
    upper = lax.dot_general(rows, up_ref[...], by_row, preferred_element_type=F32)
    hidden = (gate / (1.0 + jnp.exp(-gate)) * upper).astype(BF16)
    out = jnp.dot(hidden, down_ref[...], preferred_element_type=F32).astype(BF16)
    out_top_ref[...] = out[:half]
    out_bottom_ref[...] = out[half:]


def expert(pieces, weights):
    vmem = pl.BlockSpec(memory_space=pltpu.VMEM)
    units, width = weights[0].shape
    return pl.pallas_call(
        functools.partial(expert_kernel, len(pieces)),
        out_shape=(shape((2 * SLOTS, width), BF16),) * 2,
        in_specs=[vmem] * (len(pieces) + 3),
        out_specs=(vmem, vmem),
        compiler_params=params(28),
        cost_estimate=pl.CostEstimate(
            flops=24 * SLOTS * width * units, bytes_accessed=6 * units * width + 16 * SLOTS * width, transcendentals=0
        ),
        name="expert",
    )(*pieces, *weights)


def relay_kernel(after_ref, down_ref, before_ref, up_ref, to_after_ref, to_before_ref):
    to_after_ref[...] = (after_ref[...].astype(F32) + down_ref[...].astype(F32)).astype(BF16)
    to_before_ref[...] = (before_ref[...].astype(F32) + up_ref[...].astype(F32)).astype(BF16)


def relay(*arrays):
    vmem = pl.BlockSpec(memory_space=pltpu.VMEM)
    return pl.pallas_call(
        relay_kernel,
        out_shape=(shape(arrays[0].shape, BF16),) * 2,
        in_specs=[vmem] * 4,
        out_specs=(vmem, vmem),
        compiler_params=params(),
        cost_estimate=SMALL,
        name="relay",
    )(*arrays)


def total_kernel(near_top, top_a, top_b, near_bottom, bottom_a, bottom_b, level, *outs):
    for c in range(2):
        own, down, up, across = outs[4 * c : 4 * c + 4]
        for e in range(8):
            lanes, at = slice(e * 512 + c * 256, e * 512 + c * 256 + 256), slice(e * 256, e * 256 + 256)
            for near, a, b, first, second in (
                (near_top, top_a, top_b, own, down), (near_bottom, bottom_a, bottom_b, up, across)
            ):
                total = near[:, lanes].astype(F32) + a[:, lanes].astype(F32) + b[:, lanes].astype(F32)
                first[:, at] = total[:SLOTS].astype(BF16)
                second[:, at] = total[SLOTS:].astype(BF16)


def total(level, *arrays):
    vmem = pl.BlockSpec(memory_space=pltpu.VMEM)
    return pl.pallas_call(
        total_kernel,
        out_shape=(shape((SLOTS, arrays[0].shape[1] // 2), BF16),) * 8,
        in_specs=[vmem] * 6 + [pl.BlockSpec(memory_space=pl.ANY)],
        out_specs=(vmem,) * 8,
        compiler_params=params(),
        cost_estimate=SMALL,
        name="total",
    )(*arrays, level)


def plus(a, b):
    return (a.astype(F32) + b.astype(F32)).astype(BF16)


def after(values, *earlier):
    return lax.optimization_barrier((values, earlier))[0]


def experts(rows, weights):
    last, following = along_first(rows, 1), along_first(rows, -1)
    across_top = along_first(last[: SLOTS // 2], 1)
    across_bottom = along_first(following[SLOTS // 2 :], -1)
    bottom = jnp.concatenate([following, across_top, across_bottom], axis=0)
    before_own, after_own = along_second(rows, 1), along_second(rows, -1)
    bottom = after(bottom, before_own, after_own)
    before_last = along_second(last, 1)
    after_bottom = along_second(bottom, -1)
    far_own = along_second(before_own, 1)
    out_near_top, out_near_bottom = expert((rows, last, bottom), weights)
    before_last, after_bottom = after((before_last, after_bottom), out_near_top)
    far_last = along_second(before_last, 1)
    far_bottom = along_second(after_bottom, -1)
    out_before_top, out_after_bottom = expert((before_own, before_last, after_bottom), weights)
    later_last, later_bottom = after((last, bottom), out_before_top)
    after_last = along_second(later_last, -1)
    before_bottom = along_second(later_bottom, 1)
    far = after((far_own, far_last, far_bottom), out_before_top)
    out_far_top, out_far_bottom = expert(far, weights)
    relay_down = along_second(out_far_top, 1)
    relay_up = along_second(after(out_far_bottom, after_last), -1)
    first_back = after((out_before_top, out_after_bottom), out_far_top)
    top_a = along_second(first_back[0], -1)
    bottom_a = along_second(first_back[1], 1)
    second = after((after_own, after_last, before_bottom), out_far_top)
    out_after_top, out_before_bottom = expert(second, weights)
    to_after, to_before = relay(out_after_top, relay_down, out_before_bottom, relay_up)
    top_b = along_second(to_after, 1)
    bottom_b = along_second(to_before, -1)
    level = to_sibling(sum(array[:16, :128] for array in (top_a, bottom_a, top_b, bottom_b)))
    sums = total(level, out_near_top, top_a, top_b, out_near_bottom, bottom_a, bottom_b)
    terms = []
    for c in range(2):
        own, down, up, across = sums[4 * c : 4 * c + 4]
        terms.append((own, along_first(down, -1), along_first(up, 1), along_first(across, 2)))
    return terms


def weigh_kernel(where_ref, a_ref, b_ref, c_ref, d_ref, weight_ref, keep_ref, give_ref):
    rows = (a_ref[...].astype(F32) + b_ref[...].astype(F32)) + (c_ref[...].astype(F32) + d_ref[...].astype(F32))
    weighted = (rows * weight_ref[:, :1]).astype(BF16)
    _, mine, _, _ = place_of(where_ref)
    for core in range(2):

        @pl.when(mine == core)
        def _():
            for k in range(SIDE):
                to = slice(k * 256, (k + 1) * 256)
                for out, e in ((keep_ref, 2 * k + core), (give_ref, 2 * k + 1 - core)):
                    out[:, to] = weighted[:, e * 256 : (e + 1) * 256]


def weigh(where, terms, slot_weight):
    vmem = pl.BlockSpec(memory_space=pltpu.VMEM)
    return pl.pallas_call(
        weigh_kernel,
        out_shape=(shape((SLOTS, SIDE * 256), BF16),) * 2,
        in_specs=[pl.BlockSpec(memory_space=pltpu.SMEM)] + [vmem] * 5,
        out_specs=(vmem, vmem),
        compiler_params=params(),
        cost_estimate=SMALL,
        name="weigh",
    )(where, *terms, slot_weight)


def place_kernel(where_ref, keep_ref, got_ref, onehot_ref, own_ref, next_ref, last_ref, across_ref, scr):
    rows = jnp.concatenate([keep_ref[...], got_ref[...]], axis=0)
    placed = lax.dot_general(onehot_ref[...], rows, (((0,), (0,)), ((), ())), preferred_element_type=F32)
    for k in range(SIDE):
        scr[k] = placed[:, k * 256 : (k + 1) * 256]
    y, _, _, _ = place_of(where_ref)
    for by, out in ((0, own_ref), (1, next_ref), (3, last_ref), (2, across_ref)):
        out[...] = scr[(y + by) & 3].astype(out.dtype)


def place(where, keep, got, onehot):
    count = onehot.shape[1]
    vmem = pl.BlockSpec(memory_space=pltpu.VMEM)
    return pl.pallas_call(
        place_kernel,
        out_shape=(shape((count, 256), F32),) + (shape((count, 256), BF16),) * 3,
        in_specs=[pl.BlockSpec(memory_space=pltpu.SMEM)] + [vmem] * 3,
        out_specs=(vmem,) * 4,
        scratch_shapes=[pltpu.VMEM((SIDE, count, 256), F32)],
        compiler_params=params(),
        cost_estimate=SMALL,
        name="place",
    )(where, keep, got, onehot)


def residual_kernel(where_ref, tokens_ref, own_ref, a_ref, b_ref, c_ref, mixed_ref):
    summed = (own_ref[...] + a_ref[...].astype(F32)) + (b_ref[...].astype(F32) + c_ref[...].astype(F32))
    mixed_ref[...] = (tokens_ref[...].astype(F32) + summed).astype(BF16)


def residual(c, where, tokens, own, others):
    count, cols = own.shape
    whole = pl.BlockSpec((count, cols), lambda i, where: (0, 0))
    return pl.pallas_call(
        residual_kernel,
        out_shape=shape((count, cols), BF16),
        grid_spec=pltpu.PrefetchScalarGridSpec(
            num_scalar_prefetch=1,
            grid=(1,),
            in_specs=[pl.BlockSpec((count, cols), lambda i, where: (0, 2 * where[0] + c))] + [whole] * 4,
            out_specs=whole,
        ),
        compiler_params=params(),
        cost_estimate=SMALL,
        name="residual",
    )(where, tokens, own, *others)


def spread(per_head, lanes):
    heads = per_head.shape[1]
    pairs = []
    first = lax.broadcasted_iota(jnp.int32, (per_head.shape[0], 2 * HEAD_DIM), 1) < HEAD_DIM
    for k in range(heads // 2):
        pairs.append(jnp.where(first, per_head[:, 2 * k : 2 * k + 1], per_head[:, 2 * k + 1 : 2 * k + 2]))
    return jnp.concatenate(pairs, axis=1)


def project_kernel(c, where_ref, mine_ref, other_ref, gain_ref, in_w_ref, write_w_ref, read_w_ref, step_w_ref, *refs):
    y, core, _, _ = place_of(where_ref)
    squares, scaled, step_w = 0.0, [], []
    for e in range(8):
        away = (e // 2 + SIDE - y) & 3
        slot = jnp.where(away == 0, 0, jnp.where(away == 3, 1, away + 1))
        values = jnp.where(core == e % 2, mine_ref[slot], other_ref[slot]).astype(F32)
        squares += jnp.sum(values * values, axis=1, keepdims=True)
        scaled.append((values * gain_ref[e, c]).astype(BF16))
        step_w.append(step_w_ref[:, e * 512 + c * 256 : e * 512 + c * 256 + 256])
    scaled = jnp.concatenate(scaled, axis=1)

    def rows(ref):
        return ref[:, c].reshape(scaled.shape[1], ref.shape[3])

    write_read = jnp.concatenate([rows(write_w_ref), rows(read_w_ref)], axis=1)
    accs = [
        jnp.dot(scaled, rows(in_w_ref), preferred_element_type=F32),
        jnp.dot(scaled, write_read, preferred_element_type=F32),
        lax.dot_general(
            scaled, jnp.concatenate(step_w, axis=1), (((1,), (1,)), ((), ())), preferred_element_type=F32
        ),
        jnp.broadcast_to(squares, (squares.shape[0], 128)),
    ]
    if c == 0:
        for out, acc in zip(refs, accs):
            out[...] = acc
    else:
        before, (bias_ref, decay_ref) = refs[:4], refs[4:6]
        accs = [acc + ref[...] for acc, ref in zip(accs, before)]
        projected(where_ref, bias_ref, decay_ref, refs[6:15], accs, refs[15], 8 * 512)


def projected(where_ref, bias_ref, decay_ref, outs, accs, state_scr, width):
    in_acc, write_read, step_acc, square_acc = accs
    x_ref, write_ref, read_ref, step_ref, cum_ref = outs[:5]
    count, heads = step_acc.shape
    scale = lax.rsqrt(square_acc[:, :1] / width + EPSILON)
    x = (in_acc * scale).astype(BF16)
    x_ref[...] = x
    write = (write_read[:, :STATE] * scale).astype(BF16)
    write_ref[...] = write
    read_ref[...] = (write_read[:, STATE:] * scale).astype(BF16)
    raw = step_acc * scale + bias_ref[...]
    step = jnp.maximum(raw, 0.0) + jnp.log1p(jnp.exp(-jnp.abs(raw)))
    step_ref[...] = step
    log_decay = -step * jnp.exp(decay_ref[...])
    lower = lax.broadcasted_iota(jnp.int32, (count, count), 0) >= lax.broadcasted_iota(jnp.int32, (count, count), 1)
    cum = jnp.dot(lower.astype(F32), log_decay, preferred_element_type=F32, precision=PRECISE)
    cum_ref[...] = cum
    last = cum[count - 1 :, :]
    to_end = jnp.exp(last - cum) * step
    weighted = (x.astype(F32) * spread(to_end, x.shape[1])).astype(BF16)
    state = lax.dot_general(write, weighted, (((0,), (0,)), ((), ())), preferred_element_type=F32)
    whole = spread(last, x.shape[1])
    high = whole.astype(BF16).astype(F32)
    row = lax.broadcasted_iota(jnp.int32, (16, x.shape[1]), 0)
    log_rows = jnp.where(row == 0, high, jnp.where(row == 1, whole - high, 0.0)).astype(BF16)
    cols = x.shape[1] // SIDE
    for q in range(SIDE):
        lanes = slice(q * cols, (q + 1) * cols)
        state_scr[q, :STATE, :] = state[:, lanes].astype(BF16)
        state_scr[q, STATE:, :] = log_rows[:, lanes]
    _, _, _, at = place_of(where_ref)
    for by, out in zip((0, 1, 3, 2), outs[5:]):
        out[...] = state_scr[(at + by) & 3]


def project(c, where, mine, other, gain, weights, *more):
    _, count, cols = mine.shape
    lanes, heads = weights[0].shape[1], weights[3].shape[1]
    smem, vmem = pl.BlockSpec(memory_space=pltpu.SMEM), pl.BlockSpec(memory_space=pltpu.VMEM)
    cut = [w.reshape(8, 2, cols, w.shape[1]) for w in weights[:3]]
    if c == 0:
        outs = tuple(shape((count, n), F32) for n in (lanes, 2 * STATE, heads, 128))
        scratch = []
    else:
        quarter = (STATE + 16, lanes // SIDE)
        outs = (
            shape((count, lanes), BF16), shape((count, STATE), BF16), shape((count, STATE), BF16),
            shape((count, heads), F32), shape((count, heads), F32),
        ) + (shape(quarter, BF16),) * 4
        scratch = [pltpu.VMEM((SIDE,) + quarter, BF16)]
    return pl.pallas_call(
        functools.partial(project_kernel, c),
        out_shape=outs,
        in_specs=[smem] + [vmem] * (7 + len(more)),
        out_specs=(vmem,) * len(outs),
        scratch_shapes=scratch,
        compiler_params=params(),
        cost_estimate=pl.CostEstimate(flops=3 * 10**9, bytes_accessed=10**6, transcendentals=0),
        name="project",
    )(where, mine, other, gain.reshape(8, 2, 1, cols), *cut, weights[3].T, *more)


def inside_kernel(x_ref, write_ref, read_ref, step_ref, cum_ref, skip_ref, out_ref):
    count, heads = step_ref.shape
    span = count // 2
    scores = lax.dot_general(read_ref[...], write_ref[...], (((1,), (1,)), ((), ())), preferred_element_type=F32)
    cum = cum_ref[...]
    cum_t, step_t = cum.T, step_ref[...].T
    causal = lax.broadcasted_iota(jnp.int32, (span, span), 0) >= lax.broadcasted_iota(jnp.int32, (span, span), 1)
    low, high = slice(0, span), slice(span, count)

    def mixing(h, rows, columns):
        gaps = cum[rows, h : h + 1] - cum_t[h : h + 1, columns]
        if rows == columns:
            gaps = jnp.where(causal, gaps, -jnp.inf)
        return (scores[rows, columns] * jnp.exp(gaps) * step_t[h : h + 1, columns]).astype(BF16)

    for h in range(heads):
        lanes = slice(h * HEAD_DIM, (h + 1) * HEAD_DIM)
        x = x_ref[:, lanes]
        skipped = skip_ref[0, h] * x.astype(F32)
        top = jnp.dot(mixing(h, low, low), x[low], preferred_element_type=F32)
        below = jnp.concatenate([mixing(h, high, low), mixing(h, high, high)], axis=1)
        bottom = jnp.dot(below, x, preferred_element_type=F32)
        out_ref[:, lanes] = jnp.concatenate([top, bottom], axis=0) + skipped


def inside(x, write, read, step, cum, skip_gain):
    vmem = pl.BlockSpec(memory_space=pltpu.VMEM)
    return pl.pallas_call(
        inside_kernel,
        out_shape=shape(x.shape, F32),
        in_specs=[vmem] * 5 + [pl.BlockSpec(memory_space=pltpu.SMEM)],
        out_specs=vmem,
        compiler_params=params(),
        cost_estimate=pl.CostEstimate(flops=2 * 10**9, bytes_accessed=2 * 10**6, transcendentals=10**6),
        name="inside",
    )(x, write, read, step, cum, skip_gain.reshape(1, -1))


def log_of(ref):
    return ref[STATE : STATE + 1, :].astype(F32) + ref[STATE + 1 : STATE + 2, :].astype(F32)


def weights_before(here, places, logs):
    terms = []
    for s in places:
        between = sum(jnp.where((s < u) & (u < here), log, 0.0) for u, log in zip(places, logs))
        terms.append(jnp.where(s < here, jnp.exp(between), 0.0))
    return terms


def row_total_kernel(where_ref, own_ref, last_ref, next_ref, across_ref, total_ref):
    _, _, _, here = place_of(where_ref)
    refs = (own_ref, last_ref, next_ref, across_ref)
    places = [here, (here + 3) & 3, (here + 1) & 3, (here + 2) & 3]
    logs = [log_of(ref) for ref in refs]
    until_end = [jnp.exp(sum(jnp.where(s < u, log, 0.0) for u, log in zip(places, logs))) for s in places]
    total_ref[:STATE, :] = sum(w * ref[:STATE, :].astype(F32) for w, ref in zip(until_end, refs)).astype(BF16)
    whole = sum(logs)
    top = whole.astype(BF16).astype(F32)
    row = lax.broadcasted_iota(jnp.int32, (16, whole.shape[1]), 0)
    total_ref[STATE:, :] = jnp.where(row == 0, top, jnp.where(row == 1, whole - top, 0.0)).astype(BF16)


def row_total(where, parts):
    vmem = pl.BlockSpec(memory_space=pltpu.VMEM)
    return pl.pallas_call(
        row_total_kernel,
        out_shape=shape(parts[0].shape, BF16),
        in_specs=[pl.BlockSpec(memory_space=pltpu.SMEM)] + [vmem] * 4,
        out_specs=vmem,
        compiler_params=params(),
        cost_estimate=SMALL,
        name="row_total",
    )(where, *parts)


def carry_kernel(where_ref, *refs):
    parts, earlier, outs = refs[:4], refs[4:7], refs[7:]
    _, _, z, here = place_of(where_ref)
    rows = [(z + 3) & 3, (z + 1) & 3, (z + 2) & 3]
    before = weights_before(z, rows, [log_of(ref) for ref in earlier])
    to_row = sum(w * ref[:STATE, :].astype(F32) for w, ref in zip(before, earlier))
    places = [here, (here + 3) & 3, (here + 1) & 3, (here + 2) & 3]
    logs = [log_of(ref) for ref in parts]
    for by, out in zip((0, 1, 3, 2), outs):
        target = (here + by) & 3
        gone = sum(jnp.where(s < target, log, 0.0) for s, log in zip(places, logs))
        state = jnp.exp(gone) * to_row
        for w, ref in zip(weights_before(target, places, logs), parts):
            state += w * ref[:STATE, :].astype(F32)
        out[...] = state.astype(BF16)


def carry(where, parts, earlier):
    vmem = pl.BlockSpec(memory_space=pltpu.VMEM)
    return pl.pallas_call(
        carry_kernel,
        out_shape=(shape((STATE, parts[0].shape[1]), BF16),) * 4,
        in_specs=[pl.BlockSpec(memory_space=pltpu.SMEM)] + [vmem] * 7,
        out_specs=(vmem,) * 4,
        compiler_params=params(),
        cost_estimate=SMALL,
        name="carry",
    )(where, *parts, *earlier)


def finish_kernel(where_ref, own_ref, last_ref, next_ref, across_ref, read_ref, cum_ref, inside_ref, out_ref, scr):
    _, _, _, here = place_of(where_ref)
    for by, ref in ((0, own_ref), (3, last_ref), (1, next_ref), (2, across_ref)):
        scr[(here + by) & 3] = ref[...]
    cols = own_ref.shape[1]
    decayed = spread(jnp.exp(cum_ref[...]), SIDE * cols)
    for q in range(SIDE):
        lanes = slice(q * cols, (q + 1) * cols)
        from_prior = jnp.dot(read_ref[...], scr[q], preferred_element_type=F32)
        out_ref[:, lanes] = (inside_ref[:, lanes] + decayed[:, lanes] * from_prior).astype(BF16)


def finish(where, parts, read, cum, within):
    vmem = pl.BlockSpec(memory_space=pltpu.VMEM)
    return pl.pallas_call(
        finish_kernel,
        out_shape=shape(within.shape, BF16),
        in_specs=[pl.BlockSpec(memory_space=pltpu.SMEM)] + [vmem] * 7,
        out_specs=vmem,
        scratch_shapes=[pltpu.VMEM((SIDE,) + parts[0].shape, BF16)],
        compiler_params=params(),
        cost_estimate=SMALL,
        name="finish",
    )(where, *parts, read, cum, within)


def body(
    tokens,
    routes,
    route_weight,
    moe_gain,
    gate_weight,
    up_weight,
    down_weight,
    ssd_gain,
    input_weight,
    write_weight,
    read_weight,
    step_weight,
    step_bias,
    decay_log,
    skip_gain,
):
    where = jnp.stack([lax.axis_index("expert"), lax.axis_index("frame")]).astype(jnp.int32)
    rows, onehot, slot_weight = pick(where, tokens, routes, route_weight, moe_gain)
    halves = experts(rows, (gate_weight[0], up_weight[0], down_weight[0]))
    weights = (input_weight, write_weight, read_weight, step_weight)
    sums, order = [], ()
    for c in range(2):
        keep, give = weigh(where, after(halves[c], *order), slot_weight)
        own, to_next, to_last, to_across = place(where, keep, to_sibling(give), onehot)
        order = (own,)
        sums.append((own, (along_y(to_next, 1), along_y(to_last, -1), along_y(to_across, 2))))
    mixed, more = [], ()
    for c in range(2):
        own, others = sums[c]
        own = after(own, sums[1][1][0]) if c == 0 else own
        half = residual(c, where, tokens, own, others)
        mixed.append(half)
        mine = jnp.stack([half, along_y(half, 1), along_y(half, -1), along_y(half, 2)])
        if c == 1:
            more = (*more, step_bias.reshape(1, -1), decay_log.reshape(1, -1))
        more = project(c, where, mine, to_sibling(mine), ssd_gain, weights, *more)
    inputs, write, read, step, cum, state, to_next, to_last, to_across = more
    parts = (state, along_x(to_next, 1), along_x(to_last, -1), along_x(to_across, 2))
    row = row_total(where, parts)
    earlier = (along_z(row, 1), along_z(row, -1), along_z(row, 2))
    within = inside(inputs, write, read, step, cum, skip_gain)
    prior, to_next, to_last, to_across = carry(where, parts, earlier)
    carried = (prior, along_x(to_next, 1), along_x(to_last, -1), along_x(to_across, 2))
    ssd_out = finish(where, carried, read, cum, within)
    return (jnp.concatenate(mixed, axis=1), ssd_out)


def solution(mesh):
    placed = (
        P("frame", None),
        P("frame", None),
        P("frame", None),
        P(),
        P("expert", "frame", None),
        P("expert", "frame", None),
        P("expert", "frame", None),
        P(),
        P(None, "expert"),
        P(None, "expert"),
        P(None, "expert"),
        P(None, "expert"),
        P("expert"),
        P("expert"),
        P("expert"),
    )
    return jax.shard_map(
        body,
        mesh=mesh,
        in_specs=placed,
        out_specs=(P("frame", "expert"), P("frame", "expert")),
        check_vma=False,
    )
```

```python
import functools

import jax
import jax.numpy as jnp
from jax import lax
from jax.experimental import pallas as pl
from jax.experimental.pallas import tpu as pltpu
from jax.sharding import PartitionSpec as P

HEAD_DIM = 64
STATE = 128
SLOTS = 96
SIDE = 4
EPSILON = 1e-06
PRECISE = lax.Precision.HIGHEST
AXES = ("expert", "frame")
F32, BF16 = jnp.float32, jnp.bfloat16


def routes_of(rule):
    pairs = []
    for y in range(SIDE):
        for core in range(2):
            for z in range(SIDE):
                for x in range(SIDE):
                    ny, nc, nz, nx = rule(y, core, z, x)
                    source = (y * 2 + core) * 16 + z * SIDE + x
                    target = ((ny % SIDE) * 2 + nc % 2) * 16 + (nz % SIDE) * SIDE + nx % SIDE
                    pairs.append((source, target))
    return pairs


def send(array, rule):
    return lax.ppermute(array, AXES, routes_of(rule))


def along_first(array, by):
    return send(array, lambda y, c, z, x: (y, c, z + by * c, x + by * (1 - c)))


def along_second(array, by):
    return send(array, lambda y, c, z, x: (y, c, z + by * (1 - c), x + by * c))


def along_x(array, by):
    return send(array, lambda y, c, z, x: (y, c, z, x + by))


def along_z(array, by):
    return send(array, lambda y, c, z, x: (y, c, z + by, x))


def along_y(array, by):
    return send(array, lambda y, c, z, x: (y + by, c, z, x))


def to_sibling(array):
    return send(array, lambda y, c, z, x: (y, 1 - c, z, x))


def shape(dims, kind):
    return jax.ShapeDtypeStruct(dims, kind)


def params(mebibytes=20):
    return pltpu.CompilerParams(vmem_limit_bytes=mebibytes * 1024 * 1024)


SMALL = pl.CostEstimate(flops=10**6, bytes_accessed=10**5, transcendentals=0)


def place_of(where_ref):
    return where_ref[0] >> 1, where_ref[0] & 1, where_ref[1] >> 2, where_ref[1] & 3


def pick_kernel(where_ref, *refs):
    arrays, (rows_ref, onehot_ref, slot_weight_ref), held, sems = refs[:4], refs[4:7], refs[7:11], refs[11]
    copies = [pltpu.make_async_copy(source, to, sems.at[k]) for k, (source, to) in enumerate(zip(arrays, held))]
    for copy in copies:
        copy.start()
    tokens_ref, routes_ref, weight_ref, gain_ref = held
    count = tokens_ref.shape[0]
    upper = lax.broadcasted_iota(jnp.int32, (count, count), 0) <= lax.broadcasted_iota(jnp.int32, (count, count), 1)
    slot = lax.broadcasted_iota(jnp.int32, (SLOTS, count), 0)
    copies[1].wait()
    copies[2].wait()
    onehots = []
    for sibling in range(2):
        hits = routes_ref[...] == where_ref[0] ^ sibling
        chosen = jnp.max(hits.astype(F32), axis=0, keepdims=True)
        wide = jnp.broadcast_to(chosen, (SLOTS, count))
        place = jnp.dot(wide.astype(BF16), upper.astype(BF16), preferred_element_type=F32) - 1.0
        named = (place.astype(jnp.int32) == slot) & (wide > 0.0)
        onehots.append(jnp.where(named, 1.0, 0.0).astype(BF16))
        if sibling == 0:
            weights = jnp.sum(jnp.where(hits, weight_ref[...], 0.0), axis=0, keepdims=True)
            slot_weight = jnp.sum(jnp.where(named, weights, 0.0), axis=1, keepdims=True)
    onehot_ref[...] = jnp.concatenate(onehots, axis=0)
    slot_weight_ref[...] = jnp.broadcast_to(slot_weight, slot_weight_ref.shape)
    copies[0].wait()
    copies[3].wait()
    picked = jnp.dot(onehots[0], tokens_ref[...], preferred_element_type=F32)
    mean_sq = jnp.mean(picked * picked, axis=1, keepdims=True)
    rows_ref[...] = (picked * lax.rsqrt(mean_sq + EPSILON) * gain_ref[...]).astype(BF16)


def pick(where, tokens, routes, route_weight, gain):
    count, width = tokens.shape
    smem, vmem = pl.BlockSpec(memory_space=pltpu.SMEM), pl.BlockSpec(memory_space=pltpu.VMEM)
    arrays = (tokens, routes.T, route_weight.T, gain.reshape(1, width))
    return pl.pallas_call(
        pick_kernel,
        out_shape=(shape((SLOTS, width), BF16), shape((2 * SLOTS, count), BF16), shape((SLOTS, 128), F32)),
        in_specs=[smem] + [pl.BlockSpec(memory_space=pltpu.HBM)] * 4,
        out_specs=(vmem, vmem, vmem),
        scratch_shapes=[pltpu.VMEM(array.shape, array.dtype) for array in arrays] + [pltpu.SemaphoreType.DMA((4,))],
        compiler_params=params(60),
        name="pick",
    )(where, *arrays)


def expert_kernel(top_ref, bottom_ref, gate_ref, up_ref, down_ref, *outs):
    half = top_ref.shape[0]
    rows = jnp.concatenate([top_ref[...], bottom_ref[...]], axis=0)
    by_row = (((1,), (1,)), ((), ()))
    gate = lax.dot_general(rows, gate_ref[...], by_row, preferred_element_type=F32)
    upper = lax.dot_general(rows, up_ref[...], by_row, preferred_element_type=F32)
    hidden = (gate / (1.0 + jnp.exp(-gate)) * upper).astype(BF16)
    out = jnp.dot(hidden, down_ref[...], preferred_element_type=F32).astype(BF16)
    parts = len(outs) // 2
    for c in range(parts):
        for k, lanes in enumerate(half_columns(c, out.shape[1]) if parts == 2 else [slice(0, out.shape[1])]):
            size = lanes.stop - lanes.start
            to = slice(k * size, (k + 1) * size)
            outs[2 * c][:, to] = out[:half, lanes]
            outs[2 * c + 1][:, to] = out[half:, lanes]


def expert(top, bottom, weights, parts=1):
    vmem = pl.BlockSpec(memory_space=pltpu.VMEM)
    rows, width = top.shape
    units = weights[0].shape[0]
    return pl.pallas_call(
        expert_kernel,
        out_shape=(shape((rows, width // parts), BF16),) * (2 * parts),
        in_specs=[vmem] * 5,
        out_specs=(vmem,) * (2 * parts),
        compiler_params=params(28),
        cost_estimate=pl.CostEstimate(
            flops=12 * rows * width * units, bytes_accessed=6 * units * width + 8 * rows * width, transcendentals=0
        ),
        name="expert",
    )(top, bottom, *weights)


def half_columns(c, block):
    return [slice(k * 512 + c * 256, k * 512 + c * 256 + 256) for k in range(block // 512)]


def relay_kernel(c, after_ref, down_ref, before_ref, up_ref, to_after_ref, to_before_ref):
    for k, lanes in enumerate(half_columns(c, after_ref.shape[1])):
        to = slice(k * 256, k * 256 + 256)
        to_after_ref[:, to] = (after_ref[:, lanes].astype(F32) + down_ref[:, to].astype(F32)).astype(BF16)
        to_before_ref[:, to] = (before_ref[:, lanes].astype(F32) + up_ref[:, to].astype(F32)).astype(BF16)


def relay(c, *arrays):
    rows, width = arrays[0].shape
    vmem = pl.BlockSpec(memory_space=pltpu.VMEM)
    return pl.pallas_call(
        functools.partial(relay_kernel, c),
        out_shape=(shape((rows, width // 2), BF16),) * 2,
        in_specs=[vmem] * 4,
        out_specs=(vmem, vmem),
        compiler_params=params(),
        cost_estimate=SMALL,
        name="relay",
    )(*arrays)


def total_kernel(c, near_top, top_a, top_b, near_bottom, bottom_a, bottom_b, *refs):
    own, down, up, across = refs[-4:]
    for k, lanes in enumerate(half_columns(c, near_top.shape[1])):
        at = slice(k * 256, k * 256 + 256)
        for near, a, b, first, second in (
            (near_top, top_a, top_b, own, down), (near_bottom, bottom_a, bottom_b, up, across)
        ):
            total = near[:, lanes].astype(F32) + a[:, at].astype(F32) + b[:, at].astype(F32)
            first[:, at] = total[:SLOTS].astype(BF16)
            second[:, at] = total[SLOTS:].astype(BF16)


def total(c, *arrays):
    rows, width = arrays[0].shape
    vmem = pl.BlockSpec(memory_space=pltpu.VMEM)
    return pl.pallas_call(
        functools.partial(total_kernel, c),
        out_shape=(shape((SLOTS, width // 2), BF16),) * 4,
        in_specs=[vmem] * 6 + [pl.BlockSpec(memory_space=pl.ANY)] * (len(arrays) - 6),
        out_specs=(vmem,) * 4,
        compiler_params=params(),
        cost_estimate=SMALL,
        name="total",
    )(*arrays)


def after(values, *earlier):
    return lax.optimization_barrier((values, earlier))[0]


def experts(rows, weights):
    last, following = along_first(rows, 1), along_first(rows, -1)
    across_top = along_first(last[: SLOTS // 2], 1)
    across_bottom = along_first(following[SLOTS // 2 :], -1)
    near_top = jnp.concatenate([rows, last], axis=0)
    near_bottom = jnp.concatenate([following, across_top, across_bottom], axis=0)
    near_top = after(near_top, across_top, across_bottom)
    before_top = along_second(near_top, 1)
    after_bottom = along_second(near_bottom, -1)
    out_near_top, out_near_bottom = expert(near_top, near_bottom, weights)
    before_top, after_bottom = after((before_top, after_bottom), out_near_top)
    far_top = along_second(before_top, 1)
    far_bottom = along_second(after_bottom, -1)
    early = expert(before_top, after_bottom, weights, parts=2)
    later_top, later_bottom = after((near_top, near_bottom), early[0])
    after_top = along_second(later_top, -1)
    before_bottom = along_second(later_bottom, 1)
    out_far = expert(*after((far_top, far_bottom), early[0]), weights, parts=2)
    second = after((after_top, before_bottom), out_far[0])
    out_after_top, out_before_bottom = expert(*second, weights)
    terms, order = [], (out_far[0],)
    for c in range(2):
        top, bottom = after(out_far[2 * c : 2 * c + 2], *order)
        relay_down, relay_up = along_second(top, 1), along_second(bottom, -1)
        top, bottom = after(early[2 * c : 2 * c + 2], *order)
        top_a, bottom_a = along_second(top, -1), along_second(bottom, 1)
        to_after, to_before = relay(c, out_after_top, relay_down, out_before_bottom, relay_up)
        order = (out_after_top,)
        top_b = along_second(to_after, 1)
        bottom_b = along_second(to_before, -1)
        own, down, up, across = total(c, out_near_top, top_a, top_b, out_near_bottom, bottom_a, bottom_b)
        terms.append((own, along_first(down, -1), along_first(up, 1), along_first(across, 2)))
    return terms


def weigh_kernel(where_ref, a_ref, b_ref, c_ref, d_ref, weight_ref, keep_ref, give_ref):
    rows = (a_ref[...].astype(F32) + b_ref[...].astype(F32)) + (c_ref[...].astype(F32) + d_ref[...].astype(F32))
    weighted = (rows * weight_ref[:, :1]).astype(BF16)
    _, mine, _, _ = place_of(where_ref)
    for core in range(2):

        @pl.when(mine == core)
        def _():
            for k in range(SIDE):
                to = slice(k * 256, (k + 1) * 256)
                for out, e in ((keep_ref, 2 * k + core), (give_ref, 2 * k + 1 - core)):
                    out[:, to] = weighted[:, e * 256 : (e + 1) * 256]


def weigh(where, terms, slot_weight):
    vmem = pl.BlockSpec(memory_space=pltpu.VMEM)
    return pl.pallas_call(
        weigh_kernel,
        out_shape=(shape((SLOTS, SIDE * 256), BF16),) * 2,
        in_specs=[pl.BlockSpec(memory_space=pltpu.SMEM)] + [vmem] * 5,
        out_specs=(vmem, vmem),
        compiler_params=params(),
        cost_estimate=SMALL,
        name="weigh",
    )(where, *terms, slot_weight)


def place_kernel(where_ref, keep_ref, got_ref, onehot_ref, own_ref, next_ref, last_ref, across_ref, scr):
    rows = jnp.concatenate([keep_ref[...], got_ref[...]], axis=0)
    placed = lax.dot_general(onehot_ref[...], rows, (((0,), (0,)), ((), ())), preferred_element_type=F32)
    for k in range(SIDE):
        scr[k] = placed[:, k * 256 : (k + 1) * 256]
    y, _, _, _ = place_of(where_ref)
    for by, out in ((0, own_ref), (1, next_ref), (3, last_ref), (2, across_ref)):
        out[...] = scr[(y + by) & 3].astype(out.dtype)


def place(where, keep, got, onehot):
    count = onehot.shape[1]
    vmem = pl.BlockSpec(memory_space=pltpu.VMEM)
    return pl.pallas_call(
        place_kernel,
        out_shape=(shape((count, 256), F32),) + (shape((count, 256), BF16),) * 3,
        in_specs=[pl.BlockSpec(memory_space=pltpu.SMEM)] + [vmem] * 3,
        out_specs=(vmem,) * 4,
        scratch_shapes=[pltpu.VMEM((SIDE, count, 256), F32)],
        compiler_params=params(),
        cost_estimate=SMALL,
        name="place",
    )(where, keep, got, onehot)


def residual_kernel(where_ref, tokens_ref, own_ref, a_ref, b_ref, c_ref, mixed_ref):
    summed = (own_ref[...] + a_ref[...].astype(F32)) + (b_ref[...].astype(F32) + c_ref[...].astype(F32))
    mixed_ref[...] = (tokens_ref[...].astype(F32) + summed).astype(BF16)


def residual(c, where, tokens, own, others):
    count, cols = own.shape
    whole = pl.BlockSpec((count, cols), lambda i, where: (0, 0))
    return pl.pallas_call(
        residual_kernel,
        out_shape=shape((count, cols), BF16),
        grid_spec=pltpu.PrefetchScalarGridSpec(
            num_scalar_prefetch=1,
            grid=(1,),
            in_specs=[pl.BlockSpec((count, cols), lambda i, where: (0, 2 * where[0] + c))] + [whole] * 4,
            out_specs=whole,
        ),
        compiler_params=params(),
        cost_estimate=SMALL,
        name="residual",
    )(where, tokens, own, *others)


def spread(per_head, lanes):
    heads = per_head.shape[1]
    pairs = []
    first = lax.broadcasted_iota(jnp.int32, (per_head.shape[0], 2 * HEAD_DIM), 1) < HEAD_DIM
    for k in range(heads // 2):
        pairs.append(jnp.where(first, per_head[:, 2 * k : 2 * k + 1], per_head[:, 2 * k + 1 : 2 * k + 2]))
    return jnp.concatenate(pairs, axis=1)


def project_kernel(c, where_ref, mine_ref, other_ref, gain_ref, in_w_ref, write_w_ref, read_w_ref, step_w_ref, *refs):
    y, core, _, _ = place_of(where_ref)
    squares, scaled, step_w = 0.0, [], []
    for e in range(8):
        away = (e // 2 + SIDE - y) & 3
        slot = jnp.where(away == 0, 0, jnp.where(away == 3, 1, away + 1))
        values = jnp.where(core == e % 2, mine_ref[slot], other_ref[slot]).astype(F32)
        squares += jnp.sum(values * values, axis=1, keepdims=True)
        scaled.append((values * gain_ref[e, c]).astype(BF16))
        step_w.append(step_w_ref[:, e * 512 + c * 256 : e * 512 + c * 256 + 256])
    scaled = jnp.concatenate(scaled, axis=1)

    def rows(ref):
        return ref[:, c].reshape(scaled.shape[1], ref.shape[3])

    write_read = jnp.concatenate([rows(write_w_ref), rows(read_w_ref)], axis=1)
    accs = [
        jnp.dot(scaled, rows(in_w_ref), preferred_element_type=F32),
        jnp.dot(scaled, write_read, preferred_element_type=F32),
        lax.dot_general(
            scaled, jnp.concatenate(step_w, axis=1), (((1,), (1,)), ((), ())), preferred_element_type=F32
        ),
        jnp.broadcast_to(squares, (squares.shape[0], 128)),
    ]
    if c == 0:
        for out, acc in zip(refs, accs):
            out[...] = acc
    else:
        before, (bias_ref, decay_ref) = refs[:4], refs[4:6]
        accs = [acc + ref[...] for acc, ref in zip(accs, before)]
        projected(where_ref, bias_ref, decay_ref, refs[6:15], accs, refs[15], 8 * 512)


def projected(where_ref, bias_ref, decay_ref, outs, accs, state_scr, width):
    in_acc, write_read, step_acc, square_acc = accs
    x_ref, write_ref, read_ref, step_ref, cum_ref = outs[:5]
    count, heads = step_acc.shape
    scale = lax.rsqrt(square_acc[:, :1] / width + EPSILON)
    x = (in_acc * scale).astype(BF16)
    x_ref[...] = x
    write = (write_read[:, :STATE] * scale).astype(BF16)
    write_ref[...] = write
    read_ref[...] = (write_read[:, STATE:] * scale).astype(BF16)
    raw = step_acc * scale + bias_ref[...]
    step = jnp.maximum(raw, 0.0) + jnp.log1p(jnp.exp(-jnp.abs(raw)))
    step_ref[...] = step
    log_decay = -step * jnp.exp(decay_ref[...])
    lower = lax.broadcasted_iota(jnp.int32, (count, count), 0) >= lax.broadcasted_iota(jnp.int32, (count, count), 1)
    cum = jnp.dot(lower.astype(F32), log_decay, preferred_element_type=F32, precision=PRECISE)
    cum_ref[...] = cum
    last = cum[count - 1 :, :]
    to_end = jnp.exp(last - cum) * step
    weighted = (x.astype(F32) * spread(to_end, x.shape[1])).astype(BF16)
    state = lax.dot_general(write, weighted, (((0,), (0,)), ((), ())), preferred_element_type=F32)
    whole = spread(last, x.shape[1])
    high = whole.astype(BF16).astype(F32)
    row = lax.broadcasted_iota(jnp.int32, (16, x.shape[1]), 0)
    log_rows = jnp.where(row == 0, high, jnp.where(row == 1, whole - high, 0.0)).astype(BF16)
    cols = x.shape[1] // SIDE
    for q in range(SIDE):
        lanes = slice(q * cols, (q + 1) * cols)
        state_scr[q, :STATE, :] = state[:, lanes].astype(BF16)
        state_scr[q, STATE:, :] = log_rows[:, lanes]
    _, _, _, at = place_of(where_ref)
    for by, out in zip((0, 1, 3, 2), outs[5:]):
        out[...] = state_scr[(at + by) & 3]


def project(c, where, mine, other, gain, weights, *more):
    _, count, cols = mine.shape
    lanes, heads = weights[0].shape[1], weights[3].shape[1]
    smem, vmem = pl.BlockSpec(memory_space=pltpu.SMEM), pl.BlockSpec(memory_space=pltpu.VMEM)
    cut = [w.reshape(8, 2, cols, w.shape[1]) for w in weights[:3]]
    if c == 0:
        outs = tuple(shape((count, n), F32) for n in (lanes, 2 * STATE, heads, 128))
        scratch = []
    else:
        quarter = (STATE + 16, lanes // SIDE)
        outs = (
            shape((count, lanes), BF16), shape((count, STATE), BF16), shape((count, STATE), BF16),
            shape((count, heads), F32), shape((count, heads), F32),
        ) + (shape(quarter, BF16),) * 4
        scratch = [pltpu.VMEM((SIDE,) + quarter, BF16)]
    return pl.pallas_call(
        functools.partial(project_kernel, c),
        out_shape=outs,
        in_specs=[smem] + [vmem] * (7 + len(more)),
        out_specs=(vmem,) * len(outs),
        scratch_shapes=scratch,
        compiler_params=params(),
        cost_estimate=pl.CostEstimate(flops=3 * 10**9, bytes_accessed=10**6, transcendentals=0),
        name="project",
    )(where, mine, other, gain.reshape(8, 2, 1, cols), *cut, weights[3].T, *more)


def inside_kernel(x_ref, write_ref, read_ref, step_ref, cum_ref, skip_ref, out_ref):
    count, heads = step_ref.shape
    span = count // 2
    scores = lax.dot_general(read_ref[...], write_ref[...], (((1,), (1,)), ((), ())), preferred_element_type=F32)
    cum = cum_ref[...]
    cum_t, step_t = cum.T, step_ref[...].T
    causal = lax.broadcasted_iota(jnp.int32, (span, span), 0) >= lax.broadcasted_iota(jnp.int32, (span, span), 1)
    low, high = slice(0, span), slice(span, count)

    def mixing(h, rows, columns):
        gaps = cum[rows, h : h + 1] - cum_t[h : h + 1, columns]
        if rows == columns:
            gaps = jnp.where(causal, gaps, -jnp.inf)
        return (scores[rows, columns] * jnp.exp(gaps) * step_t[h : h + 1, columns]).astype(BF16)

    for h in range(heads):
        lanes = slice(h * HEAD_DIM, (h + 1) * HEAD_DIM)
        x = x_ref[:, lanes]
        skipped = skip_ref[0, h] * x.astype(F32)
        top = jnp.dot(mixing(h, low, low), x[low], preferred_element_type=F32)
        below = jnp.concatenate([mixing(h, high, low), mixing(h, high, high)], axis=1)
        bottom = jnp.dot(below, x, preferred_element_type=F32)
        out_ref[:, lanes] = jnp.concatenate([top, bottom], axis=0) + skipped


def inside(x, write, read, step, cum, skip_gain):
    vmem = pl.BlockSpec(memory_space=pltpu.VMEM)
    return pl.pallas_call(
        inside_kernel,
        out_shape=shape(x.shape, F32),
        in_specs=[vmem] * 5 + [pl.BlockSpec(memory_space=pltpu.SMEM)],
        out_specs=vmem,
        compiler_params=params(),
        cost_estimate=pl.CostEstimate(flops=2 * 10**9, bytes_accessed=2 * 10**6, transcendentals=10**6),
        name="inside",
    )(x, write, read, step, cum, skip_gain.reshape(1, -1))


def log_of(ref):
    return ref[STATE : STATE + 1, :].astype(F32) + ref[STATE + 1 : STATE + 2, :].astype(F32)


def weights_before(here, places, logs):
    terms = []
    for s in places:
        between = sum(jnp.where((s < u) & (u < here), log, 0.0) for u, log in zip(places, logs))
        terms.append(jnp.where(s < here, jnp.exp(between), 0.0))
    return terms


def row_total_kernel(where_ref, own_ref, last_ref, next_ref, across_ref, total_ref):
    _, _, _, here = place_of(where_ref)
    refs = (own_ref, last_ref, next_ref, across_ref)
    places = [here, (here + 3) & 3, (here + 1) & 3, (here + 2) & 3]
    logs = [log_of(ref) for ref in refs]
    until_end = [jnp.exp(sum(jnp.where(s < u, log, 0.0) for u, log in zip(places, logs))) for s in places]
    total_ref[:STATE, :] = sum(w * ref[:STATE, :].astype(F32) for w, ref in zip(until_end, refs)).astype(BF16)
    whole = sum(logs)
    top = whole.astype(BF16).astype(F32)
    row = lax.broadcasted_iota(jnp.int32, (16, whole.shape[1]), 0)
    total_ref[STATE:, :] = jnp.where(row == 0, top, jnp.where(row == 1, whole - top, 0.0)).astype(BF16)


def row_total(where, parts):
    vmem = pl.BlockSpec(memory_space=pltpu.VMEM)
    return pl.pallas_call(
        row_total_kernel,
        out_shape=shape(parts[0].shape, BF16),
        in_specs=[pl.BlockSpec(memory_space=pltpu.SMEM)] + [vmem] * 4,
        out_specs=vmem,
        compiler_params=params(),
        cost_estimate=SMALL,
        name="row_total",
    )(where, *parts)


def carry_kernel(where_ref, *refs):
    parts, earlier, outs = refs[:4], refs[4:7], refs[7:]
    _, _, z, here = place_of(where_ref)
    rows = [(z + 3) & 3, (z + 1) & 3, (z + 2) & 3]
    before = weights_before(z, rows, [log_of(ref) for ref in earlier])
    to_row = sum(w * ref[:STATE, :].astype(F32) for w, ref in zip(before, earlier))
    places = [here, (here + 3) & 3, (here + 1) & 3, (here + 2) & 3]
    logs = [log_of(ref) for ref in parts]
    for by, out in zip((0, 1, 3, 2), outs):
        target = (here + by) & 3
        gone = sum(jnp.where(s < target, log, 0.0) for s, log in zip(places, logs))
        state = jnp.exp(gone) * to_row
        for w, ref in zip(weights_before(target, places, logs), parts):
            state += w * ref[:STATE, :].astype(F32)
        out[...] = state.astype(BF16)


def carry(where, parts, earlier):
    vmem = pl.BlockSpec(memory_space=pltpu.VMEM)
    return pl.pallas_call(
        carry_kernel,
        out_shape=(shape((STATE, parts[0].shape[1]), BF16),) * 4,
        in_specs=[pl.BlockSpec(memory_space=pltpu.SMEM)] + [vmem] * 7,
        out_specs=(vmem,) * 4,
        compiler_params=params(),
        cost_estimate=SMALL,
        name="carry",
    )(where, *parts, *earlier)


def finish_kernel(where_ref, own_ref, last_ref, next_ref, across_ref, read_ref, cum_ref, inside_ref, out_ref, scr):
    _, _, _, here = place_of(where_ref)
    for by, ref in ((0, own_ref), (3, last_ref), (1, next_ref), (2, across_ref)):
        scr[(here + by) & 3] = ref[...]
    cols = own_ref.shape[1]
    decayed = spread(jnp.exp(cum_ref[...]), SIDE * cols)
    for q in range(SIDE):
        lanes = slice(q * cols, (q + 1) * cols)
        from_prior = jnp.dot(read_ref[...], scr[q], preferred_element_type=F32)
        out_ref[:, lanes] = (inside_ref[:, lanes] + decayed[:, lanes] * from_prior).astype(BF16)


def finish(where, parts, read, cum, within):
    vmem = pl.BlockSpec(memory_space=pltpu.VMEM)
    return pl.pallas_call(
        finish_kernel,
        out_shape=shape(within.shape, BF16),
        in_specs=[pl.BlockSpec(memory_space=pltpu.SMEM)] + [vmem] * 7,
        out_specs=vmem,
        scratch_shapes=[pltpu.VMEM((SIDE,) + parts[0].shape, BF16)],
        compiler_params=params(),
        cost_estimate=SMALL,
        name="finish",
    )(where, *parts, read, cum, within)


def body(
    tokens,
    routes,
    route_weight,
    moe_gain,
    gate_weight,
    up_weight,
    down_weight,
    ssd_gain,
    input_weight,
    write_weight,
    read_weight,
    step_weight,
    step_bias,
    decay_log,
    skip_gain,
):
    where = jnp.stack([lax.axis_index("expert"), lax.axis_index("frame")]).astype(jnp.int32)
    rows, onehot, slot_weight = pick(where, tokens, routes, route_weight, moe_gain)
    halves = experts(rows, (gate_weight[0], up_weight[0], down_weight[0]))
    weights = (input_weight, write_weight, read_weight, step_weight)
    mixed, more, order = [], (), ()
    for c in range(2):
        keep, give = weigh(where, after(halves[c], *order), slot_weight)
        own, to_next, to_last, to_across = place(where, keep, to_sibling(give), onehot)
        others = (along_y(to_next, 1), along_y(to_last, -1), along_y(to_across, 2))
        half = residual(c, where, tokens, own, others)
        order = (own,)
        mixed.append(half)
        mine = jnp.stack([half, along_y(half, 1), along_y(half, -1), along_y(half, 2)])
        if c == 1:
            more = (*more, step_bias.reshape(1, -1), decay_log.reshape(1, -1))
        more = project(c, where, mine, to_sibling(mine), ssd_gain, weights, *more)
    inputs, write, read, step, cum, state, to_next, to_last, to_across = more
    parts = (state, along_x(to_next, 1), along_x(to_last, -1), along_x(to_across, 2))
    row = row_total(where, parts)
    earlier = (along_z(row, 1), along_z(row, -1), along_z(row, 2))
    within = inside(inputs, write, read, step, cum, skip_gain)
    prior, to_next, to_last, to_across = carry(where, parts, earlier)
    carried = (prior, along_x(to_next, 1), along_x(to_last, -1), along_x(to_across, 2))
    ssd_out = finish(where, carried, read, cum, within)
    return (jnp.concatenate(mixed, axis=1), ssd_out)


def solution(mesh):
    placed = (
        P("frame", None),
        P("frame", None),
        P("frame", None),
        P(),
        P("expert", "frame", None),
        P("expert", "frame", None),
        P("expert", "frame", None),
        P(),
        P(None, "expert"),
        P(None, "expert"),
        P(None, "expert"),
        P(None, "expert"),
        P("expert"),
        P("expert"),
        P("expert"),
    )
    return jax.shard_map(
        body,
        mesh=mesh,
        in_specs=placed,
        out_specs=(P("frame", "expert"), P("frame", "expert")),
        check_vma=False,
    )
```

```python
import functools

import jax
import jax.numpy as jnp
from jax import lax
from jax.experimental import pallas as pl
from jax.experimental.pallas import tpu as pltpu
from jax.sharding import PartitionSpec as P

HEAD_DIM = 64
STATE = 128
SLOTS = 96
SIDE = 4
EPSILON = 1e-06
PRECISE = lax.Precision.HIGHEST
AXES = ("expert", "frame")
F32, BF16 = jnp.float32, jnp.bfloat16


def routes_of(rule):
    pairs = []
    for y in range(SIDE):
        for core in range(2):
            for z in range(SIDE):
                for x in range(SIDE):
                    ny, nc, nz, nx = rule(y, core, z, x)
                    source = (y * 2 + core) * 16 + z * SIDE + x
                    target = ((ny % SIDE) * 2 + nc % 2) * 16 + (nz % SIDE) * SIDE + nx % SIDE
                    pairs.append((source, target))
    return pairs


def send(array, rule):
    return lax.ppermute(array, AXES, routes_of(rule))


def along_first(array, by):
    return send(array, lambda y, c, z, x: (y, c, z + by * c, x + by * (1 - c)))


def along_second(array, by):
    return send(array, lambda y, c, z, x: (y, c, z + by * (1 - c), x + by * c))


def along_x(array, by):
    return send(array, lambda y, c, z, x: (y, c, z, x + by))


def along_z(array, by):
    return send(array, lambda y, c, z, x: (y, c, z + by, x))


def along_y(array, by):
    return send(array, lambda y, c, z, x: (y + by, c, z, x))


def to_sibling(array):
    return send(array, lambda y, c, z, x: (y, 1 - c, z, x))


def shape(dims, kind):
    return jax.ShapeDtypeStruct(dims, kind)


def params(mebibytes=20):
    return pltpu.CompilerParams(vmem_limit_bytes=mebibytes * 1024 * 1024)


SMALL = pl.CostEstimate(flops=10**6, bytes_accessed=10**5, transcendentals=0)


def place_of(where_ref):
    return where_ref[0] >> 1, where_ref[0] & 1, where_ref[1] >> 2, where_ref[1] & 3


def pick_kernel(where_ref, *refs):
    arrays, (rows_ref, onehot_ref, slot_weight_ref), held, sems = refs[:4], refs[4:7], refs[7:11], refs[11]
    copies = [pltpu.make_async_copy(source, to, sems.at[k]) for k, (source, to) in enumerate(zip(arrays, held))]
    for copy in copies:
        copy.start()
    tokens_ref, routes_ref, weight_ref, gain_ref = held
    count = tokens_ref.shape[0]
    upper = lax.broadcasted_iota(jnp.int32, (count, count), 0) <= lax.broadcasted_iota(jnp.int32, (count, count), 1)
    slot = lax.broadcasted_iota(jnp.int32, (SLOTS, count), 0)
    copies[1].wait()
    copies[2].wait()
    onehots = []
    for sibling in range(2):
        hits = routes_ref[...] == where_ref[0] ^ sibling
        chosen = jnp.max(hits.astype(F32), axis=0, keepdims=True)
        wide = jnp.broadcast_to(chosen, (SLOTS, count))
        place = jnp.dot(wide.astype(BF16), upper.astype(BF16), preferred_element_type=F32) - 1.0
        named = (place.astype(jnp.int32) == slot) & (wide > 0.0)
        onehots.append(jnp.where(named, 1.0, 0.0).astype(BF16))
        if sibling == 0:
            weights = jnp.sum(jnp.where(hits, weight_ref[...], 0.0), axis=0, keepdims=True)
            slot_weight = jnp.sum(jnp.where(named, weights, 0.0), axis=1, keepdims=True)
    onehot_ref[...] = jnp.concatenate(onehots, axis=0)
    slot_weight_ref[...] = jnp.broadcast_to(slot_weight, slot_weight_ref.shape)
    copies[0].wait()
    copies[3].wait()
    picked = jnp.dot(onehots[0], tokens_ref[...], preferred_element_type=F32)
    mean_sq = jnp.mean(picked * picked, axis=1, keepdims=True)
    rows_ref[...] = (picked * lax.rsqrt(mean_sq + EPSILON) * gain_ref[...]).astype(BF16)


def pick(where, tokens, routes, route_weight, gain):
    count, width = tokens.shape
    smem, vmem = pl.BlockSpec(memory_space=pltpu.SMEM), pl.BlockSpec(memory_space=pltpu.VMEM)
    arrays = (tokens, routes.T, route_weight.T, gain.reshape(1, width))
    return pl.pallas_call(
        pick_kernel,
        out_shape=(shape((SLOTS, width), BF16), shape((2 * SLOTS, count), BF16), shape((SLOTS, 128), F32)),
        in_specs=[smem] + [pl.BlockSpec(memory_space=pltpu.HBM)] * 4,
        out_specs=(vmem, vmem, vmem),
        scratch_shapes=[pltpu.VMEM(array.shape, array.dtype) for array in arrays] + [pltpu.SemaphoreType.DMA((4,))],
        compiler_params=params(60),
        name="pick",
    )(where, *arrays)


def expert_kernel(pieces, *refs):
    gate_ref, up_ref, down_ref = refs[pieces : pieces + 3]
    rows = jnp.concatenate([ref[...] for ref in refs[:pieces]], axis=0)
    by_row = (((1,), (1,)), ((), ()))
    gate = lax.dot_general(rows, gate_ref[...], by_row, preferred_element_type=F32)
    upper = lax.dot_general(rows, up_ref[...], by_row, preferred_element_type=F32)
    hidden = (gate / (1.0 + jnp.exp(-gate)) * upper).astype(BF16)
    out = jnp.dot(hidden, down_ref[...], preferred_element_type=F32).astype(BF16)
    at = 0
    for ref in refs[pieces + 3 :]:
        ref[...] = out[at : at + ref.shape[0]]
        at += ref.shape[0]


def expert(pieces, weights, devices=(2, 2)):
    vmem = pl.BlockSpec(memory_space=pltpu.VMEM)
    units, width = weights[0].shape
    return pl.pallas_call(
        functools.partial(expert_kernel, len(pieces)),
        out_shape=tuple(shape((count * SLOTS, width), BF16) for count in devices),
        in_specs=[vmem] * (len(pieces) + 3),
        out_specs=(vmem,) * len(devices),
        compiler_params=params(28),
        cost_estimate=pl.CostEstimate(
            flops=24 * SLOTS * width * units, bytes_accessed=6 * units * width + 16 * SLOTS * width, transcendentals=0
        ),
        name="expert",
    )(*pieces, *weights)


def relay_kernel(after_ref, down_ref, before_ref, up_ref, to_after_own_ref, to_after_last_ref, to_before_ref):
    to_after = (after_ref[...].astype(F32) + down_ref[...].astype(F32)).astype(BF16)
    to_after_own_ref[...] = to_after[:SLOTS]
    to_after_last_ref[...] = to_after[SLOTS:]
    to_before_ref[...] = (before_ref[...].astype(F32) + up_ref[...].astype(F32)).astype(BF16)


def relay(*arrays):
    vmem = pl.BlockSpec(memory_space=pltpu.VMEM)
    rows, width = arrays[0].shape
    return pl.pallas_call(
        relay_kernel,
        out_shape=tuple(shape((count, width), BF16) for count in (SLOTS, SLOTS, rows)),
        in_specs=[vmem] * 4,
        out_specs=(vmem,) * 3,
        compiler_params=params(),
        cost_estimate=SMALL,
        name="relay",
    )(*arrays)


def block_columns(c, e):
    return slice(e * 512 + c * 256, e * 512 + c * 256 + 256), slice(e * 256, e * 256 + 256)


def total_kernel(near_top, last_a, last_b, near_bottom, bottom_a, bottom_b, *outs):
    for c in range(2):
        down, up, across = outs[3 * c : 3 * c + 3]
        for e in range(8):
            lanes, at = block_columns(c, e)
            last = near_top[SLOTS:, lanes].astype(F32) + last_a[:, lanes].astype(F32) + last_b[:, lanes].astype(F32)
            down[:, at] = last.astype(BF16)
            bottom = near_bottom[:, lanes].astype(F32) + bottom_a[:, lanes].astype(F32) + bottom_b[:, lanes].astype(F32)
            up[:, at] = bottom[:SLOTS].astype(BF16)
            across[:, at] = bottom[SLOTS:].astype(BF16)


def total(*arrays):
    vmem = pl.BlockSpec(memory_space=pltpu.VMEM)
    return pl.pallas_call(
        total_kernel,
        out_shape=(shape((SLOTS, arrays[0].shape[1] // 2), BF16),) * 6,
        in_specs=[vmem] * 6,
        out_specs=(vmem,) * 6,
        compiler_params=params(),
        cost_estimate=SMALL,
        name="total",
    )(*arrays)


def after(values, *earlier):
    return lax.optimization_barrier((values, earlier))[0]


def experts(rows, weights):
    last, following = along_first(rows, 1), along_first(rows, -1)
    across_top = along_first(last[: SLOTS // 2], 1)
    across_bottom = along_first(following[SLOTS // 2 :], -1)
    near_top = jnp.concatenate([rows, last], axis=0)
    near_bottom = jnp.concatenate([following, across_top, across_bottom], axis=0)
    near_top = after(near_top, across_top, across_bottom)
    before_top = along_second(near_top, 1)
    after_bottom = along_second(near_bottom, -1)
    out_near_top, out_near_bottom = expert((near_top, near_bottom), weights)
    before_top, after_bottom = after((before_top, after_bottom), out_near_top)
    far_top = along_second(before_top, 1)
    far_bottom = along_second(after_bottom, -1)
    before_own, before_last, out_after_bottom = expert((before_top, after_bottom), weights, (1, 1, 2))
    later_top, later_bottom = after((near_top, near_bottom), before_own)
    after_top = along_second(later_top, -1)
    before_bottom = along_second(later_bottom, 1)
    out_far_top, out_far_bottom = expert(after((far_top, far_bottom), before_own), weights)
    relay_down = along_second(out_far_top, 1)
    relay_up = along_second(out_far_bottom, -1)
    first_last, first_bottom = after((before_last, out_after_bottom), out_far_top)
    last_a = along_second(first_last, -1)
    bottom_a = along_second(first_bottom, 1)
    second = after((after_top, before_bottom), relay_down, relay_up)
    out_after_top, out_before_bottom = expert(second, weights)
    to_after_own, to_after_last, to_before = relay(out_after_top, relay_down, out_before_bottom, relay_up)
    last_b = along_second(after(to_after_last, last_a), 1)
    bottom_b = along_second(to_before, -1)
    own_a = along_second(after(before_own, to_before), -1)
    own_b = along_second(to_after_own, 1)
    sums = total(out_near_top, last_a, last_b, out_near_bottom, bottom_a, bottom_b)
    terms = []
    for c in range(2):
        down, up, across = sums[3 * c : 3 * c + 3]
        first_ring = (along_first(down, -1), along_first(up, 1), along_first(across, 2))
        terms.append((out_near_top, own_a, own_b, *first_ring))
    return terms


def weigh_kernel(c, where_ref, near_ref, own_a, own_b, first, second, third, weight_ref, keep_ref, give_ref):
    weight = weight_ref[:, :1]
    weighted = []
    for e in range(8):
        lanes, at = block_columns(c, e)
        rows = near_ref[:SLOTS, lanes].astype(F32) + own_a[:, lanes].astype(F32) + own_b[:, lanes].astype(F32)
        rows += first[:, at].astype(F32) + second[:, at].astype(F32) + third[:, at].astype(F32)
        weighted.append((rows * weight).astype(BF16))
    _, mine, _, _ = place_of(where_ref)
    for core in range(2):

        @pl.when(mine == core)
        def _():
            for k in range(SIDE):
                to = slice(k * 256, (k + 1) * 256)
                for out, e in ((keep_ref, 2 * k + core), (give_ref, 2 * k + 1 - core)):
                    out[:, to] = weighted[e]


def weigh(c, where, terms, slot_weight):
    vmem = pl.BlockSpec(memory_space=pltpu.VMEM)
    return pl.pallas_call(
        functools.partial(weigh_kernel, c),
        out_shape=(shape((SLOTS, SIDE * 256), BF16),) * 2,
        in_specs=[pl.BlockSpec(memory_space=pltpu.SMEM)] + [vmem] * 7,
        out_specs=(vmem, vmem),
        compiler_params=params(),
        cost_estimate=SMALL,
        name="weigh",
    )(where, *terms, slot_weight)


def place_kernel(where_ref, keep_ref, got_ref, onehot_ref, own_ref, next_ref, last_ref, across_ref, scr):
    rows = jnp.concatenate([keep_ref[...], got_ref[...]], axis=0)
    placed = lax.dot_general(onehot_ref[...], rows, (((0,), (0,)), ((), ())), preferred_element_type=F32)
    for k in range(SIDE):
        scr[k] = placed[:, k * 256 : (k + 1) * 256]
    y, _, _, _ = place_of(where_ref)
    for by, out in ((0, own_ref), (1, next_ref), (3, last_ref), (2, across_ref)):
        out[...] = scr[(y + by) & 3].astype(out.dtype)


def place(where, keep, got, onehot):
    count = onehot.shape[1]
    vmem = pl.BlockSpec(memory_space=pltpu.VMEM)
    return pl.pallas_call(
        place_kernel,
        out_shape=(shape((count, 256), F32),) + (shape((count, 256), BF16),) * 3,
        in_specs=[pl.BlockSpec(memory_space=pltpu.SMEM)] + [vmem] * 3,
        out_specs=(vmem,) * 4,
        scratch_shapes=[pltpu.VMEM((SIDE, count, 256), F32)],
        compiler_params=params(),
        cost_estimate=SMALL,
        name="place",
    )(where, keep, got, onehot)


def residual_kernel(where_ref, tokens_ref, own_ref, a_ref, b_ref, c_ref, mixed_ref):
    summed = (own_ref[...] + a_ref[...].astype(F32)) + (b_ref[...].astype(F32) + c_ref[...].astype(F32))
    mixed_ref[...] = (tokens_ref[...].astype(F32) + summed).astype(BF16)


def residual(c, where, tokens, own, others):
    count, cols = own.shape
    whole = pl.BlockSpec((count, cols), lambda i, where: (0, 0))
    return pl.pallas_call(
        residual_kernel,
        out_shape=shape((count, cols), BF16),
        grid_spec=pltpu.PrefetchScalarGridSpec(
            num_scalar_prefetch=1,
            grid=(1,),
            in_specs=[pl.BlockSpec((count, cols), lambda i, where: (0, 2 * where[0] + c))] + [whole] * 4,
            out_specs=whole,
        ),
        compiler_params=params(),
        cost_estimate=SMALL,
        name="residual",
    )(where, tokens, own, *others)


def spread(per_head, lanes):
    heads = per_head.shape[1]
    pairs = []
    first = lax.broadcasted_iota(jnp.int32, (per_head.shape[0], 2 * HEAD_DIM), 1) < HEAD_DIM
    for k in range(heads // 2):
        pairs.append(jnp.where(first, per_head[:, 2 * k : 2 * k + 1], per_head[:, 2 * k + 1 : 2 * k + 2]))
    return jnp.concatenate(pairs, axis=1)


def project_kernel(c, where_ref, mine_ref, other_ref, gain_ref, in_w_ref, write_w_ref, read_w_ref, step_w_ref, *refs):
    y, core, _, _ = place_of(where_ref)
    squares, scaled, step_w = 0.0, [], []
    for e in range(8):
        away = (e // 2 + SIDE - y) & 3
        slot = jnp.where(away == 0, 0, jnp.where(away == 3, 1, away + 1))
        values = jnp.where(core == e % 2, mine_ref[slot], other_ref[slot]).astype(F32)
        squares += jnp.sum(values * values, axis=1, keepdims=True)
        scaled.append((values * gain_ref[e, c]).astype(BF16))
        step_w.append(step_w_ref[:, e * 512 + c * 256 : e * 512 + c * 256 + 256])
    scaled = jnp.concatenate(scaled, axis=1)

    def rows(ref):
        return ref[:, c].reshape(scaled.shape[1], ref.shape[3])

    write_read = jnp.concatenate([rows(write_w_ref), rows(read_w_ref)], axis=1)
    accs = [
        jnp.dot(scaled, rows(in_w_ref), preferred_element_type=F32),
        jnp.dot(scaled, write_read, preferred_element_type=F32),
        lax.dot_general(
            scaled, jnp.concatenate(step_w, axis=1), (((1,), (1,)), ((), ())), preferred_element_type=F32
        ),
        jnp.broadcast_to(squares, (squares.shape[0], 128)),
    ]
    if c == 0:
        for out, acc in zip(refs, accs):
            out[...] = acc
    else:
        before, (bias_ref, decay_ref) = refs[:4], refs[4:6]
        accs = [acc + ref[...] for acc, ref in zip(accs, before)]
        projected(where_ref, bias_ref, decay_ref, refs[6:15], accs, refs[15], 8 * 512)


def projected(where_ref, bias_ref, decay_ref, outs, accs, state_scr, width):
    in_acc, write_read, step_acc, square_acc = accs
    x_ref, write_ref, read_ref, step_ref, cum_ref = outs[:5]
    count, heads = step_acc.shape
    scale = lax.rsqrt(square_acc[:, :1] / width + EPSILON)
    x = (in_acc * scale).astype(BF16)
    x_ref[...] = x
    write = (write_read[:, :STATE] * scale).astype(BF16)
    write_ref[...] = write
    read_ref[...] = (write_read[:, STATE:] * scale).astype(BF16)
    raw = step_acc * scale + bias_ref[...]
    step = jnp.maximum(raw, 0.0) + jnp.log1p(jnp.exp(-jnp.abs(raw)))
    step_ref[...] = step
    log_decay = -step * jnp.exp(decay_ref[...])
    lower = lax.broadcasted_iota(jnp.int32, (count, count), 0) >= lax.broadcasted_iota(jnp.int32, (count, count), 1)
    cum = jnp.dot(lower.astype(F32), log_decay, preferred_element_type=F32, precision=PRECISE)
    cum_ref[...] = cum
    last = cum[count - 1 :, :]
    to_end = jnp.exp(last - cum) * step
    weighted = (x.astype(F32) * spread(to_end, x.shape[1])).astype(BF16)
    state = lax.dot_general(write, weighted, (((0,), (0,)), ((), ())), preferred_element_type=F32)
    whole = spread(last, x.shape[1])
    high = whole.astype(BF16).astype(F32)
    row = lax.broadcasted_iota(jnp.int32, (16, x.shape[1]), 0)
    log_rows = jnp.where(row == 0, high, jnp.where(row == 1, whole - high, 0.0)).astype(BF16)
    cols = x.shape[1] // SIDE
    for q in range(SIDE):
        lanes = slice(q * cols, (q + 1) * cols)
        state_scr[q, :STATE, :] = state[:, lanes].astype(BF16)
        state_scr[q, STATE:, :] = log_rows[:, lanes]
    _, _, _, at = place_of(where_ref)
    for by, out in zip((0, 1, 3, 2), outs[5:]):
        out[...] = state_scr[(at + by) & 3]


def project(c, where, mine, other, gain, weights, *more):
    _, count, cols = mine.shape
    lanes, heads = weights[0].shape[1], weights[3].shape[1]
    smem, vmem = pl.BlockSpec(memory_space=pltpu.SMEM), pl.BlockSpec(memory_space=pltpu.VMEM)
    cut = [w.reshape(8, 2, cols, w.shape[1]) for w in weights[:3]]
    if c == 0:
        outs = tuple(shape((count, n), F32) for n in (lanes, 2 * STATE, heads, 128))
        scratch = []
    else:
        quarter = (STATE + 16, lanes // SIDE)
        outs = (
            shape((count, lanes), BF16), shape((count, STATE), BF16), shape((count, STATE), BF16),
            shape((count, heads), F32), shape((count, heads), F32),
        ) + (shape(quarter, BF16),) * 4
        scratch = [pltpu.VMEM((SIDE,) + quarter, BF16)]
    return pl.pallas_call(
        functools.partial(project_kernel, c),
        out_shape=outs,
        in_specs=[smem] + [vmem] * (7 + len(more)),
        out_specs=(vmem,) * len(outs),
        scratch_shapes=scratch,
        compiler_params=params(),
        cost_estimate=pl.CostEstimate(flops=3 * 10**9, bytes_accessed=10**6, transcendentals=0),
        name="project",
    )(where, mine, other, gain.reshape(8, 2, 1, cols), *cut, weights[3].T, *more)


def inside_kernel(x_ref, write_ref, read_ref, step_ref, cum_ref, skip_ref, out_ref):
    count, heads = step_ref.shape
    span = count // 2
    scores = lax.dot_general(read_ref[...], write_ref[...], (((1,), (1,)), ((), ())), preferred_element_type=F32)
    cum = cum_ref[...]
    cum_t, step_t = cum.T, step_ref[...].T
    causal = lax.broadcasted_iota(jnp.int32, (span, span), 0) >= lax.broadcasted_iota(jnp.int32, (span, span), 1)
    low, high = slice(0, span), slice(span, count)

    def mixing(h, rows, columns):
        gaps = cum[rows, h : h + 1] - cum_t[h : h + 1, columns]
        if rows == columns:
            gaps = jnp.where(causal, gaps, -jnp.inf)
        return (scores[rows, columns] * jnp.exp(gaps) * step_t[h : h + 1, columns]).astype(BF16)

    for h in range(heads):
        lanes = slice(h * HEAD_DIM, (h + 1) * HEAD_DIM)
        x = x_ref[:, lanes]
        skipped = skip_ref[0, h] * x.astype(F32)
        top = jnp.dot(mixing(h, low, low), x[low], preferred_element_type=F32)
        below = jnp.concatenate([mixing(h, high, low), mixing(h, high, high)], axis=1)
        bottom = jnp.dot(below, x, preferred_element_type=F32)
        out_ref[:, lanes] = jnp.concatenate([top, bottom], axis=0) + skipped


def inside(x, write, read, step, cum, skip_gain):
    vmem = pl.BlockSpec(memory_space=pltpu.VMEM)
    return pl.pallas_call(
        inside_kernel,
        out_shape=shape(x.shape, F32),
        in_specs=[vmem] * 5 + [pl.BlockSpec(memory_space=pltpu.SMEM)],
        out_specs=vmem,
        compiler_params=params(),
        cost_estimate=pl.CostEstimate(flops=2 * 10**9, bytes_accessed=2 * 10**6, transcendentals=10**6),
        name="inside",
    )(x, write, read, step, cum, skip_gain.reshape(1, -1))


def log_of(ref):
    return ref[STATE : STATE + 1, :].astype(F32) + ref[STATE + 1 : STATE + 2, :].astype(F32)


def weights_before(here, places, logs):
    terms = []
    for s in places:
        between = sum(jnp.where((s < u) & (u < here), log, 0.0) for u, log in zip(places, logs))
        terms.append(jnp.where(s < here, jnp.exp(between), 0.0))
    return terms


def row_total_kernel(where_ref, own_ref, last_ref, next_ref, across_ref, total_ref):
    _, _, _, here = place_of(where_ref)
    refs = (own_ref, last_ref, next_ref, across_ref)
    places = [here, (here + 3) & 3, (here + 1) & 3, (here + 2) & 3]
    logs = [log_of(ref) for ref in refs]
    until_end = [jnp.exp(sum(jnp.where(s < u, log, 0.0) for u, log in zip(places, logs))) for s in places]
    total_ref[:STATE, :] = sum(w * ref[:STATE, :].astype(F32) for w, ref in zip(until_end, refs)).astype(BF16)
    whole = sum(logs)
    top = whole.astype(BF16).astype(F32)
    row = lax.broadcasted_iota(jnp.int32, (16, whole.shape[1]), 0)
    total_ref[STATE:, :] = jnp.where(row == 0, top, jnp.where(row == 1, whole - top, 0.0)).astype(BF16)


def row_total(where, parts):
    vmem = pl.BlockSpec(memory_space=pltpu.VMEM)
    return pl.pallas_call(
        row_total_kernel,
        out_shape=shape(parts[0].shape, BF16),
        in_specs=[pl.BlockSpec(memory_space=pltpu.SMEM)] + [vmem] * 4,
        out_specs=vmem,
        compiler_params=params(),
        cost_estimate=SMALL,
        name="row_total",
    )(where, *parts)


def carry_kernel(where_ref, *refs):
    parts, earlier, outs = refs[:4], refs[4:7], refs[7:]
    _, _, z, here = place_of(where_ref)
    rows = [(z + 3) & 3, (z + 1) & 3, (z + 2) & 3]
    before = weights_before(z, rows, [log_of(ref) for ref in earlier])
    to_row = sum(w * ref[:STATE, :].astype(F32) for w, ref in zip(before, earlier))
    places = [here, (here + 3) & 3, (here + 1) & 3, (here + 2) & 3]
    logs = [log_of(ref) for ref in parts]
    for by, out in zip((0, 1, 3, 2), outs):
        target = (here + by) & 3
        gone = sum(jnp.where(s < target, log, 0.0) for s, log in zip(places, logs))
        state = jnp.exp(gone) * to_row
        for w, ref in zip(weights_before(target, places, logs), parts):
            state += w * ref[:STATE, :].astype(F32)
        out[...] = state.astype(BF16)


def carry(where, parts, earlier):
    vmem = pl.BlockSpec(memory_space=pltpu.VMEM)
    return pl.pallas_call(
        carry_kernel,
        out_shape=(shape((STATE, parts[0].shape[1]), BF16),) * 4,
        in_specs=[pl.BlockSpec(memory_space=pltpu.SMEM)] + [vmem] * 7,
        out_specs=(vmem,) * 4,
        compiler_params=params(),
        cost_estimate=SMALL,
        name="carry",
    )(where, *parts, *earlier)


def finish_kernel(where_ref, own_ref, last_ref, next_ref, across_ref, read_ref, cum_ref, inside_ref, out_ref, scr):
    _, _, _, here = place_of(where_ref)
    for by, ref in ((0, own_ref), (3, last_ref), (1, next_ref), (2, across_ref)):
        scr[(here + by) & 3] = ref[...]
    cols = own_ref.shape[1]
    decayed = spread(jnp.exp(cum_ref[...]), SIDE * cols)
    for q in range(SIDE):
        lanes = slice(q * cols, (q + 1) * cols)
        from_prior = jnp.dot(read_ref[...], scr[q], preferred_element_type=F32)
        out_ref[:, lanes] = (inside_ref[:, lanes] + decayed[:, lanes] * from_prior).astype(BF16)


def finish(where, parts, read, cum, within):
    vmem = pl.BlockSpec(memory_space=pltpu.VMEM)
    return pl.pallas_call(
        finish_kernel,
        out_shape=shape(within.shape, BF16),
        in_specs=[pl.BlockSpec(memory_space=pltpu.SMEM)] + [vmem] * 7,
        out_specs=vmem,
        scratch_shapes=[pltpu.VMEM((SIDE,) + parts[0].shape, BF16)],
        compiler_params=params(),
        cost_estimate=SMALL,
        name="finish",
    )(where, *parts, read, cum, within)


def body(
    tokens,
    routes,
    route_weight,
    moe_gain,
    gate_weight,
    up_weight,
    down_weight,
    ssd_gain,
    input_weight,
    write_weight,
    read_weight,
    step_weight,
    step_bias,
    decay_log,
    skip_gain,
):
    where = jnp.stack([lax.axis_index("expert"), lax.axis_index("frame")]).astype(jnp.int32)
    rows, onehot, slot_weight = pick(where, tokens, routes, route_weight, moe_gain)
    halves = experts(rows, (gate_weight[0], up_weight[0], down_weight[0]))
    weights = (input_weight, write_weight, read_weight, step_weight)
    mixed, more, order = [], (), ()
    for c in range(2):
        keep, give = weigh(c, where, after(halves[c], *order), slot_weight)
        own, to_next, to_last, to_across = place(where, keep, to_sibling(give), onehot)
        others = (along_y(to_next, 1), along_y(to_last, -1), along_y(to_across, 2))
        half = residual(c, where, tokens, own, others)
        order = (own,)
        mixed.append(half)
        mine = jnp.stack([half, along_y(half, 1), along_y(half, -1), along_y(half, 2)])
        if c == 1:
            more = (*more, step_bias.reshape(1, -1), decay_log.reshape(1, -1))
        more = project(c, where, mine, to_sibling(mine), ssd_gain, weights, *more)
    inputs, write, read, step, cum, state, to_next, to_last, to_across = more
    within = inside(inputs, write, read, step, cum, skip_gain)
    parts = (after(state, within), along_x(to_next, 1), along_x(to_last, -1), along_x(to_across, 2))
    row = row_total(where, parts)
    earlier = (along_z(row, 1), along_z(row, -1), along_z(row, 2))
    prior, to_next, to_last, to_across = carry(where, parts, earlier)
    carried = (prior, along_x(to_next, 1), along_x(to_last, -1), along_x(to_across, 2))
    ssd_out = finish(where, carried, read, cum, within)
    return (jnp.concatenate(mixed, axis=1), ssd_out)


def solution(mesh):
    placed = (
        P("frame", None),
        P("frame", None),
        P("frame", None),
        P(),
        P("expert", "frame", None),
        P("expert", "frame", None),
        P("expert", "frame", None),
        P(),
        P(None, "expert"),
        P(None, "expert"),
        P(None, "expert"),
        P(None, "expert"),
        P("expert"),
        P("expert"),
        P("expert"),
    )
    return jax.shard_map(
        body,
        mesh=mesh,
        in_specs=placed,
        out_specs=(P("frame", "expert"), P("frame", "expert")),
        check_vma=False,
    )
```

```python
import functools

import jax
import jax.numpy as jnp
from jax import lax
from jax.experimental import pallas as pl
from jax.experimental.pallas import tpu as pltpu
from jax.sharding import PartitionSpec as P

HEAD_DIM = 64
STATE = 128
SLOTS = 96
SIDE = 4
EPSILON = 1e-06
PRECISE = lax.Precision.HIGHEST
AXES = ("expert", "frame")
F32, BF16 = jnp.float32, jnp.bfloat16


def routes_of(rule):
    pairs = []
    for y in range(SIDE):
        for core in range(2):
            for z in range(SIDE):
                for x in range(SIDE):
                    ny, nc, nz, nx = rule(y, core, z, x)
                    source = (y * 2 + core) * 16 + z * SIDE + x
                    target = ((ny % SIDE) * 2 + nc % 2) * 16 + (nz % SIDE) * SIDE + nx % SIDE
                    pairs.append((source, target))
    return pairs


def send(array, rule):
    return lax.ppermute(array, AXES, routes_of(rule))


def along_first(array, by):
    return send(array, lambda y, c, z, x: (y, c, z + by * c, x + by * (1 - c)))


def along_second(array, by):
    return send(array, lambda y, c, z, x: (y, c, z + by * (1 - c), x + by * c))


def along_x(array, by):
    return send(array, lambda y, c, z, x: (y, c, z, x + by))


def along_z(array, by):
    return send(array, lambda y, c, z, x: (y, c, z + by, x))


def along_y(array, by):
    return send(array, lambda y, c, z, x: (y + by, c, z, x))


def to_sibling(array):
    return send(array, lambda y, c, z, x: (y, 1 - c, z, x))


def shape(dims, kind):
    return jax.ShapeDtypeStruct(dims, kind)


def params(mebibytes=20):
    return pltpu.CompilerParams(vmem_limit_bytes=mebibytes * 1024 * 1024)


SMALL = pl.CostEstimate(flops=10**6, bytes_accessed=10**5, transcendentals=0)


def place_of(where_ref):
    return where_ref[0] >> 1, where_ref[0] & 1, where_ref[1] >> 2, where_ref[1] & 3


def pick_kernel(where_ref, *refs):
    arrays, (rows_ref, onehot_ref, slot_weight_ref), held, sems = refs[:4], refs[4:7], refs[7:11], refs[11]
    copies = [pltpu.make_async_copy(source, to, sems.at[k]) for k, (source, to) in enumerate(zip(arrays, held))]
    for copy in copies:
        copy.start()
    tokens_ref, routes_ref, weight_ref, gain_ref = held
    count = tokens_ref.shape[0]
    upper = lax.broadcasted_iota(jnp.int32, (count, count), 0) <= lax.broadcasted_iota(jnp.int32, (count, count), 1)
    slot = lax.broadcasted_iota(jnp.int32, (SLOTS, count), 0)
    copies[1].wait()
    copies[2].wait()
    onehots = []
    for sibling in range(2):
        hits = routes_ref[...] == where_ref[0] ^ sibling
        chosen = jnp.max(hits.astype(F32), axis=0, keepdims=True)
        wide = jnp.broadcast_to(chosen, (SLOTS, count))
        place = jnp.dot(wide.astype(BF16), upper.astype(BF16), preferred_element_type=F32) - 1.0
        named = (place.astype(jnp.int32) == slot) & (wide > 0.0)
        onehots.append(jnp.where(named, 1.0, 0.0).astype(BF16))
        if sibling == 0:
            weights = jnp.sum(jnp.where(hits, weight_ref[...], 0.0), axis=0, keepdims=True)
            slot_weight = jnp.sum(jnp.where(named, weights, 0.0), axis=1, keepdims=True)
    onehot_ref[...] = jnp.concatenate(onehots, axis=0)
    slot_weight_ref[...] = jnp.broadcast_to(slot_weight, slot_weight_ref.shape)
    copies[0].wait()
    copies[3].wait()
    picked = jnp.dot(onehots[0], tokens_ref[...], preferred_element_type=F32)
    mean_sq = jnp.mean(picked * picked, axis=1, keepdims=True)
    rows_ref[...] = (picked * lax.rsqrt(mean_sq + EPSILON) * gain_ref[...]).astype(BF16)


def pick(where, tokens, routes, route_weight, gain):
    count, width = tokens.shape
    smem, vmem = pl.BlockSpec(memory_space=pltpu.SMEM), pl.BlockSpec(memory_space=pltpu.VMEM)
    arrays = (tokens, routes.T, route_weight.T, gain.reshape(1, width))
    return pl.pallas_call(
        pick_kernel,
        out_shape=(shape((SLOTS, width), BF16), shape((2 * SLOTS, count), BF16), shape((SLOTS, 128), F32)),
        in_specs=[smem] + [pl.BlockSpec(memory_space=pltpu.HBM)] * 4,
        out_specs=(vmem, vmem, vmem),
        scratch_shapes=[pltpu.VMEM(array.shape, array.dtype) for array in arrays] + [pltpu.SemaphoreType.DMA((4,))],
        compiler_params=params(60),
        name="pick",
    )(where, *arrays)


def expert_kernel(top_ref, bottom_ref, gate_ref, up_ref, down_ref, out_top_ref, out_bottom_ref):
    half = top_ref.shape[0]
    rows = jnp.concatenate([top_ref[...], bottom_ref[...]], axis=0)
    by_row = (((1,), (1,)), ((), ()))
    gate = lax.dot_general(rows, gate_ref[...], by_row, preferred_element_type=F32)
    upper = lax.dot_general(rows, up_ref[...], by_row, preferred_element_type=F32)
    hidden = (gate / (1.0 + jnp.exp(-gate)) * upper).astype(BF16)
    out = jnp.dot(hidden, down_ref[...], preferred_element_type=F32).astype(BF16)
    out_top_ref[...] = out[:half]
    out_bottom_ref[...] = out[half:]


def expert(top, bottom, weights):
    vmem = pl.BlockSpec(memory_space=pltpu.VMEM)
    rows, width = top.shape
    units = weights[0].shape[0]
    return pl.pallas_call(
        expert_kernel,
        out_shape=(shape(top.shape, BF16),) * 2,
        in_specs=[vmem] * 5,
        out_specs=(vmem, vmem),
        compiler_params=params(28),
        cost_estimate=pl.CostEstimate(
            flops=12 * rows * width * units, bytes_accessed=6 * units * width + 8 * rows * width, transcendentals=0
        ),
        name="expert",
    )(top, bottom, *weights)


def relay_kernel(after_ref, down_ref, before_ref, up_ref, to_after_ref, to_before_ref):
    to_after_ref[...] = (after_ref[...].astype(F32) + down_ref[...].astype(F32)).astype(BF16)
    to_before_ref[...] = (before_ref[...].astype(F32) + up_ref[...].astype(F32)).astype(BF16)


def relay(*arrays):
    vmem = pl.BlockSpec(memory_space=pltpu.VMEM)
    return pl.pallas_call(
        relay_kernel,
        out_shape=(shape(arrays[0].shape, BF16),) * 2,
        in_specs=[vmem] * 4,
        out_specs=(vmem, vmem),
        compiler_params=params(),
        cost_estimate=SMALL,
        name="relay",
    )(*arrays)


def total_kernel(near_top, top_a, top_b, near_bottom, bottom_a, bottom_b, own, down, up, across):
    for near, a, b, first, second in (
        (near_top, top_a, top_b, own, down), (near_bottom, bottom_a, bottom_b, up, across)
    ):
        total = near[...].astype(F32) + a[...].astype(F32) + b[...].astype(F32)
        first[...] = total[:SLOTS].astype(BF16)
        second[...] = total[SLOTS:].astype(BF16)


def total(*arrays):
    vmem = pl.BlockSpec(memory_space=pltpu.VMEM)
    return pl.pallas_call(
        total_kernel,
        out_shape=(shape((SLOTS, arrays[0].shape[1]), BF16),) * 4,
        in_specs=[vmem] * 6,
        out_specs=(vmem,) * 4,
        compiler_params=params(),
        cost_estimate=SMALL,
        name="total",
    )(*arrays)


def after(values, *earlier):
    return lax.optimization_barrier((values, earlier))[0]


def experts(rows, weights):
    last, following = along_first(rows, 1), along_first(rows, -1)
    across_top = along_first(last[: SLOTS // 2], 1)
    across_bottom = along_first(following[SLOTS // 2 :], -1)
    near_top = jnp.concatenate([rows, last], axis=0)
    near_bottom = jnp.concatenate([following, across_top, across_bottom], axis=0)
    near_top = after(near_top, across_top, across_bottom)
    before_top = along_second(near_top, 1)
    after_bottom = along_second(near_bottom, -1)
    out_near_top, out_near_bottom = expert(near_top, near_bottom, weights)
    before_top, after_bottom = after((before_top, after_bottom), out_near_top)
    far_top = along_second(before_top, 1)
    far_bottom = along_second(after_bottom, -1)
    out_before_top, out_after_bottom = expert(before_top, after_bottom, weights)
    later_top, later_bottom = after((near_top, near_bottom), out_before_top)
    after_top = along_second(later_top, -1)
    before_bottom = along_second(later_bottom, 1)
    out_far_top, out_far_bottom = expert(*after((far_top, far_bottom), out_before_top), weights)
    relay_down = along_second(out_far_top, 1)
    relay_up = along_second(out_far_bottom, -1)
    first_back = after((out_before_top, out_after_bottom), out_far_top)
    top_a = along_second(first_back[0], -1)
    bottom_a = along_second(first_back[1], 1)
    second = after((after_top, before_bottom), relay_down, relay_up)
    out_after_top, out_before_bottom = expert(*second, weights)
    to_after, to_before = relay(out_after_top, relay_down, out_before_bottom, relay_up)
    top_b = along_second(to_after, 1)
    bottom_b = along_second(to_before, -1)
    own, down, up, across = total(out_near_top, top_a, top_b, out_near_bottom, bottom_a, bottom_b)
    return own, along_first(down, -1), along_first(up, 1), along_first(across, 2)


def weigh_kernel(c, where_ref, a_ref, b_ref, c_ref, d_ref, weight_ref, keep_ref, give_ref):
    weight, weighted = weight_ref[:, :1], []
    for e in range(8):
        lanes = slice(e * 512 + c * 256, e * 512 + c * 256 + 256)
        rows = a_ref[:, lanes].astype(F32) + b_ref[:, lanes].astype(F32)
        rows += c_ref[:, lanes].astype(F32) + d_ref[:, lanes].astype(F32)
        weighted.append((rows * weight).astype(BF16))
    _, mine, _, _ = place_of(where_ref)
    for core in range(2):

        @pl.when(mine == core)
        def _():
            for k in range(SIDE):
                to = slice(k * 256, (k + 1) * 256)
                for out, e in ((keep_ref, 2 * k + core), (give_ref, 2 * k + 1 - core)):
                    out[:, to] = weighted[e]


def weigh(c, where, terms, slot_weight):
    vmem = pl.BlockSpec(memory_space=pltpu.VMEM)
    return pl.pallas_call(
        functools.partial(weigh_kernel, c),
        out_shape=(shape((SLOTS, SIDE * 256), BF16),) * 2,
        in_specs=[pl.BlockSpec(memory_space=pltpu.SMEM)] + [vmem] * 5,
        out_specs=(vmem, vmem),
        compiler_params=params(),
        cost_estimate=SMALL,
        name="weigh",
    )(where, *terms, slot_weight)


def place_kernel(where_ref, keep_ref, got_ref, onehot_ref, own_ref, next_ref, last_ref, across_ref, scr):
    rows = jnp.concatenate([keep_ref[...], got_ref[...]], axis=0)
    placed = lax.dot_general(onehot_ref[...], rows, (((0,), (0,)), ((), ())), preferred_element_type=F32)
    for k in range(SIDE):
        scr[k] = placed[:, k * 256 : (k + 1) * 256]
    y, _, _, _ = place_of(where_ref)
    for by, out in ((0, own_ref), (1, next_ref), (3, last_ref), (2, across_ref)):
        out[...] = scr[(y + by) & 3].astype(out.dtype)


def place(where, keep, got, onehot):
    count = onehot.shape[1]
    vmem = pl.BlockSpec(memory_space=pltpu.VMEM)
    return pl.pallas_call(
        place_kernel,
        out_shape=(shape((count, 256), F32),) + (shape((count, 256), BF16),) * 3,
        in_specs=[pl.BlockSpec(memory_space=pltpu.SMEM)] + [vmem] * 3,
        out_specs=(vmem,) * 4,
        scratch_shapes=[pltpu.VMEM((SIDE, count, 256), F32)],
        compiler_params=params(),
        cost_estimate=SMALL,
        name="place",
    )(where, keep, got, onehot)


def residual_kernel(where_ref, tokens_ref, own_ref, a_ref, b_ref, c_ref, mixed_ref):
    summed = (own_ref[...] + a_ref[...].astype(F32)) + (b_ref[...].astype(F32) + c_ref[...].astype(F32))
    mixed_ref[...] = (tokens_ref[...].astype(F32) + summed).astype(BF16)


def residual(c, where, tokens, own, others):
    count, cols = own.shape
    whole = pl.BlockSpec((count, cols), lambda i, where: (0, 0))
    return pl.pallas_call(
        residual_kernel,
        out_shape=shape((count, cols), BF16),
        grid_spec=pltpu.PrefetchScalarGridSpec(
            num_scalar_prefetch=1,
            grid=(1,),
            in_specs=[pl.BlockSpec((count, cols), lambda i, where: (0, 2 * where[0] + c))] + [whole] * 4,
            out_specs=whole,
        ),
        compiler_params=params(),
        cost_estimate=SMALL,
        name="residual",
    )(where, tokens, own, *others)


def spread(per_head, lanes):
    heads = per_head.shape[1]
    pairs = []
    first = lax.broadcasted_iota(jnp.int32, (per_head.shape[0], 2 * HEAD_DIM), 1) < HEAD_DIM
    for k in range(heads // 2):
        pairs.append(jnp.where(first, per_head[:, 2 * k : 2 * k + 1], per_head[:, 2 * k + 1 : 2 * k + 2]))
    return jnp.concatenate(pairs, axis=1)


def project_kernel(c, where_ref, mine_ref, other_ref, gain_ref, in_w_ref, write_w_ref, read_w_ref, step_w_ref, *refs):
    y, core, _, _ = place_of(where_ref)
    squares, scaled, step_w = 0.0, [], []
    for e in range(8):
        away = (e // 2 + SIDE - y) & 3
        slot = jnp.where(away == 0, 0, jnp.where(away == 3, 1, away + 1))
        values = jnp.where(core == e % 2, mine_ref[slot], other_ref[slot]).astype(F32)
        squares += jnp.sum(values * values, axis=1, keepdims=True)
        scaled.append((values * gain_ref[e, c]).astype(BF16))
        step_w.append(step_w_ref[:, e * 512 + c * 256 : e * 512 + c * 256 + 256])
    scaled = jnp.concatenate(scaled, axis=1)

    def rows(ref):
        return ref[:, c].reshape(scaled.shape[1], ref.shape[3])

    write_read = jnp.concatenate([rows(write_w_ref), rows(read_w_ref)], axis=1)
    accs = [
        jnp.dot(scaled, rows(in_w_ref), preferred_element_type=F32),
        jnp.dot(scaled, write_read, preferred_element_type=F32),
        lax.dot_general(
            scaled, jnp.concatenate(step_w, axis=1), (((1,), (1,)), ((), ())), preferred_element_type=F32
        ),
        jnp.broadcast_to(squares, (squares.shape[0], 128)),
    ]
    if c == 0:
        for out, acc in zip(refs, accs):
            out[...] = acc
    else:
        before, (bias_ref, decay_ref) = refs[:4], refs[4:6]
        accs = [acc + ref[...] for acc, ref in zip(accs, before)]
        projected(where_ref, bias_ref, decay_ref, refs[6:15], accs, refs[15], 8 * 512)


def projected(where_ref, bias_ref, decay_ref, outs, accs, state_scr, width):
    in_acc, write_read, step_acc, square_acc = accs
    x_ref, write_ref, read_ref, step_ref, cum_ref = outs[:5]
    count, heads = step_acc.shape
    scale = lax.rsqrt(square_acc[:, :1] / width + EPSILON)
    x = (in_acc * scale).astype(BF16)
    x_ref[...] = x
    write = (write_read[:, :STATE] * scale).astype(BF16)
    write_ref[...] = write
    read_ref[...] = (write_read[:, STATE:] * scale).astype(BF16)
    raw = step_acc * scale + bias_ref[...]
    step = jnp.maximum(raw, 0.0) + jnp.log1p(jnp.exp(-jnp.abs(raw)))
    step_ref[...] = step
    log_decay = -step * jnp.exp(decay_ref[...])
    lower = lax.broadcasted_iota(jnp.int32, (count, count), 0) >= lax.broadcasted_iota(jnp.int32, (count, count), 1)
    cum = jnp.dot(lower.astype(F32), log_decay, preferred_element_type=F32, precision=PRECISE)
    cum_ref[...] = cum
    last = cum[count - 1 :, :]
    to_end = jnp.exp(last - cum) * step
    weighted = (x.astype(F32) * spread(to_end, x.shape[1])).astype(BF16)
    state = lax.dot_general(write, weighted, (((0,), (0,)), ((), ())), preferred_element_type=F32)
    whole = spread(last, x.shape[1])
    high = whole.astype(BF16).astype(F32)
    row = lax.broadcasted_iota(jnp.int32, (16, x.shape[1]), 0)
    log_rows = jnp.where(row == 0, high, jnp.where(row == 1, whole - high, 0.0)).astype(BF16)
    cols = x.shape[1] // SIDE
    for q in range(SIDE):
        lanes = slice(q * cols, (q + 1) * cols)
        state_scr[q, :STATE, :] = state[:, lanes].astype(BF16)
        state_scr[q, STATE:, :] = log_rows[:, lanes]
    _, _, _, at = place_of(where_ref)
    for by, out in zip((0, 1, 3, 2), outs[5:]):
        out[...] = state_scr[(at + by) & 3]


def project(c, where, mine, other, gain, weights, *more):
    _, count, cols = mine.shape
    lanes, heads = weights[0].shape[1], weights[3].shape[1]
    smem, vmem = pl.BlockSpec(memory_space=pltpu.SMEM), pl.BlockSpec(memory_space=pltpu.VMEM)
    cut = [w.reshape(8, 2, cols, w.shape[1]) for w in weights[:3]]
    if c == 0:
        outs = tuple(shape((count, n), F32) for n in (lanes, 2 * STATE, heads, 128))
        scratch = []
    else:
        quarter = (STATE + 16, lanes // SIDE)
        outs = (
            shape((count, lanes), BF16), shape((count, STATE), BF16), shape((count, STATE), BF16),
            shape((count, heads), F32), shape((count, heads), F32),
        ) + (shape(quarter, BF16),) * 4
        scratch = [pltpu.VMEM((SIDE,) + quarter, BF16)]
    return pl.pallas_call(
        functools.partial(project_kernel, c),
        out_shape=outs,
        in_specs=[smem] + [vmem] * (7 + len(more)),
        out_specs=(vmem,) * len(outs),
        scratch_shapes=scratch,
        compiler_params=params(),
        cost_estimate=SMALL,
        name="project",
    )(where, mine, other, gain.reshape(8, 2, 1, cols), *cut, weights[3].T, *more)


def inside_kernel(x_ref, write_ref, read_ref, step_ref, cum_ref, skip_ref, out_ref):
    count, heads = step_ref.shape
    span = count // 2
    scores = lax.dot_general(read_ref[...], write_ref[...], (((1,), (1,)), ((), ())), preferred_element_type=F32)
    cum = cum_ref[...]
    cum_t, step_t = cum.T, step_ref[...].T
    causal = lax.broadcasted_iota(jnp.int32, (span, span), 0) >= lax.broadcasted_iota(jnp.int32, (span, span), 1)
    low, high = slice(0, span), slice(span, count)

    def mixing(h, rows, columns):
        gaps = cum[rows, h : h + 1] - cum_t[h : h + 1, columns]
        if rows == columns:
            gaps = jnp.where(causal, gaps, -jnp.inf)
        return (scores[rows, columns] * jnp.exp(gaps) * step_t[h : h + 1, columns]).astype(BF16)

    for h in range(heads):
        lanes = slice(h * HEAD_DIM, (h + 1) * HEAD_DIM)
        x = x_ref[:, lanes]
        skipped = skip_ref[0, h] * x.astype(F32)
        top = jnp.dot(mixing(h, low, low), x[low], preferred_element_type=F32)
        below = jnp.concatenate([mixing(h, high, low), mixing(h, high, high)], axis=1)
        bottom = jnp.dot(below, x, preferred_element_type=F32)
        out_ref[:, lanes] = jnp.concatenate([top, bottom], axis=0) + skipped


def inside(x, write, read, step, cum, skip_gain):
    vmem = pl.BlockSpec(memory_space=pltpu.VMEM)
    return pl.pallas_call(
        inside_kernel,
        out_shape=shape(x.shape, F32),
        in_specs=[vmem] * 5 + [pl.BlockSpec(memory_space=pltpu.SMEM)],
        out_specs=vmem,
        compiler_params=params(),
        cost_estimate=pl.CostEstimate(flops=2 * 10**9, bytes_accessed=2 * 10**6, transcendentals=10**6),
        name="inside",
    )(x, write, read, step, cum, skip_gain.reshape(1, -1))


def log_of(ref):
    return ref[STATE : STATE + 1, :].astype(F32) + ref[STATE + 1 : STATE + 2, :].astype(F32)


def weights_before(here, places, logs):
    terms = []
    for s in places:
        between = sum(jnp.where((s < u) & (u < here), log, 0.0) for u, log in zip(places, logs))
        terms.append(jnp.where(s < here, jnp.exp(between), 0.0))
    return terms


def row_total_kernel(where_ref, own_ref, last_ref, next_ref, across_ref, total_ref):
    _, _, _, here = place_of(where_ref)
    refs = (own_ref, last_ref, next_ref, across_ref)
    places = [here, (here + 3) & 3, (here + 1) & 3, (here + 2) & 3]
    logs = [log_of(ref) for ref in refs]
    until_end = [jnp.exp(sum(jnp.where(s < u, log, 0.0) for u, log in zip(places, logs))) for s in places]
    total_ref[:STATE, :] = sum(w * ref[:STATE, :].astype(F32) for w, ref in zip(until_end, refs)).astype(BF16)
    whole = sum(logs)
    top = whole.astype(BF16).astype(F32)
    row = lax.broadcasted_iota(jnp.int32, (16, whole.shape[1]), 0)
    total_ref[STATE:, :] = jnp.where(row == 0, top, jnp.where(row == 1, whole - top, 0.0)).astype(BF16)


def row_total(where, parts):
    vmem = pl.BlockSpec(memory_space=pltpu.VMEM)
    return pl.pallas_call(
        row_total_kernel,
        out_shape=shape(parts[0].shape, BF16),
        in_specs=[pl.BlockSpec(memory_space=pltpu.SMEM)] + [vmem] * 4,
        out_specs=vmem,
        compiler_params=params(),
        cost_estimate=SMALL,
        name="row_total",
    )(where, *parts)


def carry_kernel(where_ref, *refs):
    parts, earlier, outs = refs[:4], refs[4:7], refs[7:]
    _, _, z, here = place_of(where_ref)
    rows = [(z + 3) & 3, (z + 1) & 3, (z + 2) & 3]
    before = weights_before(z, rows, [log_of(ref) for ref in earlier])
    to_row = sum(w * ref[:STATE, :].astype(F32) for w, ref in zip(before, earlier))
    places = [here, (here + 3) & 3, (here + 1) & 3, (here + 2) & 3]
    logs = [log_of(ref) for ref in parts]
    for by, out in zip((0, 1, 3, 2), outs):
        target = (here + by) & 3
        gone = sum(jnp.where(s < target, log, 0.0) for s, log in zip(places, logs))
        state = jnp.exp(gone) * to_row
        for w, ref in zip(weights_before(target, places, logs), parts):
            state += w * ref[:STATE, :].astype(F32)
        out[...] = state.astype(BF16)


def carry(where, parts, earlier):
    vmem = pl.BlockSpec(memory_space=pltpu.VMEM)
    return pl.pallas_call(
        carry_kernel,
        out_shape=(shape((STATE, parts[0].shape[1]), BF16),) * 4,
        in_specs=[pl.BlockSpec(memory_space=pltpu.SMEM)] + [vmem] * 7,
        out_specs=(vmem,) * 4,
        compiler_params=params(),
        cost_estimate=SMALL,
        name="carry",
    )(where, *parts, *earlier)


def finish_kernel(where_ref, own_ref, last_ref, next_ref, across_ref, read_ref, cum_ref, inside_ref, out_ref, scr):
    _, _, _, here = place_of(where_ref)
    for by, ref in ((0, own_ref), (3, last_ref), (1, next_ref), (2, across_ref)):
        scr[(here + by) & 3] = ref[...]
    cols = own_ref.shape[1]
    decayed = spread(jnp.exp(cum_ref[...]), SIDE * cols)
    for q in range(SIDE):
        lanes = slice(q * cols, (q + 1) * cols)
        from_prior = jnp.dot(read_ref[...], scr[q], preferred_element_type=F32)
        out_ref[:, lanes] = (inside_ref[:, lanes] + decayed[:, lanes] * from_prior).astype(BF16)


def finish(where, parts, read, cum, within):
    vmem = pl.BlockSpec(memory_space=pltpu.VMEM)
    return pl.pallas_call(
        finish_kernel,
        out_shape=shape(within.shape, BF16),
        in_specs=[pl.BlockSpec(memory_space=pltpu.SMEM)] + [vmem] * 7,
        out_specs=vmem,
        scratch_shapes=[pltpu.VMEM((SIDE,) + parts[0].shape, BF16)],
        compiler_params=params(),
        cost_estimate=SMALL,
        name="finish",
    )(where, *parts, read, cum, within)


def body(
    tokens,
    routes,
    route_weight,
    moe_gain,
    gate_weight,
    up_weight,
    down_weight,
    ssd_gain,
    input_weight,
    write_weight,
    read_weight,
    step_weight,
    step_bias,
    decay_log,
    skip_gain,
):
    where = jnp.stack([lax.axis_index("expert"), lax.axis_index("frame")]).astype(jnp.int32)
    rows, onehot, slot_weight = pick(where, tokens, routes, route_weight, moe_gain)
    terms = experts(rows, (gate_weight[0], up_weight[0], down_weight[0]))
    weights = (input_weight, write_weight, read_weight, step_weight)
    keeps, gives, sums, mixed, more = [], [], [], [], ()
    for c in range(2):
        keep, give = weigh(c, where, after(terms, *keeps), slot_weight)
        keeps.append(keep)
        gives.append(to_sibling(give))
    for c in range(2):
        own, to_next, to_last, to_across = place(where, after(keeps[c], keeps[1]), gives[c], onehot)
        sums.append((own, (along_y(to_next, 1), along_y(to_last, -1), along_y(to_across, 2))))
    for c, (own, others) in enumerate(sums):
        half = residual(c, where, tokens, own, others)
        mixed.append(half)
        mine = jnp.stack([half, along_y(half, 1), along_y(half, -1), along_y(half, 2)])
        if c == 1:
            more = (*more, step_bias.reshape(1, -1), decay_log.reshape(1, -1))
        more = project(c, where, mine, to_sibling(mine), ssd_gain, weights, *more)
    inputs, write, read, step, cum, state, to_next, to_last, to_across = more
    within = inside(inputs, write, read, step, cum, skip_gain)
    parts = (after(state, within), along_x(to_next, 1), along_x(to_last, -1), along_x(to_across, 2))
    row = row_total(where, parts)
    earlier = (along_z(row, 1), along_z(row, -1), along_z(row, 2))
    prior, to_next, to_last, to_across = carry(where, parts, earlier)
    carried = (prior, along_x(to_next, 1), along_x(to_last, -1), along_x(to_across, 2))
    ssd_out = finish(where, carried, read, cum, within)
    return (jnp.concatenate(mixed, axis=1), ssd_out)


def solution(mesh):
    placed = (
        P("frame", None),
        P("frame", None),
        P("frame", None),
        P(),
        P("expert", "frame", None),
        P("expert", "frame", None),
        P("expert", "frame", None),
        P(),
        P(None, "expert"),
        P(None, "expert"),
        P(None, "expert"),
        P(None, "expert"),
        P("expert"),
        P("expert"),
        P("expert"),
    )
    return jax.shard_map(
        body,
        mesh=mesh,
        in_specs=placed,
        out_specs=(P("frame", "expert"), P("frame", "expert")),
        check_vma=False,
    )
```

```python
import functools

import jax
import jax.numpy as jnp
from jax import lax
from jax.experimental import pallas as pl
from jax.experimental.pallas import tpu as pltpu
from jax.sharding import PartitionSpec as P

HEAD_DIM = 64
STATE = 128
SLOTS = 96
SIDE = 4
EPSILON = 1e-06
PRECISE = lax.Precision.HIGHEST
AXES = ("expert", "frame")
F32, BF16 = jnp.float32, jnp.bfloat16


def routes_of(rule):
    pairs = []
    for y in range(SIDE):
        for core in range(2):
            for z in range(SIDE):
                for x in range(SIDE):
                    ny, nc, nz, nx = rule(y, core, z, x)
                    source = (y * 2 + core) * 16 + z * SIDE + x
                    target = ((ny % SIDE) * 2 + nc % 2) * 16 + (nz % SIDE) * SIDE + nx % SIDE
                    pairs.append((source, target))
    return pairs


def send(array, rule):
    return lax.ppermute(array, AXES, routes_of(rule))


def along_first(array, by):
    return send(array, lambda y, c, z, x: (y, c, z + by * c, x + by * (1 - c)))


def along_second(array, by):
    return send(array, lambda y, c, z, x: (y, c, z + by * (1 - c), x + by * c))


def along_x(array, by):
    return send(array, lambda y, c, z, x: (y, c, z, x + by))


def along_z(array, by):
    return send(array, lambda y, c, z, x: (y, c, z + by, x))


def along_y(array, by):
    return send(array, lambda y, c, z, x: (y + by, c, z, x))


def to_sibling(array):
    return send(array, lambda y, c, z, x: (y, 1 - c, z, x))


def shape(dims, kind):
    return jax.ShapeDtypeStruct(dims, kind)


def params(mebibytes=20):
    return pltpu.CompilerParams(vmem_limit_bytes=mebibytes * 1024 * 1024)


SMALL = pl.CostEstimate(flops=10**6, bytes_accessed=10**5, transcendentals=0)


def place_of(where_ref):
    return where_ref[0] >> 1, where_ref[0] & 1, where_ref[1] >> 2, where_ref[1] & 3


def pick_kernel(where_ref, *refs):
    arrays, (rows_ref, onehot_ref, slot_weight_ref), held, sems = refs[:4], refs[4:7], refs[7:11], refs[11]
    copies = [pltpu.make_async_copy(source, to, sems.at[k]) for k, (source, to) in enumerate(zip(arrays, held))]
    for copy in copies:
        copy.start()
    tokens_ref, routes_ref, weight_ref, gain_ref = held
    count = tokens_ref.shape[0]
    upper = lax.broadcasted_iota(jnp.int32, (count, count), 0) <= lax.broadcasted_iota(jnp.int32, (count, count), 1)
    slot = lax.broadcasted_iota(jnp.int32, (SLOTS, count), 0)
    copies[1].wait()
    copies[2].wait()
    onehots = []
    for sibling in range(2):
        hits = routes_ref[...] == where_ref[0] ^ sibling
        chosen = jnp.max(hits.astype(F32), axis=0, keepdims=True)
        wide = jnp.broadcast_to(chosen, (SLOTS, count))
        place = jnp.dot(wide.astype(BF16), upper.astype(BF16), preferred_element_type=F32) - 1.0
        named = (place.astype(jnp.int32) == slot) & (wide > 0.0)
        onehots.append(jnp.where(named, 1.0, 0.0).astype(BF16))
        if sibling == 0:
            weights = jnp.sum(jnp.where(hits, weight_ref[...], 0.0), axis=0, keepdims=True)
            slot_weight = jnp.sum(jnp.where(named, weights, 0.0), axis=1, keepdims=True)
    onehot_ref[...] = jnp.concatenate(onehots, axis=0)
    slot_weight_ref[...] = jnp.broadcast_to(slot_weight, slot_weight_ref.shape)
    copies[0].wait()
    copies[3].wait()
    picked = jnp.dot(onehots[0], tokens_ref[...], preferred_element_type=F32)
    mean_sq = jnp.mean(picked * picked, axis=1, keepdims=True)
    rows_ref[...] = (picked * lax.rsqrt(mean_sq + EPSILON) * gain_ref[...]).astype(BF16)


def pick(where, tokens, routes, route_weight, gain):
    count, width = tokens.shape
    smem, vmem = pl.BlockSpec(memory_space=pltpu.SMEM), pl.BlockSpec(memory_space=pltpu.VMEM)
    arrays = (tokens, routes.T, route_weight.T, gain.reshape(1, width))
    return pl.pallas_call(
        pick_kernel,
        out_shape=(shape((SLOTS, width), BF16), shape((2 * SLOTS, count), BF16), shape((SLOTS, 128), F32)),
        in_specs=[smem] + [pl.BlockSpec(memory_space=pltpu.HBM)] * 4,
        out_specs=(vmem, vmem, vmem),
        scratch_shapes=[pltpu.VMEM(array.shape, array.dtype) for array in arrays] + [pltpu.SemaphoreType.DMA((4,))],
        compiler_params=params(60),
        name="pick",
    )(where, *arrays)


def expert_kernel(top_ref, bottom_ref, gate_ref, up_ref, down_ref, out_top_ref, out_bottom_ref):
    half = top_ref.shape[0]
    rows = jnp.concatenate([top_ref[...], bottom_ref[...]], axis=0)
    by_row = (((1,), (1,)), ((), ()))
    gate = lax.dot_general(rows, gate_ref[...], by_row, preferred_element_type=F32)
    upper = lax.dot_general(rows, up_ref[...], by_row, preferred_element_type=F32)
    hidden = (gate / (1.0 + jnp.exp(-gate)) * upper).astype(BF16)
    out = jnp.dot(hidden, down_ref[...], preferred_element_type=F32).astype(BF16)
    out_top_ref[...] = out[:half]
    out_bottom_ref[...] = out[half:]


def expert(top, bottom, weights):
    vmem = pl.BlockSpec(memory_space=pltpu.VMEM)
    rows, width = top.shape
    units = weights[0].shape[0]
    return pl.pallas_call(
        expert_kernel,
        out_shape=(shape(top.shape, BF16),) * 2,
        in_specs=[vmem] * 5,
        out_specs=(vmem, vmem),
        compiler_params=params(28),
        cost_estimate=pl.CostEstimate(
            flops=12 * rows * width * units, bytes_accessed=6 * units * width + 8 * rows * width, transcendentals=0
        ),
        name="expert",
    )(top, bottom, *weights)


def relay_kernel(after_ref, down_ref, before_ref, up_ref, to_after_ref, to_before_ref):
    to_after_ref[...] = (after_ref[...].astype(F32) + down_ref[...].astype(F32)).astype(BF16)
    to_before_ref[...] = (before_ref[...].astype(F32) + up_ref[...].astype(F32)).astype(BF16)


def relay(*arrays):
    vmem = pl.BlockSpec(memory_space=pltpu.VMEM)
    return pl.pallas_call(
        relay_kernel,
        out_shape=(shape(arrays[0].shape, BF16),) * 2,
        in_specs=[vmem] * 4,
        out_specs=(vmem, vmem),
        compiler_params=params(),
        cost_estimate=SMALL,
        name="relay",
    )(*arrays)


def total_kernel(near_top, top_a, top_b, near_bottom, bottom_a, bottom_b, *outs):
    for c in range(2):
        own, down, up, across = outs[4 * c : 4 * c + 4]
        for e in range(8):
            lanes, at = slice(e * 512 + c * 256, e * 512 + c * 256 + 256), slice(e * 256, e * 256 + 256)
            for near, a, b, first, second in (
                (near_top, top_a, top_b, own, down), (near_bottom, bottom_a, bottom_b, up, across)
            ):
                total = near[:, lanes].astype(F32) + a[:, lanes].astype(F32) + b[:, lanes].astype(F32)
                first[:, at] = total[:SLOTS].astype(BF16)
                second[:, at] = total[SLOTS:].astype(BF16)


def total(*arrays):
    vmem = pl.BlockSpec(memory_space=pltpu.VMEM)
    return pl.pallas_call(
        total_kernel,
        out_shape=(shape((SLOTS, arrays[0].shape[1] // 2), BF16),) * 8,
        in_specs=[vmem] * 6,
        out_specs=(vmem,) * 8,
        compiler_params=params(),
        cost_estimate=SMALL,
        name="total",
    )(*arrays)


def plus(a, b):
    return (a.astype(F32) + b.astype(F32)).astype(BF16)


def after(values, *earlier):
    return lax.optimization_barrier((values, earlier))[0]


def experts(rows, weights):
    last, following = along_first(rows, 1), along_first(rows, -1)
    across_top = along_first(last[: SLOTS // 2], 1)
    across_bottom = along_first(following[SLOTS // 2 :], -1)
    near_top = jnp.concatenate([rows, last], axis=0)
    near_bottom = jnp.concatenate([following, across_top, across_bottom], axis=0)
    near_top = after(near_top, across_top, across_bottom)
    before_top = along_second(near_top, 1)
    after_bottom = along_second(near_bottom, -1)
    out_near_top, out_near_bottom = expert(near_top, near_bottom, weights)
    before_top, after_bottom = after((before_top, after_bottom), out_near_top)
    far_top = along_second(before_top, 1)
    far_bottom = along_second(after_bottom, -1)
    out_before_top, out_after_bottom = expert(before_top, after_bottom, weights)
    later_top, later_bottom = after((near_top, near_bottom), out_before_top)
    after_top = along_second(later_top, -1)
    before_bottom = along_second(later_bottom, 1)
    out_far_top, out_far_bottom = expert(*after((far_top, far_bottom), out_before_top), weights)
    relay_down = along_second(out_far_top, 1)
    relay_up = along_second(out_far_bottom, -1)
    first_back = after((out_before_top, out_after_bottom), out_far_top)
    top_a = along_second(first_back[0], -1)
    bottom_a = along_second(first_back[1], 1)
    second = after((after_top, before_bottom), relay_down, relay_up)
    out_after_top, out_before_bottom = expert(*second, weights)
    to_after, to_before = relay(out_after_top, relay_down, out_before_bottom, relay_up)
    top_b = along_second(to_after, 1)
    bottom_b = along_second(to_before, -1)
    sums = total(out_near_top, top_a, top_b, out_near_bottom, bottom_a, bottom_b)
    terms = []
    for c in range(2):
        own, down, up, across = sums[4 * c : 4 * c + 4]
        terms.append((own, along_first(down, -1), along_first(up, 1), along_first(across, 2)))
    return terms


def weigh_kernel(where_ref, a_ref, b_ref, c_ref, d_ref, weight_ref, keep_ref, give_ref):
    rows = (a_ref[...].astype(F32) + b_ref[...].astype(F32)) + (c_ref[...].astype(F32) + d_ref[...].astype(F32))
    weighted = (rows * weight_ref[:, :1]).astype(BF16)
    _, mine, _, _ = place_of(where_ref)
    for core in range(2):

        @pl.when(mine == core)
        def _():
            for k in range(SIDE):
                to = slice(k * 256, (k + 1) * 256)
                for out, e in ((keep_ref, 2 * k + core), (give_ref, 2 * k + 1 - core)):
                    out[:, to] = weighted[:, e * 256 : (e + 1) * 256]


def weigh(where, terms, slot_weight):
    vmem = pl.BlockSpec(memory_space=pltpu.VMEM)
    return pl.pallas_call(
        weigh_kernel,
        out_shape=(shape((SLOTS, SIDE * 256), BF16),) * 2,
        in_specs=[pl.BlockSpec(memory_space=pltpu.SMEM)] + [vmem] * 5,
        out_specs=(vmem, vmem),
        compiler_params=params(),
        cost_estimate=SMALL,
        name="weigh",
    )(where, *terms, slot_weight)


def place_kernel(where_ref, keep_ref, got_ref, onehot_ref, own_ref, next_ref, last_ref, across_ref, scr):
    rows = jnp.concatenate([keep_ref[...], got_ref[...]], axis=0)
    placed = lax.dot_general(onehot_ref[...], rows, (((0,), (0,)), ((), ())), preferred_element_type=F32)
    for k in range(SIDE):
        scr[k] = placed[:, k * 256 : (k + 1) * 256]
    y, _, _, _ = place_of(where_ref)
    for by, out in ((0, own_ref), (1, next_ref), (3, last_ref), (2, across_ref)):
        out[...] = scr[(y + by) & 3].astype(out.dtype)


def place(where, keep, got, onehot):
    count = onehot.shape[1]
    vmem = pl.BlockSpec(memory_space=pltpu.VMEM)
    return pl.pallas_call(
        place_kernel,
        out_shape=(shape((count, 256), F32),) + (shape((count, 256), BF16),) * 3,
        in_specs=[pl.BlockSpec(memory_space=pltpu.SMEM)] + [vmem] * 3,
        out_specs=(vmem,) * 4,
        scratch_shapes=[pltpu.VMEM((SIDE, count, 256), F32)],
        compiler_params=params(),
        cost_estimate=SMALL,
        name="place",
    )(where, keep, got, onehot)


def residual_kernel(where_ref, tokens_ref, own_ref, a_ref, b_ref, c_ref, mixed_ref):
    summed = (own_ref[...] + a_ref[...].astype(F32)) + (b_ref[...].astype(F32) + c_ref[...].astype(F32))
    mixed_ref[...] = (tokens_ref[...].astype(F32) + summed).astype(BF16)


def residual(c, where, tokens, own, others):
    count, cols = own.shape
    whole = pl.BlockSpec((count, cols), lambda i, where: (0, 0))
    return pl.pallas_call(
        residual_kernel,
        out_shape=shape((count, cols), BF16),
        grid_spec=pltpu.PrefetchScalarGridSpec(
            num_scalar_prefetch=1,
            grid=(1,),
            in_specs=[pl.BlockSpec((count, cols), lambda i, where: (0, 2 * where[0] + c))] + [whole] * 4,
            out_specs=whole,
        ),
        compiler_params=params(),
        cost_estimate=SMALL,
        name="residual",
    )(where, tokens, own, *others)


def spread(per_head, lanes):
    heads = per_head.shape[1]
    pairs = []
    first = lax.broadcasted_iota(jnp.int32, (per_head.shape[0], 2 * HEAD_DIM), 1) < HEAD_DIM
    for k in range(heads // 2):
        pairs.append(jnp.where(first, per_head[:, 2 * k : 2 * k + 1], per_head[:, 2 * k + 1 : 2 * k + 2]))
    return jnp.concatenate(pairs, axis=1)


def project_kernel(c, where_ref, mine_ref, other_ref, gain_ref, in_w_ref, write_w_ref, read_w_ref, step_w_ref, *refs):
    y, core, _, _ = place_of(where_ref)
    squares, scaled, step_w = 0.0, [], []
    for e in range(8):
        away = (e // 2 + SIDE - y) & 3
        slot = jnp.where(away == 0, 0, jnp.where(away == 3, 1, away + 1))
        values = jnp.where(core == e % 2, mine_ref[slot], other_ref[slot]).astype(F32)
        squares += jnp.sum(values * values, axis=1, keepdims=True)
        scaled.append((values * gain_ref[e, c]).astype(BF16))
        step_w.append(step_w_ref[:, e * 512 + c * 256 : e * 512 + c * 256 + 256])
    scaled = jnp.concatenate(scaled, axis=1)

    def rows(ref):
        return ref[:, c].reshape(scaled.shape[1], ref.shape[3])

    write_read = jnp.concatenate([rows(write_w_ref), rows(read_w_ref)], axis=1)
    accs = [
        jnp.dot(scaled, rows(in_w_ref), preferred_element_type=F32),
        jnp.dot(scaled, write_read, preferred_element_type=F32),
        lax.dot_general(
            scaled, jnp.concatenate(step_w, axis=1), (((1,), (1,)), ((), ())), preferred_element_type=F32
        ),
        jnp.broadcast_to(squares, (squares.shape[0], 128)),
    ]
    if c == 0:
        for out, acc in zip(refs, accs):
            out[...] = acc
    else:
        before, (bias_ref, decay_ref) = refs[:4], refs[4:6]
        accs = [acc + ref[...] for acc, ref in zip(accs, before)]
        projected(where_ref, bias_ref, decay_ref, refs[6:15], accs, refs[15], 8 * 512)


def projected(where_ref, bias_ref, decay_ref, outs, accs, state_scr, width):
    in_acc, write_read, step_acc, square_acc = accs
    x_ref, write_ref, read_ref, step_ref, cum_ref = outs[:5]
    count, heads = step_acc.shape
    scale = lax.rsqrt(square_acc[:, :1] / width + EPSILON)
    x = (in_acc * scale).astype(BF16)
    x_ref[...] = x
    write = (write_read[:, :STATE] * scale).astype(BF16)
    write_ref[...] = write
    read_ref[...] = (write_read[:, STATE:] * scale).astype(BF16)
    raw = step_acc * scale + bias_ref[...]
    step = jnp.maximum(raw, 0.0) + jnp.log1p(jnp.exp(-jnp.abs(raw)))
    step_ref[...] = step
    log_decay = -step * jnp.exp(decay_ref[...])
    lower = lax.broadcasted_iota(jnp.int32, (count, count), 0) >= lax.broadcasted_iota(jnp.int32, (count, count), 1)
    cum = jnp.dot(lower.astype(F32), log_decay, preferred_element_type=F32, precision=PRECISE)
    cum_ref[...] = cum
    last = cum[count - 1 :, :]
    to_end = jnp.exp(last - cum) * step
    weighted = (x.astype(F32) * spread(to_end, x.shape[1])).astype(BF16)
    state = lax.dot_general(write, weighted, (((0,), (0,)), ((), ())), preferred_element_type=F32)
    whole = spread(last, x.shape[1])
    high = whole.astype(BF16).astype(F32)
    row = lax.broadcasted_iota(jnp.int32, (16, x.shape[1]), 0)
    log_rows = jnp.where(row == 0, high, jnp.where(row == 1, whole - high, 0.0)).astype(BF16)
    cols = x.shape[1] // SIDE
    for q in range(SIDE):
        lanes = slice(q * cols, (q + 1) * cols)
        state_scr[q, :STATE, :] = state[:, lanes].astype(BF16)
        state_scr[q, STATE:, :] = log_rows[:, lanes]
    _, _, _, at = place_of(where_ref)
    for by, out in zip((0, 1, 3, 2), outs[5:]):
        out[...] = state_scr[(at + by) & 3]


def project(c, where, mine, other, gain, weights, *more):
    _, count, cols = mine.shape
    lanes, heads = weights[0].shape[1], weights[3].shape[1]
    smem, vmem = pl.BlockSpec(memory_space=pltpu.SMEM), pl.BlockSpec(memory_space=pltpu.VMEM)
    cut = [w.reshape(8, 2, cols, w.shape[1]) for w in weights[:3]]
    if c == 0:
        outs = tuple(shape((count, n), F32) for n in (lanes, 2 * STATE, heads, 128))
        scratch = []
    else:
        quarter = (STATE + 16, lanes // SIDE)
        outs = (
            shape((count, lanes), BF16), shape((count, STATE), BF16), shape((count, STATE), BF16),
            shape((count, heads), F32), shape((count, heads), F32),
        ) + (shape(quarter, BF16),) * 4
        scratch = [pltpu.VMEM((SIDE,) + quarter, BF16)]
    return pl.pallas_call(
        functools.partial(project_kernel, c),
        out_shape=outs,
        in_specs=[smem] + [vmem] * (7 + len(more)),
        out_specs=(vmem,) * len(outs),
        scratch_shapes=scratch,
        compiler_params=params(),
        cost_estimate=SMALL,
        name="project",
    )(where, mine, other, gain.reshape(8, 2, 1, cols), *cut, weights[3].T, *more)


def inside_kernel(x_ref, write_ref, read_ref, step_ref, cum_ref, skip_ref, out_ref):
    count, heads = step_ref.shape
    span = count // 2
    scores = lax.dot_general(read_ref[...], write_ref[...], (((1,), (1,)), ((), ())), preferred_element_type=F32)
    cum = cum_ref[...]
    cum_t, step_t = cum.T, step_ref[...].T
    causal = lax.broadcasted_iota(jnp.int32, (span, span), 0) >= lax.broadcasted_iota(jnp.int32, (span, span), 1)
    low, high = slice(0, span), slice(span, count)

    def mixing(h, rows, columns):
        gaps = cum[rows, h : h + 1] - cum_t[h : h + 1, columns]
        if rows == columns:
            gaps = jnp.where(causal, gaps, -jnp.inf)
        return (scores[rows, columns] * jnp.exp(gaps) * step_t[h : h + 1, columns]).astype(BF16)

    for h in range(heads):
        lanes = slice(h * HEAD_DIM, (h + 1) * HEAD_DIM)
        x = x_ref[:, lanes]
        skipped = skip_ref[0, h] * x.astype(F32)
        top = jnp.dot(mixing(h, low, low), x[low], preferred_element_type=F32)
        below = jnp.concatenate([mixing(h, high, low), mixing(h, high, high)], axis=1)
        bottom = jnp.dot(below, x, preferred_element_type=F32)
        out_ref[:, lanes] = jnp.concatenate([top, bottom], axis=0) + skipped


def inside(x, write, read, step, cum, skip_gain):
    vmem = pl.BlockSpec(memory_space=pltpu.VMEM)
    return pl.pallas_call(
        inside_kernel,
        out_shape=shape(x.shape, F32),
        in_specs=[vmem] * 5 + [pl.BlockSpec(memory_space=pltpu.SMEM)],
        out_specs=vmem,
        compiler_params=params(),
        cost_estimate=pl.CostEstimate(flops=2 * 10**9, bytes_accessed=2 * 10**6, transcendentals=10**6),
        name="inside",
    )(x, write, read, step, cum, skip_gain.reshape(1, -1))


def log_of(ref):
    return ref[STATE : STATE + 1, :].astype(F32) + ref[STATE + 1 : STATE + 2, :].astype(F32)


def weights_before(here, places, logs):
    terms = []
    for s in places:
        between = sum(jnp.where((s < u) & (u < here), log, 0.0) for u, log in zip(places, logs))
        terms.append(jnp.where(s < here, jnp.exp(between), 0.0))
    return terms


def row_total_kernel(where_ref, own_ref, last_ref, next_ref, across_ref, total_ref):
    _, _, _, here = place_of(where_ref)
    refs = (own_ref, last_ref, next_ref, across_ref)
    places = [here, (here + 3) & 3, (here + 1) & 3, (here + 2) & 3]
    logs = [log_of(ref) for ref in refs]
    until_end = [jnp.exp(sum(jnp.where(s < u, log, 0.0) for u, log in zip(places, logs))) for s in places]
    total_ref[:STATE, :] = sum(w * ref[:STATE, :].astype(F32) for w, ref in zip(until_end, refs)).astype(BF16)
    whole = sum(logs)
    top = whole.astype(BF16).astype(F32)
    row = lax.broadcasted_iota(jnp.int32, (16, whole.shape[1]), 0)
    total_ref[STATE:, :] = jnp.where(row == 0, top, jnp.where(row == 1, whole - top, 0.0)).astype(BF16)


def row_total(where, parts):
    vmem = pl.BlockSpec(memory_space=pltpu.VMEM)
    return pl.pallas_call(
        row_total_kernel,
        out_shape=shape(parts[0].shape, BF16),
        in_specs=[pl.BlockSpec(memory_space=pltpu.SMEM)] + [vmem] * 4,
        out_specs=vmem,
        compiler_params=params(),
        cost_estimate=SMALL,
        name="row_total",
    )(where, *parts)


def carry_kernel(where_ref, *refs):
    parts, earlier, outs = refs[:4], refs[4:7], refs[7:]
    _, _, z, here = place_of(where_ref)
    rows = [(z + 3) & 3, (z + 1) & 3, (z + 2) & 3]
    before = weights_before(z, rows, [log_of(ref) for ref in earlier])
    to_row = sum(w * ref[:STATE, :].astype(F32) for w, ref in zip(before, earlier))
    places = [here, (here + 3) & 3, (here + 1) & 3, (here + 2) & 3]
    logs = [log_of(ref) for ref in parts]
    for by, out in zip((0, 1, 3, 2), outs):
        target = (here + by) & 3
        gone = sum(jnp.where(s < target, log, 0.0) for s, log in zip(places, logs))
        state = jnp.exp(gone) * to_row
        for w, ref in zip(weights_before(target, places, logs), parts):
            state += w * ref[:STATE, :].astype(F32)
        out[...] = state.astype(BF16)


def carry(where, parts, earlier):
    vmem = pl.BlockSpec(memory_space=pltpu.VMEM)
    return pl.pallas_call(
        carry_kernel,
        out_shape=(shape((STATE, parts[0].shape[1]), BF16),) * 4,
        in_specs=[pl.BlockSpec(memory_space=pltpu.SMEM)] + [vmem] * 7,
        out_specs=(vmem,) * 4,
        compiler_params=params(),
        cost_estimate=SMALL,
        name="carry",
    )(where, *parts, *earlier)


def finish_kernel(where_ref, own_ref, last_ref, next_ref, across_ref, read_ref, cum_ref, inside_ref, out_ref, scr):
    _, _, _, here = place_of(where_ref)
    for by, ref in ((0, own_ref), (3, last_ref), (1, next_ref), (2, across_ref)):
        scr[(here + by) & 3] = ref[...]
    cols = own_ref.shape[1]
    decayed = spread(jnp.exp(cum_ref[...]), SIDE * cols)
    for q in range(SIDE):
        lanes = slice(q * cols, (q + 1) * cols)
        from_prior = jnp.dot(read_ref[...], scr[q], preferred_element_type=F32)
        out_ref[:, lanes] = (inside_ref[:, lanes] + decayed[:, lanes] * from_prior).astype(BF16)


def finish(where, parts, read, cum, within):
    vmem = pl.BlockSpec(memory_space=pltpu.VMEM)
    return pl.pallas_call(
        finish_kernel,
        out_shape=shape(within.shape, BF16),
        in_specs=[pl.BlockSpec(memory_space=pltpu.SMEM)] + [vmem] * 7,
        out_specs=vmem,
        scratch_shapes=[pltpu.VMEM((SIDE,) + parts[0].shape, BF16)],
        compiler_params=params(),
        cost_estimate=SMALL,
        name="finish",
    )(where, *parts, read, cum, within)


def body(
    tokens,
    routes,
    route_weight,
    moe_gain,
    gate_weight,
    up_weight,
    down_weight,
    ssd_gain,
    input_weight,
    write_weight,
    read_weight,
    step_weight,
    step_bias,
    decay_log,
    skip_gain,
):
    where = jnp.stack([lax.axis_index("expert"), lax.axis_index("frame")]).astype(jnp.int32)
    rows, onehot, slot_weight = pick(where, tokens, routes, route_weight, moe_gain)
    halves = experts(rows, (gate_weight[0], up_weight[0], down_weight[0]))
    weights = (input_weight, write_weight, read_weight, step_weight)
    sums, mixed, more, order = [], [], (), ()
    for c in range(2):
        keep, give = weigh(where, after(halves[c], *order), slot_weight)
        own, to_next, to_last, to_across = place(where, keep, to_sibling(give), onehot)
        order = (own,)
        sums.append((own, (along_y(to_next, 1), along_y(to_last, -1), along_y(to_across, 2))))
    for c, (own, others) in enumerate(sums):
        half = residual(c, where, tokens, own, others)
        mixed.append(half)
        mine = jnp.stack([half, along_y(half, 1), along_y(half, -1), along_y(half, 2)])
        if c == 1:
            more = (*more, step_bias.reshape(1, -1), decay_log.reshape(1, -1))
        more = project(c, where, mine, to_sibling(mine), ssd_gain, weights, *more)
    inputs, write, read, step, cum, state, to_next, to_last, to_across = more
    within = inside(inputs, write, read, step, cum, skip_gain)
    parts = (after(state, within), along_x(to_next, 1), along_x(to_last, -1), along_x(to_across, 2))
    row = row_total(where, parts)
    earlier = (along_z(row, 1), along_z(row, -1), along_z(row, 2))
    prior, to_next, to_last, to_across = carry(where, parts, earlier)
    carried = (prior, along_x(to_next, 1), along_x(to_last, -1), along_x(to_across, 2))
    ssd_out = finish(where, carried, read, cum, within)
    return (jnp.concatenate(mixed, axis=1), ssd_out)


def solution(mesh):
    placed = (
        P("frame", None),
        P("frame", None),
        P("frame", None),
        P(),
        P("expert", "frame", None),
        P("expert", "frame", None),
        P("expert", "frame", None),
        P(),
        P(None, "expert"),
        P(None, "expert"),
        P(None, "expert"),
        P(None, "expert"),
        P("expert"),
        P("expert"),
        P("expert"),
    )
    return jax.shard_map(
        body,
        mesh=mesh,
        in_specs=placed,
        out_specs=(P("frame", "expert"), P("frame", "expert")),
        check_vma=False,
    )
```

```python
import functools

import jax
import jax.numpy as jnp
from jax import lax
from jax.experimental import pallas as pl
from jax.experimental.pallas import tpu as pltpu
from jax.sharding import PartitionSpec as P

HEAD_DIM = 64
STATE = 128
SLOTS = 96
SIDE = 4
EPSILON = 1e-06
PRECISE = lax.Precision.HIGHEST
AXES = ("expert", "frame")
F32, BF16 = jnp.float32, jnp.bfloat16


def routes_of(rule):
    pairs = []
    for y in range(SIDE):
        for core in range(2):
            for z in range(SIDE):
                for x in range(SIDE):
                    ny, nc, nz, nx = rule(y, core, z, x)
                    source = (y * 2 + core) * 16 + z * SIDE + x
                    target = ((ny % SIDE) * 2 + nc % 2) * 16 + (nz % SIDE) * SIDE + nx % SIDE
                    pairs.append((source, target))
    return pairs


def send(array, rule):
    return lax.ppermute(array, AXES, routes_of(rule))


def along_first(array, by):
    return send(array, lambda y, c, z, x: (y, c, z + by * c, x + by * (1 - c)))


def along_second(array, by):
    return send(array, lambda y, c, z, x: (y, c, z + by * (1 - c), x + by * c))


def along_x(array, by):
    return send(array, lambda y, c, z, x: (y, c, z, x + by))


def along_z(array, by):
    return send(array, lambda y, c, z, x: (y, c, z + by, x))


def along_y(array, by):
    return send(array, lambda y, c, z, x: (y + by, c, z, x))


def to_sibling(array):
    return send(array, lambda y, c, z, x: (y, 1 - c, z, x))


def shape(dims, kind):
    return jax.ShapeDtypeStruct(dims, kind)


def params(mebibytes=20):
    return pltpu.CompilerParams(vmem_limit_bytes=mebibytes * 1024 * 1024)


SMALL = pl.CostEstimate(flops=10**6, bytes_accessed=10**5, transcendentals=0)


def place_of(where_ref):
    return where_ref[0] >> 1, where_ref[0] & 1, where_ref[1] >> 2, where_ref[1] & 3


def pick_kernel(where_ref, *refs):
    arrays, (rows_ref, onehot_ref, slot_weight_ref), held, sems = refs[:4], refs[4:7], refs[7:11], refs[11]
    copies = [pltpu.make_async_copy(source, to, sems.at[k]) for k, (source, to) in enumerate(zip(arrays, held))]
    for copy in copies:
        copy.start()
    tokens_ref, routes_ref, weight_ref, gain_ref = held
    count = tokens_ref.shape[0]
    upper = lax.broadcasted_iota(jnp.int32, (count, count), 0) <= lax.broadcasted_iota(jnp.int32, (count, count), 1)
    slot = lax.broadcasted_iota(jnp.int32, (SLOTS, count), 0)
    copies[1].wait()
    copies[2].wait()
    onehots = []
    for sibling in range(2):
        hits = routes_ref[...] == where_ref[0] ^ sibling
        chosen = jnp.max(hits.astype(F32), axis=0, keepdims=True)
        wide = jnp.broadcast_to(chosen, (SLOTS, count))
        place = jnp.dot(wide.astype(BF16), upper.astype(BF16), preferred_element_type=F32) - 1.0
        named = (place.astype(jnp.int32) == slot) & (wide > 0.0)
        onehots.append(jnp.where(named, 1.0, 0.0).astype(BF16))
        if sibling == 0:
            weights = jnp.sum(jnp.where(hits, weight_ref[...], 0.0), axis=0, keepdims=True)
            slot_weight = jnp.sum(jnp.where(named, weights, 0.0), axis=1, keepdims=True)
    onehot_ref[...] = jnp.concatenate(onehots, axis=0)
    slot_weight_ref[...] = jnp.broadcast_to(slot_weight, slot_weight_ref.shape)
    copies[0].wait()
    copies[3].wait()
    picked = jnp.dot(onehots[0], tokens_ref[...], preferred_element_type=F32)
    mean_sq = jnp.mean(picked * picked, axis=1, keepdims=True)
    rows_ref[...] = (picked * lax.rsqrt(mean_sq + EPSILON) * gain_ref[...]).astype(BF16)


def pick(where, tokens, routes, route_weight, gain):
    count, width = tokens.shape
    smem, vmem = pl.BlockSpec(memory_space=pltpu.SMEM), pl.BlockSpec(memory_space=pltpu.VMEM)
    arrays = (tokens, routes.T, route_weight.T, gain.reshape(1, width))
    return pl.pallas_call(
        pick_kernel,
        out_shape=(shape((SLOTS, width), BF16), shape((2 * SLOTS, count), BF16), shape((SLOTS, 128), F32)),
        in_specs=[smem] + [pl.BlockSpec(memory_space=pltpu.HBM)] * 4,
        out_specs=(vmem, vmem, vmem),
        scratch_shapes=[pltpu.VMEM(array.shape, array.dtype) for array in arrays] + [pltpu.SemaphoreType.DMA((4,))],
        compiler_params=params(60),
        name="pick",
    )(where, *arrays)


def expert_kernel(top_ref, bottom_ref, gate_ref, up_ref, down_ref, out_top_ref, out_bottom_ref):
    half = top_ref.shape[0]
    rows = jnp.concatenate([top_ref[...], bottom_ref[...]], axis=0)
    by_row = (((1,), (1,)), ((), ()))
    gate = lax.dot_general(rows, gate_ref[...], by_row, preferred_element_type=F32)
    upper = lax.dot_general(rows, up_ref[...], by_row, preferred_element_type=F32)
    hidden = (gate / (1.0 + jnp.exp(-gate)) * upper).astype(BF16)
    out = jnp.dot(hidden, down_ref[...], preferred_element_type=F32).astype(BF16)
    out_top_ref[...] = out[:half]
    out_bottom_ref[...] = out[half:]


def expert(top, bottom, weights):
    vmem = pl.BlockSpec(memory_space=pltpu.VMEM)
    rows, width = top.shape
    units = weights[0].shape[0]
    return pl.pallas_call(
        expert_kernel,
        out_shape=(shape(top.shape, BF16),) * 2,
        in_specs=[vmem] * 5,
        out_specs=(vmem, vmem),
        compiler_params=params(28),
        cost_estimate=pl.CostEstimate(
            flops=12 * rows * width * units, bytes_accessed=6 * units * width + 8 * rows * width, transcendentals=0
        ),
        name="expert",
    )(top, bottom, *weights)


def relay_kernel(after_ref, down_ref, before_ref, up_ref, to_after_ref, to_before_ref):
    to_after_ref[...] = (after_ref[...].astype(F32) + down_ref[...].astype(F32)).astype(BF16)
    to_before_ref[...] = (before_ref[...].astype(F32) + up_ref[...].astype(F32)).astype(BF16)


def relay(*arrays):
    vmem = pl.BlockSpec(memory_space=pltpu.VMEM)
    return pl.pallas_call(
        relay_kernel,
        out_shape=(shape(arrays[0].shape, BF16),) * 2,
        in_specs=[vmem] * 4,
        out_specs=(vmem, vmem),
        compiler_params=params(),
        cost_estimate=SMALL,
        name="relay",
    )(*arrays)


def total_kernel(near_top, top_a, top_b, near_bottom, bottom_a, bottom_b, *outs):
    for c in range(2):
        own, down, up, across = outs[4 * c : 4 * c + 4]
        for e in range(8):
            lanes, at = slice(e * 512 + c * 256, e * 512 + c * 256 + 256), slice(e * 256, e * 256 + 256)
            for near, a, b, first, second in (
                (near_top, top_a, top_b, own, down), (near_bottom, bottom_a, bottom_b, up, across)
            ):
                total = near[:, lanes].astype(F32) + a[:, lanes].astype(F32) + b[:, lanes].astype(F32)
                first[:, at] = total[:SLOTS].astype(BF16)
                second[:, at] = total[SLOTS:].astype(BF16)


def total(*arrays):
    vmem = pl.BlockSpec(memory_space=pltpu.VMEM)
    return pl.pallas_call(
        total_kernel,
        out_shape=(shape((SLOTS, arrays[0].shape[1] // 2), BF16),) * 8,
        in_specs=[vmem] * 6,
        out_specs=(vmem,) * 8,
        compiler_params=params(),
        cost_estimate=SMALL,
        name="total",
    )(*arrays)


def plus(a, b):
    return (a.astype(F32) + b.astype(F32)).astype(BF16)


def after(values, *earlier):
    return lax.optimization_barrier((values, earlier))[0]


def experts(rows, weights):
    last, following = along_first(rows, 1), along_first(rows, -1)
    across_top = along_first(last[: SLOTS // 2], 1)
    across_bottom = along_first(following[SLOTS // 2 :], -1)
    near_top = jnp.concatenate([rows, last], axis=0)
    near_bottom = jnp.concatenate([following, across_top, across_bottom], axis=0)
    near_top = after(near_top, across_top, across_bottom)
    before_top = along_second(near_top, 1)
    after_bottom = along_second(near_bottom, -1)
    out_near_top, out_near_bottom = expert(near_top, near_bottom, weights)
    before_top, after_bottom = after((before_top, after_bottom), out_near_top)
    far_top = along_second(before_top, 1)
    far_bottom = along_second(after_bottom, -1)
    out_before_top, out_after_bottom = expert(before_top, after_bottom, weights)
    later_top, later_bottom = after((near_top, near_bottom), out_before_top)
    after_top = along_second(later_top, -1)
    before_bottom = along_second(later_bottom, 1)
    out_far_top, out_far_bottom = expert(*after((far_top, far_bottom), out_before_top), weights)
    relay_down = along_second(out_far_top, 1)
    relay_up = along_second(out_far_bottom, -1)
    first_back = after((out_before_top, out_after_bottom), out_far_top)
    top_a = along_second(first_back[0], -1)
    bottom_a = along_second(first_back[1], 1)
    second = after((after_top, before_bottom), relay_down, relay_up)
    out_after_top, out_before_bottom = expert(*second, weights)
    to_after, to_before = relay(out_after_top, relay_down, out_before_bottom, relay_up)
    top_b = along_second(to_after, 1)
    bottom_b = along_second(to_before, -1)
    sums = total(out_near_top, top_a, top_b, out_near_bottom, bottom_a, bottom_b)
    terms = []
    for c in range(2):
        own, down, up, across = sums[4 * c : 4 * c + 4]
        terms.append((own, along_first(down, -1), along_first(up, 1), along_first(across, 2)))
    return terms


def weigh_kernel(where_ref, a_ref, b_ref, c_ref, d_ref, weight_ref, keep_ref, give_ref):
    rows = (a_ref[...].astype(F32) + b_ref[...].astype(F32)) + (c_ref[...].astype(F32) + d_ref[...].astype(F32))
    weighted = (rows * weight_ref[:, :1]).astype(BF16)
    _, mine, _, _ = place_of(where_ref)
    for core in range(2):

        @pl.when(mine == core)
        def _():
            for k in range(SIDE):
                to = slice(k * 256, (k + 1) * 256)
                for out, e in ((keep_ref, 2 * k + core), (give_ref, 2 * k + 1 - core)):
                    out[:, to] = weighted[:, e * 256 : (e + 1) * 256]


def weigh(where, terms, slot_weight):
    vmem = pl.BlockSpec(memory_space=pltpu.VMEM)
    return pl.pallas_call(
        weigh_kernel,
        out_shape=(shape((SLOTS, SIDE * 256), BF16),) * 2,
        in_specs=[pl.BlockSpec(memory_space=pltpu.SMEM)] + [vmem] * 5,
        out_specs=(vmem, vmem),
        compiler_params=params(),
        cost_estimate=SMALL,
        name="weigh",
    )(where, *terms, slot_weight)


def place_kernel(where_ref, keep_ref, got_ref, onehot_ref, own_ref, next_ref, last_ref, across_ref, scr):
    rows = jnp.concatenate([keep_ref[...], got_ref[...]], axis=0)
    placed = lax.dot_general(onehot_ref[...], rows, (((0,), (0,)), ((), ())), preferred_element_type=F32)
    for k in range(SIDE):
        scr[k] = placed[:, k * 256 : (k + 1) * 256]
    y, _, _, _ = place_of(where_ref)
    for by, out in ((0, own_ref), (1, next_ref), (3, last_ref), (2, across_ref)):
        out[...] = scr[(y + by) & 3].astype(out.dtype)


def place(where, keep, got, onehot):
    count = onehot.shape[1]
    vmem = pl.BlockSpec(memory_space=pltpu.VMEM)
    return pl.pallas_call(
        place_kernel,
        out_shape=(shape((count, 256), F32),) + (shape((count, 256), BF16),) * 3,
        in_specs=[pl.BlockSpec(memory_space=pltpu.SMEM)] + [vmem] * 3,
        out_specs=(vmem,) * 4,
        scratch_shapes=[pltpu.VMEM((SIDE, count, 256), F32)],
        compiler_params=params(),
        cost_estimate=SMALL,
        name="place",
    )(where, keep, got, onehot)


def residual_kernel(where_ref, tokens_ref, own_ref, a_ref, b_ref, c_ref, mixed_ref):
    summed = (own_ref[...] + a_ref[...].astype(F32)) + (b_ref[...].astype(F32) + c_ref[...].astype(F32))
    mixed_ref[...] = (tokens_ref[...].astype(F32) + summed).astype(BF16)


def residual(c, where, tokens, own, others):
    count, cols = own.shape
    whole = pl.BlockSpec((count, cols), lambda i, where: (0, 0))
    return pl.pallas_call(
        residual_kernel,
        out_shape=shape((count, cols), BF16),
        grid_spec=pltpu.PrefetchScalarGridSpec(
            num_scalar_prefetch=1,
            grid=(1,),
            in_specs=[pl.BlockSpec((count, cols), lambda i, where: (0, 2 * where[0] + c))] + [whole] * 4,
            out_specs=whole,
        ),
        compiler_params=params(),
        cost_estimate=SMALL,
        name="residual",
    )(where, tokens, own, *others)


def spread(per_head, lanes):
    heads = per_head.shape[1]
    pairs = []
    first = lax.broadcasted_iota(jnp.int32, (per_head.shape[0], 2 * HEAD_DIM), 1) < HEAD_DIM
    for k in range(heads // 2):
        pairs.append(jnp.where(first, per_head[:, 2 * k : 2 * k + 1], per_head[:, 2 * k + 1 : 2 * k + 2]))
    return jnp.concatenate(pairs, axis=1)


def project_kernel(c, where_ref, mine_ref, other_ref, gain_ref, in_w_ref, write_w_ref, read_w_ref, step_w_ref, *refs):
    y, core, _, _ = place_of(where_ref)
    squares, scaled, step_w = 0.0, [], []
    for e in range(8):
        away = (e // 2 + SIDE - y) & 3
        slot = jnp.where(away == 0, 0, jnp.where(away == 3, 1, away + 1))
        values = jnp.where(core == e % 2, mine_ref[slot], other_ref[slot]).astype(F32)
        squares += jnp.sum(values * values, axis=1, keepdims=True)
        scaled.append((values * gain_ref[e, c]).astype(BF16))
        step_w.append(step_w_ref[:, e * 512 + c * 256 : e * 512 + c * 256 + 256])
    scaled = jnp.concatenate(scaled, axis=1)

    def rows(ref):
        return ref[:, c].reshape(scaled.shape[1], ref.shape[3])

    write_read = jnp.concatenate([rows(write_w_ref), rows(read_w_ref)], axis=1)
    accs = [
        jnp.dot(scaled, rows(in_w_ref), preferred_element_type=F32),
        jnp.dot(scaled, write_read, preferred_element_type=F32),
        lax.dot_general(
            scaled, jnp.concatenate(step_w, axis=1), (((1,), (1,)), ((), ())), preferred_element_type=F32
        ),
        jnp.broadcast_to(squares, (squares.shape[0], 128)),
    ]
    if c == 0:
        for out, acc in zip(refs, accs):
            out[...] = acc
    else:
        before, (bias_ref, decay_ref) = refs[:4], refs[4:6]
        accs = [acc + ref[...] for acc, ref in zip(accs, before)]
        projected(where_ref, bias_ref, decay_ref, refs[6:15], accs, refs[15], 8 * 512)


def projected(where_ref, bias_ref, decay_ref, outs, accs, state_scr, width):
    in_acc, write_read, step_acc, square_acc = accs
    x_ref, write_ref, read_ref, step_ref, cum_ref = outs[:5]
    count, heads = step_acc.shape
    scale = lax.rsqrt(square_acc[:, :1] / width + EPSILON)
    x = (in_acc * scale).astype(BF16)
    x_ref[...] = x
    write = (write_read[:, :STATE] * scale).astype(BF16)
    write_ref[...] = write
    read_ref[...] = (write_read[:, STATE:] * scale).astype(BF16)
    raw = step_acc * scale + bias_ref[...]
    step = jnp.maximum(raw, 0.0) + jnp.log1p(jnp.exp(-jnp.abs(raw)))
    step_ref[...] = step
    log_decay = -step * jnp.exp(decay_ref[...])
    lower = lax.broadcasted_iota(jnp.int32, (count, count), 0) >= lax.broadcasted_iota(jnp.int32, (count, count), 1)
    cum = jnp.dot(lower.astype(F32), log_decay, preferred_element_type=F32, precision=PRECISE)
    cum_ref[...] = cum
    last = cum[count - 1 :, :]
    to_end = jnp.exp(last - cum) * step
    weighted = (x.astype(F32) * spread(to_end, x.shape[1])).astype(BF16)
    state = lax.dot_general(write, weighted, (((0,), (0,)), ((), ())), preferred_element_type=F32)
    whole = spread(last, x.shape[1])
    high = whole.astype(BF16).astype(F32)
    row = lax.broadcasted_iota(jnp.int32, (16, x.shape[1]), 0)
    log_rows = jnp.where(row == 0, high, jnp.where(row == 1, whole - high, 0.0)).astype(BF16)
    cols = x.shape[1] // SIDE
    for q in range(SIDE):
        lanes = slice(q * cols, (q + 1) * cols)
        state_scr[q, :STATE, :] = state[:, lanes].astype(BF16)
        state_scr[q, STATE:, :] = log_rows[:, lanes]
    _, _, _, at = place_of(where_ref)
    for by, out in zip((0, 1, 3, 2), outs[5:]):
        out[...] = state_scr[(at + by) & 3]


def project(c, where, mine, other, gain, weights, *more):
    _, count, cols = mine.shape
    lanes, heads = weights[0].shape[1], weights[3].shape[1]
    smem, vmem = pl.BlockSpec(memory_space=pltpu.SMEM), pl.BlockSpec(memory_space=pltpu.VMEM)
    cut = [w.reshape(8, 2, cols, w.shape[1]) for w in weights[:3]]
    if c == 0:
        outs = tuple(shape((count, n), F32) for n in (lanes, 2 * STATE, heads, 128))
        scratch = []
    else:
        quarter = (STATE + 16, lanes // SIDE)
        outs = (
            shape((count, lanes), BF16), shape((count, STATE), BF16), shape((count, STATE), BF16),
            shape((count, heads), F32), shape((count, heads), F32),
        ) + (shape(quarter, BF16),) * 4
        scratch = [pltpu.VMEM((SIDE,) + quarter, BF16)]
    return pl.pallas_call(
        functools.partial(project_kernel, c),
        out_shape=outs,
        in_specs=[smem] + [vmem] * (7 + len(more)),
        out_specs=(vmem,) * len(outs),
        scratch_shapes=scratch,
        compiler_params=params(),
        cost_estimate=SMALL,
        name="project",
    )(where, mine, other, gain.reshape(8, 2, 1, cols), *cut, weights[3].T, *more)


def inside_kernel(x_ref, write_ref, read_ref, step_ref, cum_ref, skip_ref, out_ref, decayed_ref):
    count, heads = step_ref.shape
    span = count // 2
    scores = lax.dot_general(read_ref[...], write_ref[...], (((1,), (1,)), ((), ())), preferred_element_type=F32)
    cum = cum_ref[...]
    decayed_ref[...] = spread(jnp.exp(cum), x_ref.shape[1])
    cum_t, step_t = cum.T, step_ref[...].T
    causal = lax.broadcasted_iota(jnp.int32, (span, span), 0) >= lax.broadcasted_iota(jnp.int32, (span, span), 1)
    low, high = slice(0, span), slice(span, count)

    def mixing(h, rows, columns):
        gaps = cum[rows, h : h + 1] - cum_t[h : h + 1, columns]
        if rows == columns:
            gaps = jnp.where(causal, gaps, -jnp.inf)
        return (scores[rows, columns] * jnp.exp(gaps) * step_t[h : h + 1, columns]).astype(BF16)

    for h in range(heads):
        lanes = slice(h * HEAD_DIM, (h + 1) * HEAD_DIM)
        x = x_ref[:, lanes]
        skipped = skip_ref[0, h] * x.astype(F32)
        top = jnp.dot(mixing(h, low, low), x[low], preferred_element_type=F32)
        below = jnp.concatenate([mixing(h, high, low), mixing(h, high, high)], axis=1)
        bottom = jnp.dot(below, x, preferred_element_type=F32)
        out_ref[:, lanes] = jnp.concatenate([top, bottom], axis=0) + skipped


def inside(x, write, read, step, cum, skip_gain):
    vmem = pl.BlockSpec(memory_space=pltpu.VMEM)
    return pl.pallas_call(
        inside_kernel,
        out_shape=(shape(x.shape, F32),) * 2,
        in_specs=[vmem] * 5 + [pl.BlockSpec(memory_space=pltpu.SMEM)],
        out_specs=(vmem, vmem),
        compiler_params=params(),
        cost_estimate=pl.CostEstimate(flops=2 * 10**9, bytes_accessed=2 * 10**6, transcendentals=10**6),
        name="inside",
    )(x, write, read, step, cum, skip_gain.reshape(1, -1))


def log_of(ref):
    return ref[STATE : STATE + 1, :].astype(F32) + ref[STATE + 1 : STATE + 2, :].astype(F32)


def weights_before(here, places, logs):
    terms = []
    for s in places:
        between = sum(jnp.where((s < u) & (u < here), log, 0.0) for u, log in zip(places, logs))
        terms.append(jnp.where(s < here, jnp.exp(between), 0.0))
    return terms


def row_total_kernel(where_ref, own_ref, last_ref, next_ref, across_ref, total_ref):
    _, _, _, here = place_of(where_ref)
    refs = (own_ref, last_ref, next_ref, across_ref)
    places = [here, (here + 3) & 3, (here + 1) & 3, (here + 2) & 3]
    logs = [log_of(ref) for ref in refs]
    until_end = [jnp.exp(sum(jnp.where(s < u, log, 0.0) for u, log in zip(places, logs))) for s in places]
    total_ref[:STATE, :] = sum(w * ref[:STATE, :].astype(F32) for w, ref in zip(until_end, refs)).astype(BF16)
    whole = sum(logs)
    top = whole.astype(BF16).astype(F32)
    row = lax.broadcasted_iota(jnp.int32, (16, whole.shape[1]), 0)
    total_ref[STATE:, :] = jnp.where(row == 0, top, jnp.where(row == 1, whole - top, 0.0)).astype(BF16)


def row_total(where, parts):
    vmem = pl.BlockSpec(memory_space=pltpu.VMEM)
    return pl.pallas_call(
        row_total_kernel,
        out_shape=shape(parts[0].shape, BF16),
        in_specs=[pl.BlockSpec(memory_space=pltpu.SMEM)] + [vmem] * 4,
        out_specs=vmem,
        compiler_params=params(),
        cost_estimate=SMALL,
        name="row_total",
    )(where, *parts)


def carry_kernel(where_ref, *refs):
    parts, earlier, outs = refs[:4], refs[4:7], refs[7:]
    _, _, z, here = place_of(where_ref)
    rows = [(z + 3) & 3, (z + 1) & 3, (z + 2) & 3]
    before = weights_before(z, rows, [log_of(ref) for ref in earlier])
    to_row = sum(w * ref[:STATE, :].astype(F32) for w, ref in zip(before, earlier))
    places = [here, (here + 3) & 3, (here + 1) & 3, (here + 2) & 3]
    logs = [log_of(ref) for ref in parts]
    for by, out in zip((0, 1, 3, 2), outs):
        target = (here + by) & 3
        gone = sum(jnp.where(s < target, log, 0.0) for s, log in zip(places, logs))
        state = jnp.exp(gone) * to_row
        for w, ref in zip(weights_before(target, places, logs), parts):
            state += w * ref[:STATE, :].astype(F32)
        out[...] = state.astype(BF16)


def carry(where, parts, earlier):
    vmem = pl.BlockSpec(memory_space=pltpu.VMEM)
    return pl.pallas_call(
        carry_kernel,
        out_shape=(shape((STATE, parts[0].shape[1]), BF16),) * 4,
        in_specs=[pl.BlockSpec(memory_space=pltpu.SMEM)] + [vmem] * 7,
        out_specs=(vmem,) * 4,
        compiler_params=params(),
        cost_estimate=SMALL,
        name="carry",
    )(where, *parts, *earlier)


def finish_kernel(where_ref, own_ref, last_ref, next_ref, across_ref, read_ref, decayed_ref, inside_ref, out_ref, scr):
    _, _, _, here = place_of(where_ref)
    for by, ref in ((0, own_ref), (3, last_ref), (1, next_ref), (2, across_ref)):
        scr[(here + by) & 3] = ref[...]
    cols = own_ref.shape[1]
    for q in range(SIDE):
        lanes = slice(q * cols, (q + 1) * cols)
        from_prior = jnp.dot(read_ref[...], scr[q], preferred_element_type=F32)
        out_ref[:, lanes] = (inside_ref[:, lanes] + decayed_ref[:, lanes] * from_prior).astype(BF16)


def finish(where, parts, read, decayed, within):
    vmem = pl.BlockSpec(memory_space=pltpu.VMEM)
    return pl.pallas_call(
        finish_kernel,
        out_shape=shape(within.shape, BF16),
        in_specs=[pl.BlockSpec(memory_space=pltpu.SMEM)] + [vmem] * 7,
        out_specs=vmem,
        scratch_shapes=[pltpu.VMEM((SIDE,) + parts[0].shape, BF16)],
        compiler_params=params(),
        cost_estimate=SMALL,
        name="finish",
    )(where, *parts, read, decayed, within)


def body(
    tokens,
    routes,
    route_weight,
    moe_gain,
    gate_weight,
    up_weight,
    down_weight,
    ssd_gain,
    input_weight,
    write_weight,
    read_weight,
    step_weight,
    step_bias,
    decay_log,
    skip_gain,
):
    where = jnp.stack([lax.axis_index("expert"), lax.axis_index("frame")]).astype(jnp.int32)
    rows, onehot, slot_weight = pick(where, tokens, routes, route_weight, moe_gain)
    halves = experts(rows, (gate_weight[0], up_weight[0], down_weight[0]))
    weights = (input_weight, write_weight, read_weight, step_weight)
    sums, mixed, more, order = [], [], (), ()
    for c in range(2):
        keep, give = weigh(where, after(halves[c], *order), slot_weight)
        own, to_next, to_last, to_across = place(where, keep, to_sibling(give), onehot)
        order = (own,)
        sums.append((own, (along_y(to_next, 1), along_y(to_last, -1), along_y(to_across, 2))))
    for c, (own, others) in enumerate(sums):
        half = residual(c, where, tokens, own, others)
        mixed.append(half)
        mine = jnp.stack([half, along_y(half, 1), along_y(half, -1), along_y(half, 2)])
        if c == 1:
            more = (*more, step_bias.reshape(1, -1), decay_log.reshape(1, -1))
        more = project(c, where, mine, to_sibling(mine), ssd_gain, weights, *more)
    inputs, write, read, step, cum, state, to_next, to_last, to_across = more
    parts = (state, along_x(to_next, 1), along_x(to_last, -1), along_x(to_across, 2))
    row = row_total(where, parts)
    earlier = (along_z(row, 1), along_z(row, -1), along_z(row, 2))
    within, decayed = inside(inputs, write, read, step, cum, skip_gain)
    parts = (after(state, within), *parts[1:])
    prior, to_next, to_last, to_across = carry(where, parts, earlier)
    carried = (prior, along_x(to_next, 1), along_x(to_last, -1), along_x(to_across, 2))
    ssd_out = finish(where, carried, read, decayed, within)
    return (jnp.concatenate(mixed, axis=1), ssd_out)


def solution(mesh):
    placed = (
        P("frame", None),
        P("frame", None),
        P("frame", None),
        P(),
        P("expert", "frame", None),
        P("expert", "frame", None),
        P("expert", "frame", None),
        P(),
        P(None, "expert"),
        P(None, "expert"),
        P(None, "expert"),
        P(None, "expert"),
        P("expert"),
        P("expert"),
        P("expert"),
    )
    return jax.shard_map(
        body,
        mesh=mesh,
        in_specs=placed,
        out_specs=(P("frame", "expert"), P("frame", "expert")),
        check_vma=False,
    )
```

```python
import functools

import jax
import jax.numpy as jnp
from jax import lax
from jax.experimental import pallas as pl
from jax.experimental.pallas import tpu as pltpu
from jax.sharding import PartitionSpec as P

HEAD_DIM = 64
STATE = 128
SLOTS = 96
SIDE = 4
EPSILON = 1e-06
PRECISE = lax.Precision.HIGHEST
AXES = ("expert", "frame")
F32, BF16 = jnp.float32, jnp.bfloat16


def routes_of(rule):
    pairs = []
    for y in range(SIDE):
        for core in range(2):
            for z in range(SIDE):
                for x in range(SIDE):
                    ny, nc, nz, nx = rule(y, core, z, x)
                    source = (y * 2 + core) * 16 + z * SIDE + x
                    target = ((ny % SIDE) * 2 + nc % 2) * 16 + (nz % SIDE) * SIDE + nx % SIDE
                    pairs.append((source, target))
    return pairs


def send(array, rule):
    return lax.ppermute(array, AXES, routes_of(rule))


def along_first(array, by):
    return send(array, lambda y, c, z, x: (y, c, z + by * c, x + by * (1 - c)))


def along_second(array, by):
    return send(array, lambda y, c, z, x: (y, c, z + by * (1 - c), x + by * c))


def along_x(array, by):
    return send(array, lambda y, c, z, x: (y, c, z, x + by))


def along_z(array, by):
    return send(array, lambda y, c, z, x: (y, c, z + by, x))


def along_y(array, by):
    return send(array, lambda y, c, z, x: (y + by, c, z, x))


def to_sibling(array):
    return send(array, lambda y, c, z, x: (y, 1 - c, z, x))


def shape(dims, kind):
    return jax.ShapeDtypeStruct(dims, kind)


def params(mebibytes=20):
    return pltpu.CompilerParams(vmem_limit_bytes=mebibytes * 1024 * 1024)


SMALL = pl.CostEstimate(flops=10**6, bytes_accessed=10**5, transcendentals=0)


def place_of(where_ref):
    return where_ref[0] >> 1, where_ref[0] & 1, where_ref[1] >> 2, where_ref[1] & 3


def pick_kernel(where_ref, *refs):
    arrays, (rows_ref, onehot_ref, slot_weight_ref), held, sems = refs[:4], refs[4:7], refs[7:11], refs[11]
    copies = [pltpu.make_async_copy(source, to, sems.at[k]) for k, (source, to) in enumerate(zip(arrays, held))]
    for copy in copies:
        copy.start()
    tokens_ref, routes_ref, weight_ref, gain_ref = held
    count = tokens_ref.shape[0]
    upper = lax.broadcasted_iota(jnp.int32, (count, count), 0) <= lax.broadcasted_iota(jnp.int32, (count, count), 1)
    slot = lax.broadcasted_iota(jnp.int32, (SLOTS, count), 0)
    copies[1].wait()
    copies[2].wait()
    onehots = []
    for sibling in range(2):
        hits = routes_ref[...] == where_ref[0] ^ sibling
        chosen = jnp.max(hits.astype(F32), axis=0, keepdims=True)
        wide = jnp.broadcast_to(chosen, (SLOTS, count))
        place = jnp.dot(wide.astype(BF16), upper.astype(BF16), preferred_element_type=F32) - 1.0
        named = (place.astype(jnp.int32) == slot) & (wide > 0.0)
        onehots.append(jnp.where(named, 1.0, 0.0).astype(BF16))
        if sibling == 0:
            weights = jnp.sum(jnp.where(hits, weight_ref[...], 0.0), axis=0, keepdims=True)
            slot_weight = jnp.sum(jnp.where(named, weights, 0.0), axis=1, keepdims=True)
    onehot_ref[...] = jnp.concatenate(onehots, axis=0)
    slot_weight_ref[...] = jnp.broadcast_to(slot_weight, slot_weight_ref.shape)
    copies[0].wait()
    copies[3].wait()
    picked = jnp.dot(onehots[0], tokens_ref[...], preferred_element_type=F32)
    mean_sq = jnp.mean(picked * picked, axis=1, keepdims=True)
    rows_ref[...] = (picked * lax.rsqrt(mean_sq + EPSILON) * gain_ref[...]).astype(BF16)


def pick(where, tokens, routes, route_weight, gain):
    count, width = tokens.shape
    smem, vmem = pl.BlockSpec(memory_space=pltpu.SMEM), pl.BlockSpec(memory_space=pltpu.VMEM)
    arrays = (tokens, routes.T, route_weight.T, gain.reshape(1, width))
    return pl.pallas_call(
        pick_kernel,
        out_shape=(shape((SLOTS, width), BF16), shape((2 * SLOTS, count), BF16), shape((SLOTS, 128), F32)),
        in_specs=[smem] + [pl.BlockSpec(memory_space=pltpu.HBM)] * 4,
        out_specs=(vmem, vmem, vmem),
        scratch_shapes=[pltpu.VMEM(array.shape, array.dtype) for array in arrays] + [pltpu.SemaphoreType.DMA((4,))],
        compiler_params=params(60),
        name="pick",
    )(where, *arrays)


def expert_kernel(top_ref, bottom_ref, gate_ref, up_ref, down_ref, out_top_ref, out_bottom_ref):
    half = top_ref.shape[0]
    rows = jnp.concatenate([top_ref[...], bottom_ref[...]], axis=0)
    by_row = (((1,), (1,)), ((), ()))
    gate = lax.dot_general(rows, gate_ref[...], by_row, preferred_element_type=F32)
    upper = lax.dot_general(rows, up_ref[...], by_row, preferred_element_type=F32)
    hidden = (gate / (1.0 + jnp.exp(-gate)) * upper).astype(BF16)
    out = jnp.dot(hidden, down_ref[...], preferred_element_type=F32).astype(BF16)
    out_top_ref[...] = out[:half]
    out_bottom_ref[...] = out[half:]


def expert(top, bottom, weights):
    vmem = pl.BlockSpec(memory_space=pltpu.VMEM)
    rows, width = top.shape
    units = weights[0].shape[0]
    return pl.pallas_call(
        expert_kernel,
        out_shape=(shape(top.shape, BF16),) * 2,
        in_specs=[vmem] * 5,
        out_specs=(vmem, vmem),
        compiler_params=params(28),
        cost_estimate=pl.CostEstimate(
            flops=12 * rows * width * units, bytes_accessed=6 * units * width + 8 * rows * width, transcendentals=0
        ),
        name="expert",
    )(top, bottom, *weights)


def relay_kernel(after_ref, down_ref, before_ref, up_ref, to_after_ref, to_before_ref):
    to_after_ref[...] = (after_ref[...].astype(F32) + down_ref[...].astype(F32)).astype(BF16)
    to_before_ref[...] = (before_ref[...].astype(F32) + up_ref[...].astype(F32)).astype(BF16)


def relay(*arrays):
    vmem = pl.BlockSpec(memory_space=pltpu.VMEM)
    return pl.pallas_call(
        relay_kernel,
        out_shape=(shape(arrays[0].shape, BF16),) * 2,
        in_specs=[vmem] * 4,
        out_specs=(vmem, vmem),
        compiler_params=params(),
        cost_estimate=SMALL,
        name="relay",
    )(*arrays)


def total_kernel(c, near_top, top_a, top_b, near_bottom, bottom_a, bottom_b, own, down, up, across):
    for e in range(8):
        lanes, at = slice(e * 512 + c * 256, e * 512 + c * 256 + 256), slice(e * 256, e * 256 + 256)
        for near, a, b, first, second in (
            (near_top, top_a, top_b, own, down), (near_bottom, bottom_a, bottom_b, up, across)
        ):
            total = near[:, lanes].astype(F32) + a[:, lanes].astype(F32) + b[:, lanes].astype(F32)
            first[:, at] = total[:SLOTS].astype(BF16)
            second[:, at] = total[SLOTS:].astype(BF16)


def total(c, *arrays):
    vmem = pl.BlockSpec(memory_space=pltpu.VMEM)
    return pl.pallas_call(
        functools.partial(total_kernel, c),
        out_shape=(shape((SLOTS, arrays[0].shape[1] // 2), BF16),) * 4,
        in_specs=[vmem] * 6,
        out_specs=(vmem,) * 4,
        compiler_params=params(),
        cost_estimate=SMALL,
        name="total",
    )(*arrays)


def after(values, *earlier):
    return lax.optimization_barrier((values, earlier))[0]


def experts(rows, weights):
    last, following = along_first(rows, 1), along_first(rows, -1)
    across_top = along_first(last[: SLOTS // 2], 1)
    across_bottom = along_first(following[SLOTS // 2 :], -1)
    near_top = jnp.concatenate([rows, last], axis=0)
    near_bottom = jnp.concatenate([following, across_top, across_bottom], axis=0)
    near_top = after(near_top, across_top, across_bottom)
    before_top = along_second(near_top, 1)
    after_bottom = along_second(near_bottom, -1)
    out_near_top, out_near_bottom = expert(near_top, near_bottom, weights)
    before_top, after_bottom = after((before_top, after_bottom), out_near_top)
    far_top = along_second(before_top, 1)
    far_bottom = along_second(after_bottom, -1)
    out_before_top, out_after_bottom = expert(before_top, after_bottom, weights)
    later_top, later_bottom = after((near_top, near_bottom), out_before_top)
    after_top = along_second(later_top, -1)
    before_bottom = along_second(later_bottom, 1)
    out_far_top, out_far_bottom = expert(*after((far_top, far_bottom), out_before_top), weights)
    relay_down = along_second(out_far_top, 1)
    relay_up = along_second(out_far_bottom, -1)
    first_back = after((out_before_top, out_after_bottom), out_far_top)
    top_a = along_second(first_back[0], -1)
    bottom_a = along_second(first_back[1], 1)
    second = after((after_top, before_bottom), relay_down, relay_up)
    out_after_top, out_before_bottom = expert(*second, weights)
    to_after, to_before = relay(out_after_top, relay_down, out_before_bottom, relay_up)
    top_b = along_second(to_after, 1)
    bottom_b = along_second(to_before, -1)
    sums, terms, order = (out_near_top, top_a, top_b, out_near_bottom, bottom_a, bottom_b), [], ()
    for c in range(2):
        own, down, up, across = total(c, *after(sums, *order))
        order = (own,)
        terms.append((own, along_first(down, -1), along_first(up, 1), along_first(across, 2)))
    return terms


def weigh_kernel(where_ref, a_ref, b_ref, c_ref, d_ref, weight_ref, keep_ref, give_ref):
    rows = (a_ref[...].astype(F32) + b_ref[...].astype(F32)) + (c_ref[...].astype(F32) + d_ref[...].astype(F32))
    weighted = (rows * weight_ref[:, :1]).astype(BF16)
    _, mine, _, _ = place_of(where_ref)
    for core in range(2):

        @pl.when(mine == core)
        def _():
            for k in range(SIDE):
                to = slice(k * 256, (k + 1) * 256)
                for out, e in ((keep_ref, 2 * k + core), (give_ref, 2 * k + 1 - core)):
                    out[:, to] = weighted[:, e * 256 : (e + 1) * 256]


def weigh(where, terms, slot_weight):
    vmem = pl.BlockSpec(memory_space=pltpu.VMEM)
    return pl.pallas_call(
        weigh_kernel,
        out_shape=(shape((SLOTS, SIDE * 256), BF16),) * 2,
        in_specs=[pl.BlockSpec(memory_space=pltpu.SMEM)] + [vmem] * 5,
        out_specs=(vmem, vmem),
        compiler_params=params(),
        cost_estimate=SMALL,
        name="weigh",
    )(where, *terms, slot_weight)


def place_kernel(where_ref, keep_ref, got_ref, onehot_ref, own_ref, next_ref, last_ref, across_ref, scr):
    rows = jnp.concatenate([keep_ref[...], got_ref[...]], axis=0)
    placed = lax.dot_general(onehot_ref[...], rows, (((0,), (0,)), ((), ())), preferred_element_type=F32)
    for k in range(SIDE):
        scr[k] = placed[:, k * 256 : (k + 1) * 256]
    y, _, _, _ = place_of(where_ref)
    for by, out in ((0, own_ref), (1, next_ref), (3, last_ref), (2, across_ref)):
        out[...] = scr[(y + by) & 3].astype(out.dtype)


def place(where, keep, got, onehot):
    count = onehot.shape[1]
    vmem = pl.BlockSpec(memory_space=pltpu.VMEM)
    return pl.pallas_call(
        place_kernel,
        out_shape=(shape((count, 256), F32),) + (shape((count, 256), BF16),) * 3,
        in_specs=[pl.BlockSpec(memory_space=pltpu.SMEM)] + [vmem] * 3,
        out_specs=(vmem,) * 4,
        scratch_shapes=[pltpu.VMEM((SIDE, count, 256), F32)],
        compiler_params=params(),
        cost_estimate=SMALL,
        name="place",
    )(where, keep, got, onehot)


def residual_kernel(where_ref, tokens_ref, own_ref, a_ref, b_ref, c_ref, mixed_ref):
    summed = (own_ref[...] + a_ref[...].astype(F32)) + (b_ref[...].astype(F32) + c_ref[...].astype(F32))
    mixed_ref[...] = (tokens_ref[...].astype(F32) + summed).astype(BF16)


def residual(c, where, tokens, own, others):
    count, cols = own.shape
    whole = pl.BlockSpec((count, cols), lambda i, where: (0, 0))
    return pl.pallas_call(
        residual_kernel,
        out_shape=shape((count, cols), BF16),
        grid_spec=pltpu.PrefetchScalarGridSpec(
            num_scalar_prefetch=1,
            grid=(1,),
            in_specs=[pl.BlockSpec((count, cols), lambda i, where: (0, 2 * where[0] + c))] + [whole] * 4,
            out_specs=whole,
        ),
        compiler_params=params(),
        cost_estimate=SMALL,
        name="residual",
    )(where, tokens, own, *others)


def spread(per_head, lanes):
    heads = per_head.shape[1]
    pairs = []
    first = lax.broadcasted_iota(jnp.int32, (per_head.shape[0], 2 * HEAD_DIM), 1) < HEAD_DIM
    for k in range(heads // 2):
        pairs.append(jnp.where(first, per_head[:, 2 * k : 2 * k + 1], per_head[:, 2 * k + 1 : 2 * k + 2]))
    return jnp.concatenate(pairs, axis=1)


def project_kernel(c, where_ref, mine_ref, other_ref, gain_ref, in_w_ref, write_w_ref, read_w_ref, step_w_ref, *refs):
    y, core, _, _ = place_of(where_ref)
    squares, scaled, step_w = 0.0, [], []
    for e in range(8):
        away = (e // 2 + SIDE - y) & 3
        slot = jnp.where(away == 0, 0, jnp.where(away == 3, 1, away + 1))
        values = jnp.where(core == e % 2, mine_ref[slot], other_ref[slot]).astype(F32)
        squares += jnp.sum(values * values, axis=1, keepdims=True)
        scaled.append((values * gain_ref[e, c]).astype(BF16))
        step_w.append(step_w_ref[:, e * 512 + c * 256 : e * 512 + c * 256 + 256])
    scaled = jnp.concatenate(scaled, axis=1)

    def rows(ref):
        return ref[:, c].reshape(scaled.shape[1], ref.shape[3])

    write_read = jnp.concatenate([rows(write_w_ref), rows(read_w_ref)], axis=1)
    accs = [
        jnp.dot(scaled, rows(in_w_ref), preferred_element_type=F32),
        jnp.dot(scaled, write_read, preferred_element_type=F32),
        lax.dot_general(
            scaled, jnp.concatenate(step_w, axis=1), (((1,), (1,)), ((), ())), preferred_element_type=F32
        ),
        jnp.broadcast_to(squares, (squares.shape[0], 128)),
    ]
    if c == 0:
        for out, acc in zip(refs, accs):
            out[...] = acc
    else:
        before, (bias_ref, decay_ref) = refs[:4], refs[4:6]
        accs = [acc + ref[...] for acc, ref in zip(accs, before)]
        projected(where_ref, bias_ref, decay_ref, refs[6:15], accs, refs[15], 8 * 512)


def projected(where_ref, bias_ref, decay_ref, outs, accs, state_scr, width):
    in_acc, write_read, step_acc, square_acc = accs
    x_ref, write_ref, read_ref, step_ref, cum_ref = outs[:5]
    count, heads = step_acc.shape
    scale = lax.rsqrt(square_acc[:, :1] / width + EPSILON)
    x = (in_acc * scale).astype(BF16)
    x_ref[...] = x
    write = (write_read[:, :STATE] * scale).astype(BF16)
    write_ref[...] = write
    read_ref[...] = (write_read[:, STATE:] * scale).astype(BF16)
    raw = step_acc * scale + bias_ref[...]
    step = jnp.maximum(raw, 0.0) + jnp.log1p(jnp.exp(-jnp.abs(raw)))
    step_ref[...] = step
    log_decay = -step * jnp.exp(decay_ref[...])
    lower = lax.broadcasted_iota(jnp.int32, (count, count), 0) >= lax.broadcasted_iota(jnp.int32, (count, count), 1)
    cum = jnp.dot(lower.astype(F32), log_decay, preferred_element_type=F32, precision=PRECISE)
    cum_ref[...] = cum
    last = cum[count - 1 :, :]
    to_end = jnp.exp(last - cum) * step
    weighted = (x.astype(F32) * spread(to_end, x.shape[1])).astype(BF16)
    state = lax.dot_general(write, weighted, (((0,), (0,)), ((), ())), preferred_element_type=F32)
    whole = spread(last, x.shape[1])
    high = whole.astype(BF16).astype(F32)
    row = lax.broadcasted_iota(jnp.int32, (16, x.shape[1]), 0)
    log_rows = jnp.where(row == 0, high, jnp.where(row == 1, whole - high, 0.0)).astype(BF16)
    cols = x.shape[1] // SIDE
    for q in range(SIDE):
        lanes = slice(q * cols, (q + 1) * cols)
        state_scr[q, :STATE, :] = state[:, lanes].astype(BF16)
        state_scr[q, STATE:, :] = log_rows[:, lanes]
    _, _, _, at = place_of(where_ref)
    for by, out in zip((0, 1, 3, 2), outs[5:]):
        out[...] = state_scr[(at + by) & 3]


def project(c, where, mine, other, gain, weights, *more):
    _, count, cols = mine.shape
    lanes, heads = weights[0].shape[1], weights[3].shape[1]
    smem, vmem = pl.BlockSpec(memory_space=pltpu.SMEM), pl.BlockSpec(memory_space=pltpu.VMEM)
    cut = [w.reshape(8, 2, cols, w.shape[1]) for w in weights[:3]]
    if c == 0:
        outs = tuple(shape((count, n), F32) for n in (lanes, 2 * STATE, heads, 128))
        scratch = []
    else:
        quarter = (STATE + 16, lanes // SIDE)
        outs = (
            shape((count, lanes), BF16), shape((count, STATE), BF16), shape((count, STATE), BF16),
            shape((count, heads), F32), shape((count, heads), F32),
        ) + (shape(quarter, BF16),) * 4
        scratch = [pltpu.VMEM((SIDE,) + quarter, BF16)]
    return pl.pallas_call(
        functools.partial(project_kernel, c),
        out_shape=outs,
        in_specs=[smem] + [vmem] * (7 + len(more)),
        out_specs=(vmem,) * len(outs),
        scratch_shapes=scratch,
        compiler_params=params(),
        cost_estimate=SMALL,
        name="project",
    )(where, mine, other, gain.reshape(8, 2, 1, cols), *cut, weights[3].T, *more)


def inside_kernel(x_ref, write_ref, read_ref, step_ref, cum_ref, skip_ref, out_ref, decayed_ref):
    count, heads = step_ref.shape
    span = count // 2
    scores = lax.dot_general(read_ref[...], write_ref[...], (((1,), (1,)), ((), ())), preferred_element_type=F32)
    cum = cum_ref[...]
    decayed_ref[...] = spread(jnp.exp(cum), x_ref.shape[1])
    cum_t, step_t = cum.T, step_ref[...].T
    causal = lax.broadcasted_iota(jnp.int32, (span, span), 0) >= lax.broadcasted_iota(jnp.int32, (span, span), 1)
    low, high = slice(0, span), slice(span, count)

    def mixing(h, rows, columns):
        gaps = cum[rows, h : h + 1] - cum_t[h : h + 1, columns]
        if rows == columns:
            gaps = jnp.where(causal, gaps, -jnp.inf)
        return (scores[rows, columns] * jnp.exp(gaps) * step_t[h : h + 1, columns]).astype(BF16)

    for h in range(heads):
        lanes = slice(h * HEAD_DIM, (h + 1) * HEAD_DIM)
        x = x_ref[:, lanes]
        skipped = skip_ref[0, h] * x.astype(F32)
        top = jnp.dot(mixing(h, low, low), x[low], preferred_element_type=F32)
        below = jnp.concatenate([mixing(h, high, low), mixing(h, high, high)], axis=1)
        bottom = jnp.dot(below, x, preferred_element_type=F32)
        out_ref[:, lanes] = jnp.concatenate([top, bottom], axis=0) + skipped


def inside(x, write, read, step, cum, skip_gain):
    vmem = pl.BlockSpec(memory_space=pltpu.VMEM)
    return pl.pallas_call(
        inside_kernel,
        out_shape=(shape(x.shape, F32),) * 2,
        in_specs=[vmem] * 5 + [pl.BlockSpec(memory_space=pltpu.SMEM)],
        out_specs=(vmem, vmem),
        compiler_params=params(),
        cost_estimate=pl.CostEstimate(flops=2 * 10**9, bytes_accessed=2 * 10**6, transcendentals=10**6),
        name="inside",
    )(x, write, read, step, cum, skip_gain.reshape(1, -1))


def log_of(ref):
    return ref[STATE : STATE + 1, :].astype(F32) + ref[STATE + 1 : STATE + 2, :].astype(F32)


def weights_before(here, places, logs):
    terms = []
    for s in places:
        between = sum(jnp.where((s < u) & (u < here), log, 0.0) for u, log in zip(places, logs))
        terms.append(jnp.where(s < here, jnp.exp(between), 0.0))
    return terms


def row_total_kernel(where_ref, own_ref, last_ref, next_ref, across_ref, total_ref):
    _, _, _, here = place_of(where_ref)
    refs = (own_ref, last_ref, next_ref, across_ref)
    places = [here, (here + 3) & 3, (here + 1) & 3, (here + 2) & 3]
    logs = [log_of(ref) for ref in refs]
    until_end = [jnp.exp(sum(jnp.where(s < u, log, 0.0) for u, log in zip(places, logs))) for s in places]
    total_ref[:STATE, :] = sum(w * ref[:STATE, :].astype(F32) for w, ref in zip(until_end, refs)).astype(BF16)
    whole = sum(logs)
    top = whole.astype(BF16).astype(F32)
    row = lax.broadcasted_iota(jnp.int32, (16, whole.shape[1]), 0)
    total_ref[STATE:, :] = jnp.where(row == 0, top, jnp.where(row == 1, whole - top, 0.0)).astype(BF16)


def row_total(where, parts):
    vmem = pl.BlockSpec(memory_space=pltpu.VMEM)
    return pl.pallas_call(
        row_total_kernel,
        out_shape=shape(parts[0].shape, BF16),
        in_specs=[pl.BlockSpec(memory_space=pltpu.SMEM)] + [vmem] * 4,
        out_specs=vmem,
        compiler_params=params(),
        cost_estimate=SMALL,
        name="row_total",
    )(where, *parts)


def carry_kernel(where_ref, *refs):
    parts, earlier, outs = refs[:4], refs[4:7], refs[7:]
    _, _, z, here = place_of(where_ref)
    rows = [(z + 3) & 3, (z + 1) & 3, (z + 2) & 3]
    before = weights_before(z, rows, [log_of(ref) for ref in earlier])
    to_row = sum(w * ref[:STATE, :].astype(F32) for w, ref in zip(before, earlier))
    places = [here, (here + 3) & 3, (here + 1) & 3, (here + 2) & 3]
    logs = [log_of(ref) for ref in parts]
    for by, out in zip((0, 1, 3, 2), outs):
        target = (here + by) & 3
        gone = sum(jnp.where(s < target, log, 0.0) for s, log in zip(places, logs))
        state = jnp.exp(gone) * to_row
        for w, ref in zip(weights_before(target, places, logs), parts):
            state += w * ref[:STATE, :].astype(F32)
        out[...] = state.astype(BF16)


def carry(where, parts, earlier):
    vmem = pl.BlockSpec(memory_space=pltpu.VMEM)
    return pl.pallas_call(
        carry_kernel,
        out_shape=(shape((STATE, parts[0].shape[1]), BF16),) * 4,
        in_specs=[pl.BlockSpec(memory_space=pltpu.SMEM)] + [vmem] * 7,
        out_specs=(vmem,) * 4,
        compiler_params=params(),
        cost_estimate=SMALL,
        name="carry",
    )(where, *parts, *earlier)


def finish_kernel(where_ref, own_ref, last_ref, next_ref, across_ref, read_ref, decayed_ref, inside_ref, out_ref, scr):
    _, _, _, here = place_of(where_ref)
    for by, ref in ((0, own_ref), (3, last_ref), (1, next_ref), (2, across_ref)):
        scr[(here + by) & 3] = ref[...]
    cols = own_ref.shape[1]
    for q in range(SIDE):
        lanes = slice(q * cols, (q + 1) * cols)
        from_prior = jnp.dot(read_ref[...], scr[q], preferred_element_type=F32)
        out_ref[:, lanes] = (inside_ref[:, lanes] + decayed_ref[:, lanes] * from_prior).astype(BF16)


def finish(where, parts, read, decayed, within):
    vmem = pl.BlockSpec(memory_space=pltpu.VMEM)
    return pl.pallas_call(
        finish_kernel,
        out_shape=shape(within.shape, BF16),
        in_specs=[pl.BlockSpec(memory_space=pltpu.SMEM)] + [vmem] * 7,
        out_specs=vmem,
        scratch_shapes=[pltpu.VMEM((SIDE,) + parts[0].shape, BF16)],
        compiler_params=params(),
        cost_estimate=SMALL,
        name="finish",
    )(where, *parts, read, decayed, within)


def body(
    tokens,
    routes,
    route_weight,
    moe_gain,
    gate_weight,
    up_weight,
    down_weight,
    ssd_gain,
    input_weight,
    write_weight,
    read_weight,
    step_weight,
    step_bias,
    decay_log,
    skip_gain,
):
    where = jnp.stack([lax.axis_index("expert"), lax.axis_index("frame")]).astype(jnp.int32)
    rows, onehot, slot_weight = pick(where, tokens, routes, route_weight, moe_gain)
    halves = experts(rows, (gate_weight[0], up_weight[0], down_weight[0]))
    weights = (input_weight, write_weight, read_weight, step_weight)
    sums, mixed, more, order = [], [], (), ()
    for c in range(2):
        keep, give = weigh(where, after(halves[c], *order), slot_weight)
        own, to_next, to_last, to_across = place(where, keep, to_sibling(give), onehot)
        order = (own,)
        sums.append((own, (along_y(to_next, 1), along_y(to_last, -1), along_y(to_across, 2))))
    for c, (own, others) in enumerate(sums):
        half = residual(c, where, tokens, own, others)
        mixed.append(half)
        mine = jnp.stack([half, along_y(half, 1), along_y(half, -1), along_y(half, 2)])
        if c == 1:
            more = (*more, step_bias.reshape(1, -1), decay_log.reshape(1, -1))
        more = project(c, where, mine, to_sibling(mine), ssd_gain, weights, *more)
    inputs, write, read, step, cum, state, to_next, to_last, to_across = more
    parts = (state, along_x(to_next, 1), along_x(to_last, -1), along_x(to_across, 2))
    row = row_total(where, parts)
    earlier = (along_z(row, 1), along_z(row, -1), along_z(row, 2))
    within, decayed = inside(inputs, write, read, step, cum, skip_gain)
    parts = (after(state, within), *parts[1:])
    prior, to_next, to_last, to_across = carry(where, parts, earlier)
    carried = (prior, along_x(to_next, 1), along_x(to_last, -1), along_x(to_across, 2))
    ssd_out = finish(where, carried, read, decayed, within)
    return (jnp.concatenate(mixed, axis=1), ssd_out)


def solution(mesh):
    placed = (
        P("frame", None),
        P("frame", None),
        P("frame", None),
        P(),
        P("expert", "frame", None),
        P("expert", "frame", None),
        P("expert", "frame", None),
        P(),
        P(None, "expert"),
        P(None, "expert"),
        P(None, "expert"),
        P(None, "expert"),
        P("expert"),
        P("expert"),
        P("expert"),
    )
    return jax.shard_map(
        body,
        mesh=mesh,
        in_specs=placed,
        out_specs=(P("frame", "expert"), P("frame", "expert")),
        check_vma=False,
    )
```
